32 devices in a mesh: fsdp: 8 (over z, y), context: 2 (over x), tensor: 2 (over core).
Axes of the slice: x: 2, y: 2, z: 4, core: 2. Of those that a mesh axis runs over, the one named last changes fastest.
Arguments:
- tokens: bfloat16 [2, 8, 1024, 2048], P(None, 'fsdp', 'context'), may hold values from -6 to 6
- lengths: int32 [2, 8, 2], P(None, 'fsdp'), may hold values from 128 to 896, as said below
- block_order: int32 [2, 8, 8], P(None, 'fsdp'), may hold values from 0 to 7, each once within a row
- cotangent: bfloat16 [2, 8, 1024, 2048], P(None, 'fsdp', 'context'), may hold values from -6 to 6
- norm_gain: float32 [2048], replicated, may hold values from 0.1 to 1.9
- in_weight: bfloat16 [2048, 2, 4096], P('fsdp', None, 'tensor'), may hold values from -0.125 to 0.125
- coupling_weight: bfloat16 [2048, 256], P('fsdp'), may hold values from -0.125 to 0.125
- step_weight: bfloat16 [2048, 64], P('fsdp', 'tensor'), may hold values from -0.125 to 0.125
- out_weight: bfloat16 [4096, 2048], P('tensor', 'fsdp'), may hold values from -0.09375 to 0.09375
- conv_weight: float32 [4, 4096], P(None, 'tensor'), may hold values from -3 to 3
- conv_bias: float32 [4096], P('tensor'), may hold values from -3 to 3
- coupling_conv: float32 [4, 256], replicated, may hold values from -3 to 3
- coupling_bias: float32 [256], replicated, may hold values from -3 to 3
- step_bias: float32 [64], P('tensor'), may hold values from -1 to 1
- decay_rate: float32 [64], P('tensor'), may hold values from 0.00012207031 to 0.041666667
- skip_gain: float32 [64], P('tensor'), may hold values from 0.5 to 1.5
- inner_gain: float32 [4096], P('tensor'), may hold values from 0.1 to 1.9
Outputs:
- block_out: bfloat16 [2, 8, 1024, 2048], P(None, 'fsdp', 'context')
- input_grad: bfloat16 [2, 8, 1024, 2048], P(None, 'fsdp', 'context')
- norm_gain_grad: float32 [2048], replicated
- in_weight_grad: float32 [2048, 2, 4096], P('fsdp', None, 'tensor')
- coupling_weight_grad: float32 [2048, 256], P('fsdp')
- step_weight_grad: float32 [2048, 64], P('fsdp', 'tensor')
- out_weight_grad: float32 [4096, 2048], P('tensor', 'fsdp')
- conv_weight_grad: float32 [4, 4096], P(None, 'tensor')
- conv_bias_grad: float32 [4096], P('tensor')
- coupling_conv_grad: float32 [4, 256], replicated
- coupling_bias_grad: float32 [256], replicated
- step_bias_grad: float32 [64], P('tensor')
- decay_rate_grad: float32 [64], P('tensor')
- skip_gain_grad: float32 [64], P('tensor')
- inner_gain_grad: float32 [4096], P('tensor')
The draws below stay inside these ranges and needn't reach their ends.
Inputs may be any that keep to these rules, and one draw needn't show every extreme that they name: Each row of 1024 positions holds two packed sequences of these lengths, in this order, then padding; the longer one covers all but fewer than half of 512 positions of the row. `block_order`: each row's entries are a permutation of its 8 blocks.
All inputs are finite; a program needn't handle non-finite values.
Results may differ from the reference program's by a relative error of at most 0.00225.
The reference program's roundings to bfloat16 on the way count: a program that leaves them out, or rounds other values in their place, can miss the bound.
Values may be sent and summed in bfloat16 or wider, within the bound.
A program may use at most 768 MiB of HBM per device.

```python
import jax
import jax.numpy as jnp
from jax import lax

D = 2048
HEADS = 64
HEADDIM = 64
STATE = 128
WIDTH = 4
SPAN = 256
BLK = 128
SEQ_MIN = 128
MICRO = 2
TOK_DEV = 512
INNER = 4096
ROWS = 8
ROW = 1024
NB = 8


def draw_lengths(key, part):
    key = jax.random.fold_in(key, 11)
    key_short, key_pad, key_side = jax.random.split(key, 3)
    short_len = jax.random.randint(key_short, (MICRO, ROWS), SEQ_MIN, TOK_DEV // 4 + 1)
    pad_len = jax.random.randint(key_pad, (MICRO, ROWS), 0, TOK_DEV // 4)
    long_first = jax.random.randint(key_side, (MICRO, ROWS), 0, 2)
    long_len = ROW - short_len - pad_len
    first_len = jnp.where(long_first == 1, long_len, short_len)
    second_len = jnp.where(long_first == 1, short_len, long_len)
    return jnp.stack([first_len, second_len], axis=-1).astype(jnp.int32)


def draw_decay_rate(key, part):
    key = jax.random.fold_in(key, 23)
    key_slow, key_fast, key_pick = jax.random.split(key, 3)
    lowest = 1.0 / (8.0 * ROW)
    highest = 1.0 / 24.0
    slow_rate = jnp.exp(jax.random.uniform(key_slow, (HEADS,), jnp.float32, jnp.log(lowest), jnp.log(1.0 / (2.0 * ROW))))
    fast_rate = jnp.exp(jax.random.uniform(key_fast, (HEADS,), jnp.float32, jnp.log(1.0 / 96.0), jnp.log(highest)))
    share_slow = 0.5
    chosen = jax.random.uniform(key_pick, (HEADS,), jnp.float32) < share_slow
    return jnp.clip(jnp.where(chosen, slow_rate, fast_rate), lowest, highest).astype(jnp.float32)


def level_of(key, shape, cuts, low, high):
    factor_of, own = 1.0, jax.random.fold_in(key, 6)
    for dim, parts in cuts:
        draws = jnp.exp(jax.random.uniform(jax.random.fold_in(own, dim), (parts,), jnp.float32, low / len(cuts), high / len(cuts)))
        factor_of = factor_of * jnp.repeat(draws, shape[dim] // parts).reshape([-1 if axis == dim else 1 for axis in range(len(shape))])
    return factor_of


def normal_values(own_key, extent, scale, bound, cuts=(), kind=jnp.bfloat16):
    factor_of = level_of(own_key, extent, cuts, -0.22, 0.18) if cuts else 1.0
    values = jax.random.normal(own_key, extent, jnp.float32) * scale * factor_of
    return jnp.minimum(jnp.maximum(values, -bound), bound).astype(kind)


def setup_inputs(seed: int = 0) -> dict:
    key_list = jax.random.split(jax.random.key(seed), 18)
    tokens = normal_values(key_list[0], (MICRO, ROWS, ROW, D), 1.0, 6.0, ((1, 8), (2, 2)))
    lengths = draw_lengths(jax.random.fold_in(key_list[17], 71), 0)
    block_order = jax.vmap(lambda own: jax.random.permutation(own, NB))(jax.random.split(key_list[2], MICRO * ROWS)).reshape((MICRO, ROWS, NB)).astype(jnp.int32)
    cotangent = normal_values(key_list[3], (MICRO, ROWS, ROW, D), 1.0, 6.0, ((1, 8), (2, 2)))
    norm_gain = jnp.clip(1.0 + 0.18 * jax.random.normal(key_list[4], (D,), jnp.float32), 0.1, 1.9)
    in_weight = normal_values(key_list[5], (D, 2, INNER), D ** -0.5, 0.125, ((0, 8), (2, 2)))
    coupling_weight = normal_values(key_list[6], (D, 2 * STATE), D ** -0.5, 0.125, ((0, 8),))
    step_weight = normal_values(key_list[7], (D, HEADS), D ** -0.5, 0.125, ((0, 8), (1, 2)))
    out_weight = normal_values(key_list[8], (INNER, D), INNER ** -0.5, 0.09375, ((0, 2), (1, 8)))
    conv_weight = normal_values(key_list[9], (WIDTH, INNER), 0.5, 3.0, ((1, 2),), jnp.float32)
    conv_bias = normal_values(key_list[10], (INNER,), 0.5, 3.0, ((0, 2),), jnp.float32)
    coupling_conv = normal_values(key_list[11], (WIDTH, 2 * STATE), 0.5, 3.0, (), jnp.float32)
    coupling_bias = normal_values(key_list[12], (2 * STATE,), 0.5, 3.0, (), jnp.float32)
    step_bias = jnp.clip(jax.random.uniform(key_list[13], (HEADS,), jnp.float32, -1.0, 1.0) * level_of(key_list[13], (HEADS,), ((0, 2),), -0.4, 0.0), -1.0, 1.0)
    decay_rate = draw_decay_rate(jax.random.fold_in(key_list[17], 71), 0)
    skip_gain = jnp.clip(0.5 + 1.0 * jax.random.uniform(key_list[15], (HEADS,), jnp.float32) ** level_of(key_list[15], (HEADS,), ((0, 2),), -0.2, 0.2), 0.5, 1.5)
    inner_gain = jnp.clip(1.0 + 0.18 * jax.random.normal(key_list[16], (INNER,), jnp.float32), 0.1, 1.9)
    return dict(tokens=tokens, lengths=lengths, block_order=block_order, cotangent=cotangent, norm_gain=norm_gain, in_weight=in_weight, coupling_weight=coupling_weight, step_weight=step_weight, out_weight=out_weight, conv_weight=conv_weight, conv_bias=conv_bias, coupling_conv=coupling_conv, coupling_bias=coupling_bias, step_bias=step_bias, decay_rate=decay_rate, skip_gain=skip_gain, inner_gain=inner_gain)


epsilon = 1e-05

@jax.custom_vjp
def low(v):
    return lax.optimization_barrier(v.astype(jnp.bfloat16)).astype(jnp.float32)

@jax.custom_vjp
def low_back(v):
    return v

def low_keep(v):
    return (low(v), None)

def low_pass(kept, grad):
    return (grad,)

def back_keep(v):
    return (v, None)

def back_low(kept, grad):
    return (low(grad),)
low.defvjp(low_keep, low_pass)
low_back.defvjp(back_keep, back_low)

def segment_of(position, seq_lens):
    first_part = (position >= seq_lens[0]).astype(jnp.int32)
    second_part = (position >= seq_lens[0] + seq_lens[1]).astype(jnp.int32)
    return jnp.where(position < 0, -1, first_part + second_part).astype(jnp.int32)

def conv_apply(padded, weights, biases, same_masks):
    width_conv = weights.shape[0]
    rim_rows = width_conv - 1
    length_rows = padded.shape[0] - rim_rows
    summed = biases
    for lag_index in range(width_conv):
        start_row = rim_rows - lag_index
        summed = summed + weights[lag_index] * padded[start_row:start_row + length_rows] * same_masks[lag_index][:, None]
    return jax.nn.silu(summed)

def span_step(state_now, span_parts):
    value_part, input_part, output_part, step_part, log_part, segment_part, segment_prior = span_parts
    highest = lax.Precision.HIGHEST
    cumulative = jnp.cumsum(log_part, axis=0)
    places = jnp.arange(segment_part.shape[0])
    joined = (segment_part[:, None] == segment_part[None, :]) & (places[:, None] >= places[None, :])
    spread = jnp.where(joined[:, :, None], cumulative[:, None, :] - cumulative[None, :, :], 0.0)
    decays = jnp.where(joined[:, :, None], jnp.exp(spread), 0.0)
    gram_mat = jnp.dot(output_part, input_part.T, precision=highest)
    inside = jnp.einsum('ijh,jhp->ihp', gram_mat[:, :, None] * decays, step_part[:, :, None] * value_part, precision=highest)
    carried_in = jnp.exp(cumulative) * (segment_part == segment_prior)[:, None]
    from_state = carried_in[:, :, None] * jnp.einsum('in,hpn->ihp', output_part, state_now, precision=highest)
    tail_decay = jnp.exp(cumulative[-1][None, :] - cumulative) * (segment_part == segment_part[-1])[:, None]
    fresh_state = jnp.einsum('jh,jhp,jn->hpn', tail_decay * step_part, value_part, input_part, precision=highest)
    through = jnp.exp(cumulative[-1]) * (segment_part[-1] == segment_prior)
    return (through[:, None, None] * state_now + fresh_state, inside + from_state)

def mixer_row(parameters, x_row, seg_ids):
    norm_gain, in_weight, coupling_weight, step_weight, out_weight, conv_weight, conv_bias, coupling_conv, coupling_bias, step_bias, decay_rate, skip_gain, inner_gain = parameters
    highest = lax.Precision.HIGHEST
    inv_rms = lax.rsqrt(lax.optimization_barrier(jnp.mean(x_row * x_row, axis=-1, keepdims=True)) + epsilon)
    normed = low(x_row * inv_rms * norm_gain)
    both_proj = low_back(jnp.dot(normed, in_weight.reshape(D, 2 * INNER), precision=highest))
    gate_in = both_proj[:, :INNER]
    value_raw = both_proj[:, INNER:]
    coupling_raw = low_back(jnp.dot(normed, coupling_weight, precision=highest))
    step_raw = low_back(jnp.dot(normed, step_weight, precision=highest))
    rim_rows = WIDTH - 1
    seg_pad = jnp.concatenate([jnp.full((rim_rows,), -1, jnp.int32), seg_ids])
    same_masks = jnp.stack([(seg_pad[rim_rows - lag_index:rim_rows - lag_index + ROW] == seg_ids).astype(x_row.dtype) for lag_index in range(WIDTH)])
    value_conv = conv_apply(jnp.concatenate([jnp.zeros((rim_rows, INNER), x_row.dtype), value_raw]), conv_weight, conv_bias, same_masks)
    coupling_out = conv_apply(jnp.concatenate([jnp.zeros((rim_rows, 2 * STATE), x_row.dtype), coupling_raw]), coupling_conv, coupling_bias, same_masks)
    step_size = jax.nn.softplus(step_raw + step_bias)
    log_decay = -step_size * decay_rate
    span_count = ROW // SPAN
    value_heads = value_conv.reshape(ROW, HEADS, HEADDIM)
    segment_prior = jnp.concatenate([jnp.full((1,), -1, jnp.int32), seg_ids.reshape(span_count, SPAN)[:-1, -1]])
    span_parts = (value_heads.reshape(span_count, SPAN, HEADS, HEADDIM), coupling_out[:, :STATE].reshape(span_count, SPAN, STATE), coupling_out[:, STATE:].reshape(span_count, SPAN, STATE), step_size.reshape(span_count, SPAN, HEADS), log_decay.reshape(span_count, SPAN, HEADS), seg_ids.reshape(span_count, SPAN), segment_prior)
    start_state = jnp.zeros((HEADS, HEADDIM, STATE), x_row.dtype)
    _, span_out = lax.scan(jax.checkpoint(span_step), start_state, span_parts)
    mixer_out = span_out.reshape(ROW, HEADS, HEADDIM) + skip_gain[None, :, None] * value_heads
    gated_value = mixer_out.reshape(ROW, INNER) * jax.nn.silu(gate_in)
    gated_norm = low(gated_value * lax.rsqrt(lax.optimization_barrier(jnp.mean(gated_value * gated_value, axis=-1, keepdims=True)) + epsilon) * inner_gain)
    branch_out = jnp.dot(gated_norm, out_weight, precision=highest)
    keep_mask = (seg_ids < 2).astype(x_row.dtype)
    return x_row + keep_mask[:, None] * branch_out

def reference(tokens, lengths, block_order, cotangent, norm_gain, in_weight, coupling_weight, step_weight, out_weight, conv_weight, conv_bias, coupling_conv, coupling_bias, step_bias, decay_rate, skip_gain, inner_gain):
    parameters = tuple((item.astype(jnp.float32) for item in (norm_gain, in_weight, coupling_weight, step_weight, out_weight, conv_weight, conv_bias, coupling_conv, coupling_bias, step_bias, decay_rate, skip_gain, inner_gain)))
    rows_all = MICRO * ROWS
    tok_rows = tokens.reshape(rows_all, NB, BLK, D)
    len_rows = lengths.reshape(rows_all, 2)
    order_rows = block_order.reshape(rows_all, NB)
    cot_rows = cotangent.reshape(rows_all, ROW, D)

    def one_row(totals, row_items):
        tok_row, seq_lens, order_row, cot_row = row_items
        x_row = jnp.zeros((NB, BLK, D), jnp.float32).at[order_row].set(tok_row.astype(jnp.float32)).reshape(ROW, D)
        seg_ids = segment_of(jnp.arange(ROW, dtype=jnp.int32), seq_lens)
        row_out, pullback = jax.vjp(lambda weights, inputs: mixer_row(weights, inputs, seg_ids), parameters, x_row)
        weight_grads, input_grad = pullback(cot_row.astype(jnp.float32))
        totals = jax.tree.map(lambda left, right: left + right, totals, weight_grads)
        return (totals, (row_out.astype(jnp.bfloat16), input_grad.astype(jnp.bfloat16)))
    zero_grads = jax.tree.map(jnp.zeros_like, parameters)
    totals, (outs_rows, grad_rows) = lax.scan(one_row, zero_grads, (tok_rows, len_rows, order_rows, cot_rows))
    shape_out = (MICRO, ROWS, ROW, D)
    return (outs_rows.reshape(shape_out), grad_rows.reshape(shape_out), totals[0], totals[1], totals[2], totals[3], totals[4], totals[5], totals[6], totals[7], totals[8], totals[9], totals[10], totals[11], totals[12])
```

```python
import functools

import jax
import jax.numpy as jnp
import numpy as np
from jax import lax
from jax.experimental import pallas as pl
from jax.experimental.pallas import tpu as pltpu
from jax.sharding import PartitionSpec as P

CHUNK = 128
LANES = 128
f32 = jnp.float32
bf16 = jnp.bfloat16
epsilon = 1e-05


def split_two(value):
    high = value.astype(bf16)
    return high, (value - high.astype(f32)).astype(bf16)


def split_three(value):
    high = value.astype(bf16)
    rest = value - high.astype(f32)
    middle = rest.astype(bf16)
    return high, middle, (rest - middle.astype(f32)).astype(bf16)


def mm(left, right):
    return jnp.dot(left, right, preferred_element_type=f32)


def mm_nt(left, right):
    return lax.dot_general(left, right, (((1,), (1,)), ((), ())), preferred_element_type=f32)


def mm_three(left, right):
    wide = mm(left[0], jnp.concatenate([right[0], right[1]], axis=1))
    count = right[0].shape[1]
    return wide[:, :count] + wide[:, count:] + mm(left[1], right[0])


def mm_three_nt(left, right):
    return mm_nt(left[0], right[0]) + mm_nt(left[0], right[1]) + mm_nt(left[1], right[0])


def packed_parts(value, heads):
    high, middle, lowest = split_three(value)
    joined = (
        high.astype(f32)
        + pltpu.roll(middle.astype(f32), heads, 1)
        + pltpu.roll(lowest.astype(f32), 2 * heads, 1)
    )
    return joined.astype(bf16)


def segment_at(position, first_end, second_end):
    first_part = (position >= first_end).astype(jnp.int32)
    second_part = (position >= second_end).astype(jnp.int32)
    return jnp.where(position < 0, -1, first_part + second_part)


def chunk_frame(marks, chunk, step_raw, step_bias, rate, heads):
    first_end, second_end, base = marks[0], marks[1], marks[2]
    start = base + chunk * CHUNK
    rows = start + lax.broadcasted_iota(jnp.int32, (CHUNK, LANES), 0)
    columns = start + lax.broadcasted_iota(jnp.int32, (CHUNK, CHUNK), 1)
    seg_rows = segment_at(rows, first_end, second_end)
    seg_columns = segment_at(columns, first_end, second_end)
    seg_prior = segment_at(start - 1, first_end, second_end)
    seg_last = segment_at(start + CHUNK - 1, first_end, second_end)
    same = [
        (segment_at(rows - lag, first_end, second_end) == seg_rows).astype(f32) for lag in range(4)
    ]
    shifted = step_raw + step_bias
    step = jnp.maximum(shifted, 0.0) + jnp.log1p(jnp.exp(-jnp.abs(shifted)))
    lanes = lax.broadcasted_iota(jnp.int32, (CHUNK, LANES), 1)
    step = jnp.where(lanes < heads, step, 0.0)
    log_decay = -step * rate
    row_ids = lax.broadcasted_iota(jnp.int32, (CHUNK, CHUNK), 0)
    column_ids = lax.broadcasted_iota(jnp.int32, (CHUNK, CHUNK), 1)
    lower = (row_ids >= column_ids).astype(bf16)
    parts = split_three(log_decay)
    cumulative = mm(lower, parts[0]) + mm(lower, parts[1]) + mm(lower, parts[2])
    last = cumulative[CHUNK - 1 :, :]
    carry = jnp.exp(cumulative) * (seg_rows == seg_prior).astype(f32)
    tail = jnp.exp(last - cumulative) * (seg_rows == seg_last).astype(f32)
    live = lanes < heads
    carry = jnp.where(live, carry, 0.0)
    tail = jnp.where(live, tail, 0.0)
    return dict(
        seg_rows=seg_rows,
        seg_columns=seg_columns,
        row_ids=row_ids,
        column_ids=column_ids,
        same=same,
        step=step,
        shifted=shifted,
        cumulative=cumulative,
        carry=carry,
        tail=tail,
    )


def conv_sum(current, halo, weights, biases, same):
    full = jnp.concatenate([halo, current], axis=0)
    total = biases + weights(0) * current
    for lag in range(1, 4):
        total = total + weights(lag) * (pltpu.roll(full, lag, 0)[8:] * same[lag])
    return total


def logistic(value):
    return 1.0 / (1.0 + jnp.exp(-value))


def forward_kernel(
    heads,
    marks,
    vraw,
    vprev,
    vrim,
    craw,
    cprev,
    crim,
    sraw,
    cw,
    cb,
    ccw,
    ccb,
    sbias,
    rate,
    skip,
    sel,
    selcol,
    y_out,
    st_out,
    fin_out,
    bc_out,
    carry_out,
    cd_out,
    state,
    cumt,
    stack,
    cumpack,
    halo,
    same_s,
    bias_s,
    gram_s,
    cd_s,
    cparts,
    btparts,
):
    chunk = pl.program_id(0)
    chunks = pl.num_programs(0)
    width = state.shape[0]

    @pl.when(chunk == 0)
    def _():
        state[...] = jnp.zeros_like(state)
        cd_s[...] = jnp.ones_like(cd_s)
        cd_out[...] = jnp.zeros_like(cd_out)
        halo[...] = vrim[...]

    @pl.when(chunk > 0)
    def _():
        halo[...] = vprev[...]

    frame = chunk_frame(marks, chunk, sraw[...], sbias[...], rate[...], heads)
    same = frame["same"]
    for lag in range(1, 4):
        same_s[lag - 1] = same[lag]
    joined = (frame["seg_rows"] == frame["seg_columns"]) & (frame["row_ids"] >= frame["column_ids"])
    bias_s[...] = jnp.where(joined, 0.0, -1e30)
    stack[0:CHUNK, :] = packed_parts(frame["step"], heads)
    stack[CHUNK : 2 * CHUNK, :] = packed_parts(frame["carry"], heads)
    stack[2 * CHUNK : 3 * CHUNK, :] = packed_parts(frame["tail"], heads)
    cumpack[...] = packed_parts(frame["cumulative"], heads)
    cumt[...] = jnp.transpose(frame["cumulative"])
    coupling_halo = jnp.where(chunk == 0, crim[...], cprev[...])
    wide_same = [None] + [jnp.concatenate([same[lag], same[lag]], axis=1) for lag in range(1, 4)]
    pre = conv_sum(
        craw[...], coupling_halo, lambda lag: ccw[lag : lag + 1, :], ccb[...], wide_same
    )
    coupled = pre * logistic(pre)
    bc_out[...] = coupled
    b_part = split_two(coupled[:, :width])
    c_part = split_two(coupled[:, width:])
    gram_s[...] = mm_three_nt(c_part, b_part)
    cparts[0] = c_part[0]
    cparts[1] = c_part[1]
    turned = jnp.transpose(coupled[:, :width])
    bt_part = split_two(turned)
    btparts[0] = bt_part[0]
    btparts[1] = bt_part[1]
    lane = lax.broadcasted_iota(jnp.int32, (CHUNK, LANES), 1)
    low_half = (lane < LANES // 2).astype(f32)
    high_half = 1.0 - low_half

    def pair(index, carried):
        cols = pl.ds(pl.multiple_of(index * LANES, LANES), LANES)
        wide = pl.ds(pl.multiple_of(index * 2 * LANES, 2 * LANES), 2 * LANES)
        pre_value = conv_sum(
            vraw[:, cols],
            halo[:, cols],
            lambda lag: cw[lag : lag + 1, cols],
            cb[:, cols],
            [None] + [same_s[lag - 1] for lag in range(1, 4)],
        )
        value = pre_value * logistic(pre_value)
        spread = mm(stack[...], sel[:, cols])
        step_e = spread[:CHUNK]
        carry_e = spread[CHUNK : 2 * CHUNK]
        tail_e = spread[2 * CHUNK :]
        inputs = step_e * value
        column = mm(cumpack[...], selcol[:, wide])
        row_pair = jnp.concatenate(
            [cumt[pl.ds(2 * index, 1), :], cumt[pl.ds(2 * index + 1, 1), :]], axis=1
        )
        bias = bias_s[...]
        gram = gram_s[...]
        mixing = jnp.concatenate([gram, gram], axis=1) * jnp.exp(
            column - row_pair + jnp.concatenate([bias, bias], axis=1)
        )
        mix_high, mix_low = split_two(mixing)
        in_low = split_two(inputs * low_half)
        in_high = split_two(inputs * high_half)
        diag_high = jnp.concatenate([in_low[0], in_high[0]], axis=0)
        diag_low = jnp.concatenate([in_low[1], in_high[1]], axis=0)
        both = mm(mix_high, jnp.concatenate([diag_high, diag_low], axis=1))
        inside = both[:, :LANES] + both[:, LANES:] + mm(mix_low, diag_high)
        held = state[:, cols]
        from_state = mm_three((cparts[0], cparts[1]), split_two(held))
        y_out[:, cols] = inside + carry_e * from_state + skip[:, cols] * value
        fresh = mm_three((btparts[0], btparts[1]), split_two(tail_e * inputs))
        through = carry_e[CHUNK - 1 :, :]
        st_out[0, :, cols] = held
        renewed = through * held + fresh
        state[:, cols] = renewed
        fin_out[:, cols] = renewed
        reach = cd_s[0:1, cols]
        carry_out[:, cols] = carry_e * reach
        cd_s[0:1, cols] = reach * through
        return carried

    eight_rows = lax.broadcasted_iota(jnp.int32, cd_out.shape, 0)
    cd_out[...] = jnp.where(eight_rows == chunk, cd_s[0:1, :], cd_out[...])
    lax.fori_loop(0, heads // 2, pair, 0, unroll=4)
    cd_out[...] = jnp.where(eight_rows == chunk + 1, cd_s[0:1, :], cd_out[...])


def selectors(heads, head_size):
    inner = heads * head_size
    head_of_lane = np.arange(inner) // head_size
    narrow = np.zeros((LANES, inner), np.float32)
    wide = np.zeros((LANES, heads * LANES), np.float32)
    head_of_wide = np.arange(heads * LANES) // LANES
    for part in range(3):
        narrow[part * heads + head_of_lane, np.arange(inner)] = 1.0
        wide[part * heads + head_of_wide, np.arange(heads * LANES)] = 1.0
    return narrow, wide


def whole(shape):
    return pl.BlockSpec(shape, lambda index, *_: (0,) * len(shape))


def forward_ssd(
    marks, micro, raw, rim, inner, twice, tokens, cw, cb, ccw, ccb, sbias, rate, skip, sel, selcol
):
    width = twice // 2
    chunks = tokens // CHUNK
    heads = inner // (LANES // 2)
    eighth = CHUNK // 8
    initial = micro * chunks

    def rows(count):
        return pl.BlockSpec((CHUNK, count), lambda chunk, *_: (chunk, 0))

    def part(count, start):
        return pl.BlockSpec((CHUNK, count), lambda chunk, *_: (initial + chunk, start // count))

    def before(count, start):
        return pl.BlockSpec(
            (8, count),
            lambda chunk, *_: (jnp.maximum((initial + chunk) * eighth - 1, 0), start // count),
        )

    def edge(count, start):
        return pl.BlockSpec((8, count), lambda *_: (0, start // count))

    return pl.pallas_call(
        functools.partial(forward_kernel, heads),
        grid_spec=pltpu.PrefetchScalarGridSpec(
            num_scalar_prefetch=1,
            grid=(chunks,),
            in_specs=[
                part(inner, 0),
                before(inner, 0),
                edge(inner, 0),
                part(twice, inner),
                before(twice, inner),
                edge(twice, inner),
                part(LANES, inner + twice),
                whole(cw.shape),
                whole(cb.shape),
                whole(ccw.shape),
                whole(ccb.shape),
                whole(sbias.shape),
                whole(rate.shape),
                whole(skip.shape),
                whole(sel.shape),
                whole(selcol.shape),
            ],
            out_specs=[
                rows(inner),
                pl.BlockSpec((1, width, inner), lambda chunk, *_: (chunk, 0, 0)),
                whole((width, inner)),
                rows(twice),
                rows(inner),
                whole((8, inner)),
            ],
            scratch_shapes=[
                pltpu.VMEM((width, inner), f32),
                pltpu.VMEM((LANES, CHUNK), f32),
                pltpu.VMEM((3 * CHUNK, LANES), bf16),
                pltpu.VMEM((CHUNK, LANES), bf16),
                pltpu.VMEM((8, inner), f32),
                pltpu.VMEM((3, CHUNK, LANES), f32),
                pltpu.VMEM((CHUNK, CHUNK), f32),
                pltpu.VMEM((CHUNK, CHUNK), f32),
                pltpu.VMEM((8, inner), f32),
                pltpu.VMEM((2, CHUNK, width), bf16),
                pltpu.VMEM((2, width, CHUNK), bf16),
            ],
        ),
        out_shape=[
            jax.ShapeDtypeStruct((tokens, inner), f32),
            jax.ShapeDtypeStruct((chunks, width, inner), f32),
            jax.ShapeDtypeStruct((width, inner), f32),
            jax.ShapeDtypeStruct((tokens, twice), f32),
            jax.ShapeDtypeStruct((tokens, inner), f32),
            jax.ShapeDtypeStruct((8, inner), f32),
        ],
        compiler_params=pltpu.CompilerParams(vmem_limit_bytes=40 * 1024 * 1024),
        cost_estimate=pl.CostEstimate(
            flops=20 * tokens * inner * 128 * 2, bytes_accessed=24 * tokens * inner, transcendentals=0
        ),
    )(marks, raw, raw, rim, raw, raw, rim, raw, cw, cb, ccw, ccb, sbias, rate, skip, sel, selcol)


def backward_kernel(
    heads,
    marks,
    vraw,
    vprev,
    vrim,
    craw,
    cprev,
    crim,
    sraw,
    grad,
    mixer,
    st_now,
    st_next,
    fin,
    entering,
    cd,
    pulled,
    cw,
    cb,
    ccw,
    ccb,
    sbias,
    rate,
    skip,
    sel,
    selcol,
    selt,
    vraw_g,
    vrim_g,
    craw_g,
    crim_g,
    sraw_g,
    cw_g,
    ccw_g,
    small_g,
    skip_g,
    state,
    cumt,
    stack,
    cumpack,
    halo,
    same_s,
    bias_s,
    gram_s,
    cparts,
    bparts,
    ctparts,
    rim_s,
    crim_s,
    dgram,
    dcoup,
    dhead,
    cd_s,
):
    step_id = pl.program_id(0)
    chunks = pl.num_programs(0)
    chunk = chunks - 1 - step_id
    width = state.shape[0]

    @pl.when(step_id == 0)
    def _():
        state[...] = pulled[...]
        rim_s[...] = jnp.zeros_like(rim_s)
        crim_s[...] = jnp.zeros_like(crim_s)
        cw_g[...] = jnp.zeros_like(cw_g)
        ccw_g[...] = jnp.zeros_like(ccw_g)
        small_g[...] = jnp.zeros_like(small_g)
        skip_g[...] = jnp.zeros_like(skip_g)

    @pl.when(chunk == 0)
    def _():
        halo[...] = vrim[...]

    @pl.when(chunk > 0)
    def _():
        halo[...] = vprev[...]

    frame = chunk_frame(marks, chunk, sraw[...], sbias[...], rate[...], heads)
    same = frame["same"]
    for lag in range(1, 4):
        same_s[lag - 1] = same[lag]
    joined = (frame["seg_rows"] == frame["seg_columns"]) & (frame["row_ids"] <= frame["column_ids"])
    bias_s[...] = jnp.where(joined, 0.0, -1e30)
    stack[0:CHUNK, :] = packed_parts(frame["step"], heads)
    stack[CHUNK : 2 * CHUNK, :] = packed_parts(frame["carry"], heads)
    stack[2 * CHUNK : 3 * CHUNK, :] = packed_parts(frame["tail"], heads)
    cumpack[...] = packed_parts(frame["cumulative"], heads)
    cumt[...] = jnp.transpose(frame["cumulative"])
    coupling_halo = jnp.where(chunk == 0, crim[...], cprev[...])
    wide_same = [None] + [jnp.concatenate([same[lag], same[lag]], axis=1) for lag in range(1, 4)]
    craw_now = craw[...]
    pre = conv_sum(craw_now, coupling_halo, lambda lag: ccw[lag : lag + 1, :], ccb[...], wide_same)
    csig = logistic(pre)
    coupled = pre * csig
    b_value = coupled[:, :width]
    c_value = coupled[:, width:]
    b_part = split_two(b_value)
    c_part = split_two(c_value)
    gram_s[...] = mm_three_nt(b_part, c_part)
    cparts[0] = c_part[0]
    cparts[1] = c_part[1]
    bparts[0] = b_part[0]
    bparts[1] = b_part[1]
    ct_part = split_two(jnp.transpose(c_value))
    ctparts[0] = ct_part[0]
    ctparts[1] = ct_part[1]
    dgram[...] = jnp.zeros_like(dgram)
    dcoup[...] = jnp.zeros_like(dcoup)
    dhead[...] = jnp.zeros_like(dhead)
    lane = lax.broadcasted_iota(jnp.int32, (CHUNK, LANES), 1)
    row = lax.broadcasted_iota(jnp.int32, (CHUNK, LANES), 0)
    low_half = (lane < LANES // 2).astype(f32)
    high_half = 1.0 - low_half
    last_row = (row == CHUNK - 1).astype(f32)
    is_end = step_id == 0
    eight_rows = lax.broadcasted_iota(jnp.int32, cd.shape, 0)
    for place in range(2):
        chosen = jnp.where(eight_rows == chunk + place, cd[...], 0.0)
        cd_s[place : place + 1, :] = jnp.sum(chosen, axis=0, keepdims=True)

    def pair(index, carried):
        cols = pl.ds(pl.multiple_of(index * LANES, LANES), LANES)
        wide = pl.ds(pl.multiple_of(index * 2 * LANES, 2 * LANES), 2 * LANES)
        raw = vraw[:, cols]
        full = jnp.concatenate([halo[:, cols], raw], axis=0)
        lagged = [raw] + [pltpu.roll(full, lag, 0)[8:] * same_s[lag - 1] for lag in range(1, 4)]
        pre_value = cb[:, cols]
        for lag in range(4):
            pre_value = pre_value + cw[lag : lag + 1, cols] * lagged[lag]
        sig = logistic(pre_value)
        value = pre_value * sig
        spread = mm(stack[...], sel[:, cols])
        step_e = spread[:CHUNK]
        carry_e = spread[CHUNK : 2 * CHUNK]
        tail_e = spread[2 * CHUNK :]
        inputs = step_e * value
        grads = grad[:, cols]
        column = mm(cumpack[...], selcol[:, wide])
        row_pair = jnp.concatenate(
            [cumt[pl.ds(2 * index, 1), :], cumt[pl.ds(2 * index + 1, 1), :]], axis=1
        )
        bias = bias_s[...]
        gram = gram_s[...]
        decays = jnp.exp(row_pair - column + jnp.concatenate([bias, bias], axis=1))
        mixing = jnp.concatenate([gram, gram], axis=1) * decays
        mix_high, mix_low = split_two(mixing)
        g_low = split_two(grads * low_half)
        g_high = split_two(grads * high_half)
        diag_high = jnp.concatenate([g_low[0], g_high[0]], axis=0)
        diag_low = jnp.concatenate([g_low[1], g_high[1]], axis=0)
        both = mm(mix_high, jnp.concatenate([diag_high, diag_low], axis=1))
        input_g = both[:, :LANES] + both[:, LANES:] + mm(mix_low, diag_high)
        held_g = state[:, cols]
        held_parts = split_two(held_g)
        input_g = input_g + tail_e * mm_three((bparts[0], bparts[1]), held_parts)
        in_parts = split_two(inputs)
        outer = mm_three_nt(in_parts, (diag_high, diag_low)) * decays
        dgram[...] += outer[:, :CHUNK] + outer[:, CHUNK:]
        reach_now = cd_s[0:1, cols]
        reach_next = cd_s[1:2, cols]
        arriving = entering[:, cols]
        held = st_now[0, :, cols] + reach_now * arriving
        next_own = jnp.where(is_end, fin[:, cols], st_next[0, :, cols])
        following = next_own + reach_next * arriving
        carried_g = split_two(carry_e * grads)
        state[:, cols] = carry_e[CHUNK - 1 :, :] * held_g + mm_three(
            (ctparts[0], ctparts[1]), carried_g
        )
        dcoup[1] += mm_three_nt(carried_g, split_two(held))
        dcoup[0] += mm_three_nt(split_two(tail_e * inputs), held_parts)
        value_g = input_g * step_e + skip[:, cols] * grads
        kept = jnp.sum(held_g * following, axis=0, keepdims=True)
        balance = grads * (mixer[:, cols] - skip[:, cols] * value) - inputs * input_g
        balance = balance + last_row * kept
        sums = jnp.concatenate([balance, input_g * value], axis=0)
        sums_parts = split_three(sums)
        pick = selt[cols, :]
        dhead[...] += mm(sums_parts[0], pick) + mm(sums_parts[1], pick) + mm(sums_parts[2], pick)
        skip_g[0:1, cols] += jnp.sum(grads * value, axis=0, keepdims=True)
        pre_g = value_g * (sig * (1.0 + pre_value * (1.0 - sig)))
        cw_g[4:5, cols] += jnp.sum(pre_g, axis=0, keepdims=True)
        raw_g = cw[0:1, cols] * pre_g
        cw_g[0:1, cols] += jnp.sum(pre_g * raw, axis=0, keepdims=True)
        none = jnp.zeros((8, LANES), f32)
        edge = none
        for lag in range(1, 4):
            cw_g[lag : lag + 1, cols] += jnp.sum(pre_g * lagged[lag], axis=0, keepdims=True)
            weighted = cw[lag : lag + 1, cols] * (pre_g * same_s[lag - 1])
            padded = jnp.concatenate([none, weighted, none], axis=0)
            turned = pltpu.roll(padded, CHUNK + 16 - lag, 0)
            raw_g = raw_g + turned[8 : 8 + CHUNK]
            edge = edge + turned[:8]
        vraw_g[:, cols] = raw_g
        vraw_g[CHUNK - 8 :, cols] += rim_s[:, cols]
        rim_s[:, cols] = edge
        vrim_g[:, cols] = edge
        return carried

    lax.fori_loop(0, heads // 2, pair, 0, unroll=4)

    total = dgram[...]
    total_parts = split_two(total)
    turned_parts = split_two(jnp.transpose(total))
    b_grad = dcoup[0] + mm_three(total_parts, (cparts[0], cparts[1]))
    c_grad = dcoup[1] + mm_three(turned_parts, (bparts[0], bparts[1]))
    coupled_g = jnp.concatenate([b_grad, c_grad], axis=1)
    pre_g = coupled_g * (csig * (1.0 + pre * (1.0 - csig)))
    ccw_g[4:5, :] += jnp.sum(pre_g, axis=0, keepdims=True)
    ccw_g[0:1, :] += jnp.sum(pre_g * craw_now, axis=0, keepdims=True)
    raw_g = ccw[0:1, :] * pre_g
    full = jnp.concatenate([coupling_halo, craw_now], axis=0)
    none = jnp.zeros((8, 2 * width), f32)
    edge = none
    for lag in range(1, 4):
        masked = pre_g * wide_same[lag]
        ccw_g[lag : lag + 1, :] += jnp.sum(
            masked * pltpu.roll(full, lag, 0)[8:], axis=0, keepdims=True
        )
        padded = jnp.concatenate([none, ccw[lag : lag + 1, :] * masked, none], axis=0)
        turned = pltpu.roll(padded, CHUNK + 16 - lag, 0)
        raw_g = raw_g + turned[8 : 8 + CHUNK]
        edge = edge + turned[:8]
    craw_g[...] = raw_g
    craw_g[CHUNK - 8 :, :] += crim_s[...]
    crim_s[...] = edge
    crim_g[...] = edge

    upper = (frame["row_ids"] <= frame["column_ids"]).astype(bf16)
    parts = split_three(dhead[:CHUNK])
    decay_g = mm(upper, parts[0]) + mm(upper, parts[1]) + mm(upper, parts[2])
    step_g = (dhead[CHUNK:] - rate[...] * decay_g) * logistic(frame["shifted"])
    sraw_g[...] = step_g
    small_g[0:1, :] += jnp.sum(step_g, axis=0, keepdims=True)
    small_g[1:2, :] += jnp.sum(-frame["step"] * decay_g, axis=0, keepdims=True)


def backward_ssd(
    marks, micro, raw, rim, inner, twice, tokens, grad, mixer, states, fin, entering, cd, pulled,
    cw, cb, ccw, ccb, sbias, rate, skip, sel, selcol, selt,
):
    width = twice // 2
    chunks = tokens // CHUNK
    heads = inner // (LANES // 2)
    eighth = CHUNK // 8
    final = (micro + 1) * chunks - 1

    def rows(count):
        return pl.BlockSpec((CHUNK, count), lambda step, *_: (chunks - 1 - step, 0))

    def part(count, start):
        return pl.BlockSpec((CHUNK, count), lambda step, *_: (final - step, start // count))

    def before(count, start):
        return pl.BlockSpec(
            (8, count),
            lambda step, *_: (jnp.maximum((final - step) * eighth - 1, 0), start // count),
        )

    def edge(count, start):
        return pl.BlockSpec((8, count), lambda *_: (0, start // count))

    def held(offset):
        return pl.BlockSpec(
            (1, width, inner),
            lambda step, *_: (jnp.minimum(chunks - 1 - step + offset, chunks - 1), 0, 0),
        )

    return pl.pallas_call(
        functools.partial(backward_kernel, heads),
        grid_spec=pltpu.PrefetchScalarGridSpec(
            num_scalar_prefetch=1,
            grid=(chunks,),
            in_specs=[
                part(inner, 0),
                before(inner, 0),
                edge(inner, 0),
                part(twice, inner),
                before(twice, inner),
                edge(twice, inner),
                part(LANES, inner + twice),
                part(inner, 0),
                part(inner, 0),
                held(0),
                held(1),
                whole((width, inner)),
                whole((width, inner)),
                whole((8, inner)),
                whole((width, inner)),
                whole(cw.shape),
                whole(cb.shape),
                whole(ccw.shape),
                whole(ccb.shape),
                whole(sbias.shape),
                whole(rate.shape),
                whole(skip.shape),
                whole(sel.shape),
                whole(selcol.shape),
                whole(selt.shape),
            ],
            out_specs=[
                rows(inner),
                whole((8, inner)),
                rows(twice),
                whole((8, twice)),
                rows(LANES),
                whole((8, inner)),
                whole((8, twice)),
                whole((8, LANES)),
                whole((8, inner)),
            ],
            scratch_shapes=[
                pltpu.VMEM((width, inner), f32),
                pltpu.VMEM((LANES, CHUNK), f32),
                pltpu.VMEM((3 * CHUNK, LANES), bf16),
                pltpu.VMEM((CHUNK, LANES), bf16),
                pltpu.VMEM((8, inner), f32),
                pltpu.VMEM((3, CHUNK, LANES), f32),
                pltpu.VMEM((CHUNK, CHUNK), f32),
                pltpu.VMEM((CHUNK, CHUNK), f32),
                pltpu.VMEM((2, CHUNK, width), bf16),
                pltpu.VMEM((2, CHUNK, width), bf16),
                pltpu.VMEM((2, width, CHUNK), bf16),
                pltpu.VMEM((8, inner), f32),
                pltpu.VMEM((8, twice), f32),
                pltpu.VMEM((CHUNK, CHUNK), f32),
                pltpu.VMEM((2, CHUNK, width), f32),
                pltpu.VMEM((2 * CHUNK, LANES), f32),
                pltpu.VMEM((8, inner), f32),
            ],
        ),
        out_shape=[
            jax.ShapeDtypeStruct((tokens, inner), f32),
            jax.ShapeDtypeStruct((8, inner), f32),
            jax.ShapeDtypeStruct((tokens, twice), f32),
            jax.ShapeDtypeStruct((8, twice), f32),
            jax.ShapeDtypeStruct((tokens, LANES), f32),
            jax.ShapeDtypeStruct((8, inner), f32),
            jax.ShapeDtypeStruct((8, twice), f32),
            jax.ShapeDtypeStruct((8, LANES), f32),
            jax.ShapeDtypeStruct((8, inner), f32),
        ],
        compiler_params=pltpu.CompilerParams(vmem_limit_bytes=48 * 1024 * 1024),
        cost_estimate=pl.CostEstimate(
            flops=60 * tokens * inner * 128 * 2, bytes_accessed=32 * tokens * inner, transcendentals=0
        ),
    )(
        marks, raw, raw, rim, raw, raw, rim, raw, grad, mixer, states, states, fin, entering,
        cd, pulled, cw, cb, ccw, ccb, sbias, rate, skip, sel, selcol, selt,
    )


def passed_along(value, axis, steps):
    count = lax.axis_size(axis)
    initial, last = (max(0, -steps), min(count, count - steps))
    return lax.ppermute(value, axis, [(source, source + steps) for source in range(initial, last)])


def paired(value, axis):
    count = lax.axis_size(axis)
    return lax.ppermute(value, axis, [(source, source ^ 1) for source in range(count)])


def ring_shift(value, axis, steps):
    count = lax.axis_size(axis)
    return lax.ppermute(
        value, axis, [(source, (source + 2 * steps) % count) for source in range(count)]
    )


def gathered(shard, dim):
    pairs = lax.axis_size("fsdp") // 2
    own = lax.axis_index("fsdp")
    size = shard.shape[dim]
    shape = list(shard.shape)
    shape[dim] = size * 2 * pairs
    full = jnp.zeros(shape, shard.dtype)
    blocks = [shard]
    for _ in range(pairs - 1):
        blocks.append(ring_shift(blocks[-1], "fsdp", 1))
    for offset, block in enumerate(blocks):
        place = lax.rem(own + 2 * (pairs - offset), 2 * pairs)
        full = lax.dynamic_update_slice_in_dim(full, block, place * size, dim)
        other = paired(block, "fsdp")
        full = lax.dynamic_update_slice_in_dim(full, other, (place ^ 1) * size, dim)
    return full


def scattered(block_of):
    pairs = lax.axis_size("fsdp") // 2
    own = lax.axis_index("fsdp")
    order = list(range(1, pairs)) + [0]
    arrived = {}
    for offset in order:
        place = lax.rem(own + 2 * offset, 2 * pairs)
        arrived[offset] = paired(block_of(place ^ 1).astype(bf16), "fsdp")
    total = None
    for offset in order:
        place = lax.rem(own + 2 * offset, 2 * pairs)
        partial = block_of(place) + arrived[offset].astype(f32)
        if offset:
            partial = ring_shift(partial.astype(bf16), "fsdp", offset).astype(f32)
        total = partial if total is None else total + partial
    return total + lax.ppermute(
        total, "context", [(source, source ^ 1) for source in range(lax.axis_size("context"))]
    )


def summed_everywhere(values):
    sizes = [value.size for value in values]
    shapes = [value.shape for value in values]
    flat = jnp.concatenate([value.reshape(-1) for value in values])
    count = flat.shape[0]
    flat = jnp.pad(flat, (0, -count % 1024)).reshape(-1, 128)
    for axis in ("context", "fsdp"):
        members = lax.axis_size(axis)
        reach = 1
        while reach < members:
            flat = flat + lax.ppermute(
                flat, axis, [(source, source ^ reach) for source in range(members)]
            )
            reach *= 2
    flat = flat.reshape(-1)
    results, start = [], 0
    for size, shape in zip(sizes, shapes):
        results.append(flat[start : start + size].reshape(shape))
        start += size
    return results


def chained(own, factor, steps):
    arriving = passed_along(own, "context", steps)
    for _ in range(lax.axis_size("context") - 2):
        arriving = passed_along(factor * arriving + own, "context", steps)
    return arriving


def shards(
    tokens,
    lengths,
    block_order,
    cotangent,
    norm_gain,
    in_weight,
    coupling_weight,
    step_weight,
    out_weight,
    conv_weight,
    conv_bias,
    coupling_conv,
    coupling_bias,
    step_bias,
    decay_rate,
    skip_gain,
    inner_gain,
):
    highest = lax.Precision.HIGHEST
    micros = tokens.shape[0]
    count = tokens.shape[2]
    model = tokens.shape[3]
    inner = inner_gain.shape[0]
    heads = step_bias.shape[0]
    head_size = inner // heads
    twice = coupling_weight.shape[1]
    width = twice // 2
    blocks_row = block_order.shape[2]
    block_len = count * lax.axis_size("context") // blocks_row
    own_blocks = count // block_len
    inner_total = inner * lax.axis_size("tensor")
    side = lax.axis_index("tensor")
    place = lax.axis_index("context")
    base = place * count
    shard_rows = in_weight.shape[0]
    half = model // 2

    narrow, wide_columns = selectors(heads, head_size)
    sel = jnp.asarray(narrow, bf16)
    selcol = jnp.asarray(wide_columns, bf16)
    selt = jnp.asarray(narrow[:heads].T, bf16)
    selt = jnp.pad(selt, ((0, 0), (0, LANES - heads)))

    lead = jnp.concatenate(
        [
            in_weight[:, 1, :],
            coupling_weight,
            jnp.pad(step_weight, ((0, 0), (0, LANES - heads))),
        ],
        axis=1,
    )
    lead_full = gathered(lead, 0)
    gate_full = gathered(in_weight[:, 0, :], 0)
    out_full = gathered(out_weight, 1)

    mine = lax.dynamic_slice_in_dim(tokens[:, 0], side * half, half, 2)
    far_half = lax.ppermute(
        mine, "context", [(source, source ^ 1) for source in range(lax.axis_size("context"))]
    )
    far_other = paired(far_half, "tensor")
    far = jnp.where(
        side == 0,
        jnp.concatenate([far_half, far_other], axis=2),
        jnp.concatenate([far_other, far_half], axis=2),
    )
    near = tokens[:, 0].reshape(micros, own_blocks, block_len, model)
    far = far.reshape(micros, own_blocks, block_len, model)
    everything = jnp.where(
        place == 0, jnp.concatenate([near, far], 1), jnp.concatenate([far, near], 1)
    )
    slots = jnp.arange(blocks_row, dtype=jnp.int32)
    picked = []
    for micro in range(micros):
        for own in range(own_blocks):
            wanted = place * own_blocks + own
            slot = jnp.sum(jnp.where(block_order[micro, 0] == wanted, slots, 0))
            picked.append(
                lax.dynamic_slice(
                    everything, (micro, slot, 0, 0), (1, 1, block_len, model)
                ).reshape(block_len, model)
            )
    x_input = jnp.concatenate(picked, axis=0)
    x_float = x_input.astype(f32)
    inv_rms = lax.rsqrt(jnp.mean(x_float * x_float, axis=-1, keepdims=True) + epsilon)
    normed = (x_float * inv_rms * norm_gain).astype(bf16)

    first_end = lengths[:, 0, 0]
    second_end = first_end + lengths[:, 0, 1]
    marks = [
        jnp.stack([first_end[micro], second_end[micro], base]).astype(jnp.int32)
        for micro in range(micros)
    ]
    positions = base + jnp.arange(count, dtype=jnp.int32)
    keep = jnp.concatenate([(positions < second_end[micro]) for micro in range(micros)])
    keep = keep.astype(f32)[:, None]

    cw, cb = conv_weight, conv_bias.reshape(1, inner)
    ccw, ccb = coupling_conv, coupling_bias.reshape(1, twice)
    sbias = jnp.pad(step_bias, (0, LANES - heads)).reshape(1, LANES)
    rate = jnp.pad(decay_rate, (0, LANES - heads)).reshape(1, LANES)
    skip = jnp.repeat(skip_gain, head_size).reshape(1, inner)

    raw = jnp.dot(normed, lead_full, preferred_element_type=f32)
    rims = passed_along(
        jnp.stack([raw[(micro + 1) * count - 8 : (micro + 1) * count] for micro in range(micros)]),
        "context",
        1,
    )
    forwards = []
    for micro in range(micros):
        forwards.append(
            forward_ssd(
                marks[micro], micro, raw, rims[micro], inner, twice, count,
                cw, cb, ccw, ccb, sbias, rate, skip, sel, selcol,
            )
        )
    entering = [
        chained(forwards[micro][2], forwards[micro][5][count // CHUNK], 1)
        for micro in range(micros)
    ]
    gate_in = jnp.dot(normed, gate_full, preferred_element_type=f32)
    cot = cotangent[:, 0].reshape(micros * count, model)
    out_grad = cot * keep.astype(bf16)
    norm_grad = contract_cols(out_grad, out_full)

    mixers = []
    for micro in range(micros):
        y_own, _, _, coupled, carry, _ = forwards[micro]
        mixers.append(
            y_own + carry * jnp.dot(coupled[:, width:], entering[micro], precision=highest)
        )
    mixer = jnp.concatenate(mixers, axis=0)
    gate_sig = jax.nn.sigmoid(gate_in)
    gate_act = gate_in * gate_sig
    gated = mixer * gate_act
    scaled_grad = norm_grad * inner_gain
    row_sums = jnp.stack([jnp.sum(gated * gated, axis=-1), jnp.sum(scaled_grad * gated, axis=-1)])
    row_sums = row_sums + paired(row_sums, "tensor")
    inv_norm = lax.rsqrt(row_sums[0] / inner_total + epsilon)[:, None]
    inner_dot = row_sums[1][:, None]
    gated_norm = (gated * inv_norm * inner_gain).astype(bf16)
    inner_gain_grad = jnp.sum(norm_grad * gated * inv_norm, axis=0)
    gated_grad = scaled_grad * inv_norm - gated * (inner_dot * inv_norm**3 / inner_total)
    gate_grad = (gated_grad * mixer * gate_sig * (1.0 + gate_in * (1.0 - gate_sig))).astype(bf16)
    mixer_grad = gated_grad * gate_act

    pulled = []
    for micro in range(micros):
        part = slice(micro * count, (micro + 1) * count)
        own_pull = lax.dot_general(
            forwards[micro][3][:, width:],
            forwards[micro][4] * mixer_grad[part],
            (((0,), (0,)), ((), ())),
            precision=highest,
        )
        pulled.append(chained(own_pull, forwards[micro][5][count // CHUNK], -1))

    branch = jnp.dot(gated_norm, out_full, preferred_element_type=f32)
    branch = branch + paired(branch, "tensor")
    block_out = (x_float + keep * branch).astype(bf16)

    def out_block(index):
        columns = lax.dynamic_slice_in_dim(out_grad, index * shard_rows, shard_rows, 1)
        return contract_rows(gated_norm, columns)

    out_shard = scattered(out_block)

    def in_block(grads):
        def block(index):
            columns = lax.dynamic_slice_in_dim(normed, index * shard_rows, shard_rows, 1)
            return contract_rows(columns, grads)

        return block

    gate_shard = scattered(in_block(gate_grad))

    backs = []
    for micro in range(micros):
        y_own, states, final, coupled, carry, reach = forwards[micro]
        backs.append(
            backward_ssd(
                marks[micro], micro, raw, rims[micro], inner, twice, count, mixer_grad, mixer,
                states, final, entering[micro], reach, pulled[micro],
                cw, cb, ccw, ccb, sbias, rate, skip, sel, selcol, selt,
            )
        )
    edges = passed_along(
        jnp.stack([jnp.concatenate([back[1], back[3]], axis=1) for back in backs]), "context", -1
    )
    tail_pad = ((count - 8, 0), (0, 0))
    coupling_raw_grad = jnp.stack(
        [back[2] + jnp.pad(edges[micro][:, inner:], tail_pad) for micro, back in enumerate(backs)]
    )
    coupling_raw_grad = coupling_raw_grad + paired(coupling_raw_grad, "tensor")
    lane_ids = jnp.arange(twice, dtype=jnp.int32)
    own_lanes = ((lane_ids // width) == side).astype(bf16)
    coupling_low = coupling_raw_grad.astype(bf16) * own_lanes
    lead_grad = jnp.concatenate(
        [
            jnp.concatenate(
                [
                    (back[0] + jnp.pad(edges[micro][:, :inner], tail_pad)).astype(bf16),
                    coupling_low[micro],
                    back[4].astype(bf16),
                ],
                axis=1,
            )
            for micro, back in enumerate(backs)
        ],
        axis=0,
    )
    lead_shard = scattered(in_block(lead_grad))
    normed_part = contract_cols(gate_grad, gate_full) + contract_cols(lead_grad, lead_full)
    normed_grad = normed_part + paired(normed_part, "tensor")
    x_hat = x_float * inv_rms
    hat_grad = normed_grad * norm_gain
    input_grad = (
        cot.astype(f32)
        + inv_rms * (hat_grad - x_hat * jnp.mean(hat_grad * x_hat, axis=-1, keepdims=True))
    ).astype(bf16)
    norm_gain_grad = jnp.sum(normed_grad * x_hat, axis=0)

    value_sums = sum(back[5] for back in backs)
    coupling_sums = sum(back[6] for back in backs)
    small_sums = sum(back[7] for back in backs)
    skip_sums = sum(back[8] for back in backs)[0].reshape(heads, head_size).sum(axis=1)
    coupling_sums = coupling_sums + paired(coupling_sums, "tensor")
    (value_all, coupling_all, small_all, skip_all, inner_all, norm_all) = summed_everywhere(
        [value_sums[:5], coupling_sums[:5], small_sums[:2], skip_sums, inner_gain_grad, norm_gain_grad]
    )
    coupling_shard = lead_shard[:, inner : inner + twice]
    coupling_shard = coupling_shard + paired(coupling_shard, "tensor")
    return (
        block_out.reshape(micros, 1, count, model),
        input_grad.reshape(micros, 1, count, model),
        norm_all,
        jnp.stack([gate_shard, lead_shard[:, :inner]], axis=1),
        coupling_shard,
        lead_shard[:, inner + twice : inner + twice + heads],
        out_shard,
        value_all[:4],
        value_all[4],
        coupling_all[:4],
        coupling_all[4],
        small_all[0, :heads],
        small_all[1, :heads],
        skip_all,
        inner_all,
    )


def contract_rows(left, right):
    return lax.dot_general(
        left, right, (((0,), (0,)), ((), ())), preferred_element_type=jnp.float32
    )


def contract_cols(left, right):
    return lax.dot_general(
        left, right, (((1,), (1,)), ((), ())), preferred_element_type=jnp.float32
    )


def solution(mesh):
    return jax.shard_map(
        shards,
        mesh=mesh,
        in_specs=(
            P(None, "fsdp", "context", None),
            P(None, "fsdp", None),
            P(None, "fsdp", None),
            P(None, "fsdp", "context", None),
            P(),
            P("fsdp", None, "tensor"),
            P("fsdp", None),
            P("fsdp", "tensor"),
            P("tensor", "fsdp"),
            P(None, "tensor"),
            P("tensor"),
            P(),
            P(),
            P("tensor"),
            P("tensor"),
            P("tensor"),
            P("tensor"),
        ),
        out_specs=(
            P(None, "fsdp", "context", None),
            P(None, "fsdp", "context", None),
            P(),
            P("fsdp", None, "tensor"),
            P("fsdp", None),
            P("fsdp", "tensor"),
            P("tensor", "fsdp"),
            P(None, "tensor"),
            P("tensor"),
            P(),
            P(),
            P("tensor"),
            P("tensor"),
            P("tensor"),
            P("tensor"),
        ),
        check_vma=False,
    )
```

```python
import functools

import jax
import jax.numpy as jnp
import numpy as np
from jax import lax
from jax.experimental import pallas as pl
from jax.experimental.pallas import tpu as pltpu
from jax.sharding import PartitionSpec as P

CHUNK = 128
LANES = 128
MESH = pl.DeviceIdType.MESH
f32 = jnp.float32
bf16 = jnp.bfloat16
epsilon = 1e-05


def split_two(value):
    high = value.astype(bf16)
    return high, (value - high.astype(f32)).astype(bf16)


def split_three(value):
    high = value.astype(bf16)
    rest = value - high.astype(f32)
    middle = rest.astype(bf16)
    return high, middle, (rest - middle.astype(f32)).astype(bf16)


def mm(left, right):
    return jnp.dot(left, right, preferred_element_type=f32)


def mm_nt(left, right):
    return lax.dot_general(left, right, (((1,), (1,)), ((), ())), preferred_element_type=f32)


def mm_three(left, right):
    wide = mm(left[0], jnp.concatenate([right[0], right[1]], axis=1))
    count = right[0].shape[1]
    return wide[:, :count] + wide[:, count:] + mm(left[1], right[0])


def mm_three_nt(left, right):
    return mm_nt(left[0], right[0]) + mm_nt(left[0], right[1]) + mm_nt(left[1], right[0])


def packed_parts(value, heads):
    high, middle, lowest = split_three(value)
    joined = (
        high.astype(f32)
        + pltpu.roll(middle.astype(f32), heads, 1)
        + pltpu.roll(lowest.astype(f32), 2 * heads, 1)
    )
    return joined.astype(bf16)


def segment_at(position, first_end, second_end):
    first_part = (position >= first_end).astype(jnp.int32)
    second_part = (position >= second_end).astype(jnp.int32)
    return jnp.where(position < 0, -1, first_part + second_part)


def chunk_frame(marks, chunk, step_raw, step_bias, rate, heads):
    first_end, second_end, base = marks[0], marks[1], marks[2]
    start = base + chunk * CHUNK
    rows = start + lax.broadcasted_iota(jnp.int32, (CHUNK, LANES), 0)
    columns = start + lax.broadcasted_iota(jnp.int32, (CHUNK, CHUNK), 1)
    seg_rows = segment_at(rows, first_end, second_end)
    seg_columns = segment_at(columns, first_end, second_end)
    seg_prior = segment_at(start - 1, first_end, second_end)
    seg_last = segment_at(start + CHUNK - 1, first_end, second_end)
    same = [
        (segment_at(rows - lag, first_end, second_end) == seg_rows).astype(f32) for lag in range(4)
    ]
    shifted = step_raw + step_bias
    step = jnp.maximum(shifted, 0.0) + jnp.log1p(jnp.exp(-jnp.abs(shifted)))
    lanes = lax.broadcasted_iota(jnp.int32, (CHUNK, LANES), 1)
    step = jnp.where(lanes < heads, step, 0.0)
    log_decay = -step * rate
    row_ids = lax.broadcasted_iota(jnp.int32, (CHUNK, CHUNK), 0)
    column_ids = lax.broadcasted_iota(jnp.int32, (CHUNK, CHUNK), 1)
    lower = (row_ids >= column_ids).astype(bf16)
    parts = split_three(log_decay)
    cumulative = mm(lower, parts[0]) + mm(lower, parts[1]) + mm(lower, parts[2])
    last = cumulative[CHUNK - 1 :, :]
    carry = jnp.exp(cumulative) * (seg_rows == seg_prior).astype(f32)
    tail = jnp.exp(last - cumulative) * (seg_rows == seg_last).astype(f32)
    live = lanes < heads
    carry = jnp.where(live, carry, 0.0)
    tail = jnp.where(live, tail, 0.0)
    return dict(
        seg_rows=seg_rows,
        seg_columns=seg_columns,
        row_ids=row_ids,
        column_ids=column_ids,
        same=same,
        step=step,
        shifted=shifted,
        cumulative=cumulative,
        carry=carry,
        tail=tail,
    )


def conv_sum(current, halo, weights, biases, same):
    full = jnp.concatenate([halo, current], axis=0)
    total = biases + weights(0) * current
    for lag in range(1, 4):
        total = total + weights(lag) * (pltpu.roll(full, lag, 0)[8:] * same[lag])
    return total


def logistic(value):
    return 1.0 / (1.0 + jnp.exp(-value))


def forward_kernel(
    heads,
    marks,
    vraw,
    vprev,
    vrim,
    craw,
    cprev,
    crim,
    sraw,
    cw,
    cb,
    ccw,
    ccb,
    sbias,
    rate,
    skip,
    sel,
    selcol,
    y_out,
    st_out,
    fin_out,
    bc_out,
    carry_out,
    cd_out,
    state,
    cumt,
    stack,
    cumpack,
    halo,
    same_s,
    bias_s,
    gram_s,
    cd_s,
    cparts,
    btparts,
):
    chunk = pl.program_id(0)
    chunks = pl.num_programs(0)
    width = state.shape[0]

    @pl.when(chunk == 0)
    def _():
        state[...] = jnp.zeros_like(state)
        cd_s[...] = jnp.ones_like(cd_s)
        cd_out[...] = jnp.zeros_like(cd_out)
        halo[...] = vrim[...]

    @pl.when(chunk > 0)
    def _():
        halo[...] = vprev[...]

    frame = chunk_frame(marks, chunk, sraw[...], sbias[...], rate[...], heads)
    same = frame["same"]
    for lag in range(1, 4):
        same_s[lag - 1] = same[lag]
    joined = (frame["seg_rows"] == frame["seg_columns"]) & (frame["row_ids"] >= frame["column_ids"])
    bias_s[...] = jnp.where(joined, 0.0, -1e30)
    stack[0:CHUNK, :] = packed_parts(frame["step"], heads)
    stack[CHUNK : 2 * CHUNK, :] = packed_parts(frame["carry"], heads)
    stack[2 * CHUNK : 3 * CHUNK, :] = packed_parts(frame["tail"], heads)
    cumpack[...] = packed_parts(frame["cumulative"], heads)
    cumt[...] = jnp.transpose(frame["cumulative"])
    coupling_halo = jnp.where(chunk == 0, crim[...], cprev[...])
    wide_same = [None] + [jnp.concatenate([same[lag], same[lag]], axis=1) for lag in range(1, 4)]
    pre = conv_sum(
        craw[...], coupling_halo, lambda lag: ccw[lag : lag + 1, :], ccb[...], wide_same
    )
    coupled = pre * logistic(pre)
    bc_out[...] = coupled
    b_part = split_two(coupled[:, :width])
    c_part = split_two(coupled[:, width:])
    gram_s[...] = mm_three_nt(c_part, b_part)
    cparts[0] = c_part[0]
    cparts[1] = c_part[1]
    turned = jnp.transpose(coupled[:, :width])
    bt_part = split_two(turned)
    btparts[0] = bt_part[0]
    btparts[1] = bt_part[1]
    lane = lax.broadcasted_iota(jnp.int32, (CHUNK, LANES), 1)
    low_half = (lane < LANES // 2).astype(f32)
    high_half = 1.0 - low_half

    def pair(index, carried):
        cols = pl.ds(pl.multiple_of(index * LANES, LANES), LANES)
        wide = pl.ds(pl.multiple_of(index * 2 * LANES, 2 * LANES), 2 * LANES)
        pre_value = conv_sum(
            vraw[:, cols],
            halo[:, cols],
            lambda lag: cw[lag : lag + 1, cols],
            cb[:, cols],
            [None] + [same_s[lag - 1] for lag in range(1, 4)],
        )
        value = pre_value * logistic(pre_value)
        spread = mm(stack[...], sel[:, cols])
        step_e = spread[:CHUNK]
        carry_e = spread[CHUNK : 2 * CHUNK]
        tail_e = spread[2 * CHUNK :]
        inputs = step_e * value
        column = mm(cumpack[...], selcol[:, wide])
        row_pair = jnp.concatenate(
            [cumt[pl.ds(2 * index, 1), :], cumt[pl.ds(2 * index + 1, 1), :]], axis=1
        )
        bias = bias_s[...]
        gram = gram_s[...]
        mixing = jnp.concatenate([gram, gram], axis=1) * jnp.exp(
            column - row_pair + jnp.concatenate([bias, bias], axis=1)
        )
        mix_high, mix_low = split_two(mixing)
        in_low = split_two(inputs * low_half)
        in_high = split_two(inputs * high_half)
        diag_high = jnp.concatenate([in_low[0], in_high[0]], axis=0)
        diag_low = jnp.concatenate([in_low[1], in_high[1]], axis=0)
        both = mm(mix_high, jnp.concatenate([diag_high, diag_low], axis=1))
        inside = both[:, :LANES] + both[:, LANES:] + mm(mix_low, diag_high)
        held = state[:, cols]
        from_state = mm_three((cparts[0], cparts[1]), split_two(held))
        y_out[:, cols] = inside + carry_e * from_state + skip[:, cols] * value
        fresh = mm_three((btparts[0], btparts[1]), split_two(tail_e * inputs))
        through = carry_e[CHUNK - 1 :, :]
        st_out[0, :, cols] = held
        renewed = through * held + fresh
        state[:, cols] = renewed
        fin_out[:, cols] = renewed
        reach = cd_s[0:1, cols]
        carry_out[:, cols] = carry_e * reach
        cd_s[0:1, cols] = reach * through
        return carried

    eight_rows = lax.broadcasted_iota(jnp.int32, cd_out.shape, 0)
    cd_out[...] = jnp.where(eight_rows == chunk, cd_s[0:1, :], cd_out[...])
    lax.fori_loop(0, heads // 2, pair, 0, unroll=4)
    cd_out[...] = jnp.where(eight_rows == chunk + 1, cd_s[0:1, :], cd_out[...])


def selectors(heads, head_size):
    inner = heads * head_size
    head_of_lane = np.arange(inner) // head_size
    narrow = np.zeros((LANES, inner), np.float32)
    wide = np.zeros((LANES, heads * LANES), np.float32)
    head_of_wide = np.arange(heads * LANES) // LANES
    for part in range(3):
        narrow[part * heads + head_of_lane, np.arange(inner)] = 1.0
        wide[part * heads + head_of_wide, np.arange(heads * LANES)] = 1.0
    return narrow, wide


def whole(shape):
    return pl.BlockSpec(shape, lambda index, *_: (0,) * len(shape))


def forward_ssd(
    marks, micro, raw, rim, inner, twice, tokens, cw, cb, ccw, ccb, sbias, rate, skip, sel, selcol
):
    width = twice // 2
    chunks = tokens // CHUNK
    heads = inner // (LANES // 2)
    eighth = CHUNK // 8
    initial = micro * chunks

    def rows(count):
        return pl.BlockSpec((CHUNK, count), lambda chunk, *_: (chunk, 0))

    def part(count, start):
        return pl.BlockSpec((CHUNK, count), lambda chunk, *_: (initial + chunk, start // count))

    def before(count, start):
        return pl.BlockSpec(
            (8, count),
            lambda chunk, *_: (jnp.maximum((initial + chunk) * eighth - 1, 0), start // count),
        )

    def edge(count, start):
        return pl.BlockSpec((8, count), lambda *_: (0, start // count))

    return pl.pallas_call(
        functools.partial(forward_kernel, heads),
        grid_spec=pltpu.PrefetchScalarGridSpec(
            num_scalar_prefetch=1,
            grid=(chunks,),
            in_specs=[
                part(inner, 0),
                before(inner, 0),
                edge(inner, 0),
                part(twice, inner),
                before(twice, inner),
                edge(twice, inner),
                part(LANES, inner + twice),
                whole(cw.shape),
                whole(cb.shape),
                whole(ccw.shape),
                whole(ccb.shape),
                whole(sbias.shape),
                whole(rate.shape),
                whole(skip.shape),
                whole(sel.shape),
                whole(selcol.shape),
            ],
            out_specs=[
                rows(inner),
                pl.BlockSpec((1, width, inner), lambda chunk, *_: (chunk, 0, 0)),
                whole((width, inner)),
                rows(twice),
                rows(inner),
                whole((8, inner)),
            ],
            scratch_shapes=[
                pltpu.VMEM((width, inner), f32),
                pltpu.VMEM((LANES, CHUNK), f32),
                pltpu.VMEM((3 * CHUNK, LANES), bf16),
                pltpu.VMEM((CHUNK, LANES), bf16),
                pltpu.VMEM((8, inner), f32),
                pltpu.VMEM((3, CHUNK, LANES), f32),
                pltpu.VMEM((CHUNK, CHUNK), f32),
                pltpu.VMEM((CHUNK, CHUNK), f32),
                pltpu.VMEM((8, inner), f32),
                pltpu.VMEM((2, CHUNK, width), bf16),
                pltpu.VMEM((2, width, CHUNK), bf16),
            ],
        ),
        out_shape=[
            jax.ShapeDtypeStruct((tokens, inner), f32),
            jax.ShapeDtypeStruct((chunks, width, inner), f32),
            jax.ShapeDtypeStruct((width, inner), f32),
            jax.ShapeDtypeStruct((tokens, twice), f32),
            jax.ShapeDtypeStruct((tokens, inner), f32),
            jax.ShapeDtypeStruct((8, inner), f32),
        ],
        compiler_params=pltpu.CompilerParams(vmem_limit_bytes=40 * 1024 * 1024),
        cost_estimate=pl.CostEstimate(
            flops=20 * tokens * inner * 128 * 2, bytes_accessed=24 * tokens * inner, transcendentals=0
        ),
    )(marks, raw, raw, rim, raw, raw, rim, raw, cw, cb, ccw, ccb, sbias, rate, skip, sel, selcol)


def backward_kernel(
    heads,
    marks,
    vraw,
    vprev,
    vrim,
    craw,
    cprev,
    crim,
    sraw,
    grad,
    mixer,
    st_now,
    st_next,
    fin,
    entering,
    cd,
    pulled,
    cw,
    cb,
    ccw,
    ccb,
    sbias,
    rate,
    skip,
    sel,
    selcol,
    selt,
    vraw_g,
    vrim_g,
    craw_g,
    crim_g,
    sraw_g,
    cw_g,
    ccw_g,
    small_g,
    skip_g,
    state,
    cumt,
    stack,
    cumpack,
    halo,
    same_s,
    bias_s,
    gram_s,
    cparts,
    bparts,
    ctparts,
    rim_s,
    crim_s,
    dgram,
    dcoup,
    dhead,
    cd_s,
):
    step_id = pl.program_id(0)
    chunks = pl.num_programs(0)
    chunk = chunks - 1 - step_id
    width = state.shape[0]

    @pl.when(step_id == 0)
    def _():
        state[...] = pulled[...]
        rim_s[...] = jnp.zeros_like(rim_s)
        crim_s[...] = jnp.zeros_like(crim_s)
        cw_g[...] = jnp.zeros_like(cw_g)
        ccw_g[...] = jnp.zeros_like(ccw_g)
        small_g[...] = jnp.zeros_like(small_g)
        skip_g[...] = jnp.zeros_like(skip_g)

    @pl.when(chunk == 0)
    def _():
        halo[...] = vrim[...]

    @pl.when(chunk > 0)
    def _():
        halo[...] = vprev[...]

    frame = chunk_frame(marks, chunk, sraw[...], sbias[...], rate[...], heads)
    same = frame["same"]
    for lag in range(1, 4):
        same_s[lag - 1] = same[lag]
    joined = (frame["seg_rows"] == frame["seg_columns"]) & (frame["row_ids"] <= frame["column_ids"])
    bias_s[...] = jnp.where(joined, 0.0, -1e30)
    stack[0:CHUNK, :] = packed_parts(frame["step"], heads)
    stack[CHUNK : 2 * CHUNK, :] = packed_parts(frame["carry"], heads)
    stack[2 * CHUNK : 3 * CHUNK, :] = packed_parts(frame["tail"], heads)
    cumpack[...] = packed_parts(frame["cumulative"], heads)
    cumt[...] = jnp.transpose(frame["cumulative"])
    coupling_halo = jnp.where(chunk == 0, crim[...], cprev[...])
    wide_same = [None] + [jnp.concatenate([same[lag], same[lag]], axis=1) for lag in range(1, 4)]
    craw_now = craw[...]
    pre = conv_sum(craw_now, coupling_halo, lambda lag: ccw[lag : lag + 1, :], ccb[...], wide_same)
    csig = logistic(pre)
    coupled = pre * csig
    b_value = coupled[:, :width]
    c_value = coupled[:, width:]
    b_part = split_two(b_value)
    c_part = split_two(c_value)
    gram_s[...] = mm_three_nt(b_part, c_part)
    cparts[0] = c_part[0]
    cparts[1] = c_part[1]
    bparts[0] = b_part[0]
    bparts[1] = b_part[1]
    ct_part = split_two(jnp.transpose(c_value))
    ctparts[0] = ct_part[0]
    ctparts[1] = ct_part[1]
    dgram[...] = jnp.zeros_like(dgram)
    dcoup[...] = jnp.zeros_like(dcoup)
    dhead[...] = jnp.zeros_like(dhead)
    lane = lax.broadcasted_iota(jnp.int32, (CHUNK, LANES), 1)
    row = lax.broadcasted_iota(jnp.int32, (CHUNK, LANES), 0)
    low_half = (lane < LANES // 2).astype(f32)
    high_half = 1.0 - low_half
    last_row = (row == CHUNK - 1).astype(f32)
    is_end = step_id == 0
    eight_rows = lax.broadcasted_iota(jnp.int32, cd.shape, 0)
    for place in range(2):
        chosen = jnp.where(eight_rows == chunk + place, cd[...], 0.0)
        cd_s[place : place + 1, :] = jnp.sum(chosen, axis=0, keepdims=True)

    def pair(index, carried):
        cols = pl.ds(pl.multiple_of(index * LANES, LANES), LANES)
        wide = pl.ds(pl.multiple_of(index * 2 * LANES, 2 * LANES), 2 * LANES)
        raw = vraw[:, cols]
        full = jnp.concatenate([halo[:, cols], raw], axis=0)
        lagged = [raw] + [pltpu.roll(full, lag, 0)[8:] * same_s[lag - 1] for lag in range(1, 4)]
        pre_value = cb[:, cols]
        for lag in range(4):
            pre_value = pre_value + cw[lag : lag + 1, cols] * lagged[lag]
        sig = logistic(pre_value)
        value = pre_value * sig
        spread = mm(stack[...], sel[:, cols])
        step_e = spread[:CHUNK]
        carry_e = spread[CHUNK : 2 * CHUNK]
        tail_e = spread[2 * CHUNK :]
        inputs = step_e * value
        grads = grad[:, cols]
        column = mm(cumpack[...], selcol[:, wide])
        row_pair = jnp.concatenate(
            [cumt[pl.ds(2 * index, 1), :], cumt[pl.ds(2 * index + 1, 1), :]], axis=1
        )
        bias = bias_s[...]
        gram = gram_s[...]
        decays = jnp.exp(row_pair - column + jnp.concatenate([bias, bias], axis=1))
        mixing = jnp.concatenate([gram, gram], axis=1) * decays
        mix_high, mix_low = split_two(mixing)
        g_low = split_two(grads * low_half)
        g_high = split_two(grads * high_half)
        diag_high = jnp.concatenate([g_low[0], g_high[0]], axis=0)
        diag_low = jnp.concatenate([g_low[1], g_high[1]], axis=0)
        both = mm(mix_high, jnp.concatenate([diag_high, diag_low], axis=1))
        input_g = both[:, :LANES] + both[:, LANES:] + mm(mix_low, diag_high)
        held_g = state[:, cols]
        held_parts = split_two(held_g)
        input_g = input_g + tail_e * mm_three((bparts[0], bparts[1]), held_parts)
        in_parts = split_two(inputs)
        outer = mm_three_nt(in_parts, (diag_high, diag_low)) * decays
        dgram[...] += outer[:, :CHUNK] + outer[:, CHUNK:]
        reach_now = cd_s[0:1, cols]
        reach_next = cd_s[1:2, cols]
        arriving = entering[:, cols]
        held = st_now[0, :, cols] + reach_now * arriving
        next_own = jnp.where(is_end, fin[:, cols], st_next[0, :, cols])
        following = next_own + reach_next * arriving
        carried_g = split_two(carry_e * grads)
        state[:, cols] = carry_e[CHUNK - 1 :, :] * held_g + mm_three(
            (ctparts[0], ctparts[1]), carried_g
        )
        dcoup[1] += mm_three_nt(carried_g, split_two(held))
        dcoup[0] += mm_three_nt(split_two(tail_e * inputs), held_parts)
        value_g = input_g * step_e + skip[:, cols] * grads
        kept = jnp.sum(held_g * following, axis=0, keepdims=True)
        balance = grads * (mixer[:, cols] - skip[:, cols] * value) - inputs * input_g
        balance = balance + last_row * kept
        sums = jnp.concatenate([balance, input_g * value], axis=0)
        sums_parts = split_three(sums)
        pick = selt[cols, :]
        dhead[...] += mm(sums_parts[0], pick) + mm(sums_parts[1], pick) + mm(sums_parts[2], pick)
        skip_g[0:1, cols] += jnp.sum(grads * value, axis=0, keepdims=True)
        pre_g = value_g * (sig * (1.0 + pre_value * (1.0 - sig)))
        cw_g[4:5, cols] += jnp.sum(pre_g, axis=0, keepdims=True)
        raw_g = cw[0:1, cols] * pre_g
        cw_g[0:1, cols] += jnp.sum(pre_g * raw, axis=0, keepdims=True)
        none = jnp.zeros((8, LANES), f32)
        edge = none
        for lag in range(1, 4):
            cw_g[lag : lag + 1, cols] += jnp.sum(pre_g * lagged[lag], axis=0, keepdims=True)
            weighted = cw[lag : lag + 1, cols] * (pre_g * same_s[lag - 1])
            padded = jnp.concatenate([none, weighted, none], axis=0)
            turned = pltpu.roll(padded, CHUNK + 16 - lag, 0)
            raw_g = raw_g + turned[8 : 8 + CHUNK]
            edge = edge + turned[:8]
        vraw_g[:, cols] = raw_g
        vraw_g[CHUNK - 8 :, cols] += rim_s[:, cols]
        rim_s[:, cols] = edge
        vrim_g[:, cols] = edge
        return carried

    lax.fori_loop(0, heads // 2, pair, 0, unroll=4)

    total = dgram[...]
    total_parts = split_two(total)
    turned_parts = split_two(jnp.transpose(total))
    b_grad = dcoup[0] + mm_three(total_parts, (cparts[0], cparts[1]))
    c_grad = dcoup[1] + mm_three(turned_parts, (bparts[0], bparts[1]))
    coupled_g = jnp.concatenate([b_grad, c_grad], axis=1)
    pre_g = coupled_g * (csig * (1.0 + pre * (1.0 - csig)))
    ccw_g[4:5, :] += jnp.sum(pre_g, axis=0, keepdims=True)
    ccw_g[0:1, :] += jnp.sum(pre_g * craw_now, axis=0, keepdims=True)
    raw_g = ccw[0:1, :] * pre_g
    full = jnp.concatenate([coupling_halo, craw_now], axis=0)
    none = jnp.zeros((8, 2 * width), f32)
    edge = none
    for lag in range(1, 4):
        masked = pre_g * wide_same[lag]
        ccw_g[lag : lag + 1, :] += jnp.sum(
            masked * pltpu.roll(full, lag, 0)[8:], axis=0, keepdims=True
        )
        padded = jnp.concatenate([none, ccw[lag : lag + 1, :] * masked, none], axis=0)
        turned = pltpu.roll(padded, CHUNK + 16 - lag, 0)
        raw_g = raw_g + turned[8 : 8 + CHUNK]
        edge = edge + turned[:8]
    craw_g[...] = raw_g
    craw_g[CHUNK - 8 :, :] += crim_s[...]
    crim_s[...] = edge
    crim_g[...] = edge

    upper = (frame["row_ids"] <= frame["column_ids"]).astype(bf16)
    parts = split_three(dhead[:CHUNK])
    decay_g = mm(upper, parts[0]) + mm(upper, parts[1]) + mm(upper, parts[2])
    step_g = (dhead[CHUNK:] - rate[...] * decay_g) * logistic(frame["shifted"])
    sraw_g[...] = step_g
    small_g[0:1, :] += jnp.sum(step_g, axis=0, keepdims=True)
    small_g[1:2, :] += jnp.sum(-frame["step"] * decay_g, axis=0, keepdims=True)


def backward_ssd(
    marks, micro, raw, rim, inner, twice, tokens, grad, mixer, states, fin, entering, cd, pulled,
    cw, cb, ccw, ccb, sbias, rate, skip, sel, selcol, selt,
):
    width = twice // 2
    chunks = tokens // CHUNK
    heads = inner // (LANES // 2)
    eighth = CHUNK // 8
    final = (micro + 1) * chunks - 1

    def rows(count):
        return pl.BlockSpec((CHUNK, count), lambda step, *_: (chunks - 1 - step, 0))

    def part(count, start):
        return pl.BlockSpec((CHUNK, count), lambda step, *_: (final - step, start // count))

    def before(count, start):
        return pl.BlockSpec(
            (8, count),
            lambda step, *_: (jnp.maximum((final - step) * eighth - 1, 0), start // count),
        )

    def edge(count, start):
        return pl.BlockSpec((8, count), lambda *_: (0, start // count))

    def held(offset):
        return pl.BlockSpec(
            (1, width, inner),
            lambda step, *_: (jnp.minimum(chunks - 1 - step + offset, chunks - 1), 0, 0),
        )

    return pl.pallas_call(
        functools.partial(backward_kernel, heads),
        grid_spec=pltpu.PrefetchScalarGridSpec(
            num_scalar_prefetch=1,
            grid=(chunks,),
            in_specs=[
                part(inner, 0),
                before(inner, 0),
                edge(inner, 0),
                part(twice, inner),
                before(twice, inner),
                edge(twice, inner),
                part(LANES, inner + twice),
                part(inner, 0),
                part(inner, 0),
                held(0),
                held(1),
                whole((width, inner)),
                whole((width, inner)),
                whole((8, inner)),
                whole((width, inner)),
                whole(cw.shape),
                whole(cb.shape),
                whole(ccw.shape),
                whole(ccb.shape),
                whole(sbias.shape),
                whole(rate.shape),
                whole(skip.shape),
                whole(sel.shape),
                whole(selcol.shape),
                whole(selt.shape),
            ],
            out_specs=[
                rows(inner),
                whole((8, inner)),
                rows(twice),
                whole((8, twice)),
                rows(LANES),
                whole((8, inner)),
                whole((8, twice)),
                whole((8, LANES)),
                whole((8, inner)),
            ],
            scratch_shapes=[
                pltpu.VMEM((width, inner), f32),
                pltpu.VMEM((LANES, CHUNK), f32),
                pltpu.VMEM((3 * CHUNK, LANES), bf16),
                pltpu.VMEM((CHUNK, LANES), bf16),
                pltpu.VMEM((8, inner), f32),
                pltpu.VMEM((3, CHUNK, LANES), f32),
                pltpu.VMEM((CHUNK, CHUNK), f32),
                pltpu.VMEM((CHUNK, CHUNK), f32),
                pltpu.VMEM((2, CHUNK, width), bf16),
                pltpu.VMEM((2, CHUNK, width), bf16),
                pltpu.VMEM((2, width, CHUNK), bf16),
                pltpu.VMEM((8, inner), f32),
                pltpu.VMEM((8, twice), f32),
                pltpu.VMEM((CHUNK, CHUNK), f32),
                pltpu.VMEM((2, CHUNK, width), f32),
                pltpu.VMEM((2 * CHUNK, LANES), f32),
                pltpu.VMEM((8, inner), f32),
            ],
        ),
        out_shape=[
            jax.ShapeDtypeStruct((tokens, inner), f32),
            jax.ShapeDtypeStruct((8, inner), f32),
            jax.ShapeDtypeStruct((tokens, twice), f32),
            jax.ShapeDtypeStruct((8, twice), f32),
            jax.ShapeDtypeStruct((tokens, LANES), f32),
            jax.ShapeDtypeStruct((8, inner), f32),
            jax.ShapeDtypeStruct((8, twice), f32),
            jax.ShapeDtypeStruct((8, LANES), f32),
            jax.ShapeDtypeStruct((8, inner), f32),
        ],
        compiler_params=pltpu.CompilerParams(vmem_limit_bytes=48 * 1024 * 1024),
        cost_estimate=pl.CostEstimate(
            flops=60 * tokens * inner * 128 * 2, bytes_accessed=32 * tokens * inner, transcendentals=0
        ),
    )(
        marks, raw, raw, rim, raw, raw, rim, raw, grad, mixer, states, states, fin, entering,
        cd, pulled, cw, cb, ccw, ccb, sbias, rate, skip, sel, selcol, selt,
    )


def gather_kernel(arrays, shared, *refs):
    weights, tokens = refs[:arrays], refs[arrays]
    fulls, far = refs[arrays + 1 : 2 * arrays + 1], refs[2 * arrays + 1]
    refs = refs[2 * arrays + 2 :]
    ring_send, ring_recv, pair_send, pair_recv, cross_send, cross_recv, extra_send, extra_recv, local_sem = refs
    count = lax.axis_size("fsdp")
    pairs = count // 2
    own, place, side = lax.axis_index("fsdp"), lax.axis_index("context"), lax.axis_index("tensor")
    pair, member = own // 2, lax.rem(own, 2)
    rows = weights[0].shape[0]
    moved = rows - shared

    def at(offset, which):
        there = lax.rem(pair + pairs - offset, pairs)
        return 2 * there + (member if which == 0 else 1 - member)

    ahead = (2 * lax.rem(pair + 1, pairs) + member, place, side)
    behind = (2 * lax.rem(pair + pairs - 1, pairs) + member, place, side)
    partner = (2 * pair + 1 - member, place, side)
    across = (own, 1 - place, side)
    beside = (own, place, 1 - side)
    barrier = pltpu.get_barrier_semaphore()
    greeted = [ahead, behind, partner, across, beside]
    for device in greeted:
        pl.semaphore_signal(barrier, inc=1, device_id=device, device_id_type=MESH)
    pl.semaphore_wait(barrier, len(greeted))

    def part(index, j, start, size):
        return fulls[j].at[pl.ds(pl.multiple_of(index * rows + start, 16), size), :]

    moved_start = pl.multiple_of(place * shared, 16)
    shared_start = pl.multiple_of(place * moved, 16)

    started = []

    def send(src, dst, send_sem, recv_sem, device):
        copy = pltpu.make_async_remote_copy(
            src_ref=src, dst_ref=dst, send_sem=send_sem, recv_sem=recv_sem,
            device_id=device, device_id_type=MESH,
        )
        copy.start()
        started.append(copy)
        return copy

    kept = []
    for j in range(arrays):
        kept.append(
            pltpu.make_async_copy(
                weights[j], fulls[j].at[pl.ds(pl.multiple_of(own * rows, 16), rows), :], local_sem.at[j]
            )
        )
        kept[-1].start()

    def from_own(j):
        return weights[j].at[pl.ds(moved_start, moved), :]

    ring, within, crossed = {}, {}, []

    def start_ring(j, k):
        dst = part(at(k, 0), j, moved_start, moved)
        ring[j, k] = send(
            from_own(j) if k == 0 else dst, dst, ring_send.at[j, k], ring_recv.at[j, k], ahead
        )

    def start_pair(j, k):
        dst = part(at(k, 0), j, moved_start, moved)
        within[j, k] = send(
            from_own(j) if k == 0 else dst, dst, pair_send.at[j, k], pair_recv.at[j, k], partner
        )

    def start_cross(j, k, which):
        here = part(at(k, which), j, shared_start, shared)
        slot = 2 * k + which
        crossed.append(
            send(here, here, cross_send.at[j, slot], cross_recv.at[j, slot], across)
        )

    half = tokens.shape[2] // 2
    lanes = pl.ds(pl.multiple_of(side * half, 128), half)
    token_copy = send(
        tokens.at[:, :, lanes], far.at[:, :, lanes], extra_send.at[0], extra_recv.at[0], across
    )
    steps = [(j, k) for j in range(arrays) for k in range(pairs)]
    waiting = []
    forwarded = None
    for number, (j, k) in enumerate(steps):
        if k > 0:
            ring[j, k - 1].wait_recv()
        if k < pairs - 1:
            start_ring(j, k)
        start_pair(j, k)
        if k > 0:
            start_cross(j, k, 0)
        waiting.append((j, k))
        if len(waiting) > 2:
            wj, wk = waiting.pop(0)
            within[wj, wk].wait_recv()
            start_cross(wj, wk, 1)
        if number == min(pairs, len(steps) - 1):
            token_copy.wait_recv()
            forwarded = send(
                far.at[:, :, lanes], far.at[:, :, lanes], extra_send.at[1], extra_recv.at[1], beside
            )
    for wj, wk in waiting:
        within[wj, wk].wait_recv()
        start_cross(wj, wk, 1)
    forwarded.wait_recv()
    for copy in crossed:
        copy.wait_recv()
    for copy in started:
        copy.wait_send()
    for copy in kept:
        copy.wait()


def gather_weights(shards, tokens, shared, collective_id):
    rows = shards[0].shape[0]
    pairs = lax.axis_size("fsdp") // 2
    count = len(shards)
    hbm = pl.BlockSpec(memory_space=pl.ANY)
    dma = pltpu.SemaphoreType.DMA
    return pl.pallas_call(
        functools.partial(gather_kernel, count, shared),
        out_shape=[
            jax.ShapeDtypeStruct((2 * pairs * rows, shard.shape[1]), shard.dtype) for shard in shards
        ]
        + [jax.ShapeDtypeStruct(tokens.shape, tokens.dtype)],
        in_specs=[hbm] * (count + 1),
        out_specs=[hbm] * (count + 1),
        scratch_shapes=[
            dma((count, max(pairs - 1, 1))),
            dma((count, max(pairs - 1, 1))),
            dma((count, pairs)),
            dma((count, pairs)),
            dma((count, 2 * pairs)),
            dma((count, 2 * pairs)),
            dma((2,)),
            dma((2,)),
            dma((count,)),
        ],
        compiler_params=pltpu.CompilerParams(collective_id=collective_id, has_side_effects=True),
    )(*shards, tokens)


class Reduction:
    def __init__(self, rows, pairs, columns, lag):
        self.rows, self.pairs, self.columns, self.lag = rows, pairs, columns, lag
        self.shared = rows // 4
        self.moved = rows - self.shared
        self.counts = [count // LANES for count in columns]
        self.count = sum(self.counts)
        self.steps = self.count + 4 * lag

    def scratch(self):
        shared, moved, pairs, count = self.shared, self.moved, self.pairs, self.count
        cross, pair, ring = 2 * pairs * shared + 16, pairs * moved + 16, moved + 16
        i16, dma = jnp.int16, pltpu.SemaphoreType.DMA
        return [
            pltpu.VMEM((count, cross, LANES), i16),
            pltpu.VMEM((count, pair, LANES), i16),
            pltpu.VMEM((count, pairs - 1, ring, LANES), i16),
            pltpu.VMEM((count, ring, LANES), i16),
            pltpu.VMEM((2, cross, LANES), i16),
            pltpu.VMEM((2, pair, LANES), i16),
            pltpu.VMEM((2, pairs - 1, ring, LANES), i16),
            pltpu.VMEM((2, ring, LANES), i16),
            pltpu.VMEM((2, pairs, 2, shared, LANES), f32),
            pltpu.VMEM((2, pairs, moved, LANES), f32),
            pltpu.VMEM((2, pairs, moved, LANES), f32),
            pltpu.VMEM((2 * self.lag, moved, LANES), f32),
            pltpu.VMEM((2 * self.lag, moved, LANES), f32),
            pltpu.VMEM((2, self.rows, LANES), f32),
            dma((count,)),
            dma((count,)),
            dma((pairs - 1, count)),
            dma((count,)),
            dma((2,)),
            dma((2,)),
            dma((pairs - 1, 2)),
            dma((2,)),
            dma((3, 2)),
            dma((2,)),
        ]

    def bind(self, terms, outs, scratch):
        self.terms, self.outs = terms, outs
        (
            self.cross_in, self.pair_in, self.ring_in, self.last_in,
            self.cross_out, self.pair_out, self.ring_out, self.last_out,
            self.cross_term, self.pair_term, self.ring_term,
            self.kept, self.held, self.result,
            self.cross_recv, self.pair_recv, self.ring_recv, self.last_recv,
            self.cross_sent, self.pair_sent, self.ring_sent, self.last_sent,
            self.loaded, self.stored,
        ) = scratch
        self.own, self.place = lax.axis_index("fsdp"), lax.axis_index("context")
        self.side = lax.axis_index("tensor")
        self.pair, self.member = self.own // 2, lax.rem(self.own, 2)
        self.across = (self.own, 1 - self.place, self.side)
        self.partner = (2 * self.pair + 1 - self.member, self.place, self.side)
        self.inset = pl.multiple_of(self.place * (self.moved - self.shared), 16)
        self.start = pl.multiple_of(self.place * self.shared, 16)

    def peer(self, offset):
        there = lax.rem(self.pair + offset, self.pairs)
        return (2 * there + self.member, self.place, self.side)

    def greet(self):
        barrier = pltpu.get_barrier_semaphore()
        devices = [self.across, self.partner] + [self.peer(k) for k in range(1, self.pairs)]
        for device in devices:
            pl.semaphore_signal(barrier, inc=1, device_id=device, device_id_type=MESH)
        pl.semaphore_wait(barrier, len(devices))

    def cross_copy(self, chunk):
        slot = lax.rem(chunk, 2)
        return pltpu.make_async_remote_copy(
            src_ref=self.cross_out.at[slot], dst_ref=self.cross_in.at[chunk],
            send_sem=self.cross_sent.at[slot], recv_sem=self.cross_recv.at[chunk],
            device_id=self.across, device_id_type=MESH,
        )

    def pair_copy(self, chunk):
        slot = lax.rem(chunk, 2)
        return pltpu.make_async_remote_copy(
            src_ref=self.pair_out.at[slot], dst_ref=self.pair_in.at[chunk],
            send_sem=self.pair_sent.at[slot], recv_sem=self.pair_recv.at[chunk],
            device_id=self.partner, device_id_type=MESH,
        )

    def ring_copy(self, chunk, offset):
        slot = lax.rem(chunk, 2)
        return pltpu.make_async_remote_copy(
            src_ref=self.ring_out.at[slot, offset - 1], dst_ref=self.ring_in.at[chunk, offset - 1],
            send_sem=self.ring_sent.at[offset - 1, slot],
            recv_sem=self.ring_recv.at[offset - 1, chunk],
            device_id=self.peer(offset), device_id_type=MESH,
        )

    def last_copy(self, chunk):
        slot = lax.rem(chunk, 2)
        return pltpu.make_async_remote_copy(
            src_ref=self.last_out.at[slot], dst_ref=self.last_in.at[chunk],
            send_sem=self.last_sent.at[slot], recv_sem=self.last_recv.at[chunk],
            device_id=self.across, device_id_type=MESH,
        )

    def load_copy(self, stage, term, cols, slot):
        if stage == 0:
            rows = pl.ds(pl.multiple_of((1 - self.place) * self.moved, 16), self.shared)
            src, dst = term.at[:, :, rows, cols], self.cross_term.at[slot]
        elif stage == 1:
            src = term.at[:, 1 - self.member, pl.ds(self.start, self.moved), cols]
            dst = self.pair_term.at[slot]
        else:
            src = term.at[:, self.member, pl.ds(self.start, self.moved), cols]
            dst = self.ring_term.at[slot]
        return pltpu.make_async_copy(src, dst, self.loaded.at[stage, slot])

    def each_array(self, chunk, act):
        first = 0
        for number, count in enumerate(self.counts):
            inside = (chunk >= first) & (chunk < first + count)
            offset = first

            @pl.when(inside)
            def _(number=number, offset=offset):
                act(number, pl.ds(pl.multiple_of((chunk - offset) * LANES, LANES), LANES))

            first += count

    def load(self, stage, chunk):
        @pl.when((chunk >= 0) & (chunk < self.count))
        def _():
            self.each_array(
                chunk,
                lambda number, cols: self.load_copy(
                    stage, self.terms[number], cols, lax.rem(chunk, 2)
                ).start(),
            )

    def loaded_now(self, stage, chunk):
        self.load_copy(stage, self.terms[0], pl.ds(0, LANES), lax.rem(chunk, 2)).wait()

    @staticmethod
    def encode(value, out, place):
        count = value.shape[0]
        peak = jnp.maximum(jnp.max(jnp.abs(value), axis=0, keepdims=True), 1e-30)
        exponent = jnp.ceil(jnp.log(peak) * 1.4426950408889634)
        factor = jnp.exp(exponent * -0.6931471805599453) * 32000.0
        out[place + (pl.ds(0, count), slice(None))] = (
            jnp.round(value * factor).astype(jnp.int32).astype(jnp.int16)
        )
        out[place + (pl.ds(count, 16), slice(None))] = (
            jnp.broadcast_to(exponent, (16, LANES)).astype(jnp.int32).astype(jnp.int16)
        )

    @staticmethod
    def unit(ref, place, count):
        exponents = ref[place + (pl.ds(count, 16), slice(None))].astype(jnp.int32).astype(f32)
        return jnp.exp(exponents[:1] * 0.6931471805599453) * (1.0 / 32000.0)

    @staticmethod
    def decode(ref, place, first, count, unit):
        first = pl.multiple_of(first, 16) if not isinstance(first, int) else first
        return ref[place + (pl.ds(first, count), slice(None))].astype(jnp.int32).astype(f32) * unit

    def step(self, number):
        lag, pairs, shared, moved = self.lag, self.pairs, self.shared, self.moved

        @pl.when(number == 0)
        def _():
            self.load(0, number)

        self.load(0, number + 1)
        self.load(1, number + 1 - lag)
        self.load(2, number + 1 - 2 * lag)

        def stage(index, act):
            chunk = number - index * lag

            @pl.when((chunk >= 0) & (chunk < self.count))
            def _():
                act(chunk, lax.rem(chunk, 2))

        def cross(chunk, slot):
            self.loaded_now(0, chunk)

            @pl.when(chunk >= 2)
            def _():
                self.cross_copy(chunk - 2).wait_send()

            value = self.cross_term[slot].reshape(2 * pairs * shared, LANES)
            self.encode(value, self.cross_out, (slot,))
            self.cross_copy(chunk).start()

        def pair(chunk, slot):
            self.loaded_now(1, chunk)
            self.cross_copy(chunk).wait_recv()

            @pl.when(chunk >= 2)
            def _():
                self.pair_copy(chunk - 2).wait_send()

            unit = self.unit(self.cross_in, (chunk,), 2 * pairs * shared)
            for there in range(pairs):
                first = (2 * there + 1 - self.member) * shared
                self.pair_term[slot, there, pl.ds(self.inset, shared), :] += self.decode(
                    self.cross_in, (chunk,), first, shared, unit
                )
            value = self.pair_term[slot].reshape(pairs * moved, LANES)
            self.encode(value, self.pair_out, (slot,))
            self.pair_copy(chunk).start()

        def ring(chunk, slot):
            self.loaded_now(2, chunk)
            self.pair_copy(chunk).wait_recv()

            @pl.when(chunk >= 2)
            def _():
                for offset in range(1, pairs):
                    self.ring_copy(chunk - 2, offset).wait_send()

            cross_unit = self.unit(self.cross_in, (chunk,), 2 * pairs * shared)
            pair_unit = self.unit(self.pair_in, (chunk,), pairs * moved)
            for offset in list(range(1, pairs)) + [0]:
                there = lax.rem(self.pair + offset, pairs)
                first = (2 * there + self.member) * shared
                self.ring_term[slot, there, pl.ds(self.inset, shared), :] += self.decode(
                    self.cross_in, (chunk,), first, shared, cross_unit
                )
                value = self.ring_term[slot, there] + self.decode(
                    self.pair_in, (chunk,), there * moved, moved, pair_unit
                )
                if offset:
                    self.encode(value, self.ring_out, (slot, offset - 1))
                    self.ring_copy(chunk, offset).start()
                else:
                    self.kept[lax.rem(chunk, 2 * lag)] = value

        def last(chunk, slot):
            for offset in range(1, pairs):
                self.ring_copy(chunk, offset).wait_recv()

            @pl.when(chunk >= 2)
            def _():
                self.last_copy(chunk - 2).wait_send()

            total = self.kept[lax.rem(chunk, 2 * lag)]
            for offset in range(1, pairs):
                place = (chunk, offset - 1)
                total = total + self.decode(
                    self.ring_in, place, 0, moved, self.unit(self.ring_in, place, moved)
                )
            self.encode(total, self.last_out, (slot,))
            self.held[lax.rem(chunk, 2 * lag)] = self.decode(
                self.last_out, (slot,), 0, moved, self.unit(self.last_out, (slot,), moved)
            )
            self.last_copy(chunk).start()

        def write_copy(number, cols, slot):
            return pltpu.make_async_copy(
                self.result.at[slot], self.outs[number].at[:, cols], self.stored.at[slot]
            )

        def write(chunk, slot):
            self.last_copy(chunk).wait_recv()

            @pl.when(chunk >= 2)
            def _():
                write_copy(0, pl.ds(0, LANES), slot).wait()

            mine = self.held[lax.rem(chunk, 2 * lag)]
            other = self.decode(
                self.last_in, (chunk,), 0, moved, self.unit(self.last_in, (chunk,), moved)
            )
            low = jnp.where(self.place == 0, mine, other)
            high = jnp.where(self.place == 0, other, mine)
            self.result[slot, pl.ds(0, shared), :] = low[:shared]
            self.result[slot, pl.ds(shared, moved - shared), :] = (
                low[shared:] + high[: moved - shared]
            )
            self.result[slot, pl.ds(moved, shared), :] = high[moved - shared :]
            self.each_array(chunk, lambda which, cols: write_copy(which, cols, slot).start())

        stage(4, write)
        stage(3, last)
        stage(2, ring)
        stage(1, pair)
        stage(0, cross)

        @pl.when(number == self.steps - 1)
        def _():
            for slot in range(2):
                write_copy(0, pl.ds(0, LANES), slot).wait()
                self.cross_copy(jnp.int32(self.count - 2 + slot)).wait_send()
                self.pair_copy(jnp.int32(self.count - 2 + slot)).wait_send()
                self.last_copy(jnp.int32(self.count - 2 + slot)).wait_send()
                for offset in range(1, pairs):
                    self.ring_copy(jnp.int32(self.count - 2 + slot), offset).wait_send()


def reduce_kernel(plan, arrays, *refs):
    plan.bind(refs[:arrays], refs[arrays : 2 * arrays], refs[2 * arrays :])
    plan.greet()

    def body(number, carried):
        plan.step(number)
        return carried

    lax.fori_loop(0, plan.steps, body, 0)


def reduce_terms(terms, lag, collective_id):
    pairs = lax.axis_size("fsdp") // 2
    rows = terms[0].shape[0] // (2 * pairs)
    columns = [term.shape[1] for term in terms]
    plan = Reduction(rows, pairs, columns, lag)
    hbm = pl.BlockSpec(memory_space=pl.ANY)
    arrays = len(terms)
    return pl.pallas_call(
        functools.partial(reduce_kernel, plan, arrays),
        out_shape=[jax.ShapeDtypeStruct((rows, count), f32) for count in columns],
        in_specs=[hbm] * arrays,
        out_specs=[hbm] * arrays,
        scratch_shapes=plan.scratch(),
        compiler_params=pltpu.CompilerParams(
            collective_id=collective_id, has_side_effects=True, vmem_limit_bytes=58 * 1024 * 1024
        ),
    )(*[term.reshape(pairs, 2, rows, -1) for term in terms])


def passed_along(value, axis, steps):
    count = lax.axis_size(axis)
    initial, last = (max(0, -steps), min(count, count - steps))
    return lax.ppermute(value, axis, [(source, source + steps) for source in range(initial, last)])


def paired(value, axis):
    count = lax.axis_size(axis)
    return lax.ppermute(value, axis, [(source, source ^ 1) for source in range(count)])


def ring_shift(value, axis, steps):
    count = lax.axis_size(axis)
    return lax.ppermute(
        value, axis, [(source, (source + 2 * steps) % count) for source in range(count)]
    )


def summed_everywhere(values):
    sizes = [value.size for value in values]
    shapes = [value.shape for value in values]
    flat = jnp.concatenate([value.reshape(-1) for value in values])
    count = flat.shape[0]
    flat = jnp.pad(flat, (0, -count % 1024)).reshape(-1, 128)
    for axis in ("context", "fsdp"):
        members = lax.axis_size(axis)
        reach = 1
        while reach < members:
            flat = flat + lax.ppermute(
                flat, axis, [(source, source ^ reach) for source in range(members)]
            )
            reach *= 2
    flat = flat.reshape(-1)
    results, start = [], 0
    for size, shape in zip(sizes, shapes):
        results.append(flat[start : start + size].reshape(shape))
        start += size
    return results


def chained(own, factor, steps):
    arriving = passed_along(own, "context", steps)
    for _ in range(lax.axis_size("context") - 2):
        arriving = passed_along(factor * arriving + own, "context", steps)
    return arriving


def shards(
    tokens,
    lengths,
    block_order,
    cotangent,
    norm_gain,
    in_weight,
    coupling_weight,
    step_weight,
    out_weight,
    conv_weight,
    conv_bias,
    coupling_conv,
    coupling_bias,
    step_bias,
    decay_rate,
    skip_gain,
    inner_gain,
):
    highest = lax.Precision.HIGHEST
    micros = tokens.shape[0]
    count = tokens.shape[2]
    model = tokens.shape[3]
    inner = inner_gain.shape[0]
    heads = step_bias.shape[0]
    head_size = inner // heads
    twice = coupling_weight.shape[1]
    width = twice // 2
    blocks_row = block_order.shape[2]
    block_len = count * lax.axis_size("context") // blocks_row
    own_blocks = count // block_len
    inner_total = inner * lax.axis_size("tensor")
    side = lax.axis_index("tensor")
    place = lax.axis_index("context")
    base = place * count
    shard_rows = in_weight.shape[0]

    narrow, wide_columns = selectors(heads, head_size)
    sel = jnp.asarray(narrow, bf16)
    selcol = jnp.asarray(wide_columns, bf16)
    selt = jnp.asarray(narrow[:heads].T, bf16)
    selt = jnp.pad(selt, ((0, 0), (0, LANES - heads)))

    lead = jnp.concatenate(
        [
            in_weight[:, 1, :],
            coupling_weight,
            jnp.pad(step_weight, ((0, 0), (0, LANES - heads))),
        ],
        axis=1,
    )
    shared_rows = max(shard_rows * 5 // 16 // 16 * 16, 16)
    lead_full, gate_full, out_full, far = gather_weights(
        [lead, in_weight[:, 0, :], jnp.transpose(out_weight)], tokens[:, 0], shared_rows, 1
    )

    near = tokens[:, 0].reshape(micros, own_blocks, block_len, model)
    far = far.reshape(micros, own_blocks, block_len, model)
    everything = jnp.where(
        place == 0, jnp.concatenate([near, far], 1), jnp.concatenate([far, near], 1)
    )
    slots = jnp.arange(blocks_row, dtype=jnp.int32)
    picked = []
    for micro in range(micros):
        for own in range(own_blocks):
            wanted = place * own_blocks + own
            slot = jnp.sum(jnp.where(block_order[micro, 0] == wanted, slots, 0))
            picked.append(
                lax.dynamic_slice(
                    everything, (micro, slot, 0, 0), (1, 1, block_len, model)
                ).reshape(block_len, model)
            )
    x_input = jnp.concatenate(picked, axis=0)
    x_float = x_input.astype(f32)
    inv_rms = lax.rsqrt(jnp.mean(x_float * x_float, axis=-1, keepdims=True) + epsilon)
    normed = (x_float * inv_rms * norm_gain).astype(bf16)

    first_end = lengths[:, 0, 0]
    second_end = first_end + lengths[:, 0, 1]
    marks = [
        jnp.stack([first_end[micro], second_end[micro], base]).astype(jnp.int32)
        for micro in range(micros)
    ]
    positions = base + jnp.arange(count, dtype=jnp.int32)
    keep = jnp.concatenate([(positions < second_end[micro]) for micro in range(micros)])
    keep = keep.astype(f32)[:, None]

    cw, cb = conv_weight, conv_bias.reshape(1, inner)
    ccw, ccb = coupling_conv, coupling_bias.reshape(1, twice)
    sbias = jnp.pad(step_bias, (0, LANES - heads)).reshape(1, LANES)
    rate = jnp.pad(decay_rate, (0, LANES - heads)).reshape(1, LANES)
    skip = jnp.repeat(skip_gain, head_size).reshape(1, inner)

    raw = jnp.dot(normed, lead_full, preferred_element_type=f32)
    rims = passed_along(
        jnp.stack([raw[(micro + 1) * count - 8 : (micro + 1) * count] for micro in range(micros)]),
        "context",
        1,
    )
    forwards = []
    for micro in range(micros):
        forwards.append(
            forward_ssd(
                marks[micro], micro, raw, rims[micro], inner, twice, count,
                cw, cb, ccw, ccb, sbias, rate, skip, sel, selcol,
            )
        )
    entering = [
        chained(forwards[micro][2], forwards[micro][5][count // CHUNK], 1)
        for micro in range(micros)
    ]
    gate_in = jnp.dot(normed, gate_full, preferred_element_type=f32)
    cot = cotangent[:, 0].reshape(micros * count, model)
    out_grad = cot * keep.astype(bf16)
    norm_grad = jnp.dot(out_grad, out_full, preferred_element_type=f32)

    mixers = []
    for micro in range(micros):
        y_own, _, _, coupled, carry, _ = forwards[micro]
        mixers.append(
            y_own + carry * jnp.dot(coupled[:, width:], entering[micro], precision=highest)
        )
    mixer = jnp.concatenate(mixers, axis=0)
    gate_sig = jax.nn.sigmoid(gate_in)
    gate_act = gate_in * gate_sig
    gated = mixer * gate_act
    scaled_grad = norm_grad * inner_gain
    row_sums = jnp.stack([jnp.sum(gated * gated, axis=-1), jnp.sum(scaled_grad * gated, axis=-1)])
    row_sums = row_sums + paired(row_sums, "tensor")
    inv_norm = lax.rsqrt(row_sums[0] / inner_total + epsilon)[:, None]
    inner_dot = row_sums[1][:, None]
    gated_norm = (gated * inv_norm * inner_gain).astype(bf16)
    inner_gain_grad = jnp.sum(norm_grad * gated * inv_norm, axis=0)
    gated_grad = scaled_grad * inv_norm - gated * (inner_dot * inv_norm**3 / inner_total)
    gate_grad = (gated_grad * mixer * gate_sig * (1.0 + gate_in * (1.0 - gate_sig))).astype(bf16)
    mixer_grad = gated_grad * gate_act

    pulled = []
    for micro in range(micros):
        part = slice(micro * count, (micro + 1) * count)
        own_pull = lax.dot_general(
            forwards[micro][3][:, width:],
            forwards[micro][4] * mixer_grad[part],
            (((0,), (0,)), ((), ())),
            precision=highest,
        )
        pulled.append(chained(own_pull, forwards[micro][5][count // CHUNK], -1))

    branch = contract_cols(gated_norm, out_full)
    branch = branch + paired(branch, "tensor")
    block_out = (x_float + keep * branch).astype(bf16)

    out_term = contract_rows(out_grad, gated_norm)
    gate_term = contract_rows(normed, gate_grad)

    backs = []
    for micro in range(micros):
        y_own, states, final, coupled, carry, reach = forwards[micro]
        backs.append(
            backward_ssd(
                marks[micro], micro, raw, rims[micro], inner, twice, count, mixer_grad, mixer,
                states, final, entering[micro], reach, pulled[micro],
                cw, cb, ccw, ccb, sbias, rate, skip, sel, selcol, selt,
            )
        )
    edges = passed_along(
        jnp.stack([jnp.concatenate([back[1], back[3]], axis=1) for back in backs]), "context", -1
    )
    tail_pad = ((count - 8, 0), (0, 0))
    coupling_raw_grad = jnp.stack(
        [back[2] + jnp.pad(edges[micro][:, inner:], tail_pad) for micro, back in enumerate(backs)]
    )
    coupling_raw_grad = coupling_raw_grad + paired(coupling_raw_grad, "tensor")
    lane_ids = jnp.arange(twice, dtype=jnp.int32)
    own_lanes = ((lane_ids // width) == side).astype(bf16)
    coupling_low = coupling_raw_grad.astype(bf16) * own_lanes
    lead_grad = jnp.concatenate(
        [
            jnp.concatenate(
                [
                    (back[0] + jnp.pad(edges[micro][:, :inner], tail_pad)).astype(bf16),
                    coupling_low[micro],
                    back[4].astype(bf16),
                ],
                axis=1,
            )
            for micro, back in enumerate(backs)
        ],
        axis=0,
    )
    out_shard, gate_shard, lead_shard = reduce_terms(
        [out_term, gate_term, contract_rows(normed, lead_grad)], 2, 2
    )
    normed_part = contract_cols(gate_grad, gate_full) + contract_cols(lead_grad, lead_full)
    normed_grad = normed_part + paired(normed_part, "tensor")
    x_hat = x_float * inv_rms
    hat_grad = normed_grad * norm_gain
    input_grad = (
        cot.astype(f32)
        + inv_rms * (hat_grad - x_hat * jnp.mean(hat_grad * x_hat, axis=-1, keepdims=True))
    ).astype(bf16)
    norm_gain_grad = jnp.sum(normed_grad * x_hat, axis=0)

    value_sums = sum(back[5] for back in backs)
    coupling_sums = sum(back[6] for back in backs)
    small_sums = sum(back[7] for back in backs)
    skip_sums = sum(back[8] for back in backs)[0].reshape(heads, head_size).sum(axis=1)
    coupling_sums = coupling_sums + paired(coupling_sums, "tensor")
    (value_all, coupling_all, small_all, skip_all, inner_all, norm_all) = summed_everywhere(
        [value_sums[:5], coupling_sums[:5], small_sums[:2], skip_sums, inner_gain_grad, norm_gain_grad]
    )
    coupling_shard = lead_shard[:, inner : inner + twice]
    coupling_shard = coupling_shard + paired(coupling_shard, "tensor")
    return (
        block_out.reshape(micros, 1, count, model),
        input_grad.reshape(micros, 1, count, model),
        norm_all,
        jnp.stack([gate_shard, lead_shard[:, :inner]], axis=1),
        coupling_shard,
        lead_shard[:, inner + twice : inner + twice + heads],
        jnp.transpose(out_shard),
        value_all[:4],
        value_all[4],
        coupling_all[:4],
        coupling_all[4],
        small_all[0, :heads],
        small_all[1, :heads],
        skip_all,
        inner_all,
    )


def contract_rows(left, right):
    return lax.dot_general(
        left, right, (((0,), (0,)), ((), ())), preferred_element_type=jnp.float32
    )


def contract_cols(left, right):
    return lax.dot_general(
        left, right, (((1,), (1,)), ((), ())), preferred_element_type=jnp.float32
    )


def solution(mesh):
    return jax.shard_map(
        shards,
        mesh=mesh,
        in_specs=(
            P(None, "fsdp", "context", None),
            P(None, "fsdp", None),
            P(None, "fsdp", None),
            P(None, "fsdp", "context", None),
            P(),
            P("fsdp", None, "tensor"),
            P("fsdp", None),
            P("fsdp", "tensor"),
            P("tensor", "fsdp"),
            P(None, "tensor"),
            P("tensor"),
            P(),
            P(),
            P("tensor"),
            P("tensor"),
            P("tensor"),
            P("tensor"),
        ),
        out_specs=(
            P(None, "fsdp", "context", None),
            P(None, "fsdp", "context", None),
            P(),
            P("fsdp", None, "tensor"),
            P("fsdp", None),
            P("fsdp", "tensor"),
            P("tensor", "fsdp"),
            P(None, "tensor"),
            P("tensor"),
            P(),
            P(),
            P("tensor"),
            P("tensor"),
            P("tensor"),
            P("tensor"),
        ),
        check_vma=False,
    )
```

```python
import functools

import jax
import jax.numpy as jnp
import numpy as np
from jax import lax
from jax.experimental import pallas as pl
from jax.experimental.pallas import tpu as pltpu
from jax.sharding import PartitionSpec as P

CHUNK = 128
LANES = 128
MESH = pl.DeviceIdType.MESH
f32 = jnp.float32
bf16 = jnp.bfloat16
epsilon = 1e-05


def split_two(value):
    high = value.astype(bf16)
    return high, (value - high.astype(f32)).astype(bf16)


def split_three(value):
    high = value.astype(bf16)
    rest = value - high.astype(f32)
    middle = rest.astype(bf16)
    return high, middle, (rest - middle.astype(f32)).astype(bf16)


def mm(left, right):
    return jnp.dot(left, right, preferred_element_type=f32)


def mm_nt(left, right):
    return lax.dot_general(left, right, (((1,), (1,)), ((), ())), preferred_element_type=f32)


def mm_three(left, right):
    wide = mm(left[0], jnp.concatenate([right[0], right[1]], axis=1))
    count = right[0].shape[1]
    return wide[:, :count] + wide[:, count:] + mm(left[1], right[0])


def mm_three_nt(left, right):
    return mm_nt(left[0], right[0]) + mm_nt(left[0], right[1]) + mm_nt(left[1], right[0])


def packed_parts(value, heads):
    high, middle, lowest = split_three(value)
    joined = (
        high.astype(f32)
        + pltpu.roll(middle.astype(f32), heads, 1)
        + pltpu.roll(lowest.astype(f32), 2 * heads, 1)
    )
    return joined.astype(bf16)


def segment_at(position, first_end, second_end):
    first_part = (position >= first_end).astype(jnp.int32)
    second_part = (position >= second_end).astype(jnp.int32)
    return jnp.where(position < 0, -1, first_part + second_part)


def chunk_frame(marks, chunk, step_raw, step_bias, rate, heads):
    first_end, second_end, base = marks[0], marks[1], marks[2]
    start = base + chunk * CHUNK
    rows = start + lax.broadcasted_iota(jnp.int32, (CHUNK, LANES), 0)
    columns = start + lax.broadcasted_iota(jnp.int32, (CHUNK, CHUNK), 1)
    seg_rows = segment_at(rows, first_end, second_end)
    seg_columns = segment_at(columns, first_end, second_end)
    seg_prior = segment_at(start - 1, first_end, second_end)
    seg_last = segment_at(start + CHUNK - 1, first_end, second_end)
    same = [
        (segment_at(rows - lag, first_end, second_end) == seg_rows).astype(f32) for lag in range(4)
    ]
    shifted = step_raw + step_bias
    step = jnp.maximum(shifted, 0.0) + jnp.log1p(jnp.exp(-jnp.abs(shifted)))
    lanes = lax.broadcasted_iota(jnp.int32, (CHUNK, LANES), 1)
    step = jnp.where(lanes < heads, step, 0.0)
    log_decay = -step * rate
    row_ids = lax.broadcasted_iota(jnp.int32, (CHUNK, CHUNK), 0)
    column_ids = lax.broadcasted_iota(jnp.int32, (CHUNK, CHUNK), 1)
    lower = (row_ids >= column_ids).astype(bf16)
    parts = split_three(log_decay)
    cumulative = mm(lower, parts[0]) + mm(lower, parts[1]) + mm(lower, parts[2])
    last = cumulative[CHUNK - 1 :, :]
    carry = jnp.exp(cumulative) * (seg_rows == seg_prior).astype(f32)
    tail = jnp.exp(last - cumulative) * (seg_rows == seg_last).astype(f32)
    live = lanes < heads
    carry = jnp.where(live, carry, 0.0)
    tail = jnp.where(live, tail, 0.0)
    return dict(
        seg_rows=seg_rows,
        seg_columns=seg_columns,
        row_ids=row_ids,
        column_ids=column_ids,
        same=same,
        step=step,
        shifted=shifted,
        cumulative=cumulative,
        carry=carry,
        tail=tail,
    )


def conv_sum(current, halo, weights, biases, same):
    full = jnp.concatenate([halo, current], axis=0)
    total = biases + weights(0) * current
    for lag in range(1, 4):
        total = total + weights(lag) * (pltpu.roll(full, lag, 0)[8:] * same[lag])
    return total


def logistic(value):
    return 1.0 / (1.0 + jnp.exp(-value))


def forward_kernel(
    heads,
    extra,
    marks,
    vraw,
    vprev,
    vrim,
    craw,
    cprev,
    crim,
    sraw,
    cw,
    cb,
    ccw,
    ccb,
    sbias,
    rate,
    skip,
    sel,
    selcol,
    *refs,
):
    y_out, st_out, fin_out, bc_out, carry_out, cd_out = refs[extra : extra + 6]
    (state, cumt, stack, cumpack, halo, same_s, bias_s, gram_s, cd_s, cparts, btparts) = refs[
        extra + 6 :
    ]
    chunk = pl.program_id(0)
    chunks = pl.num_programs(0)
    width = state.shape[0]

    @pl.when(chunk == 0)
    def _():
        state[...] = jnp.zeros_like(state)
        cd_s[...] = jnp.ones_like(cd_s)
        cd_out[...] = jnp.zeros_like(cd_out)
        halo[...] = vrim[...]

    @pl.when(chunk > 0)
    def _():
        halo[...] = vprev[...]

    frame = chunk_frame(marks, chunk, sraw[...], sbias[...], rate[...], heads)
    same = frame["same"]
    for lag in range(1, 4):
        same_s[lag - 1] = same[lag]
    joined = (frame["seg_rows"] == frame["seg_columns"]) & (frame["row_ids"] >= frame["column_ids"])
    bias_s[...] = jnp.where(joined, 0.0, -1e30)
    stack[0:CHUNK, :] = packed_parts(frame["step"], heads)
    stack[CHUNK : 2 * CHUNK, :] = packed_parts(frame["carry"], heads)
    stack[2 * CHUNK : 3 * CHUNK, :] = packed_parts(frame["tail"], heads)
    cumpack[...] = packed_parts(frame["cumulative"], heads)
    cumt[...] = jnp.transpose(frame["cumulative"])
    coupling_halo = jnp.where(chunk == 0, crim[...], cprev[...])
    wide_same = [None] + [jnp.concatenate([same[lag], same[lag]], axis=1) for lag in range(1, 4)]
    pre = conv_sum(
        craw[...], coupling_halo, lambda lag: ccw[lag : lag + 1, :], ccb[...], wide_same
    )
    coupled = pre * logistic(pre)
    bc_out[...] = coupled
    b_part = split_two(coupled[:, :width])
    c_part = split_two(coupled[:, width:])
    gram_s[...] = mm_three_nt(c_part, b_part)
    cparts[0] = c_part[0]
    cparts[1] = c_part[1]
    turned = jnp.transpose(coupled[:, :width])
    bt_part = split_two(turned)
    btparts[0] = bt_part[0]
    btparts[1] = bt_part[1]
    lane = lax.broadcasted_iota(jnp.int32, (CHUNK, LANES), 1)
    low_half = (lane < LANES // 2).astype(f32)
    high_half = 1.0 - low_half

    def pair(index, carried):
        cols = pl.ds(pl.multiple_of(index * LANES, LANES), LANES)
        wide = pl.ds(pl.multiple_of(index * 2 * LANES, 2 * LANES), 2 * LANES)
        pre_value = conv_sum(
            vraw[:, cols],
            halo[:, cols],
            lambda lag: cw[lag : lag + 1, cols],
            cb[:, cols],
            [None] + [same_s[lag - 1] for lag in range(1, 4)],
        )
        value = pre_value * logistic(pre_value)
        spread = mm(stack[...], sel[:, cols])
        step_e = spread[:CHUNK]
        carry_e = spread[CHUNK : 2 * CHUNK]
        tail_e = spread[2 * CHUNK :]
        inputs = step_e * value
        column = mm(cumpack[...], selcol[:, wide])
        row_pair = jnp.concatenate(
            [cumt[pl.ds(2 * index, 1), :], cumt[pl.ds(2 * index + 1, 1), :]], axis=1
        )
        bias = bias_s[...]
        gram = gram_s[...]
        mixing = jnp.concatenate([gram, gram], axis=1) * jnp.exp(
            column - row_pair + jnp.concatenate([bias, bias], axis=1)
        )
        mix_high, mix_low = split_two(mixing)
        in_low = split_two(inputs * low_half)
        in_high = split_two(inputs * high_half)
        diag_high = jnp.concatenate([in_low[0], in_high[0]], axis=0)
        diag_low = jnp.concatenate([in_low[1], in_high[1]], axis=0)
        both = mm(mix_high, jnp.concatenate([diag_high, diag_low], axis=1))
        inside = both[:, :LANES] + both[:, LANES:] + mm(mix_low, diag_high)
        held = state[:, cols]
        from_state = mm_three((cparts[0], cparts[1]), split_two(held))
        y_out[:, cols] = inside + carry_e * from_state + skip[:, cols] * value
        fresh = mm_three((btparts[0], btparts[1]), split_two(tail_e * inputs))
        through = carry_e[CHUNK - 1 :, :]
        st_out[0, :, cols] = held
        renewed = through * held + fresh
        state[:, cols] = renewed
        fin_out[:, cols] = renewed
        reach = cd_s[0:1, cols]
        carry_out[:, cols] = carry_e * reach
        cd_s[0:1, cols] = reach * through
        return carried

    eight_rows = lax.broadcasted_iota(jnp.int32, cd_out.shape, 0)
    cd_out[...] = jnp.where(eight_rows == chunk, cd_s[0:1, :], cd_out[...])
    lax.fori_loop(0, heads // 2, pair, 0, unroll=4)
    cd_out[...] = jnp.where(eight_rows == chunk + 1, cd_s[0:1, :], cd_out[...])


def selectors(heads, head_size):
    inner = heads * head_size
    head_of_lane = np.arange(inner) // head_size
    narrow = np.zeros((LANES, inner), np.float32)
    wide = np.zeros((LANES, heads * LANES), np.float32)
    head_of_wide = np.arange(heads * LANES) // LANES
    for part in range(3):
        narrow[part * heads + head_of_lane, np.arange(inner)] = 1.0
        wide[part * heads + head_of_wide, np.arange(heads * LANES)] = 1.0
    return narrow, wide


def whole(shape):
    return pl.BlockSpec(shape, lambda index, *_: (0,) * len(shape))


def forward_ssd(
    marks, micro, micros, before_this, raw, rim, inner, twice, tokens,
    cw, cb, ccw, ccb, sbias, rate, skip, sel, selcol,
):
    width = twice // 2
    chunks = tokens // CHUNK
    heads = inner // (LANES // 2)
    eighth = CHUNK // 8
    initial = micro * chunks

    def part(count, start):
        return pl.BlockSpec((CHUNK, count), lambda chunk, *_: (initial + chunk, start // count))

    def before(count, start):
        return pl.BlockSpec(
            (8, count),
            lambda chunk, *_: (jnp.maximum((initial + chunk) * eighth - 1, 0), start // count),
        )

    def edge(count, start):
        return pl.BlockSpec((8, count), lambda *_: (0, start // count))

    return pl.pallas_call(
        functools.partial(forward_kernel, heads, len(before_this)),
        grid_spec=pltpu.PrefetchScalarGridSpec(
            num_scalar_prefetch=1,
            grid=(chunks,),
            in_specs=[
                part(inner, 0),
                before(inner, 0),
                edge(inner, 0),
                part(twice, inner),
                before(twice, inner),
                edge(twice, inner),
                part(LANES, inner + twice),
                whole(cw.shape),
                whole(cb.shape),
                whole(ccw.shape),
                whole(ccb.shape),
                whole(sbias.shape),
                whole(rate.shape),
                whole(skip.shape),
                whole(sel.shape),
                whole(selcol.shape),
            ]
            + [pl.BlockSpec(memory_space=pl.ANY)] * len(before_this),
            out_specs=[
                part(inner, 0),
                pl.BlockSpec((1, width, inner), lambda chunk, *_: (initial + chunk, 0, 0)),
                whole((width, inner)),
                part(twice, 0),
                part(inner, 0),
                pl.BlockSpec((None, 8, inner), lambda *_: (micro, 0, 0)),
            ],
            scratch_shapes=[
                pltpu.VMEM((width, inner), f32),
                pltpu.VMEM((LANES, CHUNK), f32),
                pltpu.VMEM((3 * CHUNK, LANES), bf16),
                pltpu.VMEM((CHUNK, LANES), bf16),
                pltpu.VMEM((8, inner), f32),
                pltpu.VMEM((3, CHUNK, LANES), f32),
                pltpu.VMEM((CHUNK, CHUNK), f32),
                pltpu.VMEM((CHUNK, CHUNK), f32),
                pltpu.VMEM((8, inner), f32),
                pltpu.VMEM((2, CHUNK, width), bf16),
                pltpu.VMEM((2, width, CHUNK), bf16),
            ],
        ),
        out_shape=[
            jax.ShapeDtypeStruct((micros * tokens, inner), f32),
            jax.ShapeDtypeStruct((micros * chunks, width, inner), f32),
            jax.ShapeDtypeStruct((width, inner), f32),
            jax.ShapeDtypeStruct((micros * tokens, twice), f32),
            jax.ShapeDtypeStruct((micros * tokens, inner), f32),
            jax.ShapeDtypeStruct((micros, 8, inner), f32),
        ],
        input_output_aliases={
            17 + number: where for number, where in enumerate([0, 1, 3, 4, 5][: len(before_this)])
        },
        compiler_params=pltpu.CompilerParams(vmem_limit_bytes=40 * 1024 * 1024),
        cost_estimate=pl.CostEstimate(
            flops=20 * tokens * inner * 128 * 2, bytes_accessed=24 * tokens * inner, transcendentals=0
        ),
    )(
        marks, raw, raw, rim, raw, raw, rim, raw, cw, cb, ccw, ccb, sbias, rate, skip, sel, selcol,
        *before_this,
    )


def backward_kernel(heads, chunks, plan, *refs):
    (
        marks, vraw, vprev, vrim, craw, cprev, crim, sraw, grad, mixer, st_now, st_next, fin,
        entering, cd, pulled, cw, cb, ccw, ccb, sbias, rate, skip, sel, selcol, selt,
    ) = refs[:26]
    arrays = len(plan.counts)
    refs = refs[26:]
    terms, refs = refs[:arrays], refs[arrays:]
    (
        lead_g, vtail_g, vrim_g, craw_g, crim_g, cw_g, ccw_g, small_g, skip_g,
    ) = refs[:9]
    outs, refs = refs[9 : 9 + arrays], refs[9 + arrays :]
    (
        state, cumt, stack, cumpack, halo, same_s, bias_s, gram_s, cparts, bparts, ctparts,
        rim_s, crim_s, dgram, dcoup, dhead, cd_s,
    ) = refs[:17]
    plan.bind(terms, outs, refs[17:])
    grid_step = pl.program_id(0)
    step_id = lax.rem(grid_step, chunks)
    micro = grid_step // chunks
    chunk = chunks - 1 - step_id
    width = state.shape[0]
    inner = state.shape[1]
    per_step = -(-plan.steps // pl.num_programs(0))

    @pl.when(grid_step == 0)
    def _():
        plan.greet()
        cw_g[...] = jnp.zeros_like(cw_g)
        ccw_g[...] = jnp.zeros_like(ccw_g)
        small_g[...] = jnp.zeros_like(small_g)
        skip_g[...] = jnp.zeros_like(skip_g)

    def reduce_steps(first, count):
        def one(number, carried):
            plan.step(number)
            return carried

        start = grid_step * per_step + first
        lax.fori_loop(start, jnp.minimum(start + count, plan.steps), one, 0)

    @pl.when(step_id == 0)
    def _():
        state[...] = pulled[...]
        rim_s[...] = jnp.zeros_like(rim_s)
        crim_s[...] = jnp.zeros_like(crim_s)

    @pl.when(chunk == 0)
    def _():
        halo[...] = vrim[...]

    @pl.when(chunk > 0)
    def _():
        halo[...] = vprev[...]

    frame = chunk_frame([marks[micro, place] for place in range(3)], chunk, sraw[...], sbias[...], rate[...], heads)
    same = frame["same"]
    for lag in range(1, 4):
        same_s[lag - 1] = same[lag]
    joined = (frame["seg_rows"] == frame["seg_columns"]) & (frame["row_ids"] <= frame["column_ids"])
    bias_s[...] = jnp.where(joined, 0.0, -1e30)
    stack[0:CHUNK, :] = packed_parts(frame["step"], heads)
    stack[CHUNK : 2 * CHUNK, :] = packed_parts(frame["carry"], heads)
    stack[2 * CHUNK : 3 * CHUNK, :] = packed_parts(frame["tail"], heads)
    cumpack[...] = packed_parts(frame["cumulative"], heads)
    cumt[...] = jnp.transpose(frame["cumulative"])
    coupling_halo = jnp.where(chunk == 0, crim[...], cprev[...])
    wide_same = [None] + [jnp.concatenate([same[lag], same[lag]], axis=1) for lag in range(1, 4)]
    craw_now = craw[...]
    pre = conv_sum(craw_now, coupling_halo, lambda lag: ccw[lag : lag + 1, :], ccb[...], wide_same)
    csig = logistic(pre)
    coupled = pre * csig
    b_value = coupled[:, :width]
    c_value = coupled[:, width:]
    b_part = split_two(b_value)
    c_part = split_two(c_value)
    gram_s[...] = mm_three_nt(b_part, c_part)
    cparts[0] = c_part[0]
    cparts[1] = c_part[1]
    bparts[0] = b_part[0]
    bparts[1] = b_part[1]
    ct_part = split_two(jnp.transpose(c_value))
    ctparts[0] = ct_part[0]
    ctparts[1] = ct_part[1]
    dgram[...] = jnp.zeros_like(dgram)
    dcoup[...] = jnp.zeros_like(dcoup)
    dhead[...] = jnp.zeros_like(dhead)
    lane = lax.broadcasted_iota(jnp.int32, (CHUNK, LANES), 1)
    row = lax.broadcasted_iota(jnp.int32, (CHUNK, LANES), 0)
    low_half = (lane < LANES // 2).astype(f32)
    high_half = 1.0 - low_half
    last_row = (row == CHUNK - 1).astype(f32)
    is_end = step_id == 0
    eight_rows = lax.broadcasted_iota(jnp.int32, cd.shape, 0)
    for place in range(2):
        chosen = jnp.where(eight_rows == chunk + place, cd[...], 0.0)
        cd_s[place : place + 1, :] = jnp.sum(chosen, axis=0, keepdims=True)

    def pair(index):
        cols = pl.ds(pl.multiple_of(index * LANES, LANES), LANES)
        wide = pl.ds(pl.multiple_of(index * 2 * LANES, 2 * LANES), 2 * LANES)
        raw = vraw[:, cols]
        full = jnp.concatenate([halo[:, cols], raw], axis=0)
        lagged = [raw] + [pltpu.roll(full, lag, 0)[8:] * same_s[lag - 1] for lag in range(1, 4)]
        pre_value = cb[:, cols]
        for lag in range(4):
            pre_value = pre_value + cw[lag : lag + 1, cols] * lagged[lag]
        sig = logistic(pre_value)
        value = pre_value * sig
        spread = mm(stack[...], sel[:, cols])
        step_e = spread[:CHUNK]
        carry_e = spread[CHUNK : 2 * CHUNK]
        tail_e = spread[2 * CHUNK :]
        inputs = step_e * value
        grads = grad[:, cols]
        column = mm(cumpack[...], selcol[:, wide])
        row_pair = jnp.concatenate(
            [cumt[pl.ds(2 * index, 1), :], cumt[pl.ds(2 * index + 1, 1), :]], axis=1
        )
        bias = bias_s[...]
        gram = gram_s[...]
        decays = jnp.exp(row_pair - column + jnp.concatenate([bias, bias], axis=1))
        mixing = jnp.concatenate([gram, gram], axis=1) * decays
        mix_high, mix_low = split_two(mixing)
        g_low = split_two(grads * low_half)
        g_high = split_two(grads * high_half)
        diag_high = jnp.concatenate([g_low[0], g_high[0]], axis=0)
        diag_low = jnp.concatenate([g_low[1], g_high[1]], axis=0)
        both = mm(mix_high, jnp.concatenate([diag_high, diag_low], axis=1))
        input_g = both[:, :LANES] + both[:, LANES:] + mm(mix_low, diag_high)
        held_g = state[:, cols]
        held_parts = split_two(held_g)
        input_g = input_g + tail_e * mm_three((bparts[0], bparts[1]), held_parts)
        in_parts = split_two(inputs)
        outer = mm_three_nt(in_parts, (diag_high, diag_low)) * decays
        dgram[...] += outer[:, :CHUNK] + outer[:, CHUNK:]
        reach_now = cd_s[0:1, cols]
        reach_next = cd_s[1:2, cols]
        arriving = entering[:, cols]
        held = st_now[0, :, cols] + reach_now * arriving
        next_own = jnp.where(is_end, fin[:, cols], st_next[0, :, cols])
        following = next_own + reach_next * arriving
        carried_g = split_two(carry_e * grads)
        state[:, cols] = carry_e[CHUNK - 1 :, :] * held_g + mm_three(
            (ctparts[0], ctparts[1]), carried_g
        )
        dcoup[1] += mm_three_nt(carried_g, split_two(held))
        dcoup[0] += mm_three_nt(split_two(tail_e * inputs), held_parts)
        value_g = input_g * step_e + skip[:, cols] * grads
        kept = jnp.sum(held_g * following, axis=0, keepdims=True)
        balance = grads * (mixer[:, cols] - skip[:, cols] * value) - inputs * input_g
        balance = balance + last_row * kept
        sums = jnp.concatenate([balance, input_g * value], axis=0)
        sums_parts = split_three(sums)
        pick = selt[cols, :]
        dhead[...] += mm(sums_parts[0], pick) + mm(sums_parts[1], pick) + mm(sums_parts[2], pick)
        skip_g[0:1, cols] += jnp.sum(grads * value, axis=0, keepdims=True)
        pre_g = value_g * (sig * (1.0 + pre_value * (1.0 - sig)))
        cw_g[4:5, cols] += jnp.sum(pre_g, axis=0, keepdims=True)
        raw_g = cw[0:1, cols] * pre_g
        cw_g[0:1, cols] += jnp.sum(pre_g * raw, axis=0, keepdims=True)
        none = jnp.zeros((8, LANES), f32)
        edge = none
        for lag in range(1, 4):
            cw_g[lag : lag + 1, cols] += jnp.sum(pre_g * lagged[lag], axis=0, keepdims=True)
            weighted = cw[lag : lag + 1, cols] * (pre_g * same_s[lag - 1])
            padded = jnp.concatenate([none, weighted, none], axis=0)
            turned = pltpu.roll(padded, CHUNK + 16 - lag, 0)
            raw_g = raw_g + turned[8 : 8 + CHUNK]
            edge = edge + turned[:8]
        last_rows = raw_g[CHUNK - 8 :] + rim_s[:, cols]
        lead_g[:, cols] = jnp.concatenate([raw_g[: CHUNK - 8], last_rows], axis=0).astype(bf16)

        @pl.when(step_id == 0)
        def _():
            vtail_g[:, cols] = last_rows

        rim_s[:, cols] = edge
        vrim_g[:, cols] = edge

    groups = 4
    per_group = heads // 2 // groups

    def group(number, carried):
        for inside in range(per_group):
            pair(number * per_group + inside)
        share = per_step // (groups + 1)
        reduce_steps(number * share, share)
        return carried

    lax.fori_loop(0, groups, group, 0)
    used = groups * (per_step // (groups + 1))
    reduce_steps(used, per_step - used)

    total = dgram[...]
    total_parts = split_two(total)
    turned_parts = split_two(jnp.transpose(total))
    b_grad = dcoup[0] + mm_three(total_parts, (cparts[0], cparts[1]))
    c_grad = dcoup[1] + mm_three(turned_parts, (bparts[0], bparts[1]))
    coupled_g = jnp.concatenate([b_grad, c_grad], axis=1)
    pre_g = coupled_g * (csig * (1.0 + pre * (1.0 - csig)))
    ccw_g[4:5, :] += jnp.sum(pre_g, axis=0, keepdims=True)
    ccw_g[0:1, :] += jnp.sum(pre_g * craw_now, axis=0, keepdims=True)
    raw_g = ccw[0:1, :] * pre_g
    full = jnp.concatenate([coupling_halo, craw_now], axis=0)
    none = jnp.zeros((8, 2 * width), f32)
    edge = none
    for lag in range(1, 4):
        masked = pre_g * wide_same[lag]
        ccw_g[lag : lag + 1, :] += jnp.sum(
            masked * pltpu.roll(full, lag, 0)[8:], axis=0, keepdims=True
        )
        padded = jnp.concatenate([none, ccw[lag : lag + 1, :] * masked, none], axis=0)
        turned = pltpu.roll(padded, CHUNK + 16 - lag, 0)
        raw_g = raw_g + turned[8 : 8 + CHUNK]
        edge = edge + turned[:8]
    craw_g[...] = raw_g
    craw_g[CHUNK - 8 :, :] += crim_s[...]
    crim_s[...] = edge
    crim_g[...] = edge

    upper = (frame["row_ids"] <= frame["column_ids"]).astype(bf16)
    parts = split_three(dhead[:CHUNK])
    decay_g = mm(upper, parts[0]) + mm(upper, parts[1]) + mm(upper, parts[2])
    step_g = (dhead[CHUNK:] - rate[...] * decay_g) * logistic(frame["shifted"])
    lead_g[:, inner : inner + 2 * width] = jnp.zeros((CHUNK, 2 * width), bf16)
    lead_g[:, inner + 2 * width :] = step_g.astype(bf16)
    small_g[0:1, :] += jnp.sum(step_g, axis=0, keepdims=True)
    small_g[1:2, :] += jnp.sum(-frame["step"] * decay_g, axis=0, keepdims=True)


def backward_ssd(
    marks, micros, raw, rims, inner, twice, tokens, grad, mixer, states, fin, entering, cd, pulled,
    cw, cb, ccw, ccb, sbias, rate, skip, sel, selcol, selt, terms, collective_id,
):
    width = twice // 2
    chunks = tokens // CHUNK
    heads = inner // (LANES // 2)
    eighth = CHUNK // 8
    pairs = lax.axis_size("fsdp") // 2
    shard_rows = terms[0].shape[0] // (2 * pairs)
    plan = Reduction(shard_rows, pairs, [term.shape[1] for term in terms], 2)
    lead = inner + twice + LANES

    def row(step):
        return step // chunks * chunks + chunks - 1 - lax.rem(step, chunks)

    def part(count, start):
        return pl.BlockSpec((CHUNK, count), lambda step: (row(step), start // count))

    def before(count, start):
        return pl.BlockSpec(
            (8, count), lambda step: (jnp.maximum(row(step) * eighth - 1, 0), start // count)
        )

    def edge(count, start):
        return pl.BlockSpec(
            (None, 8, count), lambda step: (step // chunks, 0, start // count)
        )

    def held(offset):
        return pl.BlockSpec(
            (1, width, inner),
            lambda step: (
                jnp.minimum(row(step) + offset, (step // chunks + 1) * chunks - 1), 0, 0,
            ),
        )

    def each(*shape):
        return pl.BlockSpec((None, *shape), lambda step: (step // chunks, 0, 0))

    hbm = pl.BlockSpec(memory_space=pl.ANY)
    return pl.pallas_call(
        functools.partial(backward_kernel, heads, chunks, plan),
        grid=(micros * chunks,),
        in_specs=[
            pl.BlockSpec(memory_space=pltpu.SMEM),
            part(inner, 0),
            before(inner, 0),
            edge(inner, 0),
            part(twice, inner),
            before(twice, inner),
            edge(twice, inner),
            part(LANES, inner + twice),
            part(inner, 0),
            part(inner, 0),
            held(0),
            held(1),
            each(width, inner),
            each(width, inner),
            each(8, inner),
            each(width, inner),
            whole(cw.shape),
            whole(cb.shape),
            whole(ccw.shape),
            whole(ccb.shape),
            whole(sbias.shape),
            whole(rate.shape),
            whole(skip.shape),
            whole(sel.shape),
            whole(selcol.shape),
            whole(selt.shape),
        ]
        + [hbm] * len(terms),
        out_specs=[
            part(lead, 0),
            each(8, inner),
            each(8, inner),
            part(twice, 0),
            each(8, twice),
            whole((8, inner)),
            whole((8, twice)),
            whole((8, LANES)),
            whole((8, inner)),
        ]
        + [hbm] * len(terms),
        scratch_shapes=[
            pltpu.VMEM((width, inner), f32),
            pltpu.VMEM((LANES, CHUNK), f32),
            pltpu.VMEM((3 * CHUNK, LANES), bf16),
            pltpu.VMEM((CHUNK, LANES), bf16),
            pltpu.VMEM((8, inner), f32),
            pltpu.VMEM((3, CHUNK, LANES), f32),
            pltpu.VMEM((CHUNK, CHUNK), f32),
            pltpu.VMEM((CHUNK, CHUNK), f32),
            pltpu.VMEM((2, CHUNK, width), bf16),
            pltpu.VMEM((2, CHUNK, width), bf16),
            pltpu.VMEM((2, width, CHUNK), bf16),
            pltpu.VMEM((8, inner), f32),
            pltpu.VMEM((8, twice), f32),
            pltpu.VMEM((CHUNK, CHUNK), f32),
            pltpu.VMEM((2, CHUNK, width), f32),
            pltpu.VMEM((2 * CHUNK, LANES), f32),
            pltpu.VMEM((8, inner), f32),
        ]
        + plan.scratch(),
        out_shape=[
            jax.ShapeDtypeStruct((micros * tokens, lead), bf16),
            jax.ShapeDtypeStruct((micros, 8, inner), f32),
            jax.ShapeDtypeStruct((micros, 8, inner), f32),
            jax.ShapeDtypeStruct((micros * tokens, twice), f32),
            jax.ShapeDtypeStruct((micros, 8, twice), f32),
            jax.ShapeDtypeStruct((8, inner), f32),
            jax.ShapeDtypeStruct((8, twice), f32),
            jax.ShapeDtypeStruct((8, LANES), f32),
            jax.ShapeDtypeStruct((8, inner), f32),
        ]
        + [jax.ShapeDtypeStruct((shard_rows, term.shape[1]), f32) for term in terms],
        compiler_params=pltpu.CompilerParams(
            collective_id=collective_id, has_side_effects=True, vmem_limit_bytes=60 * 1024 * 1024
        ),
    )(
        marks, raw, raw, rims, raw, raw, rims, raw, grad, mixer, states, states, fin, entering,
        cd, pulled, cw, cb, ccw, ccb, sbias, rate, skip, sel, selcol, selt,
        *[term.reshape(pairs, 2, shard_rows, -1) for term in terms],
    )


def gather_kernel(arrays, shared, *refs):
    weights, tokens = refs[:arrays], refs[arrays]
    fulls, far = refs[arrays + 1 : 2 * arrays + 1], refs[2 * arrays + 1]
    refs = refs[2 * arrays + 2 :]
    ring_send, ring_recv, pair_send, pair_recv, cross_send, cross_recv, extra_send, extra_recv, local_sem = refs
    count = lax.axis_size("fsdp")
    pairs = count // 2
    own, place, side = lax.axis_index("fsdp"), lax.axis_index("context"), lax.axis_index("tensor")
    pair, member = own // 2, lax.rem(own, 2)
    rows = weights[0].shape[0]
    moved = rows - shared

    def at(offset, which):
        there = lax.rem(pair + pairs - offset, pairs)
        return 2 * there + (member if which == 0 else 1 - member)

    ahead = (2 * lax.rem(pair + 1, pairs) + member, place, side)
    behind = (2 * lax.rem(pair + pairs - 1, pairs) + member, place, side)
    partner = (2 * pair + 1 - member, place, side)
    across = (own, 1 - place, side)
    beside = (own, place, 1 - side)
    barrier = pltpu.get_barrier_semaphore()
    greeted = [ahead, behind, partner, across, beside]
    for device in greeted:
        pl.semaphore_signal(barrier, inc=1, device_id=device, device_id_type=MESH)
    pl.semaphore_wait(barrier, len(greeted))

    def part(index, j, start, size):
        return fulls[j].at[pl.ds(pl.multiple_of(index * rows + start, 16), size), :]

    moved_start = pl.multiple_of(place * shared, 16)
    shared_start = pl.multiple_of(place * moved, 16)

    started = []

    def send(src, dst, send_sem, recv_sem, device):
        copy = pltpu.make_async_remote_copy(
            src_ref=src, dst_ref=dst, send_sem=send_sem, recv_sem=recv_sem,
            device_id=device, device_id_type=MESH,
        )
        copy.start()
        started.append(copy)
        return copy

    kept = []
    for j in range(arrays):
        kept.append(
            pltpu.make_async_copy(
                weights[j], fulls[j].at[pl.ds(pl.multiple_of(own * rows, 16), rows), :], local_sem.at[j]
            )
        )
        kept[-1].start()

    def from_own(j):
        return weights[j].at[pl.ds(moved_start, moved), :]

    ring, within, crossed = {}, {}, []

    def start_ring(j, k):
        dst = part(at(k, 0), j, moved_start, moved)
        ring[j, k] = send(
            from_own(j) if k == 0 else dst, dst, ring_send.at[j, k], ring_recv.at[j, k], ahead
        )

    def start_pair(j, k):
        dst = part(at(k, 0), j, moved_start, moved)
        within[j, k] = send(
            from_own(j) if k == 0 else dst, dst, pair_send.at[j, k], pair_recv.at[j, k], partner
        )

    def start_cross(j, k, which):
        here = part(at(k, which), j, shared_start, shared)
        slot = 2 * k + which
        crossed.append(
            send(here, here, cross_send.at[j, slot], cross_recv.at[j, slot], across)
        )

    half = tokens.shape[2] // 2
    lanes = pl.ds(pl.multiple_of(side * half, 128), half)
    token_copy = send(
        tokens.at[:, :, lanes], far.at[:, :, lanes], extra_send.at[0], extra_recv.at[0], across
    )
    steps = [(j, k) for j in range(arrays) for k in range(pairs)]
    waiting = []
    forwarded = None
    for number, (j, k) in enumerate(steps):
        if k > 0:
            ring[j, k - 1].wait_recv()
        if k < pairs - 1:
            start_ring(j, k)
        start_pair(j, k)
        if k > 0:
            start_cross(j, k, 0)
        waiting.append((j, k))
        if len(waiting) > 2:
            wj, wk = waiting.pop(0)
            within[wj, wk].wait_recv()
            start_cross(wj, wk, 1)
        if number == min(pairs, len(steps) - 1):
            token_copy.wait_recv()
            forwarded = send(
                far.at[:, :, lanes], far.at[:, :, lanes], extra_send.at[1], extra_recv.at[1], beside
            )
    for wj, wk in waiting:
        within[wj, wk].wait_recv()
        start_cross(wj, wk, 1)
    forwarded.wait_recv()
    for copy in crossed:
        copy.wait_recv()
    for copy in started:
        copy.wait_send()
    for copy in kept:
        copy.wait()


def gather_weights(shards, tokens, shared, collective_id):
    rows = shards[0].shape[0]
    pairs = lax.axis_size("fsdp") // 2
    count = len(shards)
    hbm = pl.BlockSpec(memory_space=pl.ANY)
    dma = pltpu.SemaphoreType.DMA
    return pl.pallas_call(
        functools.partial(gather_kernel, count, shared),
        out_shape=[
            jax.ShapeDtypeStruct((2 * pairs * rows, shard.shape[1]), shard.dtype) for shard in shards
        ]
        + [jax.ShapeDtypeStruct(tokens.shape, tokens.dtype)],
        in_specs=[hbm] * (count + 1),
        out_specs=[hbm] * (count + 1),
        scratch_shapes=[
            dma((count, max(pairs - 1, 1))),
            dma((count, max(pairs - 1, 1))),
            dma((count, pairs)),
            dma((count, pairs)),
            dma((count, 2 * pairs)),
            dma((count, 2 * pairs)),
            dma((2,)),
            dma((2,)),
            dma((count,)),
        ],
        compiler_params=pltpu.CompilerParams(collective_id=collective_id, has_side_effects=True),
    )(*shards, tokens)


class Reduction:
    def __init__(self, rows, pairs, columns, lag):
        self.rows, self.pairs, self.columns, self.lag = rows, pairs, columns, lag
        self.shared = rows // 4
        self.moved = rows - self.shared
        self.counts = [count // LANES for count in columns]
        self.count = sum(self.counts)
        self.steps = self.count + 4 * lag

    def scratch(self):
        shared, moved, pairs, count = self.shared, self.moved, self.pairs, self.count
        cross, pair, ring = 2 * pairs * shared + 16, pairs * moved + 16, moved + 16
        i16, dma = jnp.int16, pltpu.SemaphoreType.DMA
        return [
            pltpu.VMEM((count, cross, LANES), i16),
            pltpu.VMEM((count, pair, LANES), i16),
            pltpu.VMEM((count, pairs - 1, ring, LANES), i16),
            pltpu.VMEM((count, ring, LANES), i16),
            pltpu.VMEM((2, cross, LANES), i16),
            pltpu.VMEM((2, pair, LANES), i16),
            pltpu.VMEM((2, pairs - 1, ring, LANES), i16),
            pltpu.VMEM((2, ring, LANES), i16),
            pltpu.VMEM((2, pairs, 2, shared, LANES), f32),
            pltpu.VMEM((2, pairs, moved, LANES), f32),
            pltpu.VMEM((2, pairs, moved, LANES), f32),
            pltpu.VMEM((2 * self.lag, moved, LANES), f32),
            pltpu.VMEM((2 * self.lag, moved, LANES), f32),
            pltpu.VMEM((2, self.rows, LANES), f32),
            dma((count,)),
            dma((count,)),
            dma((pairs - 1, count)),
            dma((count,)),
            dma((2,)),
            dma((2,)),
            dma((pairs - 1, 2)),
            dma((2,)),
            dma((3, 2)),
            dma((2,)),
        ]

    def bind(self, terms, outs, scratch):
        self.terms, self.outs = terms, outs
        (
            self.cross_in, self.pair_in, self.ring_in, self.last_in,
            self.cross_out, self.pair_out, self.ring_out, self.last_out,
            self.cross_term, self.pair_term, self.ring_term,
            self.kept, self.held, self.result,
            self.cross_recv, self.pair_recv, self.ring_recv, self.last_recv,
            self.cross_sent, self.pair_sent, self.ring_sent, self.last_sent,
            self.loaded, self.stored,
        ) = scratch
        self.own, self.place = lax.axis_index("fsdp"), lax.axis_index("context")
        self.side = lax.axis_index("tensor")
        self.pair, self.member = self.own // 2, lax.rem(self.own, 2)
        self.across = (self.own, 1 - self.place, self.side)
        self.partner = (2 * self.pair + 1 - self.member, self.place, self.side)
        self.inset = pl.multiple_of(self.place * (self.moved - self.shared), 16)
        self.start = pl.multiple_of(self.place * self.shared, 16)

    def peer(self, offset):
        there = lax.rem(self.pair + offset, self.pairs)
        return (2 * there + self.member, self.place, self.side)

    def greet(self):
        barrier = pltpu.get_barrier_semaphore()
        devices = [self.across, self.partner] + [self.peer(k) for k in range(1, self.pairs)]
        for device in devices:
            pl.semaphore_signal(barrier, inc=1, device_id=device, device_id_type=MESH)
        pl.semaphore_wait(barrier, len(devices))

    def cross_copy(self, chunk):
        slot = lax.rem(chunk, 2)
        return pltpu.make_async_remote_copy(
            src_ref=self.cross_out.at[slot], dst_ref=self.cross_in.at[chunk],
            send_sem=self.cross_sent.at[slot], recv_sem=self.cross_recv.at[chunk],
            device_id=self.across, device_id_type=MESH,
        )

    def pair_copy(self, chunk):
        slot = lax.rem(chunk, 2)
        return pltpu.make_async_remote_copy(
            src_ref=self.pair_out.at[slot], dst_ref=self.pair_in.at[chunk],
            send_sem=self.pair_sent.at[slot], recv_sem=self.pair_recv.at[chunk],
            device_id=self.partner, device_id_type=MESH,
        )

    def ring_copy(self, chunk, offset):
        slot = lax.rem(chunk, 2)
        return pltpu.make_async_remote_copy(
            src_ref=self.ring_out.at[slot, offset - 1], dst_ref=self.ring_in.at[chunk, offset - 1],
            send_sem=self.ring_sent.at[offset - 1, slot],
            recv_sem=self.ring_recv.at[offset - 1, chunk],
            device_id=self.peer(offset), device_id_type=MESH,
        )

    def last_copy(self, chunk):
        slot = lax.rem(chunk, 2)
        return pltpu.make_async_remote_copy(
            src_ref=self.last_out.at[slot], dst_ref=self.last_in.at[chunk],
            send_sem=self.last_sent.at[slot], recv_sem=self.last_recv.at[chunk],
            device_id=self.across, device_id_type=MESH,
        )

    def load_copy(self, stage, term, cols, slot):
        if stage == 0:
            rows = pl.ds(pl.multiple_of((1 - self.place) * self.moved, 16), self.shared)
            src, dst = term.at[:, :, rows, cols], self.cross_term.at[slot]
        elif stage == 1:
            src = term.at[:, 1 - self.member, pl.ds(self.start, self.moved), cols]
            dst = self.pair_term.at[slot]
        else:
            src = term.at[:, self.member, pl.ds(self.start, self.moved), cols]
            dst = self.ring_term.at[slot]
        return pltpu.make_async_copy(src, dst, self.loaded.at[stage, slot])

    def each_array(self, chunk, act):
        first = 0
        for number, count in enumerate(self.counts):
            inside = (chunk >= first) & (chunk < first + count)
            offset = first

            @pl.when(inside)
            def _(number=number, offset=offset):
                act(number, pl.ds(pl.multiple_of((chunk - offset) * LANES, LANES), LANES))

            first += count

    def load(self, stage, chunk):
        @pl.when((chunk >= 0) & (chunk < self.count))
        def _():
            self.each_array(
                chunk,
                lambda number, cols: self.load_copy(
                    stage, self.terms[number], cols, lax.rem(chunk, 2)
                ).start(),
            )

    def loaded_now(self, stage, chunk):
        self.load_copy(stage, self.terms[0], pl.ds(0, LANES), lax.rem(chunk, 2)).wait()

    @staticmethod
    def encode(value, out, place):
        count = value.shape[0]
        peak = jnp.maximum(jnp.max(jnp.abs(value), axis=0, keepdims=True), 1e-30)
        exponent = jnp.ceil(jnp.log(peak) * 1.4426950408889634)
        factor = jnp.exp(exponent * -0.6931471805599453) * 32000.0
        out[place + (pl.ds(0, count), slice(None))] = (
            jnp.round(value * factor).astype(jnp.int32).astype(jnp.int16)
        )
        out[place + (pl.ds(count, 16), slice(None))] = (
            jnp.broadcast_to(exponent, (16, LANES)).astype(jnp.int32).astype(jnp.int16)
        )

    @staticmethod
    def unit(ref, place, count):
        exponents = ref[place + (pl.ds(count, 16), slice(None))].astype(jnp.int32).astype(f32)
        return jnp.exp(exponents[:1] * 0.6931471805599453) * (1.0 / 32000.0)

    @staticmethod
    def decode(ref, place, first, count, unit):
        first = pl.multiple_of(first, 16) if not isinstance(first, int) else first
        return ref[place + (pl.ds(first, count), slice(None))].astype(jnp.int32).astype(f32) * unit

    def step(self, number):
        lag, pairs, shared, moved = self.lag, self.pairs, self.shared, self.moved

        @pl.when(number == 0)
        def _():
            self.load(0, number)

        self.load(0, number + 1)
        self.load(1, number + 1 - lag)
        self.load(2, number + 1 - 2 * lag)

        def stage(index, act):
            chunk = number - index * lag

            @pl.when((chunk >= 0) & (chunk < self.count))
            def _():
                act(chunk, lax.rem(chunk, 2))

        def cross(chunk, slot):
            self.loaded_now(0, chunk)

            @pl.when(chunk >= 2)
            def _():
                self.cross_copy(chunk - 2).wait_send()

            value = self.cross_term[slot].reshape(2 * pairs * shared, LANES)
            self.encode(value, self.cross_out, (slot,))
            self.cross_copy(chunk).start()

        def pair(chunk, slot):
            self.loaded_now(1, chunk)
            self.cross_copy(chunk).wait_recv()

            @pl.when(chunk >= 2)
            def _():
                self.pair_copy(chunk - 2).wait_send()

            unit = self.unit(self.cross_in, (chunk,), 2 * pairs * shared)
            for there in range(pairs):
                first = (2 * there + 1 - self.member) * shared
                self.pair_term[slot, there, pl.ds(self.inset, shared), :] += self.decode(
                    self.cross_in, (chunk,), first, shared, unit
                )
            value = self.pair_term[slot].reshape(pairs * moved, LANES)
            self.encode(value, self.pair_out, (slot,))
            self.pair_copy(chunk).start()

        def ring(chunk, slot):
            self.loaded_now(2, chunk)
            self.pair_copy(chunk).wait_recv()

            @pl.when(chunk >= 2)
            def _():
                for offset in range(1, pairs):
                    self.ring_copy(chunk - 2, offset).wait_send()

            cross_unit = self.unit(self.cross_in, (chunk,), 2 * pairs * shared)
            pair_unit = self.unit(self.pair_in, (chunk,), pairs * moved)
            for offset in list(range(1, pairs)) + [0]:
                there = lax.rem(self.pair + offset, pairs)
                first = (2 * there + self.member) * shared
                self.ring_term[slot, there, pl.ds(self.inset, shared), :] += self.decode(
                    self.cross_in, (chunk,), first, shared, cross_unit
                )
                value = self.ring_term[slot, there] + self.decode(
                    self.pair_in, (chunk,), there * moved, moved, pair_unit
                )
                if offset:
                    self.encode(value, self.ring_out, (slot, offset - 1))
                    self.ring_copy(chunk, offset).start()
                else:
                    self.kept[lax.rem(chunk, 2 * lag)] = value

        def last(chunk, slot):
            for offset in range(1, pairs):
                self.ring_copy(chunk, offset).wait_recv()

            @pl.when(chunk >= 2)
            def _():
                self.last_copy(chunk - 2).wait_send()

            total = self.kept[lax.rem(chunk, 2 * lag)]
            for offset in range(1, pairs):
                place = (chunk, offset - 1)
                total = total + self.decode(
                    self.ring_in, place, 0, moved, self.unit(self.ring_in, place, moved)
                )
            self.encode(total, self.last_out, (slot,))
            self.held[lax.rem(chunk, 2 * lag)] = self.decode(
                self.last_out, (slot,), 0, moved, self.unit(self.last_out, (slot,), moved)
            )
            self.last_copy(chunk).start()

        def write_copy(number, cols, slot):
            return pltpu.make_async_copy(
                self.result.at[slot], self.outs[number].at[:, cols], self.stored.at[slot]
            )

        def write(chunk, slot):
            self.last_copy(chunk).wait_recv()

            @pl.when(chunk >= 2)
            def _():
                write_copy(0, pl.ds(0, LANES), slot).wait()

            mine = self.held[lax.rem(chunk, 2 * lag)]
            other = self.decode(
                self.last_in, (chunk,), 0, moved, self.unit(self.last_in, (chunk,), moved)
            )
            low = jnp.where(self.place == 0, mine, other)
            high = jnp.where(self.place == 0, other, mine)
            self.result[slot, pl.ds(0, shared), :] = low[:shared]
            self.result[slot, pl.ds(shared, moved - shared), :] = (
                low[shared:] + high[: moved - shared]
            )
            self.result[slot, pl.ds(moved, shared), :] = high[moved - shared :]
            self.each_array(chunk, lambda which, cols: write_copy(which, cols, slot).start())

        stage(4, write)
        stage(3, last)
        stage(2, ring)
        stage(1, pair)
        stage(0, cross)

        @pl.when(number == self.steps - 1)
        def _():
            for slot in range(2):
                write_copy(0, pl.ds(0, LANES), slot).wait()
                self.cross_copy(jnp.int32(self.count - 2 + slot)).wait_send()
                self.pair_copy(jnp.int32(self.count - 2 + slot)).wait_send()
                self.last_copy(jnp.int32(self.count - 2 + slot)).wait_send()
                for offset in range(1, pairs):
                    self.ring_copy(jnp.int32(self.count - 2 + slot), offset).wait_send()


def reduce_kernel(plan, arrays, *refs):
    plan.bind(refs[:arrays], refs[arrays : 2 * arrays], refs[2 * arrays :])
    plan.greet()

    def body(number, carried):
        plan.step(number)
        return carried

    lax.fori_loop(0, plan.steps, body, 0)


def reduce_terms(terms, lag, collective_id):
    pairs = lax.axis_size("fsdp") // 2
    rows = terms[0].shape[0] // (2 * pairs)
    columns = [term.shape[1] for term in terms]
    plan = Reduction(rows, pairs, columns, lag)
    hbm = pl.BlockSpec(memory_space=pl.ANY)
    arrays = len(terms)
    return pl.pallas_call(
        functools.partial(reduce_kernel, plan, arrays),
        out_shape=[jax.ShapeDtypeStruct((rows, count), f32) for count in columns],
        in_specs=[hbm] * arrays,
        out_specs=[hbm] * arrays,
        scratch_shapes=plan.scratch(),
        compiler_params=pltpu.CompilerParams(
            collective_id=collective_id, has_side_effects=True, vmem_limit_bytes=58 * 1024 * 1024
        ),
    )(*[term.reshape(pairs, 2, rows, -1) for term in terms])


def passed_along(value, axis, steps):
    count = lax.axis_size(axis)
    initial, last = (max(0, -steps), min(count, count - steps))
    return lax.ppermute(value, axis, [(source, source + steps) for source in range(initial, last)])


def paired(value, axis):
    count = lax.axis_size(axis)
    return lax.ppermute(value, axis, [(source, source ^ 1) for source in range(count)])


def ring_shift(value, axis, steps):
    count = lax.axis_size(axis)
    return lax.ppermute(
        value, axis, [(source, (source + 2 * steps) % count) for source in range(count)]
    )


def summed_everywhere(values):
    sizes = [value.size for value in values]
    shapes = [value.shape for value in values]
    flat = jnp.concatenate([value.reshape(-1) for value in values])
    count = flat.shape[0]
    flat = jnp.pad(flat, (0, -count % 1024)).reshape(-1, 128)
    for axis in ("context", "fsdp"):
        members = lax.axis_size(axis)
        reach = 1
        while reach < members:
            flat = flat + lax.ppermute(
                flat, axis, [(source, source ^ reach) for source in range(members)]
            )
            reach *= 2
    flat = flat.reshape(-1)
    results, start = [], 0
    for size, shape in zip(sizes, shapes):
        results.append(flat[start : start + size].reshape(shape))
        start += size
    return results


def chained(own, factor, steps):
    arriving = passed_along(own, "context", steps)
    for _ in range(lax.axis_size("context") - 2):
        arriving = passed_along(factor * arriving + own, "context", steps)
    return arriving


def shards(
    tokens,
    lengths,
    block_order,
    cotangent,
    norm_gain,
    in_weight,
    coupling_weight,
    step_weight,
    out_weight,
    conv_weight,
    conv_bias,
    coupling_conv,
    coupling_bias,
    step_bias,
    decay_rate,
    skip_gain,
    inner_gain,
):
    highest = lax.Precision.HIGHEST
    micros = tokens.shape[0]
    count = tokens.shape[2]
    model = tokens.shape[3]
    inner = inner_gain.shape[0]
    heads = step_bias.shape[0]
    head_size = inner // heads
    twice = coupling_weight.shape[1]
    width = twice // 2
    blocks_row = block_order.shape[2]
    block_len = count * lax.axis_size("context") // blocks_row
    own_blocks = count // block_len
    inner_total = inner * lax.axis_size("tensor")
    side = lax.axis_index("tensor")
    place = lax.axis_index("context")
    base = place * count
    shard_rows = in_weight.shape[0]

    narrow, wide_columns = selectors(heads, head_size)
    sel = jnp.asarray(narrow, bf16)
    selcol = jnp.asarray(wide_columns, bf16)
    selt = jnp.asarray(narrow[:heads].T, bf16)
    selt = jnp.pad(selt, ((0, 0), (0, LANES - heads)))

    lead = jnp.concatenate(
        [
            in_weight[:, 1, :],
            coupling_weight,
            jnp.pad(step_weight, ((0, 0), (0, LANES - heads))),
        ],
        axis=1,
    )
    shared_rows = max(shard_rows * 5 // 16 // 16 * 16, 16)
    lead_full, gate_full, out_full, far = gather_weights(
        [lead, in_weight[:, 0, :], jnp.transpose(out_weight)], tokens[:, 0], shared_rows, 1
    )

    near = tokens[:, 0].reshape(micros, own_blocks, block_len, model)
    far = far.reshape(micros, own_blocks, block_len, model)
    everything = jnp.where(
        place == 0, jnp.concatenate([near, far], 1), jnp.concatenate([far, near], 1)
    )
    slots = jnp.arange(blocks_row, dtype=jnp.int32)
    picked = []
    for micro in range(micros):
        for own in range(own_blocks):
            wanted = place * own_blocks + own
            slot = jnp.sum(jnp.where(block_order[micro, 0] == wanted, slots, 0))
            picked.append(
                lax.dynamic_slice(
                    everything, (micro, slot, 0, 0), (1, 1, block_len, model)
                ).reshape(block_len, model)
            )
    x_input = jnp.concatenate(picked, axis=0)
    x_float = x_input.astype(f32)
    inv_rms = lax.rsqrt(jnp.mean(x_float * x_float, axis=-1, keepdims=True) + epsilon)
    normed = (x_float * inv_rms * norm_gain).astype(bf16)

    first_end = lengths[:, 0, 0]
    second_end = first_end + lengths[:, 0, 1]
    marks = [
        jnp.stack([first_end[micro], second_end[micro], base]).astype(jnp.int32)
        for micro in range(micros)
    ]
    positions = base + jnp.arange(count, dtype=jnp.int32)
    keep = jnp.concatenate([(positions < second_end[micro]) for micro in range(micros)])
    keep = keep.astype(f32)[:, None]

    cw, cb = conv_weight, conv_bias.reshape(1, inner)
    ccw, ccb = coupling_conv, coupling_bias.reshape(1, twice)
    sbias = jnp.pad(step_bias, (0, LANES - heads)).reshape(1, LANES)
    rate = jnp.pad(decay_rate, (0, LANES - heads)).reshape(1, LANES)
    skip = jnp.repeat(skip_gain, head_size).reshape(1, inner)

    raw = jnp.dot(normed, lead_full, preferred_element_type=f32)
    rims = passed_along(
        jnp.stack([raw[(micro + 1) * count - 8 : (micro + 1) * count] for micro in range(micros)]),
        "context",
        1,
    )
    chunk_count = count // CHUNK
    written, finals, entering = (), [], []
    for micro in range(micros):
        y_own, states, final, coupled, carry, reach = forward_ssd(
            marks[micro], micro, micros, written, raw, rims[micro], inner, twice, count,
            cw, cb, ccw, ccb, sbias, rate, skip, sel, selcol,
        )
        written = (y_own, states, coupled, carry, reach)
        finals.append(final)
        entering.append(chained(final, reach[micro, chunk_count], 1))
    entering = jnp.stack(entering)
    coupled_c = coupled[:, width:].reshape(micros, count, width)
    gate_in = jnp.dot(normed, gate_full, preferred_element_type=f32)
    cot = cotangent[:, 0].reshape(micros * count, model)
    out_grad = cot * keep.astype(bf16)
    norm_grad = jnp.dot(out_grad, out_full, preferred_element_type=f32)

    arrived = jnp.concatenate(
        [jnp.dot(coupled_c[micro], entering[micro], precision=highest) for micro in range(micros)],
        axis=0,
    )
    mixer = y_own + carry * arrived
    gate_sig = jax.nn.sigmoid(gate_in)
    gate_act = gate_in * gate_sig
    gated = mixer * gate_act
    scaled_grad = norm_grad * inner_gain
    row_sums = jnp.stack([jnp.sum(gated * gated, axis=-1), jnp.sum(scaled_grad * gated, axis=-1)])
    row_sums = row_sums + paired(row_sums, "tensor")
    inv_norm = lax.rsqrt(row_sums[0] / inner_total + epsilon)[:, None]
    inner_dot = row_sums[1][:, None]
    gated_norm = (gated * inv_norm * inner_gain).astype(bf16)
    inner_gain_grad = jnp.sum(norm_grad * gated * inv_norm, axis=0)
    gated_grad = scaled_grad * inv_norm - gated * (inner_dot * inv_norm**3 / inner_total)
    gate_grad = (gated_grad * mixer * gate_sig * (1.0 + gate_in * (1.0 - gate_sig))).astype(bf16)
    mixer_grad = gated_grad * gate_act

    out_term = contract_rows(out_grad, gated_norm)
    gate_term = contract_rows(normed, gate_grad)
    pulled = []
    for micro in range(micros):
        part = slice(micro * count, (micro + 1) * count)
        own_pull = lax.dot_general(
            coupled_c[micro],
            carry[part] * mixer_grad[part],
            (((0,), (0,)), ((), ())),
            precision=highest,
        )
        pulled.append(chained(own_pull, reach[micro, chunk_count], -1))

    branch = contract_cols(gated_norm, out_full)
    branch = branch + paired(branch, "tensor")
    block_out = (x_float + keep * branch).astype(bf16)

    (
        lead_grad, tails, rims_grad, coupling_raw_grad, coupling_rims_grad,
        value_sums, coupling_sums, small_sums, skip_sums, out_shard, gate_shard,
    ) = backward_ssd(
        jnp.stack(marks), micros, raw, rims, inner, twice, count, mixer_grad, mixer, states,
        jnp.stack(finals), entering, reach, jnp.stack(pulled),
        cw, cb, ccw, ccb, sbias, rate, skip, sel, selcol, selt, [out_term, gate_term], 2,
    )
    edges = passed_along(jnp.concatenate([rims_grad, coupling_rims_grad], axis=2), "context", -1)
    coupling_raw_grad = coupling_raw_grad.reshape(micros, count, twice) + jnp.pad(
        edges[:, :, inner:], ((0, 0), (count - 8, 0), (0, 0))
    )
    coupling_raw_grad = coupling_raw_grad + paired(coupling_raw_grad, "tensor")
    lane_ids = jnp.arange(twice, dtype=jnp.int32)
    own_lanes = ((lane_ids // width) == side).astype(bf16)
    coupling_low = (coupling_raw_grad.astype(bf16) * own_lanes).reshape(micros * count, twice)
    lead_grad = lax.dynamic_update_slice(lead_grad, coupling_low, (0, inner))
    tails = (tails + edges[:, :, :inner]).astype(bf16)
    for micro in range(micros):
        lead_grad = lax.dynamic_update_slice(
            lead_grad, tails[micro], ((micro + 1) * count - 8, 0)
        )
    (lead_shard,) = reduce_terms([contract_rows(normed, lead_grad)], 2, 3)
    normed_part = contract_cols(gate_grad, gate_full) + contract_cols(lead_grad, lead_full)
    normed_grad = normed_part + paired(normed_part, "tensor")
    x_hat = x_float * inv_rms
    hat_grad = normed_grad * norm_gain
    input_grad = (
        cot.astype(f32)
        + inv_rms * (hat_grad - x_hat * jnp.mean(hat_grad * x_hat, axis=-1, keepdims=True))
    ).astype(bf16)
    norm_gain_grad = jnp.sum(normed_grad * x_hat, axis=0)

    skip_sums = skip_sums[0].reshape(heads, head_size).sum(axis=1)
    coupling_sums = coupling_sums + paired(coupling_sums, "tensor")
    (value_all, coupling_all, small_all, skip_all, inner_all, norm_all) = summed_everywhere(
        [value_sums[:5], coupling_sums[:5], small_sums[:2], skip_sums, inner_gain_grad, norm_gain_grad]
    )
    coupling_shard = lead_shard[:, inner : inner + twice]
    coupling_shard = coupling_shard + paired(coupling_shard, "tensor")
    return (
        block_out.reshape(micros, 1, count, model),
        input_grad.reshape(micros, 1, count, model),
        norm_all,
        jnp.stack([gate_shard, lead_shard[:, :inner]], axis=1),
        coupling_shard,
        lead_shard[:, inner + twice : inner + twice + heads],
        jnp.transpose(out_shard),
        value_all[:4],
        value_all[4],
        coupling_all[:4],
        coupling_all[4],
        small_all[0, :heads],
        small_all[1, :heads],
        skip_all,
        inner_all,
    )


def contract_rows(left, right):
    return lax.dot_general(
        left, right, (((0,), (0,)), ((), ())), preferred_element_type=jnp.float32
    )


def contract_cols(left, right):
    return lax.dot_general(
        left, right, (((1,), (1,)), ((), ())), preferred_element_type=jnp.float32
    )


def solution(mesh):
    return jax.shard_map(
        shards,
        mesh=mesh,
        in_specs=(
            P(None, "fsdp", "context", None),
            P(None, "fsdp", None),
            P(None, "fsdp", None),
            P(None, "fsdp", "context", None),
            P(),
            P("fsdp", None, "tensor"),
            P("fsdp", None),
            P("fsdp", "tensor"),
            P("tensor", "fsdp"),
            P(None, "tensor"),
            P("tensor"),
            P(),
            P(),
            P("tensor"),
            P("tensor"),
            P("tensor"),
            P("tensor"),
        ),
        out_specs=(
            P(None, "fsdp", "context", None),
            P(None, "fsdp", "context", None),
            P(),
            P("fsdp", None, "tensor"),
            P("fsdp", None),
            P("fsdp", "tensor"),
            P("tensor", "fsdp"),
            P(None, "tensor"),
            P("tensor"),
            P(),
            P(),
            P("tensor"),
            P("tensor"),
            P("tensor"),
            P("tensor"),
        ),
        check_vma=False,
    )
```

```python
import functools

import jax
import jax.numpy as jnp
import numpy as np
from jax import lax
from jax.experimental import pallas as pl
from jax.experimental.pallas import tpu as pltpu
from jax.sharding import PartitionSpec as P

CHUNK = 128
LANES = 128
MESH = pl.DeviceIdType.MESH
f32 = jnp.float32
bf16 = jnp.bfloat16
epsilon = 1e-05


def split_two(value):
    high = value.astype(bf16)
    return high, (value - high.astype(f32)).astype(bf16)


def split_three(value):
    high = value.astype(bf16)
    rest = value - high.astype(f32)
    middle = rest.astype(bf16)
    return high, middle, (rest - middle.astype(f32)).astype(bf16)


def mm(left, right):
    return jnp.dot(left, right, preferred_element_type=f32)


def mm_nt(left, right):
    return lax.dot_general(left, right, (((1,), (1,)), ((), ())), preferred_element_type=f32)


def mm_three(left, right):
    wide = mm(left[0], jnp.concatenate([right[0], right[1]], axis=1))
    count = right[0].shape[1]
    return wide[:, :count] + wide[:, count:] + mm(left[1], right[0])


def mm_three_nt(left, right):
    return mm_nt(left[0], right[0]) + mm_nt(left[0], right[1]) + mm_nt(left[1], right[0])


def packed_parts(value, heads):
    high, middle, lowest = split_three(value)
    joined = (
        high.astype(f32)
        + pltpu.roll(middle.astype(f32), heads, 1)
        + pltpu.roll(lowest.astype(f32), 2 * heads, 1)
    )
    return joined.astype(bf16)


def segment_at(position, first_end, second_end):
    first_part = (position >= first_end).astype(jnp.int32)
    second_part = (position >= second_end).astype(jnp.int32)
    return jnp.where(position < 0, -1, first_part + second_part)


def chunk_frame(marks, chunk, step_raw, step_bias, rate, heads):
    first_end, second_end, base = marks[0], marks[1], marks[2]
    start = base + chunk * CHUNK
    rows = start + lax.broadcasted_iota(jnp.int32, (CHUNK, LANES), 0)
    columns = start + lax.broadcasted_iota(jnp.int32, (CHUNK, CHUNK), 1)
    seg_rows = segment_at(rows, first_end, second_end)
    seg_columns = segment_at(columns, first_end, second_end)
    seg_prior = segment_at(start - 1, first_end, second_end)
    seg_last = segment_at(start + CHUNK - 1, first_end, second_end)
    same = [
        (segment_at(rows - lag, first_end, second_end) == seg_rows).astype(f32) for lag in range(4)
    ]
    shifted = step_raw + step_bias
    step = jnp.maximum(shifted, 0.0) + jnp.log1p(jnp.exp(-jnp.abs(shifted)))
    lanes = lax.broadcasted_iota(jnp.int32, (CHUNK, LANES), 1)
    step = jnp.where(lanes < heads, step, 0.0)
    log_decay = -step * rate
    row_ids = lax.broadcasted_iota(jnp.int32, (CHUNK, CHUNK), 0)
    column_ids = lax.broadcasted_iota(jnp.int32, (CHUNK, CHUNK), 1)
    lower = (row_ids >= column_ids).astype(bf16)
    parts = split_three(log_decay)
    cumulative = mm(lower, parts[0]) + mm(lower, parts[1]) + mm(lower, parts[2])
    last = cumulative[CHUNK - 1 :, :]
    carry = jnp.exp(cumulative) * (seg_rows == seg_prior).astype(f32)
    tail = jnp.exp(last - cumulative) * (seg_rows == seg_last).astype(f32)
    live = lanes < heads
    carry = jnp.where(live, carry, 0.0)
    tail = jnp.where(live, tail, 0.0)
    return dict(
        seg_rows=seg_rows,
        seg_columns=seg_columns,
        row_ids=row_ids,
        column_ids=column_ids,
        same=same,
        step=step,
        shifted=shifted,
        cumulative=cumulative,
        carry=carry,
        tail=tail,
    )


def conv_sum(current, halo, weights, biases, same):
    full = jnp.concatenate([halo, current], axis=0)
    total = biases + weights(0) * current
    for lag in range(1, 4):
        total = total + weights(lag) * (pltpu.roll(full, lag, 0)[8:] * same[lag])
    return total


def logistic(value):
    return 1.0 / (1.0 + jnp.exp(-value))


def forward_kernel(heads, chunks, plan, *refs):
    (
        marks, vraw, vprev, vrim, craw, cprev, crim, sraw, cw, cb, ccw, ccb, sbias, rate, skip,
        sel, selcol,
    ) = refs[:17]
    arrays = plan.arrays
    weights, refs = refs[17 : 17 + arrays], refs[17 + arrays :]
    y_out, st_out, fin_out, bc_out, carry_out, cd_out, entering = refs[:7]
    fulls, refs = refs[7 : 7 + arrays], refs[7 + arrays :]
    (
        state, cumt, stack, cumpack, halo, same_s, bias_s, gram_s, cd_s, cparts, btparts,
        leaving, leave_send, leave_recv,
    ) = refs[:14]
    plan.bind(weights, fulls, refs[14:])
    grid_step = pl.program_id(0)
    steps = pl.num_programs(0)
    chunk = lax.rem(grid_step, chunks)
    micro = grid_step // chunks
    width = state.shape[0]
    early = {0: range(0, arrays), 3: range(arrays, arrays + 1), 5: range(arrays + 1, arrays + 2)}
    placed = max(early[5])

    def leave_copy(which):
        return pltpu.make_async_remote_copy(
            src_ref=leaving.at[which], dst_ref=entering.at[which],
            send_sem=leave_send.at[which], recv_sem=leave_recv.at[which],
            device_id=plan.across, device_id_type=MESH,
        )

    for when, numbers in early.items():

        @pl.when(grid_step == when)
        def _(when=when, numbers=numbers):
            if when == 0:
                plan.greet()
            for number in numbers:
                plan.event(number)

    @pl.when(chunk == 0)
    def _():
        state[...] = jnp.zeros_like(state)
        cd_s[...] = jnp.ones_like(cd_s)
        cd_out[...] = jnp.zeros_like(cd_out)
        halo[...] = vrim[...]

    @pl.when(chunk > 0)
    def _():
        halo[...] = vprev[...]

    frame = chunk_frame([marks[micro, place] for place in range(3)], chunk, sraw[...], sbias[...], rate[...], heads)
    same = frame["same"]
    for lag in range(1, 4):
        same_s[lag - 1] = same[lag]
    joined = (frame["seg_rows"] == frame["seg_columns"]) & (frame["row_ids"] >= frame["column_ids"])
    bias_s[...] = jnp.where(joined, 0.0, -1e30)
    stack[0:CHUNK, :] = packed_parts(frame["step"], heads)
    stack[CHUNK : 2 * CHUNK, :] = packed_parts(frame["carry"], heads)
    stack[2 * CHUNK : 3 * CHUNK, :] = packed_parts(frame["tail"], heads)
    cumpack[...] = packed_parts(frame["cumulative"], heads)
    cumt[...] = jnp.transpose(frame["cumulative"])
    coupling_halo = jnp.where(chunk == 0, crim[...], cprev[...])
    wide_same = [None] + [jnp.concatenate([same[lag], same[lag]], axis=1) for lag in range(1, 4)]
    pre = conv_sum(
        craw[...], coupling_halo, lambda lag: ccw[lag : lag + 1, :], ccb[...], wide_same
    )
    coupled = pre * logistic(pre)
    bc_out[...] = coupled
    b_part = split_two(coupled[:, :width])
    c_part = split_two(coupled[:, width:])
    gram_s[...] = mm_three_nt(c_part, b_part)
    cparts[0] = c_part[0]
    cparts[1] = c_part[1]
    turned = jnp.transpose(coupled[:, :width])
    bt_part = split_two(turned)
    btparts[0] = bt_part[0]
    btparts[1] = bt_part[1]
    lane = lax.broadcasted_iota(jnp.int32, (CHUNK, LANES), 1)
    low_half = (lane < LANES // 2).astype(f32)
    high_half = 1.0 - low_half

    def pair(index, carried):
        cols = pl.ds(pl.multiple_of(index * LANES, LANES), LANES)
        wide = pl.ds(pl.multiple_of(index * 2 * LANES, 2 * LANES), 2 * LANES)
        pre_value = conv_sum(
            vraw[:, cols],
            halo[:, cols],
            lambda lag: cw[lag : lag + 1, cols],
            cb[:, cols],
            [None] + [same_s[lag - 1] for lag in range(1, 4)],
        )
        value = pre_value * logistic(pre_value)
        spread = mm(stack[...], sel[:, cols])
        step_e = spread[:CHUNK]
        carry_e = spread[CHUNK : 2 * CHUNK]
        tail_e = spread[2 * CHUNK :]
        inputs = step_e * value
        column = mm(cumpack[...], selcol[:, wide])
        row_pair = jnp.concatenate(
            [cumt[pl.ds(2 * index, 1), :], cumt[pl.ds(2 * index + 1, 1), :]], axis=1
        )
        bias = bias_s[...]
        gram = gram_s[...]
        mixing = jnp.concatenate([gram, gram], axis=1) * jnp.exp(
            column - row_pair + jnp.concatenate([bias, bias], axis=1)
        )
        mix_high, mix_low = split_two(mixing)
        in_low = split_two(inputs * low_half)
        in_high = split_two(inputs * high_half)
        diag_high = jnp.concatenate([in_low[0], in_high[0]], axis=0)
        diag_low = jnp.concatenate([in_low[1], in_high[1]], axis=0)
        both = mm(mix_high, jnp.concatenate([diag_high, diag_low], axis=1))
        inside = both[:, :LANES] + both[:, LANES:] + mm(mix_low, diag_high)
        held = state[:, cols]
        from_state = mm_three((cparts[0], cparts[1]), split_two(held))
        y_out[:, cols] = inside + carry_e * from_state + skip[:, cols] * value
        fresh = mm_three((btparts[0], btparts[1]), split_two(tail_e * inputs))
        through = carry_e[CHUNK - 1 :, :]
        st_out[0, :, cols] = held
        renewed = through * held + fresh
        state[:, cols] = renewed
        fin_out[:, cols] = renewed
        reach = cd_s[0:1, cols]
        carry_out[:, cols] = carry_e * reach
        cd_s[0:1, cols] = reach * through
        return carried

    eight_rows = lax.broadcasted_iota(jnp.int32, cd_out.shape, 0)
    cd_out[...] = jnp.where(eight_rows == chunk, cd_s[0:1, :], cd_out[...])
    lax.fori_loop(0, heads // 2, pair, 0, unroll=4)
    cd_out[...] = jnp.where(eight_rows == chunk + 1, cd_s[0:1, :], cd_out[...])

    @pl.when(chunk == chunks - 1)
    def _():
        leaving[micro] = state[...]
        leave_copy(micro).start()

    @pl.when(grid_step == steps - 1)
    def _():
        for number in range(placed + 1, len(plan.order)):
            plan.event(number)
        plan.finish()
        for which in range(leaving.shape[0]):
            leave_copy(which).wait()


def selectors(heads, head_size):
    inner = heads * head_size
    head_of_lane = np.arange(inner) // head_size
    narrow = np.zeros((LANES, inner), np.float32)
    wide = np.zeros((LANES, heads * LANES), np.float32)
    head_of_wide = np.arange(heads * LANES) // LANES
    for part in range(3):
        narrow[part * heads + head_of_lane, np.arange(inner)] = 1.0
        wide[part * heads + head_of_wide, np.arange(heads * LANES)] = 1.0
    return narrow, wide


def whole(shape):
    return pl.BlockSpec(shape, lambda index, *_: (0,) * len(shape))


def forward_ssd(
    marks, micros, raw, rims, inner, twice, tokens,
    cw, cb, ccw, ccb, sbias, rate, skip, sel, selcol, shards, shared, collective_id,
):
    width = twice // 2
    chunks = tokens // CHUNK
    heads = inner // (LANES // 2)
    eighth = CHUNK // 8
    pairs = lax.axis_size("fsdp") // 2
    shard_rows = shards[0].shape[0]
    plan = Gathering(shard_rows, pairs, len(shards), shared)

    def part(count, start):
        return pl.BlockSpec((CHUNK, count), lambda step: (step, start // count))

    def before(count, start):
        return pl.BlockSpec(
            (8, count), lambda step: (jnp.maximum(step * eighth - 1, 0), start // count)
        )

    def edge(count, start):
        return pl.BlockSpec((None, 8, count), lambda step: (step // chunks, 0, start // count))

    def each(*shape):
        return pl.BlockSpec((None, *shape), lambda step: (step // chunks, 0, 0))

    hbm = pl.BlockSpec(memory_space=pl.ANY)
    dma = pltpu.SemaphoreType.DMA
    return pl.pallas_call(
        functools.partial(forward_kernel, heads, chunks, plan),
        grid=(micros * chunks,),
        in_specs=[
            pl.BlockSpec(memory_space=pltpu.SMEM),
            part(inner, 0),
            before(inner, 0),
            edge(inner, 0),
            part(twice, inner),
            before(twice, inner),
            edge(twice, inner),
            part(LANES, inner + twice),
            whole(cw.shape),
            whole(cb.shape),
            whole(ccw.shape),
            whole(ccb.shape),
            whole(sbias.shape),
            whole(rate.shape),
            whole(skip.shape),
            whole(sel.shape),
            whole(selcol.shape),
        ]
        + [hbm] * len(shards),
        out_specs=[
            part(inner, 0),
            pl.BlockSpec((1, width, inner), lambda step: (step, 0, 0)),
            each(width, inner),
            part(twice, 0),
            part(inner, 0),
            each(8, inner),
            hbm,
        ]
        + [hbm] * len(shards),
        scratch_shapes=[
            pltpu.VMEM((width, inner), f32),
            pltpu.VMEM((LANES, CHUNK), f32),
            pltpu.VMEM((3 * CHUNK, LANES), bf16),
            pltpu.VMEM((CHUNK, LANES), bf16),
            pltpu.VMEM((8, inner), f32),
            pltpu.VMEM((3, CHUNK, LANES), f32),
            pltpu.VMEM((CHUNK, CHUNK), f32),
            pltpu.VMEM((CHUNK, CHUNK), f32),
            pltpu.VMEM((8, inner), f32),
            pltpu.VMEM((2, CHUNK, width), bf16),
            pltpu.VMEM((2, width, CHUNK), bf16),
            pltpu.VMEM((micros, width, inner), f32),
            dma((micros,)),
            dma((micros,)),
        ]
        + plan.scratch(),
        out_shape=[
            jax.ShapeDtypeStruct((micros * tokens, inner), f32),
            jax.ShapeDtypeStruct((micros * chunks, width, inner), f32),
            jax.ShapeDtypeStruct((micros, width, inner), f32),
            jax.ShapeDtypeStruct((micros * tokens, twice), f32),
            jax.ShapeDtypeStruct((micros * tokens, inner), f32),
            jax.ShapeDtypeStruct((micros, 8, inner), f32),
            jax.ShapeDtypeStruct((micros, width, inner), f32),
        ]
        + [
            jax.ShapeDtypeStruct((2 * pairs * shard_rows, shard.shape[1]), shard.dtype)
            for shard in shards
        ],
        compiler_params=pltpu.CompilerParams(
            collective_id=collective_id, has_side_effects=True, vmem_limit_bytes=48 * 1024 * 1024
        ),
    )(
        marks, raw, raw, rims, raw, raw, rims, raw, cw, cb, ccw, ccb, sbias, rate, skip, sel, selcol,
        *shards,
    )


def backward_kernel(heads, chunks, plan, waited, *refs):
    (
        marks, vraw, vprev, vrim, craw, cprev, crim, sraw, grad, mixer, st_now, st_next, fin,
        entering, cd, pulled, cw, cb, ccw, ccb, sbias, rate, skip, sel, selcol, selt,
    ) = refs[:26]
    arrays = len(plan.counts)
    refs = refs[26:]
    terms, refs = refs[:arrays], refs[arrays + waited :]
    (
        lead_g, vtail_g, vrim_g, craw_g, crim_g, cw_g, ccw_g, small_g, skip_g,
    ) = refs[:9]
    outs, refs = refs[9 : 9 + arrays], refs[9 + arrays :]
    (
        state, cumt, stack, cumpack, halo, same_s, bias_s, gram_s, cparts, bparts, ctparts,
        rim_s, crim_s, dgram, dcoup, dhead, cd_s,
    ) = refs[:17]
    plan.bind(terms, outs, refs[17:])
    grid_step = pl.program_id(0)
    step_id = lax.rem(grid_step, chunks)
    micro = grid_step // chunks
    chunk = chunks - 1 - step_id
    width = state.shape[0]
    inner = state.shape[1]
    per_step = -(-plan.steps // pl.num_programs(0))

    @pl.when(grid_step == 0)
    def _():
        plan.greet()
        cw_g[...] = jnp.zeros_like(cw_g)
        ccw_g[...] = jnp.zeros_like(ccw_g)
        small_g[...] = jnp.zeros_like(small_g)
        skip_g[...] = jnp.zeros_like(skip_g)

    def reduce_steps(first, count):
        def one(number, carried):
            plan.step(number)
            return carried

        start = grid_step * per_step + first
        lax.fori_loop(start, jnp.minimum(start + count, plan.steps), one, 0)

    @pl.when(step_id == 0)
    def _():
        state[...] = pulled[...]
        rim_s[...] = jnp.zeros_like(rim_s)
        crim_s[...] = jnp.zeros_like(crim_s)

    @pl.when(chunk == 0)
    def _():
        halo[...] = vrim[...]

    @pl.when(chunk > 0)
    def _():
        halo[...] = vprev[...]

    frame = chunk_frame([marks[micro, place] for place in range(3)], chunk, sraw[...], sbias[...], rate[...], heads)
    same = frame["same"]
    for lag in range(1, 4):
        same_s[lag - 1] = same[lag]
    joined = (frame["seg_rows"] == frame["seg_columns"]) & (frame["row_ids"] <= frame["column_ids"])
    bias_s[...] = jnp.where(joined, 0.0, -1e30)
    stack[0:CHUNK, :] = packed_parts(frame["step"], heads)
    stack[CHUNK : 2 * CHUNK, :] = packed_parts(frame["carry"], heads)
    stack[2 * CHUNK : 3 * CHUNK, :] = packed_parts(frame["tail"], heads)
    cumpack[...] = packed_parts(frame["cumulative"], heads)
    cumt[...] = jnp.transpose(frame["cumulative"])
    coupling_halo = jnp.where(chunk == 0, crim[...], cprev[...])
    wide_same = [None] + [jnp.concatenate([same[lag], same[lag]], axis=1) for lag in range(1, 4)]
    craw_now = craw[...]
    pre = conv_sum(craw_now, coupling_halo, lambda lag: ccw[lag : lag + 1, :], ccb[...], wide_same)
    csig = logistic(pre)
    coupled = pre * csig
    b_value = coupled[:, :width]
    c_value = coupled[:, width:]
    b_part = split_two(b_value)
    c_part = split_two(c_value)
    gram_s[...] = mm_three_nt(b_part, c_part)
    cparts[0] = c_part[0]
    cparts[1] = c_part[1]
    bparts[0] = b_part[0]
    bparts[1] = b_part[1]
    ct_part = split_two(jnp.transpose(c_value))
    ctparts[0] = ct_part[0]
    ctparts[1] = ct_part[1]
    dgram[...] = jnp.zeros_like(dgram)
    dcoup[...] = jnp.zeros_like(dcoup)
    dhead[...] = jnp.zeros_like(dhead)
    lane = lax.broadcasted_iota(jnp.int32, (CHUNK, LANES), 1)
    row = lax.broadcasted_iota(jnp.int32, (CHUNK, LANES), 0)
    low_half = (lane < LANES // 2).astype(f32)
    high_half = 1.0 - low_half
    last_row = (row == CHUNK - 1).astype(f32)
    is_end = step_id == 0
    eight_rows = lax.broadcasted_iota(jnp.int32, cd.shape, 0)
    for place in range(2):
        chosen = jnp.where(eight_rows == chunk + place, cd[...], 0.0)
        cd_s[place : place + 1, :] = jnp.sum(chosen, axis=0, keepdims=True)

    def pair(index):
        cols = pl.ds(pl.multiple_of(index * LANES, LANES), LANES)
        wide = pl.ds(pl.multiple_of(index * 2 * LANES, 2 * LANES), 2 * LANES)
        raw = vraw[:, cols]
        full = jnp.concatenate([halo[:, cols], raw], axis=0)
        lagged = [raw] + [pltpu.roll(full, lag, 0)[8:] * same_s[lag - 1] for lag in range(1, 4)]
        pre_value = cb[:, cols]
        for lag in range(4):
            pre_value = pre_value + cw[lag : lag + 1, cols] * lagged[lag]
        sig = logistic(pre_value)
        value = pre_value * sig
        spread = mm(stack[...], sel[:, cols])
        step_e = spread[:CHUNK]
        carry_e = spread[CHUNK : 2 * CHUNK]
        tail_e = spread[2 * CHUNK :]
        inputs = step_e * value
        grads = grad[:, cols]
        column = mm(cumpack[...], selcol[:, wide])
        row_pair = jnp.concatenate(
            [cumt[pl.ds(2 * index, 1), :], cumt[pl.ds(2 * index + 1, 1), :]], axis=1
        )
        bias = bias_s[...]
        gram = gram_s[...]
        decays = jnp.exp(row_pair - column + jnp.concatenate([bias, bias], axis=1))
        mixing = jnp.concatenate([gram, gram], axis=1) * decays
        mix_high, mix_low = split_two(mixing)
        g_low = split_two(grads * low_half)
        g_high = split_two(grads * high_half)
        diag_high = jnp.concatenate([g_low[0], g_high[0]], axis=0)
        diag_low = jnp.concatenate([g_low[1], g_high[1]], axis=0)
        both = mm(mix_high, jnp.concatenate([diag_high, diag_low], axis=1))
        input_g = both[:, :LANES] + both[:, LANES:] + mm(mix_low, diag_high)
        held_g = state[:, cols]
        held_parts = split_two(held_g)
        input_g = input_g + tail_e * mm_three((bparts[0], bparts[1]), held_parts)
        in_parts = split_two(inputs)
        outer = mm_three_nt(in_parts, (diag_high, diag_low)) * decays
        dgram[...] += outer[:, :CHUNK] + outer[:, CHUNK:]
        reach_now = cd_s[0:1, cols]
        reach_next = cd_s[1:2, cols]
        arriving = entering[:, cols]
        held = st_now[0, :, cols] + reach_now * arriving
        next_own = jnp.where(is_end, fin[:, cols], st_next[0, :, cols])
        following = next_own + reach_next * arriving
        carried_g = split_two(carry_e * grads)
        state[:, cols] = carry_e[CHUNK - 1 :, :] * held_g + mm_three(
            (ctparts[0], ctparts[1]), carried_g
        )
        dcoup[1] += mm_three_nt(carried_g, split_two(held))
        dcoup[0] += mm_three_nt(split_two(tail_e * inputs), held_parts)
        value_g = input_g * step_e + skip[:, cols] * grads
        kept = jnp.sum(held_g * following, axis=0, keepdims=True)
        balance = grads * (mixer[:, cols] - skip[:, cols] * value) - inputs * input_g
        balance = balance + last_row * kept
        sums = jnp.concatenate([balance, input_g * value], axis=0)
        sums_parts = split_three(sums)
        pick = selt[cols, :]
        dhead[...] += mm(sums_parts[0], pick) + mm(sums_parts[1], pick) + mm(sums_parts[2], pick)
        skip_g[0:1, cols] += jnp.sum(grads * value, axis=0, keepdims=True)
        pre_g = value_g * (sig * (1.0 + pre_value * (1.0 - sig)))
        cw_g[4:5, cols] += jnp.sum(pre_g, axis=0, keepdims=True)
        raw_g = cw[0:1, cols] * pre_g
        cw_g[0:1, cols] += jnp.sum(pre_g * raw, axis=0, keepdims=True)
        none = jnp.zeros((8, LANES), f32)
        edge = none
        for lag in range(1, 4):
            cw_g[lag : lag + 1, cols] += jnp.sum(pre_g * lagged[lag], axis=0, keepdims=True)
            weighted = cw[lag : lag + 1, cols] * (pre_g * same_s[lag - 1])
            padded = jnp.concatenate([none, weighted, none], axis=0)
            turned = pltpu.roll(padded, CHUNK + 16 - lag, 0)
            raw_g = raw_g + turned[8 : 8 + CHUNK]
            edge = edge + turned[:8]
        last_rows = raw_g[CHUNK - 8 :] + rim_s[:, cols]
        lead_g[:, cols] = jnp.concatenate([raw_g[: CHUNK - 8], last_rows], axis=0).astype(bf16)

        @pl.when(step_id == 0)
        def _():
            vtail_g[:, cols] = last_rows

        rim_s[:, cols] = edge
        vrim_g[:, cols] = edge

    groups = 4
    per_group = heads // 2 // groups

    def group(number, carried):
        for inside in range(per_group):
            pair(number * per_group + inside)
        share = per_step // (groups + 1)
        reduce_steps(number * share, share)
        return carried

    lax.fori_loop(0, groups, group, 0)
    used = groups * (per_step // (groups + 1))
    reduce_steps(used, per_step - used)

    total = dgram[...]
    total_parts = split_two(total)
    turned_parts = split_two(jnp.transpose(total))
    b_grad = dcoup[0] + mm_three(total_parts, (cparts[0], cparts[1]))
    c_grad = dcoup[1] + mm_three(turned_parts, (bparts[0], bparts[1]))
    coupled_g = jnp.concatenate([b_grad, c_grad], axis=1)
    pre_g = coupled_g * (csig * (1.0 + pre * (1.0 - csig)))
    ccw_g[4:5, :] += jnp.sum(pre_g, axis=0, keepdims=True)
    ccw_g[0:1, :] += jnp.sum(pre_g * craw_now, axis=0, keepdims=True)
    raw_g = ccw[0:1, :] * pre_g
    full = jnp.concatenate([coupling_halo, craw_now], axis=0)
    none = jnp.zeros((8, 2 * width), f32)
    edge = none
    for lag in range(1, 4):
        masked = pre_g * wide_same[lag]
        ccw_g[lag : lag + 1, :] += jnp.sum(
            masked * pltpu.roll(full, lag, 0)[8:], axis=0, keepdims=True
        )
        padded = jnp.concatenate([none, ccw[lag : lag + 1, :] * masked, none], axis=0)
        turned = pltpu.roll(padded, CHUNK + 16 - lag, 0)
        raw_g = raw_g + turned[8 : 8 + CHUNK]
        edge = edge + turned[:8]
    craw_g[...] = raw_g
    craw_g[CHUNK - 8 :, :] += crim_s[...]
    crim_s[...] = edge
    crim_g[...] = edge

    upper = (frame["row_ids"] <= frame["column_ids"]).astype(bf16)
    parts = split_three(dhead[:CHUNK])
    decay_g = mm(upper, parts[0]) + mm(upper, parts[1]) + mm(upper, parts[2])
    step_g = (dhead[CHUNK:] - rate[...] * decay_g) * logistic(frame["shifted"])
    lead_g[:, inner : inner + 2 * width] = jnp.zeros((CHUNK, 2 * width), bf16)
    lead_g[:, inner + 2 * width :] = step_g.astype(bf16)
    small_g[0:1, :] += jnp.sum(step_g, axis=0, keepdims=True)
    small_g[1:2, :] += jnp.sum(-frame["step"] * decay_g, axis=0, keepdims=True)


def backward_ssd(
    marks, micros, raw, rims, inner, twice, tokens, grad, mixer, states, fin, entering, cd, pulled,
    cw, cb, ccw, ccb, sbias, rate, skip, sel, selcol, selt, terms, first, collective_id,
):
    width = twice // 2
    chunks = tokens // CHUNK
    heads = inner // (LANES // 2)
    eighth = CHUNK // 8
    pairs = lax.axis_size("fsdp") // 2
    shard_rows = terms[0].shape[0] // (2 * pairs)
    plan = Reduction(shard_rows, pairs, [term.shape[1] for term in terms], 2)
    lead = inner + twice + LANES

    def row(step):
        return step // chunks * chunks + chunks - 1 - lax.rem(step, chunks)

    def part(count, start):
        return pl.BlockSpec((CHUNK, count), lambda step: (row(step), start // count))

    def before(count, start):
        return pl.BlockSpec(
            (8, count), lambda step: (jnp.maximum(row(step) * eighth - 1, 0), start // count)
        )

    def edge(count, start):
        return pl.BlockSpec(
            (None, 8, count), lambda step: (step // chunks, 0, start // count)
        )

    def held(offset):
        return pl.BlockSpec(
            (1, width, inner),
            lambda step: (
                jnp.minimum(row(step) + offset, (step // chunks + 1) * chunks - 1), 0, 0,
            ),
        )

    def each(*shape):
        return pl.BlockSpec((None, *shape), lambda step: (step // chunks, 0, 0))

    hbm = pl.BlockSpec(memory_space=pl.ANY)
    return pl.pallas_call(
        functools.partial(backward_kernel, heads, chunks, plan, len(first)),
        grid=(micros * chunks,),
        in_specs=[
            pl.BlockSpec(memory_space=pltpu.SMEM),
            part(inner, 0),
            before(inner, 0),
            edge(inner, 0),
            part(twice, inner),
            before(twice, inner),
            edge(twice, inner),
            part(LANES, inner + twice),
            part(inner, 0),
            part(inner, 0),
            held(0),
            held(1),
            each(width, inner),
            each(width, inner),
            each(8, inner),
            each(width, inner),
            whole(cw.shape),
            whole(cb.shape),
            whole(ccw.shape),
            whole(ccb.shape),
            whole(sbias.shape),
            whole(rate.shape),
            whole(skip.shape),
            whole(sel.shape),
            whole(selcol.shape),
            whole(selt.shape),
        ]
        + [hbm] * (len(terms) + len(first)),
        out_specs=[
            part(lead, 0),
            each(8, inner),
            each(8, inner),
            part(twice, 0),
            each(8, twice),
            whole((8, inner)),
            whole((8, twice)),
            whole((8, LANES)),
            whole((8, inner)),
        ]
        + [hbm] * len(terms),
        scratch_shapes=[
            pltpu.VMEM((width, inner), f32),
            pltpu.VMEM((LANES, CHUNK), f32),
            pltpu.VMEM((3 * CHUNK, LANES), bf16),
            pltpu.VMEM((CHUNK, LANES), bf16),
            pltpu.VMEM((8, inner), f32),
            pltpu.VMEM((3, CHUNK, LANES), f32),
            pltpu.VMEM((CHUNK, CHUNK), f32),
            pltpu.VMEM((CHUNK, CHUNK), f32),
            pltpu.VMEM((2, CHUNK, width), bf16),
            pltpu.VMEM((2, CHUNK, width), bf16),
            pltpu.VMEM((2, width, CHUNK), bf16),
            pltpu.VMEM((8, inner), f32),
            pltpu.VMEM((8, twice), f32),
            pltpu.VMEM((CHUNK, CHUNK), f32),
            pltpu.VMEM((2, CHUNK, width), f32),
            pltpu.VMEM((2 * CHUNK, LANES), f32),
            pltpu.VMEM((8, inner), f32),
        ]
        + plan.scratch(),
        out_shape=[
            jax.ShapeDtypeStruct((micros * tokens, lead), bf16),
            jax.ShapeDtypeStruct((micros, 8, inner), f32),
            jax.ShapeDtypeStruct((micros, 8, inner), f32),
            jax.ShapeDtypeStruct((micros * tokens, twice), f32),
            jax.ShapeDtypeStruct((micros, 8, twice), f32),
            jax.ShapeDtypeStruct((8, inner), f32),
            jax.ShapeDtypeStruct((8, twice), f32),
            jax.ShapeDtypeStruct((8, LANES), f32),
            jax.ShapeDtypeStruct((8, inner), f32),
        ]
        + [jax.ShapeDtypeStruct((shard_rows, term.shape[1]), f32) for term in terms],
        compiler_params=pltpu.CompilerParams(
            collective_id=collective_id, has_side_effects=True, vmem_limit_bytes=60 * 1024 * 1024
        ),
    )(
        marks, raw, raw, rims, raw, raw, rims, raw, grad, mixer, states, states, fin, entering,
        cd, pulled, cw, cb, ccw, ccb, sbias, rate, skip, sel, selcol, selt,
        *[term.reshape(pairs, 2, shard_rows, -1) for term in terms], *first,
    )


class Gathering:
    def __init__(self, rows, pairs, arrays, shared):
        self.rows, self.pairs, self.arrays, self.shared = rows, pairs, arrays, shared
        self.moved = rows - shared
        self.order = [(j, k) for k in range(pairs) for j in range(arrays)]
        self.lag = max(arrays, 2)

    def scratch(self):
        dma, pairs, arrays = pltpu.SemaphoreType.DMA, self.pairs, self.arrays
        return [
            dma((arrays, max(pairs - 1, 1))),
            dma((arrays, max(pairs - 1, 1))),
            dma((arrays, pairs)),
            dma((arrays, pairs)),
            dma((arrays, 2 * pairs)),
            dma((arrays, 2 * pairs)),
            dma((arrays,)),
        ]

    def bind(self, weights, fulls, scratch):
        self.weights, self.fulls = weights, fulls
        (
            self.ring_send, self.ring_recv, self.pair_send, self.pair_recv,
            self.cross_send, self.cross_recv, self.local,
        ) = scratch
        self.own, self.place = lax.axis_index("fsdp"), lax.axis_index("context")
        self.side = lax.axis_index("tensor")
        self.pair, self.member = self.own // 2, lax.rem(self.own, 2)
        pairs, pair, member = self.pairs, self.pair, self.member
        self.ahead = (2 * lax.rem(pair + 1, pairs) + member, self.place, self.side)
        self.behind = (2 * lax.rem(pair + pairs - 1, pairs) + member, self.place, self.side)
        self.partner = (2 * pair + 1 - member, self.place, self.side)
        self.across = (self.own, 1 - self.place, self.side)
        self.beside = (self.own, self.place, 1 - self.side)
        self.moved_start = pl.multiple_of(self.place * self.shared, 16)
        self.shared_start = pl.multiple_of(self.place * self.moved, 16)

    def greet(self, *others):
        barrier = pltpu.get_barrier_semaphore()
        devices = [self.ahead, self.behind, self.partner, self.across, *others]
        for device in devices:
            pl.semaphore_signal(barrier, inc=1, device_id=device, device_id_type=MESH)
        pl.semaphore_wait(barrier, len(devices))

    def part(self, j, k, which, start, size):
        there = lax.rem(self.pair + self.pairs - k, self.pairs)
        index = 2 * there + (self.member if which == 0 else 1 - self.member)
        return self.fulls[j].at[pl.ds(pl.multiple_of(index * self.rows + start, 16), size), :]

    def source(self, j, k):
        if k == 0:
            return self.weights[j].at[pl.ds(self.moved_start, self.moved), :]
        return self.part(j, k, 0, self.moved_start, self.moved)

    def ring_copy(self, j, k):
        return pltpu.make_async_remote_copy(
            src_ref=self.source(j, k), dst_ref=self.part(j, k, 0, self.moved_start, self.moved),
            send_sem=self.ring_send.at[j, k], recv_sem=self.ring_recv.at[j, k],
            device_id=self.ahead, device_id_type=MESH,
        )

    def pair_copy(self, j, k):
        return pltpu.make_async_remote_copy(
            src_ref=self.source(j, k), dst_ref=self.part(j, k, 0, self.moved_start, self.moved),
            send_sem=self.pair_send.at[j, k], recv_sem=self.pair_recv.at[j, k],
            device_id=self.partner, device_id_type=MESH,
        )

    def cross_copy(self, j, k, which):
        here = self.part(j, k, which, self.shared_start, self.shared)
        return pltpu.make_async_remote_copy(
            src_ref=here, dst_ref=here,
            send_sem=self.cross_send.at[j, 2 * k + which], recv_sem=self.cross_recv.at[j, 2 * k + which],
            device_id=self.across, device_id_type=MESH,
        )

    def keep_copy(self, j):
        rows = pl.ds(pl.multiple_of(self.own * self.rows, 16), self.rows)
        return pltpu.make_async_copy(self.weights[j], self.fulls[j].at[rows, :], self.local.at[j])

    def event(self, number):
        j, k = self.order[number]
        if k > 0:
            self.ring_copy(j, k - 1).wait_recv()
        else:
            self.keep_copy(j).start()
        if k < self.pairs - 1:
            self.ring_copy(j, k).start()
        self.pair_copy(j, k).start()
        if k > 0:
            self.cross_copy(j, k, 0).start()
        if number >= self.lag:
            self.share(number - self.lag)

    def share(self, number):
        j, k = self.order[number]
        self.pair_copy(j, k).wait_recv()
        self.cross_copy(j, k, 1).start()

    def finish(self):
        for number in range(max(len(self.order) - self.lag, 0), len(self.order)):
            self.share(number)
        crossed = [(j, k, which) for j, k in self.order for which in range(2) if k or which]
        for item in crossed:
            self.cross_copy(*item).wait_recv()
        for j, k in self.order:
            if k < self.pairs - 1:
                self.ring_copy(j, k).wait_send()
            self.pair_copy(j, k).wait_send()
        for item in crossed:
            self.cross_copy(*item).wait_send()
        for j in range(self.arrays):
            self.keep_copy(j).wait()


def gather_kernel(plan, *refs):
    arrays = plan.arrays
    weights, tokens = refs[:arrays], refs[arrays]
    fulls, far = refs[arrays + 1 : 2 * arrays + 1], refs[2 * arrays + 1]
    extra_send, extra_recv = refs[2 * arrays + 2 : 2 * arrays + 4]
    plan.bind(weights, fulls, refs[2 * arrays + 4 :])
    plan.greet(plan.beside)
    half = tokens.shape[2] // 2
    lanes = pl.ds(pl.multiple_of(plan.side * half, 128), half)

    def token_copy(src, number, device):
        return pltpu.make_async_remote_copy(
            src_ref=src.at[:, :, lanes], dst_ref=far.at[:, :, lanes],
            send_sem=extra_send.at[number], recv_sem=extra_recv.at[number],
            device_id=device, device_id_type=MESH,
        )

    first, second = token_copy(tokens, 0, plan.across), token_copy(far, 1, plan.beside)
    first.start()
    for number in range(len(plan.order)):
        plan.event(number)
        if number == min(2, len(plan.order) - 1):
            first.wait_recv()
            second.start()
    second.wait_recv()
    plan.finish()
    first.wait_send()
    second.wait_send()


def gather_weights(shards, tokens, shared, collective_id):
    rows = shards[0].shape[0]
    pairs = lax.axis_size("fsdp") // 2
    count = len(shards)
    plan = Gathering(rows, pairs, count, shared)
    hbm = pl.BlockSpec(memory_space=pl.ANY)
    dma = pltpu.SemaphoreType.DMA
    return pl.pallas_call(
        functools.partial(gather_kernel, plan),
        out_shape=[
            jax.ShapeDtypeStruct((2 * pairs * rows, shard.shape[1]), shard.dtype) for shard in shards
        ]
        + [jax.ShapeDtypeStruct(tokens.shape, tokens.dtype)],
        in_specs=[hbm] * (count + 1),
        out_specs=[hbm] * (count + 1),
        scratch_shapes=[dma((2,)), dma((2,))] + plan.scratch(),
        compiler_params=pltpu.CompilerParams(collective_id=collective_id, has_side_effects=True),
    )(*shards, tokens)


def order_kernel(near_index, far_index, is_near, near, far, gain, x_out, normed_out, scale_out):
    step = pl.program_id(0)
    near_now = is_near[step] == 1
    x = jnp.where(near_now, near[...], far[...])
    x_out[...] = x
    value = x.astype(f32)
    mean = jnp.sum(value * value, axis=-1, keepdims=True) * (1.0 / value.shape[-1])
    scale = lax.rsqrt(mean + epsilon)
    normed_out[...] = (value * scale * gain[...]).astype(bf16)
    scale_out[...] = jnp.broadcast_to(scale, scale_out.shape)


def ordered(near, far, near_index, far_index, is_near, gain):
    micros, count, length, model = near.shape
    blocks = micros * count

    def block(spec_index):
        return pl.BlockSpec((None, None, length, model), spec_index)

    def rows(lanes):
        return pl.BlockSpec((length, lanes), lambda step, *_: (step, 0))

    return pl.pallas_call(
        order_kernel,
        grid_spec=pltpu.PrefetchScalarGridSpec(
            num_scalar_prefetch=3,
            grid=(blocks,),
            in_specs=[
                block(lambda step, near_at, far_at, flags: (step // count, near_at[step], 0, 0)),
                block(lambda step, near_at, far_at, flags: (step // count, far_at[step], 0, 0)),
                pl.BlockSpec((1, model), lambda *_: (0, 0)),
            ],
            out_specs=[rows(model), rows(model), rows(LANES)],
        ),
        out_shape=[
            jax.ShapeDtypeStruct((blocks * length, model), bf16),
            jax.ShapeDtypeStruct((blocks * length, model), bf16),
            jax.ShapeDtypeStruct((blocks * length, LANES), f32),
        ],
        compiler_params=pltpu.CompilerParams(vmem_limit_bytes=32 * 1024 * 1024),
    )(near_index, far_index, is_near, near, far, gain)


def gate_kernel(
    normed, out_grad, gate_weight, out_weight, y_own, carry, coupled, entering, gain,
    mixer_out, gate_out, grad_out, sums_out,
):
    gate_in = mm(normed[...], gate_weight[...])
    grads = mm(out_grad[...], out_weight[...])
    width = entering.shape[0]
    arrived = mm_three(split_two(coupled[:, width:]), split_two(entering[...]))
    mixer = y_own[...] + carry[...] * arrived
    gated = mixer * (gate_in * logistic(gate_in))
    mixer_out[...] = mixer
    gate_out[...] = gate_in
    grad_out[...] = grads
    square = jnp.sum(gated * gated, axis=-1, keepdims=True)
    product = jnp.sum(grads * gain[...] * gated, axis=-1, keepdims=True)
    lane = lax.broadcasted_iota(jnp.int32, sums_out.shape, 1)
    sums_out[...] = jnp.where(lane == 0, square, jnp.where(lane == 1, product, 0.0))


def gate_stage(normed, out_grad, gate_weight, out_weight, y_own, carry, coupled, entering, gain):
    rows, model = normed.shape
    inner = y_own.shape[1]
    twice = coupled.shape[1]
    micros, width, _ = entering.shape
    size = 2 * CHUNK
    per_micro = rows // micros // size

    def block(lanes):
        return pl.BlockSpec((size, lanes), lambda step: (step, 0))

    return pl.pallas_call(
        gate_kernel,
        grid=(rows // size,),
        in_specs=[
            block(model),
            block(model),
            pl.BlockSpec((model, inner), lambda step: (0, 0), pipeline_mode=pl.Buffered(1)),
            pl.BlockSpec((model, inner), lambda step: (0, 0), pipeline_mode=pl.Buffered(1)),
            block(inner),
            block(inner),
            block(twice),
            pl.BlockSpec((None, width, inner), lambda step: (step // per_micro, 0, 0)),
            pl.BlockSpec((1, inner), lambda step: (0, 0)),
        ],
        out_specs=[block(inner), block(inner), block(inner), block(LANES)],
        out_shape=[jax.ShapeDtypeStruct((rows, inner), f32)] * 3
        + [jax.ShapeDtypeStruct((rows, LANES), f32)],
        compiler_params=pltpu.CompilerParams(vmem_limit_bytes=60 * 1024 * 1024),
        cost_estimate=pl.CostEstimate(
            flops=4 * rows * model * inner, bytes_accessed=24 * rows * inner, transcendentals=0
        ),
    )(normed, out_grad, gate_weight, out_weight, y_own, carry, coupled, entering, gain)


def gate_back_kernel(
    inner_total, per_micro, mixer, gate_in, grads, carry, coupled, sums, gain,
    norm_out, gate_out, mixer_out, pull_out, gain_out,
):
    step = pl.program_id(0)
    width = pull_out.shape[0]
    inv_norm = lax.rsqrt(sums[:, 0:1] / inner_total + epsilon)
    inner_dot = sums[:, 1:2] * (inv_norm * inv_norm * inv_norm) / inner_total
    mixer_now, gate_now, grad_now = mixer[...], gate_in[...], grads[...]
    sig = logistic(gate_now)
    act = gate_now * sig
    gated = mixer_now * act
    norm_out[...] = (gated * inv_norm * gain[...]).astype(bf16)
    gated_grad = grad_now * gain[...] * inv_norm - gated * inner_dot
    gate_out[...] = (gated_grad * mixer_now * sig * (1.0 + gate_now * (1.0 - sig))).astype(bf16)
    mixer_grad = gated_grad * act
    mixer_out[...] = mixer_grad

    @pl.when(step == 0)
    def _():
        gain_out[...] = jnp.zeros_like(gain_out)

    gain_out[0:1, :] += jnp.sum(grad_now * gated * inv_norm, axis=0, keepdims=True)

    @pl.when(lax.rem(step, per_micro) == 0)
    def _():
        pull_out[...] = jnp.zeros_like(pull_out)

    turned = split_two(jnp.transpose(coupled[:, width:]))
    pull_out[...] += mm_three(turned, split_two(carry[...] * mixer_grad))


def gate_back_stage(mixer, gate_in, grads, carry, coupled, sums, gain, micros, inner_total):
    rows, inner = mixer.shape
    twice = coupled.shape[1]
    width = twice // 2
    per_micro = rows // micros // CHUNK

    def block(lanes):
        return pl.BlockSpec((CHUNK, lanes), lambda step: (step, 0))

    return pl.pallas_call(
        functools.partial(gate_back_kernel, inner_total, per_micro),
        grid=(rows // CHUNK,),
        in_specs=[
            block(inner),
            block(inner),
            block(inner),
            block(inner),
            block(twice),
            block(LANES),
            pl.BlockSpec((1, inner), lambda step: (0, 0)),
        ],
        out_specs=[
            block(inner),
            block(inner),
            block(inner),
            pl.BlockSpec((None, width, inner), lambda step: (step // per_micro, 0, 0)),
            pl.BlockSpec((8, inner), lambda step: (0, 0)),
        ],
        out_shape=[
            jax.ShapeDtypeStruct((rows, inner), bf16),
            jax.ShapeDtypeStruct((rows, inner), bf16),
            jax.ShapeDtypeStruct((rows, inner), f32),
            jax.ShapeDtypeStruct((micros, width, inner), f32),
            jax.ShapeDtypeStruct((8, inner), f32),
        ],
        compiler_params=pltpu.CompilerParams(vmem_limit_bytes=48 * 1024 * 1024),
        cost_estimate=pl.CostEstimate(
            flops=8 * rows * width * inner, bytes_accessed=24 * rows * inner, transcendentals=0
        ),
    )(mixer, gate_in, grads, carry, coupled, sums, gain)


def weave_kernel(first, second, out):
    out[:, 0, :] = first[...]
    out[:, 1, :] = second[...]


def woven(first, second, columns):
    rows = first.shape[0]
    size = 32
    block = pl.BlockSpec((size, columns), lambda step: (step, 0))
    return pl.pallas_call(
        weave_kernel,
        grid=(rows // size,),
        in_specs=[block, block],
        out_specs=pl.BlockSpec((size, 2, columns), lambda step: (step, 0, 0)),
        out_shape=jax.ShapeDtypeStruct((rows, 2, columns), first.dtype),
    )(first, second)


class Reduction:
    def __init__(self, rows, pairs, columns, lag):
        self.rows, self.pairs, self.columns, self.lag = rows, pairs, columns, lag
        self.shared = rows // 4
        self.moved = rows - self.shared
        self.counts = [count // LANES for count in columns]
        self.count = sum(self.counts)
        self.steps = self.count + 4 * lag

    def scratch(self):
        shared, moved, pairs, count = self.shared, self.moved, self.pairs, self.count
        cross, pair, ring = 2 * pairs * shared + 16, pairs * moved + 16, moved + 16
        i16, dma = jnp.int16, pltpu.SemaphoreType.DMA
        return [
            pltpu.VMEM((count, cross, LANES), i16),
            pltpu.VMEM((count, pair, LANES), i16),
            pltpu.VMEM((count, pairs - 1, ring, LANES), i16),
            pltpu.VMEM((count, ring, LANES), i16),
            pltpu.VMEM((2, cross, LANES), i16),
            pltpu.VMEM((2, pair, LANES), i16),
            pltpu.VMEM((2, pairs - 1, ring, LANES), i16),
            pltpu.VMEM((2, ring, LANES), i16),
            pltpu.VMEM((2, pairs, 2, shared, LANES), f32),
            pltpu.VMEM((2, pairs, moved, LANES), f32),
            pltpu.VMEM((2, pairs, moved, LANES), f32),
            pltpu.VMEM((2 * self.lag, moved, LANES), f32),
            pltpu.VMEM((2 * self.lag, moved, LANES), f32),
            pltpu.VMEM((2, self.rows, LANES), f32),
            dma((count,)),
            dma((count,)),
            dma((pairs - 1, count)),
            dma((count,)),
            dma((2,)),
            dma((2,)),
            dma((pairs - 1, 2)),
            dma((2,)),
            dma((3, 2)),
            dma((2,)),
        ]

    def bind(self, terms, outs, scratch):
        self.terms, self.outs = terms, outs
        (
            self.cross_in, self.pair_in, self.ring_in, self.last_in,
            self.cross_out, self.pair_out, self.ring_out, self.last_out,
            self.cross_term, self.pair_term, self.ring_term,
            self.kept, self.held, self.result,
            self.cross_recv, self.pair_recv, self.ring_recv, self.last_recv,
            self.cross_sent, self.pair_sent, self.ring_sent, self.last_sent,
            self.loaded, self.stored,
        ) = scratch
        self.own, self.place = lax.axis_index("fsdp"), lax.axis_index("context")
        self.side = lax.axis_index("tensor")
        self.pair, self.member = self.own // 2, lax.rem(self.own, 2)
        self.across = (self.own, 1 - self.place, self.side)
        self.partner = (2 * self.pair + 1 - self.member, self.place, self.side)
        self.inset = pl.multiple_of(self.place * (self.moved - self.shared), 16)
        self.start = pl.multiple_of(self.place * self.shared, 16)

    def peer(self, offset):
        there = lax.rem(self.pair + offset, self.pairs)
        return (2 * there + self.member, self.place, self.side)

    def greet(self):
        barrier = pltpu.get_barrier_semaphore()
        devices = [self.across, self.partner] + [self.peer(k) for k in range(1, self.pairs)]
        for device in devices:
            pl.semaphore_signal(barrier, inc=1, device_id=device, device_id_type=MESH)
        pl.semaphore_wait(barrier, len(devices))

    def cross_copy(self, chunk):
        slot = lax.rem(chunk, 2)
        return pltpu.make_async_remote_copy(
            src_ref=self.cross_out.at[slot], dst_ref=self.cross_in.at[chunk],
            send_sem=self.cross_sent.at[slot], recv_sem=self.cross_recv.at[chunk],
            device_id=self.across, device_id_type=MESH,
        )

    def pair_copy(self, chunk):
        slot = lax.rem(chunk, 2)
        return pltpu.make_async_remote_copy(
            src_ref=self.pair_out.at[slot], dst_ref=self.pair_in.at[chunk],
            send_sem=self.pair_sent.at[slot], recv_sem=self.pair_recv.at[chunk],
            device_id=self.partner, device_id_type=MESH,
        )

    def ring_copy(self, chunk, offset):
        slot = lax.rem(chunk, 2)
        return pltpu.make_async_remote_copy(
            src_ref=self.ring_out.at[slot, offset - 1], dst_ref=self.ring_in.at[chunk, offset - 1],
            send_sem=self.ring_sent.at[offset - 1, slot],
            recv_sem=self.ring_recv.at[offset - 1, chunk],
            device_id=self.peer(offset), device_id_type=MESH,
        )

    def last_copy(self, chunk):
        slot = lax.rem(chunk, 2)
        return pltpu.make_async_remote_copy(
            src_ref=self.last_out.at[slot], dst_ref=self.last_in.at[chunk],
            send_sem=self.last_sent.at[slot], recv_sem=self.last_recv.at[chunk],
            device_id=self.across, device_id_type=MESH,
        )

    def load_copy(self, stage, term, cols, slot):
        if stage == 0:
            rows = pl.ds(pl.multiple_of((1 - self.place) * self.moved, 16), self.shared)
            src, dst = term.at[:, :, rows, cols], self.cross_term.at[slot]
        elif stage == 1:
            src = term.at[:, 1 - self.member, pl.ds(self.start, self.moved), cols]
            dst = self.pair_term.at[slot]
        else:
            src = term.at[:, self.member, pl.ds(self.start, self.moved), cols]
            dst = self.ring_term.at[slot]
        return pltpu.make_async_copy(src, dst, self.loaded.at[stage, slot])

    def each_array(self, chunk, act):
        first = 0
        for number, count in enumerate(self.counts):
            inside = (chunk >= first) & (chunk < first + count)
            offset = first

            @pl.when(inside)
            def _(number=number, offset=offset):
                act(number, pl.ds(pl.multiple_of((chunk - offset) * LANES, LANES), LANES))

            first += count

    def load(self, stage, chunk):
        @pl.when((chunk >= 0) & (chunk < self.count))
        def _():
            self.each_array(
                chunk,
                lambda number, cols: self.load_copy(
                    stage, self.terms[number], cols, lax.rem(chunk, 2)
                ).start(),
            )

    def loaded_now(self, stage, chunk):
        self.load_copy(stage, self.terms[0], pl.ds(0, LANES), lax.rem(chunk, 2)).wait()

    @staticmethod
    def encode(value, out, place):
        count = value.shape[0]
        peak = jnp.maximum(jnp.max(jnp.abs(value), axis=0, keepdims=True), 1e-30)
        exponent = jnp.ceil(jnp.log(peak) * 1.4426950408889634)
        factor = jnp.exp(exponent * -0.6931471805599453) * 32000.0
        out[place + (pl.ds(0, count), slice(None))] = (
            (value * factor + 12582912.0 - 12582912.0).astype(jnp.int32).astype(jnp.int16)
        )
        out[place + (pl.ds(count, 16), slice(None))] = (
            jnp.broadcast_to(exponent, (16, LANES)).astype(jnp.int32).astype(jnp.int16)
        )

    @staticmethod
    def unit(ref, place, count):
        exponents = ref[place + (pl.ds(count, 16), slice(None))].astype(jnp.int32).astype(f32)
        return jnp.exp(exponents[:1] * 0.6931471805599453) * (1.0 / 32000.0)

    @staticmethod
    def decode(ref, place, first, count, unit):
        first = pl.multiple_of(first, 16) if not isinstance(first, int) else first
        return ref[place + (pl.ds(first, count), slice(None))].astype(jnp.int32).astype(f32) * unit

    def step(self, number):
        lag, pairs, shared, moved = self.lag, self.pairs, self.shared, self.moved

        @pl.when(number == 0)
        def _():
            self.load(0, number)

        self.load(0, number + 1)
        self.load(1, number + 1 - lag)
        self.load(2, number + 1 - 2 * lag)

        def stage(index, act):
            chunk = number - index * lag

            @pl.when((chunk >= 0) & (chunk < self.count))
            def _():
                act(chunk, lax.rem(chunk, 2))

        def cross(chunk, slot):
            self.loaded_now(0, chunk)

            @pl.when(chunk >= 2)
            def _():
                self.cross_copy(chunk - 2).wait_send()

            value = self.cross_term[slot].reshape(2 * pairs * shared, LANES)
            self.encode(value, self.cross_out, (slot,))
            self.cross_copy(chunk).start()

        def pair(chunk, slot):
            self.loaded_now(1, chunk)
            self.cross_copy(chunk).wait_recv()

            @pl.when(chunk >= 2)
            def _():
                self.pair_copy(chunk - 2).wait_send()

            unit = self.unit(self.cross_in, (chunk,), 2 * pairs * shared)
            for there in range(pairs):
                first = (2 * there + 1 - self.member) * shared
                self.pair_term[slot, there, pl.ds(self.inset, shared), :] += self.decode(
                    self.cross_in, (chunk,), first, shared, unit
                )
            value = self.pair_term[slot].reshape(pairs * moved, LANES)
            self.encode(value, self.pair_out, (slot,))
            self.pair_copy(chunk).start()

        def ring(chunk, slot):
            self.loaded_now(2, chunk)
            self.pair_copy(chunk).wait_recv()

            @pl.when(chunk >= 2)
            def _():
                for offset in range(1, pairs):
                    self.ring_copy(chunk - 2, offset).wait_send()

            cross_unit = self.unit(self.cross_in, (chunk,), 2 * pairs * shared)
            pair_unit = self.unit(self.pair_in, (chunk,), pairs * moved)
            for offset in list(range(1, pairs)) + [0]:
                there = lax.rem(self.pair + offset, pairs)
                first = (2 * there + self.member) * shared
                self.ring_term[slot, there, pl.ds(self.inset, shared), :] += self.decode(
                    self.cross_in, (chunk,), first, shared, cross_unit
                )
                value = self.ring_term[slot, there] + self.decode(
                    self.pair_in, (chunk,), there * moved, moved, pair_unit
                )
                if offset:
                    self.encode(value, self.ring_out, (slot, offset - 1))
                    self.ring_copy(chunk, offset).start()
                else:
                    self.kept[lax.rem(chunk, 2 * lag)] = value

        def last(chunk, slot):
            for offset in range(1, pairs):
                self.ring_copy(chunk, offset).wait_recv()

            @pl.when(chunk >= 2)
            def _():
                self.last_copy(chunk - 2).wait_send()

            total = self.kept[lax.rem(chunk, 2 * lag)]
            for offset in range(1, pairs):
                place = (chunk, offset - 1)
                total = total + self.decode(
                    self.ring_in, place, 0, moved, self.unit(self.ring_in, place, moved)
                )
            self.encode(total, self.last_out, (slot,))
            self.held[lax.rem(chunk, 2 * lag)] = self.decode(
                self.last_out, (slot,), 0, moved, self.unit(self.last_out, (slot,), moved)
            )
            self.last_copy(chunk).start()

        def write_copy(number, cols, slot):
            return pltpu.make_async_copy(
                self.result.at[slot], self.outs[number].at[:, cols], self.stored.at[slot]
            )

        def write(chunk, slot):
            self.last_copy(chunk).wait_recv()

            @pl.when(chunk >= 2)
            def _():
                write_copy(0, pl.ds(0, LANES), slot).wait()

            mine = self.held[lax.rem(chunk, 2 * lag)]
            other = self.decode(
                self.last_in, (chunk,), 0, moved, self.unit(self.last_in, (chunk,), moved)
            )
            low = jnp.where(self.place == 0, mine, other)
            high = jnp.where(self.place == 0, other, mine)
            self.result[slot, pl.ds(0, shared), :] = low[:shared]
            self.result[slot, pl.ds(shared, moved - shared), :] = (
                low[shared:] + high[: moved - shared]
            )
            self.result[slot, pl.ds(moved, shared), :] = high[moved - shared :]
            self.each_array(chunk, lambda which, cols: write_copy(which, cols, slot).start())

        stage(4, write)
        stage(3, last)
        stage(2, ring)
        stage(1, pair)
        stage(0, cross)

        @pl.when(number == self.steps - 1)
        def _():
            for slot in range(2):
                write_copy(0, pl.ds(0, LANES), slot).wait()
                self.cross_copy(jnp.int32(self.count - 2 + slot)).wait_send()
                self.pair_copy(jnp.int32(self.count - 2 + slot)).wait_send()
                self.last_copy(jnp.int32(self.count - 2 + slot)).wait_send()
                for offset in range(1, pairs):
                    self.ring_copy(jnp.int32(self.count - 2 + slot), offset).wait_send()


def reduce_kernel(plan, arrays, *refs):
    plan.bind(refs[:arrays], refs[arrays : 2 * arrays], refs[2 * arrays :])
    plan.greet()

    def body(number, carried):
        plan.step(number)
        return carried

    lax.fori_loop(0, plan.steps, body, 0)


def reduce_terms(terms, lag, collective_id):
    pairs = lax.axis_size("fsdp") // 2
    rows = terms[0].shape[0] // (2 * pairs)
    columns = [term.shape[1] for term in terms]
    plan = Reduction(rows, pairs, columns, lag)
    hbm = pl.BlockSpec(memory_space=pl.ANY)
    arrays = len(terms)
    return pl.pallas_call(
        functools.partial(reduce_kernel, plan, arrays),
        out_shape=[jax.ShapeDtypeStruct((rows, count), f32) for count in columns],
        in_specs=[hbm] * arrays,
        out_specs=[hbm] * arrays,
        scratch_shapes=plan.scratch(),
        compiler_params=pltpu.CompilerParams(
            collective_id=collective_id, has_side_effects=True, vmem_limit_bytes=58 * 1024 * 1024
        ),
    )(*[term.reshape(pairs, 2, rows, -1) for term in terms])


def passed_along(value, axis, steps):
    count = lax.axis_size(axis)
    initial, last = (max(0, -steps), min(count, count - steps))
    return lax.ppermute(value, axis, [(source, source + steps) for source in range(initial, last)])


def paired(value, axis):
    count = lax.axis_size(axis)
    return lax.ppermute(value, axis, [(source, source ^ 1) for source in range(count)])


def ring_shift(value, axis, steps):
    count = lax.axis_size(axis)
    return lax.ppermute(
        value, axis, [(source, (source + 2 * steps) % count) for source in range(count)]
    )


def summed_everywhere(values):
    sizes = [value.size for value in values]
    shapes = [value.shape for value in values]
    flat = jnp.concatenate([value.reshape(-1) for value in values])
    count = flat.shape[0]
    flat = jnp.pad(flat, (0, -count % 1024)).reshape(-1, 128)
    for axis in ("context", "fsdp"):
        members = lax.axis_size(axis)
        reach = 1
        while reach < members:
            flat = flat + lax.ppermute(
                flat, axis, [(source, source ^ reach) for source in range(members)]
            )
            reach *= 2
    flat = flat.reshape(-1)
    results, start = [], 0
    for size, shape in zip(sizes, shapes):
        results.append(flat[start : start + size].reshape(shape))
        start += size
    return results


def shards(
    tokens,
    lengths,
    block_order,
    cotangent,
    norm_gain,
    in_weight,
    coupling_weight,
    step_weight,
    out_weight,
    conv_weight,
    conv_bias,
    coupling_conv,
    coupling_bias,
    step_bias,
    decay_rate,
    skip_gain,
    inner_gain,
):
    micros = tokens.shape[0]
    count = tokens.shape[2]
    model = tokens.shape[3]
    inner = inner_gain.shape[0]
    heads = step_bias.shape[0]
    head_size = inner // heads
    twice = coupling_weight.shape[1]
    width = twice // 2
    blocks_row = block_order.shape[2]
    block_len = count * lax.axis_size("context") // blocks_row
    own_blocks = count // block_len
    inner_total = inner * lax.axis_size("tensor")
    side = lax.axis_index("tensor")
    place = lax.axis_index("context")
    base = place * count
    shard_rows = in_weight.shape[0]

    narrow, wide_columns = selectors(heads, head_size)
    sel = jnp.asarray(narrow, bf16)
    selcol = jnp.asarray(wide_columns, bf16)
    selt = jnp.asarray(narrow[:heads].T, bf16)
    selt = jnp.pad(selt, ((0, 0), (0, LANES - heads)))

    lead = jnp.concatenate(
        [
            in_weight[:, 1, :],
            coupling_weight,
            jnp.pad(step_weight, ((0, 0), (0, LANES - heads))),
        ],
        axis=1,
    )
    def sharing(parts):
        return max(shard_rows * parts // 16 // 16 * 16, 16)

    lead_full, far = gather_weights([lead], tokens[:, 0], sharing(3), 1)

    near = tokens[:, 0].reshape(micros, own_blocks, block_len, model)
    far = far.reshape(micros, own_blocks, block_len, model)
    slots = jnp.arange(blocks_row, dtype=jnp.int32)
    wanted = place * own_blocks + jnp.arange(own_blocks, dtype=jnp.int32)
    found = block_order[:, 0, None, :] == wanted[None, :, None]
    slot = jnp.sum(jnp.where(found, slots, 0), axis=2).reshape(-1)
    is_near = (slot // own_blocks == place).astype(jnp.int32)
    inside = slot % own_blocks
    x_input, normed, scales = ordered(
        near, far, inside * is_near, inside * (1 - is_near), is_near, norm_gain.reshape(1, model)
    )
    x_float = x_input.astype(f32)
    inv_rms = scales[:, :1]

    first_end = lengths[:, 0, 0]
    second_end = first_end + lengths[:, 0, 1]
    marks = [
        jnp.stack([first_end[micro], second_end[micro], base]).astype(jnp.int32)
        for micro in range(micros)
    ]
    positions = base + jnp.arange(count, dtype=jnp.int32)
    keep = jnp.concatenate([(positions < second_end[micro]) for micro in range(micros)])
    keep = keep.astype(f32)[:, None]

    cw, cb = conv_weight, conv_bias.reshape(1, inner)
    ccw, ccb = coupling_conv, coupling_bias.reshape(1, twice)
    sbias = jnp.pad(step_bias, (0, LANES - heads)).reshape(1, LANES)
    rate = jnp.pad(decay_rate, (0, LANES - heads)).reshape(1, LANES)
    skip = jnp.dot(
        skip_gain.reshape(1, heads), jnp.asarray(narrow[:heads], f32), precision=lax.Precision.HIGHEST
    )

    raw = jnp.dot(normed, lead_full, preferred_element_type=f32)
    rims = passed_along(
        jnp.stack([raw[(micro + 1) * count - 8 : (micro + 1) * count] for micro in range(micros)]),
        "context",
        1,
    )
    (y_own, states, finals, coupled, carry, reach, entering, gate_full, out_full) = forward_ssd(
        jnp.stack(marks), micros, raw, rims, inner, twice, count,
        cw, cb, ccw, ccb, sbias, rate, skip, sel, selcol,
        [in_weight[:, 0, :], jnp.transpose(out_weight)], sharing(4), 3,
    )
    entering = jnp.where(place == 0, 0.0, entering)
    cot = cotangent[:, 0].reshape(micros * count, model)
    out_grad = cot * keep.astype(bf16)
    gain_row = inner_gain.reshape(1, inner)
    mixer, gate_in, norm_grad, row_sums = gate_stage(
        normed, out_grad, gate_full, out_full, y_own, carry, coupled, entering, gain_row
    )
    row_sums = row_sums + paired(row_sums, "tensor")
    gated_norm, gate_grad, mixer_grad, own_pulls, inner_gain_rows = gate_back_stage(
        mixer, gate_in, norm_grad, carry, coupled, row_sums, gain_row, micros, inner_total
    )
    pulled = passed_along(own_pulls, "context", -1)
    out_term = contract_rows(out_grad, gated_norm)
    gate_term = contract_rows(normed, gate_grad)
    branch = contract_cols(gated_norm, out_full)
    gate_part = contract_cols(gate_grad, gate_full)
    branch_other = paired(branch, "tensor")

    (
        lead_grad, tails, rims_grad, coupling_raw_grad, coupling_rims_grad,
        value_sums, coupling_sums, small_sums, skip_sums, out_shard, gate_shard,
    ) = backward_ssd(
        jnp.stack(marks), micros, raw, rims, inner, twice, count, mixer_grad, mixer, states,
        finals, entering, reach, pulled,
        cw, cb, ccw, ccb, sbias, rate, skip, sel, selcol, selt, [out_term, gate_term], [branch, gate_part], 2,
    )
    edges = passed_along(jnp.concatenate([rims_grad, coupling_rims_grad], axis=2), "context", -1)
    coupling_raw_grad = coupling_raw_grad.reshape(micros, count, twice) + jnp.pad(
        edges[:, :, inner:], ((0, 0), (count - 8, 0), (0, 0))
    )
    coupling_raw_grad = coupling_raw_grad + paired(coupling_raw_grad, "tensor")
    lane_ids = jnp.arange(twice, dtype=jnp.int32)
    own_lanes = ((lane_ids // width) == side).astype(bf16)
    coupling_low = (coupling_raw_grad.astype(bf16) * own_lanes).reshape(micros * count, twice)
    lead_grad = lax.dynamic_update_slice(lead_grad, coupling_low, (0, inner))
    tails = (tails + edges[:, :, :inner]).astype(bf16)
    for micro in range(micros):
        lead_grad = lax.dynamic_update_slice(
            lead_grad, tails[micro], ((micro + 1) * count - 8, 0)
        )
    (lead_shard,) = reduce_terms([contract_rows(normed, lead_grad)], 2, 4)
    normed_part = gate_part + contract_cols(lead_grad, lead_full)
    block_out = (x_float + keep * (branch + branch_other)).astype(bf16)
    normed_grad = normed_part + paired(normed_part, "tensor")
    x_hat = x_float * inv_rms
    hat_grad = normed_grad * norm_gain
    input_grad = (
        cot.astype(f32)
        + inv_rms * (hat_grad - x_hat * jnp.mean(hat_grad * x_hat, axis=-1, keepdims=True))
    ).astype(bf16)
    norm_gain_grad = jnp.sum(normed_grad * x_hat, axis=0)

    skip_sums = skip_sums[0].reshape(heads, head_size).sum(axis=1)
    coupling_sums = coupling_sums + paired(coupling_sums, "tensor")
    (value_all, coupling_all, small_all, skip_all, inner_all, norm_all) = summed_everywhere(
        [value_sums[:5], coupling_sums[:5], small_sums[:2], skip_sums, inner_gain_rows[0], norm_gain_grad]
    )
    coupling_shard = lead_shard[:, inner : inner + twice]
    coupling_shard = coupling_shard + paired(coupling_shard, "tensor")
    return (
        block_out.reshape(micros, 1, count, model),
        input_grad.reshape(micros, 1, count, model),
        norm_all,
        woven(gate_shard, lead_shard, inner),
        coupling_shard,
        lead_shard[:, inner + twice : inner + twice + heads],
        jnp.transpose(out_shard),
        value_all[:4],
        value_all[4],
        coupling_all[:4],
        coupling_all[4],
        small_all[0, :heads],
        small_all[1, :heads],
        skip_all,
        inner_all,
    )


def contract_rows(left, right):
    return lax.dot_general(
        left, right, (((0,), (0,)), ((), ())), preferred_element_type=jnp.float32
    )


def contract_cols(left, right):
    return lax.dot_general(
        left, right, (((1,), (1,)), ((), ())), preferred_element_type=jnp.float32
    )


def solution(mesh):
    return jax.shard_map(
        shards,
        mesh=mesh,
        in_specs=(
            P(None, "fsdp", "context", None),
            P(None, "fsdp", None),
            P(None, "fsdp", None),
            P(None, "fsdp", "context", None),
            P(),
            P("fsdp", None, "tensor"),
            P("fsdp", None),
            P("fsdp", "tensor"),
            P("tensor", "fsdp"),
            P(None, "tensor"),
            P("tensor"),
            P(),
            P(),
            P("tensor"),
            P("tensor"),
            P("tensor"),
            P("tensor"),
        ),
        out_specs=(
            P(None, "fsdp", "context", None),
            P(None, "fsdp", "context", None),
            P(),
            P("fsdp", None, "tensor"),
            P("fsdp", None),
            P("fsdp", "tensor"),
            P("tensor", "fsdp"),
            P(None, "tensor"),
            P("tensor"),
            P(),
            P(),
            P("tensor"),
            P("tensor"),
            P("tensor"),
            P("tensor"),
        ),
        check_vma=False,
    )
```

```python
import functools

import jax
import jax.numpy as jnp
import numpy as np
from jax import lax
from jax.experimental import pallas as pl
from jax.experimental.pallas import tpu as pltpu
from jax.sharding import PartitionSpec as P

CHUNK = 128
LANES = 128
MESH = pl.DeviceIdType.MESH
f32 = jnp.float32
bf16 = jnp.bfloat16
epsilon = 1e-05


def split_two(value):
    high = value.astype(bf16)
    return high, (value - high.astype(f32)).astype(bf16)


def split_three(value):
    high = value.astype(bf16)
    rest = value - high.astype(f32)
    middle = rest.astype(bf16)
    return high, middle, (rest - middle.astype(f32)).astype(bf16)


def mm(left, right):
    return jnp.dot(left, right, preferred_element_type=f32)


def mm_nt(left, right):
    return lax.dot_general(left, right, (((1,), (1,)), ((), ())), preferred_element_type=f32)


def mm_three(left, right):
    wide = mm(left[0], jnp.concatenate([right[0], right[1]], axis=1))
    count = right[0].shape[1]
    return wide[:, :count] + wide[:, count:] + mm(left[1], right[0])


def mm_three_nt(left, right):
    return mm_nt(left[0], right[0]) + mm_nt(left[0], right[1]) + mm_nt(left[1], right[0])


def packed_parts(value, heads):
    high, middle, lowest = split_three(value)
    joined = (
        high.astype(f32)
        + pltpu.roll(middle.astype(f32), heads, 1)
        + pltpu.roll(lowest.astype(f32), 2 * heads, 1)
    )
    return joined.astype(bf16)


def segment_at(position, first_end, second_end):
    first_part = (position >= first_end).astype(jnp.int32)
    second_part = (position >= second_end).astype(jnp.int32)
    return jnp.where(position < 0, -1, first_part + second_part)


def chunk_frame(marks, chunk, step_raw, step_bias, rate, heads):
    first_end, second_end, base = marks[0], marks[1], marks[2]
    start = base + chunk * CHUNK
    rows = start + lax.broadcasted_iota(jnp.int32, (CHUNK, LANES), 0)
    columns = start + lax.broadcasted_iota(jnp.int32, (CHUNK, CHUNK), 1)
    seg_rows = segment_at(rows, first_end, second_end)
    seg_columns = segment_at(columns, first_end, second_end)
    seg_prior = segment_at(start - 1, first_end, second_end)
    seg_last = segment_at(start + CHUNK - 1, first_end, second_end)
    same = [
        (segment_at(rows - lag, first_end, second_end) == seg_rows).astype(f32) for lag in range(4)
    ]
    shifted = step_raw + step_bias
    step = jnp.maximum(shifted, 0.0) + jnp.log1p(jnp.exp(-jnp.abs(shifted)))
    lanes = lax.broadcasted_iota(jnp.int32, (CHUNK, LANES), 1)
    step = jnp.where(lanes < heads, step, 0.0)
    log_decay = -step * rate
    row_ids = lax.broadcasted_iota(jnp.int32, (CHUNK, CHUNK), 0)
    column_ids = lax.broadcasted_iota(jnp.int32, (CHUNK, CHUNK), 1)
    lower = (row_ids >= column_ids).astype(bf16)
    parts = split_three(log_decay)
    cumulative = mm(lower, parts[0]) + mm(lower, parts[1]) + mm(lower, parts[2])
    last = cumulative[CHUNK - 1 :, :]
    carry = jnp.exp(cumulative) * (seg_rows == seg_prior).astype(f32)
    tail = jnp.exp(last - cumulative) * (seg_rows == seg_last).astype(f32)
    live = lanes < heads
    carry = jnp.where(live, carry, 0.0)
    tail = jnp.where(live, tail, 0.0)
    return dict(
        seg_rows=seg_rows,
        seg_columns=seg_columns,
        row_ids=row_ids,
        column_ids=column_ids,
        same=same,
        step=step,
        shifted=shifted,
        cumulative=cumulative,
        carry=carry,
        tail=tail,
    )


def conv_sum(current, halo, weights, biases, same):
    full = jnp.concatenate([halo, current], axis=0)
    total = biases + weights(0) * current
    for lag in range(1, 4):
        total = total + weights(lag) * (pltpu.roll(full, lag, 0)[8:] * same[lag])
    return total


def logistic(value):
    return 1.0 / (1.0 + jnp.exp(-value))


def forward_kernel(heads, chunks, plan, *refs):
    (
        marks, vraw, vprev, vrim, craw, cprev, crim, sraw, cw, cb, ccw, ccb, sbias, rate, skip,
        sel, selcol,
    ) = refs[:17]
    arrays = plan.arrays
    weights, refs = refs[17 : 17 + arrays], refs[17 + arrays :]
    y_out, st_out, fin_out, bc_out, carry_out, cd_out, entering = refs[:7]
    fulls, refs = refs[7 : 7 + arrays], refs[7 + arrays :]
    (
        state, cumt, stack, cumpack, halo, same_s, bias_s, gram_s, cd_s, cparts, btparts,
        leaving, leave_send, leave_recv,
    ) = refs[:14]
    plan.bind(weights, fulls, refs[14:])
    grid_step = pl.program_id(0)
    steps = pl.num_programs(0)
    chunk = lax.rem(grid_step, chunks)
    micro = grid_step // chunks
    width = state.shape[0]
    early = {0: range(2)}
    for when in range(1, min(2 * chunks - 1, len(plan.order) - 1)):
        early[when] = [when + 1]
    placed = len(early)

    def leave_copy(which):
        return pltpu.make_async_remote_copy(
            src_ref=leaving.at[which], dst_ref=entering.at[which],
            send_sem=leave_send.at[which], recv_sem=leave_recv.at[which],
            device_id=plan.across, device_id_type=MESH,
        )

    for when, numbers in early.items():

        @pl.when(grid_step == when)
        def _(when=when, numbers=numbers):
            if when == 0:
                plan.greet()
            for number in numbers:
                plan.event(number)

    @pl.when(chunk == 0)
    def _():
        state[...] = jnp.zeros_like(state)
        cd_s[...] = jnp.ones_like(cd_s)
        cd_out[...] = jnp.zeros_like(cd_out)
        halo[...] = vrim[...]

    @pl.when(chunk > 0)
    def _():
        halo[...] = vprev[...]

    frame = chunk_frame([marks[micro, place] for place in range(3)], chunk, sraw[...], sbias[...], rate[...], heads)
    same = frame["same"]
    for lag in range(1, 4):
        same_s[lag - 1] = same[lag]
    joined = (frame["seg_rows"] == frame["seg_columns"]) & (frame["row_ids"] >= frame["column_ids"])
    bias_s[...] = jnp.where(joined, 0.0, -1e30)
    stack[0:CHUNK, :] = packed_parts(frame["step"], heads)
    stack[CHUNK : 2 * CHUNK, :] = packed_parts(frame["carry"], heads)
    stack[2 * CHUNK : 3 * CHUNK, :] = packed_parts(frame["tail"], heads)
    cumpack[...] = packed_parts(frame["cumulative"], heads)
    cumt[...] = jnp.transpose(frame["cumulative"])
    coupling_halo = jnp.where(chunk == 0, crim[...], cprev[...])
    wide_same = [None] + [jnp.concatenate([same[lag], same[lag]], axis=1) for lag in range(1, 4)]
    pre = conv_sum(
        craw[...], coupling_halo, lambda lag: ccw[lag : lag + 1, :], ccb[...], wide_same
    )
    coupled = pre * logistic(pre)
    bc_out[...] = coupled
    b_part = split_two(coupled[:, :width])
    c_part = split_two(coupled[:, width:])
    gram_s[...] = mm_three_nt(c_part, b_part)
    cparts[0] = c_part[0]
    cparts[1] = c_part[1]
    turned = jnp.transpose(coupled[:, :width])
    bt_part = split_two(turned)
    btparts[0] = bt_part[0]
    btparts[1] = bt_part[1]
    lane = lax.broadcasted_iota(jnp.int32, (CHUNK, LANES), 1)
    low_half = (lane < LANES // 2).astype(f32)
    high_half = 1.0 - low_half

    def pair(index, carried):
        cols = pl.ds(pl.multiple_of(index * LANES, LANES), LANES)
        wide = pl.ds(pl.multiple_of(index * 2 * LANES, 2 * LANES), 2 * LANES)
        pre_value = conv_sum(
            vraw[:, cols],
            halo[:, cols],
            lambda lag: cw[lag : lag + 1, cols],
            cb[:, cols],
            [None] + [same_s[lag - 1] for lag in range(1, 4)],
        )
        value = pre_value * logistic(pre_value)
        spread = mm(stack[...], sel[:, cols])
        step_e = spread[:CHUNK]
        carry_e = spread[CHUNK : 2 * CHUNK]
        tail_e = spread[2 * CHUNK :]
        inputs = step_e * value
        column = mm(cumpack[...], selcol[:, wide])
        row_pair = jnp.concatenate(
            [cumt[pl.ds(2 * index, 1), :], cumt[pl.ds(2 * index + 1, 1), :]], axis=1
        )
        bias = bias_s[...]
        gram = gram_s[...]
        mixing = jnp.concatenate([gram, gram], axis=1) * jnp.exp(
            column - row_pair + jnp.concatenate([bias, bias], axis=1)
        )
        mix_high, mix_low = split_two(mixing)
        in_low = split_two(inputs * low_half)
        in_high = split_two(inputs * high_half)
        diag_high = jnp.concatenate([in_low[0], in_high[0]], axis=0)
        diag_low = jnp.concatenate([in_low[1], in_high[1]], axis=0)
        both = mm(mix_high, jnp.concatenate([diag_high, diag_low], axis=1))
        inside = both[:, :LANES] + both[:, LANES:] + mm(mix_low, diag_high)
        held = state[:, cols]
        from_state = mm_three((cparts[0], cparts[1]), split_two(held))
        y_out[:, cols] = inside + carry_e * from_state + skip[:, cols] * value
        fresh = mm_three((btparts[0], btparts[1]), split_two(tail_e * inputs))
        through = carry_e[CHUNK - 1 :, :]
        st_out[0, :, cols] = held
        renewed = through * held + fresh
        state[:, cols] = renewed
        fin_out[:, cols] = renewed
        reach = cd_s[0:1, cols]
        carry_out[:, cols] = carry_e * reach
        cd_s[0:1, cols] = reach * through
        return carried

    eight_rows = lax.broadcasted_iota(jnp.int32, cd_out.shape, 0)
    cd_out[...] = jnp.where(eight_rows == chunk, cd_s[0:1, :], cd_out[...])
    lax.fori_loop(0, heads // 2, pair, 0, unroll=4)
    cd_out[...] = jnp.where(eight_rows == chunk + 1, cd_s[0:1, :], cd_out[...])

    @pl.when(chunk == chunks - 1)
    def _():
        leaving[micro] = state[...]
        leave_copy(micro).start()

    @pl.when(grid_step == steps - 1)
    def _():
        for number in range(placed + 1, len(plan.order)):
            plan.event(number)
        plan.finish()
        for which in range(leaving.shape[0]):
            leave_copy(which).wait()


def selectors(heads, head_size):
    inner = heads * head_size
    head_of_lane = np.arange(inner) // head_size
    narrow = np.zeros((LANES, inner), np.float32)
    wide = np.zeros((LANES, heads * LANES), np.float32)
    head_of_wide = np.arange(heads * LANES) // LANES
    for part in range(3):
        narrow[part * heads + head_of_lane, np.arange(inner)] = 1.0
        wide[part * heads + head_of_wide, np.arange(heads * LANES)] = 1.0
    return narrow, wide


def whole(shape):
    return pl.BlockSpec(shape, lambda index, *_: (0,) * len(shape))


def forward_ssd(
    marks, micros, raw, rims, inner, twice, tokens,
    cw, cb, ccw, ccb, sbias, rate, skip, sel, selcol, shards, shared, collective_id,
):
    width = twice // 2
    chunks = tokens // CHUNK
    heads = inner // (LANES // 2)
    eighth = CHUNK // 8
    pairs = lax.axis_size("fsdp") // 2
    shard_rows = shards[0].shape[0]
    plan = Gathering(shard_rows, pairs, [shard.shape[1] for shard in shards], 2, shared)

    def part(count, start):
        return pl.BlockSpec((CHUNK, count), lambda step: (step, start // count))

    def before(count, start):
        return pl.BlockSpec(
            (8, count), lambda step: (jnp.maximum(step * eighth - 1, 0), start // count)
        )

    def edge(count, start):
        return pl.BlockSpec((None, 8, count), lambda step: (step // chunks, 0, start // count))

    def each(*shape):
        return pl.BlockSpec((None, *shape), lambda step: (step // chunks, 0, 0))

    hbm = pl.BlockSpec(memory_space=pl.ANY)
    dma = pltpu.SemaphoreType.DMA
    return pl.pallas_call(
        functools.partial(forward_kernel, heads, chunks, plan),
        grid=(micros * chunks,),
        in_specs=[
            pl.BlockSpec(memory_space=pltpu.SMEM),
            part(inner, 0),
            before(inner, 0),
            edge(inner, 0),
            part(twice, inner),
            before(twice, inner),
            edge(twice, inner),
            part(LANES, inner + twice),
            whole(cw.shape),
            whole(cb.shape),
            whole(ccw.shape),
            whole(ccb.shape),
            whole(sbias.shape),
            whole(rate.shape),
            whole(skip.shape),
            whole(sel.shape),
            whole(selcol.shape),
        ]
        + [hbm] * len(shards),
        out_specs=[
            part(inner, 0),
            pl.BlockSpec((1, width, inner), lambda step: (step, 0, 0)),
            each(width, inner),
            part(twice, 0),
            part(inner, 0),
            each(8, inner),
            hbm,
        ]
        + [hbm] * len(shards),
        scratch_shapes=[
            pltpu.VMEM((width, inner), f32),
            pltpu.VMEM((LANES, CHUNK), f32),
            pltpu.VMEM((3 * CHUNK, LANES), bf16),
            pltpu.VMEM((CHUNK, LANES), bf16),
            pltpu.VMEM((8, inner), f32),
            pltpu.VMEM((3, CHUNK, LANES), f32),
            pltpu.VMEM((CHUNK, CHUNK), f32),
            pltpu.VMEM((CHUNK, CHUNK), f32),
            pltpu.VMEM((8, inner), f32),
            pltpu.VMEM((2, CHUNK, width), bf16),
            pltpu.VMEM((2, width, CHUNK), bf16),
            pltpu.VMEM((micros, width, inner), f32),
            dma((micros,)),
            dma((micros,)),
        ]
        + plan.scratch(),
        out_shape=[
            jax.ShapeDtypeStruct((micros * tokens, inner), f32),
            jax.ShapeDtypeStruct((micros * chunks, width, inner), f32),
            jax.ShapeDtypeStruct((micros, width, inner), f32),
            jax.ShapeDtypeStruct((micros * tokens, twice), f32),
            jax.ShapeDtypeStruct((micros * tokens, inner), f32),
            jax.ShapeDtypeStruct((micros, 8, inner), f32),
            jax.ShapeDtypeStruct((micros, width, inner), f32),
        ]
        + [
            jax.ShapeDtypeStruct((2 * pairs * shard_rows, shard.shape[1]), shard.dtype)
            for shard in shards
        ],
        compiler_params=pltpu.CompilerParams(
            collective_id=collective_id, has_side_effects=True, vmem_limit_bytes=48 * 1024 * 1024
        ),
    )(
        marks, raw, raw, rims, raw, raw, rims, raw, cw, cb, ccw, ccb, sbias, rate, skip, sel, selcol,
        *shards,
    )


def backward_kernel(heads, chunks, plan, waited, *refs):
    (
        marks, vraw, vprev, vrim, craw, cprev, crim, sraw, grad, mixer, st_now, st_next, fin,
        entering, cd, pulled, cw, cb, ccw, ccb, sbias, rate, skip, sel, selcol, selt,
    ) = refs[:26]
    arrays = len(plan.counts)
    refs = refs[26:]
    terms, refs = refs[:arrays], refs[arrays + waited :]
    (
        lead_g, vtail_g, vrim_g, craw_g, crim_g, cw_g, ccw_g, small_g, skip_g,
    ) = refs[:9]
    outs, refs = refs[9 : 9 + arrays], refs[9 + arrays :]
    (
        state, cumt, stack, cumpack, halo, same_s, bias_s, gram_s, cparts, bparts, ctparts,
        rim_s, crim_s, dgram, dcoup, dhead, cd_s,
    ) = refs[:17]
    plan.bind(terms, outs, refs[17:])
    grid_step = pl.program_id(0)
    step_id = lax.rem(grid_step, chunks)
    micro = grid_step // chunks
    chunk = chunks - 1 - step_id
    width = state.shape[0]
    inner = state.shape[1]
    per_step = -(-plan.steps // pl.num_programs(0))

    @pl.when(grid_step == 0)
    def _():
        plan.greet()
        cw_g[...] = jnp.zeros_like(cw_g)
        ccw_g[...] = jnp.zeros_like(ccw_g)
        small_g[...] = jnp.zeros_like(small_g)
        skip_g[...] = jnp.zeros_like(skip_g)

    def reduce_steps(first, count):
        def one(number, carried):
            plan.step(number)
            return carried

        start = grid_step * per_step + first
        lax.fori_loop(start, jnp.minimum(start + count, plan.steps), one, 0)

    @pl.when(step_id == 0)
    def _():
        state[...] = pulled[...]
        rim_s[...] = jnp.zeros_like(rim_s)
        crim_s[...] = jnp.zeros_like(crim_s)

    @pl.when(chunk == 0)
    def _():
        halo[...] = vrim[...]

    @pl.when(chunk > 0)
    def _():
        halo[...] = vprev[...]

    frame = chunk_frame([marks[micro, place] for place in range(3)], chunk, sraw[...], sbias[...], rate[...], heads)
    same = frame["same"]
    for lag in range(1, 4):
        same_s[lag - 1] = same[lag]
    joined = (frame["seg_rows"] == frame["seg_columns"]) & (frame["row_ids"] <= frame["column_ids"])
    bias_s[...] = jnp.where(joined, 0.0, -1e30)
    stack[0:CHUNK, :] = packed_parts(frame["step"], heads)
    stack[CHUNK : 2 * CHUNK, :] = packed_parts(frame["carry"], heads)
    stack[2 * CHUNK : 3 * CHUNK, :] = packed_parts(frame["tail"], heads)
    cumpack[...] = packed_parts(frame["cumulative"], heads)
    cumt[...] = jnp.transpose(frame["cumulative"])
    coupling_halo = jnp.where(chunk == 0, crim[...], cprev[...])
    wide_same = [None] + [jnp.concatenate([same[lag], same[lag]], axis=1) for lag in range(1, 4)]
    craw_now = craw[...]
    pre = conv_sum(craw_now, coupling_halo, lambda lag: ccw[lag : lag + 1, :], ccb[...], wide_same)
    csig = logistic(pre)
    coupled = pre * csig
    b_value = coupled[:, :width]
    c_value = coupled[:, width:]
    b_part = split_two(b_value)
    c_part = split_two(c_value)
    gram_s[...] = mm_three_nt(b_part, c_part)
    cparts[0] = c_part[0]
    cparts[1] = c_part[1]
    bparts[0] = b_part[0]
    bparts[1] = b_part[1]
    ct_part = split_two(jnp.transpose(c_value))
    ctparts[0] = ct_part[0]
    ctparts[1] = ct_part[1]
    dgram[...] = jnp.zeros_like(dgram)
    dcoup[...] = jnp.zeros_like(dcoup)
    dhead[...] = jnp.zeros_like(dhead)
    lane = lax.broadcasted_iota(jnp.int32, (CHUNK, LANES), 1)
    row = lax.broadcasted_iota(jnp.int32, (CHUNK, LANES), 0)
    low_half = (lane < LANES // 2).astype(f32)
    high_half = 1.0 - low_half
    last_row = (row == CHUNK - 1).astype(f32)
    is_end = step_id == 0
    eight_rows = lax.broadcasted_iota(jnp.int32, cd.shape, 0)
    for place in range(2):
        chosen = jnp.where(eight_rows == chunk + place, cd[...], 0.0)
        cd_s[place : place + 1, :] = jnp.sum(chosen, axis=0, keepdims=True)

    def pair(index):
        cols = pl.ds(pl.multiple_of(index * LANES, LANES), LANES)
        wide = pl.ds(pl.multiple_of(index * 2 * LANES, 2 * LANES), 2 * LANES)
        raw = vraw[:, cols]
        full = jnp.concatenate([halo[:, cols], raw], axis=0)
        lagged = [raw] + [pltpu.roll(full, lag, 0)[8:] * same_s[lag - 1] for lag in range(1, 4)]
        pre_value = cb[:, cols]
        for lag in range(4):
            pre_value = pre_value + cw[lag : lag + 1, cols] * lagged[lag]
        sig = logistic(pre_value)
        value = pre_value * sig
        spread = mm(stack[...], sel[:, cols])
        step_e = spread[:CHUNK]
        carry_e = spread[CHUNK : 2 * CHUNK]
        tail_e = spread[2 * CHUNK :]
        inputs = step_e * value
        grads = grad[:, cols]
        column = mm(cumpack[...], selcol[:, wide])
        row_pair = jnp.concatenate(
            [cumt[pl.ds(2 * index, 1), :], cumt[pl.ds(2 * index + 1, 1), :]], axis=1
        )
        bias = bias_s[...]
        gram = gram_s[...]
        decays = jnp.exp(row_pair - column + jnp.concatenate([bias, bias], axis=1))
        mixing = jnp.concatenate([gram, gram], axis=1) * decays
        mix_high, mix_low = split_two(mixing)
        g_low = split_two(grads * low_half)
        g_high = split_two(grads * high_half)
        diag_high = jnp.concatenate([g_low[0], g_high[0]], axis=0)
        diag_low = jnp.concatenate([g_low[1], g_high[1]], axis=0)
        both = mm(mix_high, jnp.concatenate([diag_high, diag_low], axis=1))
        input_g = both[:, :LANES] + both[:, LANES:] + mm(mix_low, diag_high)
        held_g = state[:, cols]
        held_parts = split_two(held_g)
        input_g = input_g + tail_e * mm_three((bparts[0], bparts[1]), held_parts)
        in_parts = split_two(inputs)
        outer = mm_three_nt(in_parts, (diag_high, diag_low)) * decays
        dgram[...] += outer[:, :CHUNK] + outer[:, CHUNK:]
        reach_now = cd_s[0:1, cols]
        reach_next = cd_s[1:2, cols]
        arriving = entering[:, cols]
        held = st_now[0, :, cols] + reach_now * arriving
        next_own = jnp.where(is_end, fin[:, cols], st_next[0, :, cols])
        following = next_own + reach_next * arriving
        carried_g = split_two(carry_e * grads)
        state[:, cols] = carry_e[CHUNK - 1 :, :] * held_g + mm_three(
            (ctparts[0], ctparts[1]), carried_g
        )
        dcoup[1] += mm_three_nt(carried_g, split_two(held))
        dcoup[0] += mm_three_nt(split_two(tail_e * inputs), held_parts)
        value_g = input_g * step_e + skip[:, cols] * grads
        kept = jnp.sum(held_g * following, axis=0, keepdims=True)
        balance = grads * (mixer[:, cols] - skip[:, cols] * value) - inputs * input_g
        balance = balance + last_row * kept
        sums = jnp.concatenate([balance, input_g * value], axis=0)
        sums_parts = split_three(sums)
        pick = selt[cols, :]
        dhead[...] += mm(sums_parts[0], pick) + mm(sums_parts[1], pick) + mm(sums_parts[2], pick)
        skip_g[0:1, cols] += jnp.sum(grads * value, axis=0, keepdims=True)
        pre_g = value_g * (sig * (1.0 + pre_value * (1.0 - sig)))
        cw_g[4:5, cols] += jnp.sum(pre_g, axis=0, keepdims=True)
        raw_g = cw[0:1, cols] * pre_g
        cw_g[0:1, cols] += jnp.sum(pre_g * raw, axis=0, keepdims=True)
        none = jnp.zeros((8, LANES), f32)
        edge = none
        for lag in range(1, 4):
            cw_g[lag : lag + 1, cols] += jnp.sum(pre_g * lagged[lag], axis=0, keepdims=True)
            weighted = cw[lag : lag + 1, cols] * (pre_g * same_s[lag - 1])
            padded = jnp.concatenate([none, weighted, none], axis=0)
            turned = pltpu.roll(padded, CHUNK + 16 - lag, 0)
            raw_g = raw_g + turned[8 : 8 + CHUNK]
            edge = edge + turned[:8]
        last_rows = raw_g[CHUNK - 8 :] + rim_s[:, cols]
        lead_g[:, cols] = jnp.concatenate([raw_g[: CHUNK - 8], last_rows], axis=0).astype(bf16)

        @pl.when(step_id == 0)
        def _():
            vtail_g[:, cols] = last_rows

        rim_s[:, cols] = edge
        vrim_g[:, cols] = edge

    groups = 4
    per_group = heads // 2 // groups

    def group(number, carried):
        for inside in range(per_group):
            pair(number * per_group + inside)
        share = per_step // (groups + 1)
        reduce_steps(number * share, share)
        return carried

    lax.fori_loop(0, groups, group, 0)
    used = groups * (per_step // (groups + 1))
    reduce_steps(used, per_step - used)

    total = dgram[...]
    total_parts = split_two(total)
    turned_parts = split_two(jnp.transpose(total))
    b_grad = dcoup[0] + mm_three(total_parts, (cparts[0], cparts[1]))
    c_grad = dcoup[1] + mm_three(turned_parts, (bparts[0], bparts[1]))
    coupled_g = jnp.concatenate([b_grad, c_grad], axis=1)
    pre_g = coupled_g * (csig * (1.0 + pre * (1.0 - csig)))
    ccw_g[4:5, :] += jnp.sum(pre_g, axis=0, keepdims=True)
    ccw_g[0:1, :] += jnp.sum(pre_g * craw_now, axis=0, keepdims=True)
    raw_g = ccw[0:1, :] * pre_g
    full = jnp.concatenate([coupling_halo, craw_now], axis=0)
    none = jnp.zeros((8, 2 * width), f32)
    edge = none
    for lag in range(1, 4):
        masked = pre_g * wide_same[lag]
        ccw_g[lag : lag + 1, :] += jnp.sum(
            masked * pltpu.roll(full, lag, 0)[8:], axis=0, keepdims=True
        )
        padded = jnp.concatenate([none, ccw[lag : lag + 1, :] * masked, none], axis=0)
        turned = pltpu.roll(padded, CHUNK + 16 - lag, 0)
        raw_g = raw_g + turned[8 : 8 + CHUNK]
        edge = edge + turned[:8]
    craw_g[...] = raw_g
    craw_g[CHUNK - 8 :, :] += crim_s[...]
    crim_s[...] = edge
    crim_g[...] = edge

    upper = (frame["row_ids"] <= frame["column_ids"]).astype(bf16)
    parts = split_three(dhead[:CHUNK])
    decay_g = mm(upper, parts[0]) + mm(upper, parts[1]) + mm(upper, parts[2])
    step_g = (dhead[CHUNK:] - rate[...] * decay_g) * logistic(frame["shifted"])
    lead_g[:, inner : inner + 2 * width] = jnp.zeros((CHUNK, 2 * width), bf16)
    lead_g[:, inner + 2 * width :] = step_g.astype(bf16)
    small_g[0:1, :] += jnp.sum(step_g, axis=0, keepdims=True)
    small_g[1:2, :] += jnp.sum(-frame["step"] * decay_g, axis=0, keepdims=True)


def backward_ssd(
    marks, micros, raw, rims, inner, twice, tokens, grad, mixer, states, fin, entering, cd, pulled,
    cw, cb, ccw, ccb, sbias, rate, skip, sel, selcol, selt, terms, first, collective_id,
):
    width = twice // 2
    chunks = tokens // CHUNK
    heads = inner // (LANES // 2)
    eighth = CHUNK // 8
    pairs = lax.axis_size("fsdp") // 2
    shard_rows = terms[0].shape[0] // (2 * pairs)
    plan = Reduction(shard_rows, pairs, [term.shape[1] for term in terms], 2)
    lead = inner + twice + LANES

    def row(step):
        return step // chunks * chunks + chunks - 1 - lax.rem(step, chunks)

    def part(count, start):
        return pl.BlockSpec((CHUNK, count), lambda step: (row(step), start // count))

    def before(count, start):
        return pl.BlockSpec(
            (8, count), lambda step: (jnp.maximum(row(step) * eighth - 1, 0), start // count)
        )

    def edge(count, start):
        return pl.BlockSpec(
            (None, 8, count), lambda step: (step // chunks, 0, start // count)
        )

    def held(offset):
        return pl.BlockSpec(
            (1, width, inner),
            lambda step: (
                jnp.minimum(row(step) + offset, (step // chunks + 1) * chunks - 1), 0, 0,
            ),
        )

    def each(*shape):
        return pl.BlockSpec((None, *shape), lambda step: (step // chunks, 0, 0))

    hbm = pl.BlockSpec(memory_space=pl.ANY)
    return pl.pallas_call(
        functools.partial(backward_kernel, heads, chunks, plan, len(first)),
        grid=(micros * chunks,),
        in_specs=[
            pl.BlockSpec(memory_space=pltpu.SMEM),
            part(inner, 0),
            before(inner, 0),
            edge(inner, 0),
            part(twice, inner),
            before(twice, inner),
            edge(twice, inner),
            part(LANES, inner + twice),
            part(inner, 0),
            part(inner, 0),
            held(0),
            held(1),
            each(width, inner),
            each(width, inner),
            each(8, inner),
            each(width, inner),
            whole(cw.shape),
            whole(cb.shape),
            whole(ccw.shape),
            whole(ccb.shape),
            whole(sbias.shape),
            whole(rate.shape),
            whole(skip.shape),
            whole(sel.shape),
            whole(selcol.shape),
            whole(selt.shape),
        ]
        + [hbm] * (len(terms) + len(first)),
        out_specs=[
            part(lead, 0),
            each(8, inner),
            each(8, inner),
            part(twice, 0),
            each(8, twice),
            whole((8, inner)),
            whole((8, twice)),
            whole((8, LANES)),
            whole((8, inner)),
        ]
        + [hbm] * len(terms),
        scratch_shapes=[
            pltpu.VMEM((width, inner), f32),
            pltpu.VMEM((LANES, CHUNK), f32),
            pltpu.VMEM((3 * CHUNK, LANES), bf16),
            pltpu.VMEM((CHUNK, LANES), bf16),
            pltpu.VMEM((8, inner), f32),
            pltpu.VMEM((3, CHUNK, LANES), f32),
            pltpu.VMEM((CHUNK, CHUNK), f32),
            pltpu.VMEM((CHUNK, CHUNK), f32),
            pltpu.VMEM((2, CHUNK, width), bf16),
            pltpu.VMEM((2, CHUNK, width), bf16),
            pltpu.VMEM((2, width, CHUNK), bf16),
            pltpu.VMEM((8, inner), f32),
            pltpu.VMEM((8, twice), f32),
            pltpu.VMEM((CHUNK, CHUNK), f32),
            pltpu.VMEM((2, CHUNK, width), f32),
            pltpu.VMEM((2 * CHUNK, LANES), f32),
            pltpu.VMEM((8, inner), f32),
        ]
        + plan.scratch(),
        out_shape=[
            jax.ShapeDtypeStruct((micros * tokens, lead), bf16),
            jax.ShapeDtypeStruct((micros, 8, inner), f32),
            jax.ShapeDtypeStruct((micros, 8, inner), f32),
            jax.ShapeDtypeStruct((micros * tokens, twice), f32),
            jax.ShapeDtypeStruct((micros, 8, twice), f32),
            jax.ShapeDtypeStruct((8, inner), f32),
            jax.ShapeDtypeStruct((8, twice), f32),
            jax.ShapeDtypeStruct((8, LANES), f32),
            jax.ShapeDtypeStruct((8, inner), f32),
        ]
        + [jax.ShapeDtypeStruct((shard_rows, term.shape[1]), f32) for term in terms],
        compiler_params=pltpu.CompilerParams(
            collective_id=collective_id, has_side_effects=True, vmem_limit_bytes=60 * 1024 * 1024
        ),
    )(
        marks, raw, raw, rims, raw, raw, rims, raw, grad, mixer, states, states, fin, entering,
        cd, pulled, cw, cb, ccw, ccb, sbias, rate, skip, sel, selcol, selt,
        *[term.reshape(pairs, 2, shard_rows, -1) for term in terms], *first,
    )


class Gathering:
    def __init__(self, rows, pairs, widths, cuts, shared):
        self.rows, self.pairs, self.shared = rows, pairs, shared
        self.arrays = len(widths)
        self.pieces = []
        for array, width in enumerate(widths):
            size = -(-width // LANES // cuts) * LANES
            self.pieces += [
                (array, start, min(size, width - start)) for start in range(0, width, size)
            ]
        self.moved = rows - shared
        self.early = min(rows // 8, self.moved - shared) // 16 * 16
        self.late = self.moved - self.early
        self.order = [(j, k) for j in range(len(self.pieces)) for k in range(pairs)]
        if pairs > 1:
            self.order.sort(key=lambda item: (item[0] * pairs + (item[1] or -0.5 - (item[0] > 0))))
        self.lag = 2

    def scratch(self):
        dma, pairs, arrays = pltpu.SemaphoreType.DMA, self.pairs, len(self.pieces)
        return [
            dma((arrays, max(pairs - 1, 1))),
            dma((arrays, max(pairs - 1, 1))),
            dma((arrays, pairs)),
            dma((arrays, pairs)),
            dma((arrays, 2 * pairs)),
            dma((arrays, 2 * pairs)),
            dma((arrays, 2 * pairs)),
            dma((arrays, 2 * pairs)),
            dma((arrays,)),
        ]

    def bind(self, weights, fulls, scratch):
        self.weights, self.fulls = weights, fulls
        (
            self.ring_send, self.ring_recv, self.pair_send, self.pair_recv,
            self.cross_send, self.cross_recv, self.early_send, self.early_recv, self.local,
        ) = scratch
        self.own, self.place = lax.axis_index("fsdp"), lax.axis_index("context")
        self.side = lax.axis_index("tensor")
        self.pair, self.member = self.own // 2, lax.rem(self.own, 2)
        pairs, pair, member = self.pairs, self.pair, self.member
        self.ahead = (2 * lax.rem(pair + 1, pairs) + member, self.place, self.side)
        self.behind = (2 * lax.rem(pair + pairs - 1, pairs) + member, self.place, self.side)
        self.partner = (2 * pair + 1 - member, self.place, self.side)
        self.across = (self.own, 1 - self.place, self.side)
        self.beside = (self.own, self.place, 1 - self.side)
        self.late_start = pl.multiple_of(self.place * (self.shared + self.early), 16)
        self.early_start = pl.multiple_of(
            self.place * self.shared + (1 - self.place) * self.late, 16
        )
        self.shared_start = pl.multiple_of(self.place * self.moved, 16)

    def greet(self, *others):
        barrier = pltpu.get_barrier_semaphore()
        devices = [self.ahead, self.behind, self.partner, self.across, *others]
        for device in devices:
            pl.semaphore_signal(barrier, inc=1, device_id=device, device_id_type=MESH)
        pl.semaphore_wait(barrier, len(devices))

    def part(self, j, k, which, start, size):
        there = lax.rem(self.pair + self.pairs - k, self.pairs)
        index = 2 * there + (self.member if which == 0 else 1 - self.member)
        array, first, width = self.pieces[j]
        rows = pl.ds(pl.multiple_of(index * self.rows + start, 16), size)
        return self.fulls[array].at[rows, pl.ds(first, width)]

    def source(self, j, k, which, start, size):
        if k == 0 and which == 0:
            array, first, width = self.pieces[j]
            return self.weights[array].at[pl.ds(start, size), pl.ds(first, width)]
        return self.part(j, k, which, start, size)

    def ring_copy(self, j, k):
        return pltpu.make_async_remote_copy(
            src_ref=self.source(j, k, 0, self.late_start, self.late),
            dst_ref=self.part(j, k, 0, self.late_start, self.late),
            send_sem=self.ring_send.at[j, k], recv_sem=self.ring_recv.at[j, k],
            device_id=self.ahead, device_id_type=MESH,
        )

    def pair_copy(self, j, k):
        return pltpu.make_async_remote_copy(
            src_ref=self.source(j, k, 0, self.late_start, self.late),
            dst_ref=self.part(j, k, 0, self.late_start, self.late),
            send_sem=self.pair_send.at[j, k], recv_sem=self.pair_recv.at[j, k],
            device_id=self.partner, device_id_type=MESH,
        )

    def early_copy(self, j, k, which):
        own = k == self.pairs - 1
        k = 0 if own else k
        slot = 2 * self.pairs - 2 if own else 2 * k + which
        return pltpu.make_async_remote_copy(
            src_ref=self.source(j, k, which, self.early_start, self.early),
            dst_ref=self.part(j, k, which, self.early_start, self.early),
            send_sem=self.early_send.at[j, slot], recv_sem=self.early_recv.at[j, slot],
            device_id=self.partner if own else self.ahead, device_id_type=MESH,
        )

    def early_event(self, j, k):
        last = self.pairs - 1
        if k == 0:
            self.early_copy(j, last, 0).start()
        else:
            self.early_copy(j, k - 1, 0).wait_recv()
        if k < last:
            self.early_copy(j, k, 0).start()
        if k == 1:
            self.early_copy(j, last, 0).wait_recv()
        elif k > 1:
            self.early_copy(j, k - 2, 1).wait_recv()
        if k > 0:
            self.early_copy(j, k - 1, 1).start()

    def cross_copy(self, j, k, which):
        here = self.part(j, k, which, self.shared_start, self.shared)
        return pltpu.make_async_remote_copy(
            src_ref=here, dst_ref=here,
            send_sem=self.cross_send.at[j, 2 * k + which], recv_sem=self.cross_recv.at[j, 2 * k + which],
            device_id=self.across, device_id_type=MESH,
        )

    def keep_copy(self, j):
        rows = pl.ds(pl.multiple_of(self.own * self.rows, 16), self.rows)
        return pltpu.make_async_copy(self.weights[j], self.fulls[j].at[rows, :], self.local.at[j])

    def event(self, number):
        j, k = self.order[number]
        if k > 0:
            self.ring_copy(j, k - 1).wait_recv()
        if number == 0:
            for array in range(self.arrays):
                self.keep_copy(array).start()
        if k < self.pairs - 1:
            self.ring_copy(j, k).start()
        self.pair_copy(j, k).start()
        if k > 0:
            self.cross_copy(j, k, 0).start()
        if self.early:
            self.early_event(j, k)
        if number >= self.lag:
            self.share(number - self.lag)

    def share(self, number):
        j, k = self.order[number]
        self.pair_copy(j, k).wait_recv()
        self.cross_copy(j, k, 1).start()

    def finish(self):
        for number in range(max(len(self.order) - self.lag, 0), len(self.order)):
            self.share(number)
        crossed = [(j, k, which) for j, k in self.order for which in range(2) if k or which]
        for item in crossed:
            self.cross_copy(*item).wait_recv()
        for j, k in self.order:
            if k < self.pairs - 1:
                self.ring_copy(j, k).wait_send()
            self.pair_copy(j, k).wait_send()
        for item in crossed:
            self.cross_copy(*item).wait_send()
        for j in range(len(self.pieces)):
            if self.early:
                last = self.pairs - 1
                if last:
                    self.early_copy(j, last - 1, 1).wait_recv()
                else:
                    self.early_copy(j, last, 0).wait_recv()
                self.early_copy(j, last, 0).wait_send()
                for k in range(last):
                    for which in range(2):
                        self.early_copy(j, k, which).wait_send()
        for array in range(self.arrays):
            self.keep_copy(array).wait()


def gather_kernel(plan, *refs):
    arrays = plan.arrays
    weights, tokens = refs[:arrays], refs[arrays]
    fulls, far = refs[arrays + 1 : 2 * arrays + 1], refs[2 * arrays + 1]
    extra_send, extra_recv = refs[2 * arrays + 2 : 2 * arrays + 4]
    plan.bind(weights, fulls, refs[2 * arrays + 4 :])
    plan.greet(plan.beside)
    half = tokens.shape[2] // 2
    lanes = pl.ds(pl.multiple_of(plan.side * half, 128), half)

    def token_copy(src, number, device):
        return pltpu.make_async_remote_copy(
            src_ref=src.at[:, :, lanes], dst_ref=far.at[:, :, lanes],
            send_sem=extra_send.at[number], recv_sem=extra_recv.at[number],
            device_id=device, device_id_type=MESH,
        )

    first, second = token_copy(tokens, 0, plan.across), token_copy(far, 1, plan.beside)
    first.start()
    for number in range(len(plan.order)):
        plan.event(number)
        if number == min(5, len(plan.order) - 1):
            first.wait_recv()
            second.start()
    second.wait_recv()
    plan.finish()
    first.wait_send()
    second.wait_send()


def gather_weights(shards, tokens, shared, collective_id):
    rows = shards[0].shape[0]
    pairs = lax.axis_size("fsdp") // 2
    count = len(shards)
    plan = Gathering(rows, pairs, [shard.shape[1] for shard in shards], 2, shared)
    hbm = pl.BlockSpec(memory_space=pl.ANY)
    dma = pltpu.SemaphoreType.DMA
    return pl.pallas_call(
        functools.partial(gather_kernel, plan),
        out_shape=[
            jax.ShapeDtypeStruct((2 * pairs * rows, shard.shape[1]), shard.dtype) for shard in shards
        ]
        + [jax.ShapeDtypeStruct(tokens.shape, tokens.dtype)],
        in_specs=[hbm] * (count + 1),
        out_specs=[hbm] * (count + 1),
        scratch_shapes=[dma((2,)), dma((2,))] + plan.scratch(),
        compiler_params=pltpu.CompilerParams(collective_id=collective_id, has_side_effects=True),
    )(*shards, tokens)


def order_kernel(near_index, far_index, is_near, near, far, gain, x_out, normed_out, scale_out):
    step = pl.program_id(0)
    near_now = is_near[step] == 1
    x = jnp.where(near_now, near[...], far[...])
    x_out[...] = x
    value = x.astype(f32)
    mean = jnp.sum(value * value, axis=-1, keepdims=True) * (1.0 / value.shape[-1])
    scale = lax.rsqrt(mean + epsilon)
    normed_out[...] = (value * scale * gain[...]).astype(bf16)
    scale_out[...] = jnp.broadcast_to(scale, scale_out.shape)


def ordered(near, far, near_index, far_index, is_near, gain):
    micros, count, length, model = near.shape
    blocks = micros * count

    def block(spec_index):
        return pl.BlockSpec((None, None, length, model), spec_index)

    def rows(lanes):
        return pl.BlockSpec((length, lanes), lambda step, *_: (step, 0))

    return pl.pallas_call(
        order_kernel,
        grid_spec=pltpu.PrefetchScalarGridSpec(
            num_scalar_prefetch=3,
            grid=(blocks,),
            in_specs=[
                block(lambda step, near_at, far_at, flags: (step // count, near_at[step], 0, 0)),
                block(lambda step, near_at, far_at, flags: (step // count, far_at[step], 0, 0)),
                pl.BlockSpec((1, model), lambda *_: (0, 0)),
            ],
            out_specs=[rows(model), rows(model), rows(LANES)],
        ),
        out_shape=[
            jax.ShapeDtypeStruct((blocks * length, model), bf16),
            jax.ShapeDtypeStruct((blocks * length, model), bf16),
            jax.ShapeDtypeStruct((blocks * length, LANES), f32),
        ],
        compiler_params=pltpu.CompilerParams(vmem_limit_bytes=32 * 1024 * 1024),
    )(near_index, far_index, is_near, near, far, gain)


def gate_kernel(
    normed, out_grad, gate_weight, out_weight, y_own, carry, coupled, entering, gain,
    mixer_out, gate_out, grad_out, sums_out,
):
    gate_in = mm(normed[...], gate_weight[...])
    grads = mm(out_grad[...], out_weight[...])
    width = entering.shape[0]
    arrived = mm_three(split_two(coupled[:, width:]), split_two(entering[...]))
    mixer = y_own[...] + carry[...] * arrived
    gated = mixer * (gate_in * logistic(gate_in))
    mixer_out[...] = mixer
    gate_out[...] = gate_in
    grad_out[...] = grads
    square = jnp.sum(gated * gated, axis=-1, keepdims=True)
    product = jnp.sum(grads * gain[...] * gated, axis=-1, keepdims=True)
    lane = lax.broadcasted_iota(jnp.int32, sums_out.shape, 1)
    sums_out[...] = jnp.where(lane == 0, square, jnp.where(lane == 1, product, 0.0))


def gate_stage(normed, out_grad, gate_weight, out_weight, y_own, carry, coupled, entering, gain):
    rows, model = normed.shape
    inner = y_own.shape[1]
    twice = coupled.shape[1]
    micros, width, _ = entering.shape
    size = 2 * CHUNK
    per_micro = rows // micros // size

    def block(lanes):
        return pl.BlockSpec((size, lanes), lambda step: (step, 0))

    return pl.pallas_call(
        gate_kernel,
        grid=(rows // size,),
        in_specs=[
            block(model),
            block(model),
            pl.BlockSpec((model, inner), lambda step: (0, 0), pipeline_mode=pl.Buffered(1)),
            pl.BlockSpec((model, inner), lambda step: (0, 0), pipeline_mode=pl.Buffered(1)),
            block(inner),
            block(inner),
            block(twice),
            pl.BlockSpec((None, width, inner), lambda step: (step // per_micro, 0, 0)),
            pl.BlockSpec((1, inner), lambda step: (0, 0)),
        ],
        out_specs=[block(inner), block(inner), block(inner), block(LANES)],
        out_shape=[jax.ShapeDtypeStruct((rows, inner), f32)] * 3
        + [jax.ShapeDtypeStruct((rows, LANES), f32)],
        compiler_params=pltpu.CompilerParams(vmem_limit_bytes=60 * 1024 * 1024),
        cost_estimate=pl.CostEstimate(
            flops=4 * rows * model * inner, bytes_accessed=24 * rows * inner, transcendentals=0
        ),
    )(normed, out_grad, gate_weight, out_weight, y_own, carry, coupled, entering, gain)


def gate_back_kernel(
    inner_total, per_micro, mixer, gate_in, grads, carry, coupled, sums, gain,
    norm_out, gate_out, mixer_out, pull_out, gain_out,
):
    step = pl.program_id(0)
    width = pull_out.shape[0]
    inv_norm = lax.rsqrt(sums[:, 0:1] / inner_total + epsilon)
    inner_dot = sums[:, 1:2] * (inv_norm * inv_norm * inv_norm) / inner_total
    mixer_now, gate_now, grad_now = mixer[...], gate_in[...], grads[...]
    sig = logistic(gate_now)
    act = gate_now * sig
    gated = mixer_now * act
    norm_out[...] = (gated * inv_norm * gain[...]).astype(bf16)
    gated_grad = grad_now * gain[...] * inv_norm - gated * inner_dot
    gate_out[...] = (gated_grad * mixer_now * sig * (1.0 + gate_now * (1.0 - sig))).astype(bf16)
    mixer_grad = gated_grad * act
    mixer_out[...] = mixer_grad

    @pl.when(step == 0)
    def _():
        gain_out[...] = jnp.zeros_like(gain_out)

    gain_out[0:1, :] += jnp.sum(grad_now * gated * inv_norm, axis=0, keepdims=True)

    @pl.when(lax.rem(step, per_micro) == 0)
    def _():
        pull_out[...] = jnp.zeros_like(pull_out)

    turned = split_two(jnp.transpose(coupled[:, width:]))
    pull_out[...] += mm_three(turned, split_two(carry[...] * mixer_grad))


def gate_back_stage(mixer, gate_in, grads, carry, coupled, sums, gain, micros, inner_total):
    rows, inner = mixer.shape
    twice = coupled.shape[1]
    width = twice // 2
    per_micro = rows // micros // CHUNK

    def block(lanes):
        return pl.BlockSpec((CHUNK, lanes), lambda step: (step, 0))

    return pl.pallas_call(
        functools.partial(gate_back_kernel, inner_total, per_micro),
        grid=(rows // CHUNK,),
        in_specs=[
            block(inner),
            block(inner),
            block(inner),
            block(inner),
            block(twice),
            block(LANES),
            pl.BlockSpec((1, inner), lambda step: (0, 0)),
        ],
        out_specs=[
            block(inner),
            block(inner),
            block(inner),
            pl.BlockSpec((None, width, inner), lambda step: (step // per_micro, 0, 0)),
            pl.BlockSpec((8, inner), lambda step: (0, 0)),
        ],
        out_shape=[
            jax.ShapeDtypeStruct((rows, inner), bf16),
            jax.ShapeDtypeStruct((rows, inner), bf16),
            jax.ShapeDtypeStruct((rows, inner), f32),
            jax.ShapeDtypeStruct((micros, width, inner), f32),
            jax.ShapeDtypeStruct((8, inner), f32),
        ],
        compiler_params=pltpu.CompilerParams(vmem_limit_bytes=48 * 1024 * 1024),
        cost_estimate=pl.CostEstimate(
            flops=8 * rows * width * inner, bytes_accessed=24 * rows * inner, transcendentals=0
        ),
    )(mixer, gate_in, grads, carry, coupled, sums, gain)


def weave_kernel(first, second, out):
    out[:, 0, :] = first[...]
    out[:, 1, :] = second[...]


def woven(first, second, columns):
    rows = first.shape[0]
    size = 32
    block = pl.BlockSpec((size, columns), lambda step: (step, 0))
    return pl.pallas_call(
        weave_kernel,
        grid=(rows // size,),
        in_specs=[block, block],
        out_specs=pl.BlockSpec((size, 2, columns), lambda step: (step, 0, 0)),
        out_shape=jax.ShapeDtypeStruct((rows, 2, columns), first.dtype),
    )(first, second)


class Reduction:
    def __init__(self, rows, pairs, columns, lag):
        self.rows, self.pairs, self.columns, self.lag = rows, pairs, columns, lag
        self.shared = rows // 4
        self.moved = rows - self.shared
        self.counts = [count // LANES for count in columns]
        self.count = sum(self.counts)
        self.steps = self.count + 4 * lag

    def scratch(self):
        shared, moved, pairs, count = self.shared, self.moved, self.pairs, self.count
        cross, pair, ring = 2 * pairs * shared + 16, pairs * moved + 16, moved + 16
        i16, dma = jnp.int16, pltpu.SemaphoreType.DMA
        return [
            pltpu.VMEM((count, cross, LANES), i16),
            pltpu.VMEM((count, pair, LANES), i16),
            pltpu.VMEM((count, pairs - 1, ring, LANES), i16),
            pltpu.VMEM((count, ring, LANES), i16),
            pltpu.VMEM((2, cross, LANES), i16),
            pltpu.VMEM((2, pair, LANES), i16),
            pltpu.VMEM((2, pairs - 1, ring, LANES), i16),
            pltpu.VMEM((2, ring, LANES), i16),
            pltpu.VMEM((2, pairs, 2, shared, LANES), f32),
            pltpu.VMEM((2, pairs, moved, LANES), f32),
            pltpu.VMEM((2, pairs, moved, LANES), f32),
            pltpu.VMEM((2 * self.lag, moved, LANES), f32),
            pltpu.VMEM((2 * self.lag, moved, LANES), f32),
            pltpu.VMEM((2, self.rows, LANES), f32),
            dma((count,)),
            dma((count,)),
            dma((pairs - 1, count)),
            dma((count,)),
            dma((2,)),
            dma((2,)),
            dma((pairs - 1, 2)),
            dma((2,)),
            dma((3, 2)),
            dma((2,)),
        ]

    def bind(self, terms, outs, scratch):
        self.terms, self.outs = terms, outs
        (
            self.cross_in, self.pair_in, self.ring_in, self.last_in,
            self.cross_out, self.pair_out, self.ring_out, self.last_out,
            self.cross_term, self.pair_term, self.ring_term,
            self.kept, self.held, self.result,
            self.cross_recv, self.pair_recv, self.ring_recv, self.last_recv,
            self.cross_sent, self.pair_sent, self.ring_sent, self.last_sent,
            self.loaded, self.stored,
        ) = scratch
        self.own, self.place = lax.axis_index("fsdp"), lax.axis_index("context")
        self.side = lax.axis_index("tensor")
        self.pair, self.member = self.own // 2, lax.rem(self.own, 2)
        self.across = (self.own, 1 - self.place, self.side)
        self.partner = (2 * self.pair + 1 - self.member, self.place, self.side)
        self.inset = pl.multiple_of(self.place * (self.moved - self.shared), 16)
        self.start = pl.multiple_of(self.place * self.shared, 16)

    def peer(self, offset):
        there = lax.rem(self.pair + offset, self.pairs)
        return (2 * there + self.member, self.place, self.side)

    def greet(self):
        barrier = pltpu.get_barrier_semaphore()
        devices = [self.across, self.partner] + [self.peer(k) for k in range(1, self.pairs)]
        for device in devices:
            pl.semaphore_signal(barrier, inc=1, device_id=device, device_id_type=MESH)
        pl.semaphore_wait(barrier, len(devices))

    def cross_copy(self, chunk):
        slot = lax.rem(chunk, 2)
        return pltpu.make_async_remote_copy(
            src_ref=self.cross_out.at[slot], dst_ref=self.cross_in.at[chunk],
            send_sem=self.cross_sent.at[slot], recv_sem=self.cross_recv.at[chunk],
            device_id=self.across, device_id_type=MESH,
        )

    def pair_copy(self, chunk):
        slot = lax.rem(chunk, 2)
        return pltpu.make_async_remote_copy(
            src_ref=self.pair_out.at[slot], dst_ref=self.pair_in.at[chunk],
            send_sem=self.pair_sent.at[slot], recv_sem=self.pair_recv.at[chunk],
            device_id=self.partner, device_id_type=MESH,
        )

    def ring_copy(self, chunk, offset):
        slot = lax.rem(chunk, 2)
        return pltpu.make_async_remote_copy(
            src_ref=self.ring_out.at[slot, offset - 1], dst_ref=self.ring_in.at[chunk, offset - 1],
            send_sem=self.ring_sent.at[offset - 1, slot],
            recv_sem=self.ring_recv.at[offset - 1, chunk],
            device_id=self.peer(offset), device_id_type=MESH,
        )

    def last_copy(self, chunk):
        slot = lax.rem(chunk, 2)
        return pltpu.make_async_remote_copy(
            src_ref=self.last_out.at[slot], dst_ref=self.last_in.at[chunk],
            send_sem=self.last_sent.at[slot], recv_sem=self.last_recv.at[chunk],
            device_id=self.across, device_id_type=MESH,
        )

    def load_copy(self, stage, term, cols, slot):
        if stage == 0:
            rows = pl.ds(pl.multiple_of((1 - self.place) * self.moved, 16), self.shared)
            src, dst = term.at[:, :, rows, cols], self.cross_term.at[slot]
        elif stage == 1:
            src = term.at[:, 1 - self.member, pl.ds(self.start, self.moved), cols]
            dst = self.pair_term.at[slot]
        else:
            src = term.at[:, self.member, pl.ds(self.start, self.moved), cols]
            dst = self.ring_term.at[slot]
        return pltpu.make_async_copy(src, dst, self.loaded.at[stage, slot])

    def each_array(self, chunk, act):
        first = 0
        for number, count in enumerate(self.counts):
            inside = (chunk >= first) & (chunk < first + count)
            offset = first

            @pl.when(inside)
            def _(number=number, offset=offset):
                act(number, pl.ds(pl.multiple_of((chunk - offset) * LANES, LANES), LANES))

            first += count

    def load(self, stage, chunk):
        @pl.when((chunk >= 0) & (chunk < self.count))
        def _():
            self.each_array(
                chunk,
                lambda number, cols: self.load_copy(
                    stage, self.terms[number], cols, lax.rem(chunk, 2)
                ).start(),
            )

    def loaded_now(self, stage, chunk):
        self.load_copy(stage, self.terms[0], pl.ds(0, LANES), lax.rem(chunk, 2)).wait()

    @staticmethod
    def encode(value, out, place):
        count = value.shape[0]
        peak = jnp.maximum(jnp.max(jnp.abs(value), axis=0, keepdims=True), 1e-30)
        exponent = jnp.ceil(jnp.log(peak) * 1.4426950408889634)
        factor = jnp.exp(exponent * -0.6931471805599453) * 32000.0
        out[place + (pl.ds(0, count), slice(None))] = (
            (value * factor + 12582912.0 - 12582912.0).astype(jnp.int32).astype(jnp.int16)
        )
        out[place + (pl.ds(count, 16), slice(None))] = (
            jnp.broadcast_to(exponent, (16, LANES)).astype(jnp.int32).astype(jnp.int16)
        )

    @staticmethod
    def unit(ref, place, count):
        exponents = ref[place + (pl.ds(count, 16), slice(None))].astype(jnp.int32).astype(f32)
        return jnp.exp(exponents[:1] * 0.6931471805599453) * (1.0 / 32000.0)

    @staticmethod
    def decode(ref, place, first, count, unit):
        first = pl.multiple_of(first, 16) if not isinstance(first, int) else first
        return ref[place + (pl.ds(first, count), slice(None))].astype(jnp.int32).astype(f32) * unit

    def step(self, number):
        lag, pairs, shared, moved = self.lag, self.pairs, self.shared, self.moved

        @pl.when(number == 0)
        def _():
            self.load(0, number)

        self.load(0, number + 1)
        self.load(1, number + 1 - lag)
        self.load(2, number + 1 - 2 * lag)

        def stage(index, act):
            chunk = number - index * lag

            @pl.when((chunk >= 0) & (chunk < self.count))
            def _():
                act(chunk, lax.rem(chunk, 2))

        def cross(chunk, slot):
            self.loaded_now(0, chunk)

            @pl.when(chunk >= 2)
            def _():
                self.cross_copy(chunk - 2).wait_send()

            value = self.cross_term[slot].reshape(2 * pairs * shared, LANES)
            self.encode(value, self.cross_out, (slot,))
            self.cross_copy(chunk).start()

        def pair(chunk, slot):
            self.loaded_now(1, chunk)
            self.cross_copy(chunk).wait_recv()

            @pl.when(chunk >= 2)
            def _():
                self.pair_copy(chunk - 2).wait_send()

            unit = self.unit(self.cross_in, (chunk,), 2 * pairs * shared)
            for there in range(pairs):
                first = (2 * there + 1 - self.member) * shared
                self.pair_term[slot, there, pl.ds(self.inset, shared), :] += self.decode(
                    self.cross_in, (chunk,), first, shared, unit
                )
            value = self.pair_term[slot].reshape(pairs * moved, LANES)
            self.encode(value, self.pair_out, (slot,))
            self.pair_copy(chunk).start()

        def ring(chunk, slot):
            self.loaded_now(2, chunk)
            self.pair_copy(chunk).wait_recv()

            @pl.when(chunk >= 2)
            def _():
                for offset in range(1, pairs):
                    self.ring_copy(chunk - 2, offset).wait_send()

            cross_unit = self.unit(self.cross_in, (chunk,), 2 * pairs * shared)
            pair_unit = self.unit(self.pair_in, (chunk,), pairs * moved)
            for offset in list(range(1, pairs)) + [0]:
                there = lax.rem(self.pair + offset, pairs)
                first = (2 * there + self.member) * shared
                self.ring_term[slot, there, pl.ds(self.inset, shared), :] += self.decode(
                    self.cross_in, (chunk,), first, shared, cross_unit
                )
                value = self.ring_term[slot, there] + self.decode(
                    self.pair_in, (chunk,), there * moved, moved, pair_unit
                )
                if offset:
                    self.encode(value, self.ring_out, (slot, offset - 1))
                    self.ring_copy(chunk, offset).start()
                else:
                    self.kept[lax.rem(chunk, 2 * lag)] = value

        def last(chunk, slot):
            for offset in range(1, pairs):
                self.ring_copy(chunk, offset).wait_recv()

            @pl.when(chunk >= 2)
            def _():
                self.last_copy(chunk - 2).wait_send()

            total = self.kept[lax.rem(chunk, 2 * lag)]
            for offset in range(1, pairs):
                place = (chunk, offset - 1)
                total = total + self.decode(
                    self.ring_in, place, 0, moved, self.unit(self.ring_in, place, moved)
                )
            self.encode(total, self.last_out, (slot,))
            self.held[lax.rem(chunk, 2 * lag)] = self.decode(
                self.last_out, (slot,), 0, moved, self.unit(self.last_out, (slot,), moved)
            )
            self.last_copy(chunk).start()

        def write_copy(number, cols, slot):
            return pltpu.make_async_copy(
                self.result.at[slot], self.outs[number].at[:, cols], self.stored.at[slot]
            )

        def write(chunk, slot):
            self.last_copy(chunk).wait_recv()

            @pl.when(chunk >= 2)
            def _():
                write_copy(0, pl.ds(0, LANES), slot).wait()

            mine = self.held[lax.rem(chunk, 2 * lag)]
            other = self.decode(
                self.last_in, (chunk,), 0, moved, self.unit(self.last_in, (chunk,), moved)
            )
            low = jnp.where(self.place == 0, mine, other)
            high = jnp.where(self.place == 0, other, mine)
            self.result[slot, pl.ds(0, shared), :] = low[:shared]
            self.result[slot, pl.ds(shared, moved - shared), :] = (
                low[shared:] + high[: moved - shared]
            )
            self.result[slot, pl.ds(moved, shared), :] = high[moved - shared :]
            self.each_array(chunk, lambda which, cols: write_copy(which, cols, slot).start())

        stage(4, write)
        stage(3, last)
        stage(2, ring)
        stage(1, pair)
        stage(0, cross)

        @pl.when(number == self.steps - 1)
        def _():
            for slot in range(2):
                write_copy(0, pl.ds(0, LANES), slot).wait()
                self.cross_copy(jnp.int32(self.count - 2 + slot)).wait_send()
                self.pair_copy(jnp.int32(self.count - 2 + slot)).wait_send()
                self.last_copy(jnp.int32(self.count - 2 + slot)).wait_send()
                for offset in range(1, pairs):
                    self.ring_copy(jnp.int32(self.count - 2 + slot), offset).wait_send()


def reduce_kernel(plan, arrays, *refs):
    plan.bind(refs[:arrays], refs[arrays : 2 * arrays], refs[2 * arrays :])
    plan.greet()

    def body(number, carried):
        plan.step(number)
        return carried

    lax.fori_loop(0, plan.steps, body, 0)


def reduce_terms(terms, lag, collective_id):
    pairs = lax.axis_size("fsdp") // 2
    rows = terms[0].shape[0] // (2 * pairs)
    columns = [term.shape[1] for term in terms]
    plan = Reduction(rows, pairs, columns, lag)
    hbm = pl.BlockSpec(memory_space=pl.ANY)
    arrays = len(terms)
    return pl.pallas_call(
        functools.partial(reduce_kernel, plan, arrays),
        out_shape=[jax.ShapeDtypeStruct((rows, count), f32) for count in columns],
        in_specs=[hbm] * arrays,
        out_specs=[hbm] * arrays,
        scratch_shapes=plan.scratch(),
        compiler_params=pltpu.CompilerParams(
            collective_id=collective_id, has_side_effects=True, vmem_limit_bytes=58 * 1024 * 1024
        ),
    )(*[term.reshape(pairs, 2, rows, -1) for term in terms])


def passed_along(value, axis, steps):
    count = lax.axis_size(axis)
    initial, last = (max(0, -steps), min(count, count - steps))
    return lax.ppermute(value, axis, [(source, source + steps) for source in range(initial, last)])


def paired(value, axis):
    count = lax.axis_size(axis)
    return lax.ppermute(value, axis, [(source, source ^ 1) for source in range(count)])


def ring_shift(value, axis, steps):
    count = lax.axis_size(axis)
    return lax.ppermute(
        value, axis, [(source, (source + 2 * steps) % count) for source in range(count)]
    )


def summed_everywhere(values):
    sizes = [value.size for value in values]
    shapes = [value.shape for value in values]
    flat = jnp.concatenate([value.reshape(-1) for value in values])
    count = flat.shape[0]
    flat = jnp.pad(flat, (0, -count % 1024)).reshape(-1, 128)
    for axis in ("context", "fsdp"):
        members = lax.axis_size(axis)
        reach = 1
        while reach < members:
            flat = flat + lax.ppermute(
                flat, axis, [(source, source ^ reach) for source in range(members)]
            )
            reach *= 2
    flat = flat.reshape(-1)
    results, start = [], 0
    for size, shape in zip(sizes, shapes):
        results.append(flat[start : start + size].reshape(shape))
        start += size
    return results


def shards(
    tokens,
    lengths,
    block_order,
    cotangent,
    norm_gain,
    in_weight,
    coupling_weight,
    step_weight,
    out_weight,
    conv_weight,
    conv_bias,
    coupling_conv,
    coupling_bias,
    step_bias,
    decay_rate,
    skip_gain,
    inner_gain,
):
    micros = tokens.shape[0]
    count = tokens.shape[2]
    model = tokens.shape[3]
    inner = inner_gain.shape[0]
    heads = step_bias.shape[0]
    head_size = inner // heads
    twice = coupling_weight.shape[1]
    width = twice // 2
    blocks_row = block_order.shape[2]
    block_len = count * lax.axis_size("context") // blocks_row
    own_blocks = count // block_len
    inner_total = inner * lax.axis_size("tensor")
    side = lax.axis_index("tensor")
    place = lax.axis_index("context")
    base = place * count
    shard_rows = in_weight.shape[0]

    narrow, wide_columns = selectors(heads, head_size)
    sel = jnp.asarray(narrow, bf16)
    selcol = jnp.asarray(wide_columns, bf16)
    selt = jnp.asarray(narrow[:heads].T, bf16)
    selt = jnp.pad(selt, ((0, 0), (0, LANES - heads)))

    lead = jnp.concatenate(
        [
            in_weight[:, 1, :],
            coupling_weight,
            jnp.pad(step_weight, ((0, 0), (0, LANES - heads))),
        ],
        axis=1,
    )
    def sharing(parts):
        return max(shard_rows * parts // 16 // 16 * 16, 16)

    lead_full, far = gather_weights([lead], tokens[:, 0], sharing(3), 1)

    near = tokens[:, 0].reshape(micros, own_blocks, block_len, model)
    far = far.reshape(micros, own_blocks, block_len, model)
    slots = jnp.arange(blocks_row, dtype=jnp.int32)
    wanted = place * own_blocks + jnp.arange(own_blocks, dtype=jnp.int32)
    found = block_order[:, 0, None, :] == wanted[None, :, None]
    slot = jnp.sum(jnp.where(found, slots, 0), axis=2).reshape(-1)
    is_near = (slot // own_blocks == place).astype(jnp.int32)
    inside = slot % own_blocks
    x_input, normed, scales = ordered(
        near, far, inside * is_near, inside * (1 - is_near), is_near, norm_gain.reshape(1, model)
    )
    x_float = x_input.astype(f32)
    inv_rms = scales[:, :1]

    first_end = lengths[:, 0, 0]
    second_end = first_end + lengths[:, 0, 1]
    marks = [
        jnp.stack([first_end[micro], second_end[micro], base]).astype(jnp.int32)
        for micro in range(micros)
    ]
    positions = base + jnp.arange(count, dtype=jnp.int32)
    keep = jnp.concatenate([(positions < second_end[micro]) for micro in range(micros)])
    keep = keep.astype(f32)[:, None]

    cw, cb = conv_weight, conv_bias.reshape(1, inner)
    ccw, ccb = coupling_conv, coupling_bias.reshape(1, twice)
    sbias = jnp.pad(step_bias, (0, LANES - heads)).reshape(1, LANES)
    rate = jnp.pad(decay_rate, (0, LANES - heads)).reshape(1, LANES)
    skip = jnp.dot(
        skip_gain.reshape(1, heads), jnp.asarray(narrow[:heads], f32), precision=lax.Precision.HIGHEST
    )

    raw = jnp.dot(normed, lead_full, preferred_element_type=f32)
    rims = passed_along(
        jnp.stack([raw[(micro + 1) * count - 8 : (micro + 1) * count] for micro in range(micros)]),
        "context",
        1,
    )
    (y_own, states, finals, coupled, carry, reach, entering, gate_full, out_full) = forward_ssd(
        jnp.stack(marks), micros, raw, rims, inner, twice, count,
        cw, cb, ccw, ccb, sbias, rate, skip, sel, selcol,
        [in_weight[:, 0, :], jnp.transpose(out_weight)], sharing(4), 3,
    )
    entering = jnp.where(place == 0, 0.0, entering)
    cot = cotangent[:, 0].reshape(micros * count, model)
    out_grad = cot * keep.astype(bf16)
    gain_row = inner_gain.reshape(1, inner)
    mixer, gate_in, norm_grad, row_sums = gate_stage(
        normed, out_grad, gate_full, out_full, y_own, carry, coupled, entering, gain_row
    )
    row_sums = row_sums + paired(row_sums, "tensor")
    gated_norm, gate_grad, mixer_grad, own_pulls, inner_gain_rows = gate_back_stage(
        mixer, gate_in, norm_grad, carry, coupled, row_sums, gain_row, micros, inner_total
    )
    pulled = passed_along(own_pulls, "context", -1)
    out_term = contract_rows(out_grad, gated_norm)
    gate_term = contract_rows(normed, gate_grad)
    branch = contract_cols(gated_norm, out_full)
    gate_part = contract_cols(gate_grad, gate_full)
    branch_other = paired(branch, "tensor")

    (
        lead_grad, tails, rims_grad, coupling_raw_grad, coupling_rims_grad,
        value_sums, coupling_sums, small_sums, skip_sums, out_shard, gate_shard,
    ) = backward_ssd(
        jnp.stack(marks), micros, raw, rims, inner, twice, count, mixer_grad, mixer, states,
        finals, entering, reach, pulled,
        cw, cb, ccw, ccb, sbias, rate, skip, sel, selcol, selt, [out_term, gate_term], [branch, gate_part], 2,
    )
    edges = passed_along(jnp.concatenate([rims_grad, coupling_rims_grad], axis=2), "context", -1)
    coupling_raw_grad = coupling_raw_grad.reshape(micros, count, twice) + jnp.pad(
        edges[:, :, inner:], ((0, 0), (count - 8, 0), (0, 0))
    )
    coupling_raw_grad = coupling_raw_grad + paired(coupling_raw_grad, "tensor")
    lane_ids = jnp.arange(twice, dtype=jnp.int32)
    own_lanes = ((lane_ids // width) == side).astype(bf16)
    coupling_low = (coupling_raw_grad.astype(bf16) * own_lanes).reshape(micros * count, twice)
    lead_grad = lax.dynamic_update_slice(lead_grad, coupling_low, (0, inner))
    tails = (tails + edges[:, :, :inner]).astype(bf16)
    for micro in range(micros):
        lead_grad = lax.dynamic_update_slice(
            lead_grad, tails[micro], ((micro + 1) * count - 8, 0)
        )
    (lead_shard,) = reduce_terms([contract_rows(normed, lead_grad)], 2, 4)
    normed_part = gate_part + contract_cols(lead_grad, lead_full)
    block_out = (x_float + keep * (branch + branch_other)).astype(bf16)
    normed_grad = normed_part + paired(normed_part, "tensor")
    x_hat = x_float * inv_rms
    hat_grad = normed_grad * norm_gain
    input_grad = (
        cot.astype(f32)
        + inv_rms * (hat_grad - x_hat * jnp.mean(hat_grad * x_hat, axis=-1, keepdims=True))
    ).astype(bf16)
    norm_gain_grad = jnp.sum(normed_grad * x_hat, axis=0)

    skip_sums = skip_sums[0].reshape(heads, head_size).sum(axis=1)
    coupling_sums = coupling_sums + paired(coupling_sums, "tensor")
    (value_all, coupling_all, small_all, skip_all, inner_all, norm_all) = summed_everywhere(
        [value_sums[:5], coupling_sums[:5], small_sums[:2], skip_sums, inner_gain_rows[0], norm_gain_grad]
    )
    coupling_shard = lead_shard[:, inner : inner + twice]
    coupling_shard = coupling_shard + paired(coupling_shard, "tensor")
    return (
        block_out.reshape(micros, 1, count, model),
        input_grad.reshape(micros, 1, count, model),
        norm_all,
        woven(gate_shard, lead_shard, inner),
        coupling_shard,
        lead_shard[:, inner + twice : inner + twice + heads],
        jnp.transpose(out_shard),
        value_all[:4],
        value_all[4],
        coupling_all[:4],
        coupling_all[4],
        small_all[0, :heads],
        small_all[1, :heads],
        skip_all,
        inner_all,
    )


def contract_rows(left, right):
    return lax.dot_general(
        left, right, (((0,), (0,)), ((), ())), preferred_element_type=jnp.float32
    )


def contract_cols(left, right):
    return lax.dot_general(
        left, right, (((1,), (1,)), ((), ())), preferred_element_type=jnp.float32
    )


def solution(mesh):
    return jax.shard_map(
        shards,
        mesh=mesh,
        in_specs=(
            P(None, "fsdp", "context", None),
            P(None, "fsdp", None),
            P(None, "fsdp", None),
            P(None, "fsdp", "context", None),
            P(),
            P("fsdp", None, "tensor"),
            P("fsdp", None),
            P("fsdp", "tensor"),
            P("tensor", "fsdp"),
            P(None, "tensor"),
            P("tensor"),
            P(),
            P(),
            P("tensor"),
            P("tensor"),
            P("tensor"),
            P("tensor"),
        ),
        out_specs=(
            P(None, "fsdp", "context", None),
            P(None, "fsdp", "context", None),
            P(),
            P("fsdp", None, "tensor"),
            P("fsdp", None),
            P("fsdp", "tensor"),
            P("tensor", "fsdp"),
            P(None, "tensor"),
            P("tensor"),
            P(),
            P(),
            P("tensor"),
            P("tensor"),
            P("tensor"),
            P("tensor"),
        ),
        check_vma=False,
    )
```

```python
import functools

import jax
import jax.numpy as jnp
import numpy as np
from jax import lax
from jax.experimental import pallas as pl
from jax.experimental.pallas import tpu as pltpu
from jax.sharding import PartitionSpec as P

CHUNK = 128
LANES = 128
MESH = pl.DeviceIdType.MESH
f32 = jnp.float32
bf16 = jnp.bfloat16
epsilon = 1e-05


def split_two(value):
    high = value.astype(bf16)
    return high, (value - high.astype(f32)).astype(bf16)


def split_three(value):
    high = value.astype(bf16)
    rest = value - high.astype(f32)
    middle = rest.astype(bf16)
    return high, middle, (rest - middle.astype(f32)).astype(bf16)


def mm(left, right):
    return jnp.dot(left, right, preferred_element_type=f32)


def mm_nt(left, right):
    return lax.dot_general(left, right, (((1,), (1,)), ((), ())), preferred_element_type=f32)


def mm_three(left, right):
    wide = mm(left[0], jnp.concatenate([right[0], right[1]], axis=1))
    count = right[0].shape[1]
    return wide[:, :count] + wide[:, count:] + mm(left[1], right[0])


def mm_three_nt(left, right):
    return mm_nt(left[0], right[0]) + mm_nt(left[0], right[1]) + mm_nt(left[1], right[0])


def packed_parts(value, heads):
    high, middle, lowest = split_three(value)
    joined = (
        high.astype(f32)
        + pltpu.roll(middle.astype(f32), heads, 1)
        + pltpu.roll(lowest.astype(f32), 2 * heads, 1)
    )
    return joined.astype(bf16)


def segment_at(position, first_end, second_end):
    first_part = (position >= first_end).astype(jnp.int32)
    second_part = (position >= second_end).astype(jnp.int32)
    return jnp.where(position < 0, -1, first_part + second_part)


def chunk_frame(marks, chunk, step_raw, step_bias, rate, heads):
    first_end, second_end, base = marks[0], marks[1], marks[2]
    start = base + chunk * CHUNK
    rows = start + lax.broadcasted_iota(jnp.int32, (CHUNK, LANES), 0)
    columns = start + lax.broadcasted_iota(jnp.int32, (CHUNK, CHUNK), 1)
    seg_rows = segment_at(rows, first_end, second_end)
    seg_columns = segment_at(columns, first_end, second_end)
    seg_prior = segment_at(start - 1, first_end, second_end)
    seg_last = segment_at(start + CHUNK - 1, first_end, second_end)
    same = [
        (segment_at(rows - lag, first_end, second_end) == seg_rows).astype(f32) for lag in range(4)
    ]
    shifted = step_raw + step_bias
    step = jnp.maximum(shifted, 0.0) + jnp.log1p(jnp.exp(-jnp.abs(shifted)))
    lanes = lax.broadcasted_iota(jnp.int32, (CHUNK, LANES), 1)
    step = jnp.where(lanes < heads, step, 0.0)
    log_decay = -step * rate
    row_ids = lax.broadcasted_iota(jnp.int32, (CHUNK, CHUNK), 0)
    column_ids = lax.broadcasted_iota(jnp.int32, (CHUNK, CHUNK), 1)
    lower = (row_ids >= column_ids).astype(bf16)
    parts = split_three(log_decay)
    cumulative = mm(lower, parts[0]) + mm(lower, parts[1]) + mm(lower, parts[2])
    last = cumulative[CHUNK - 1 :, :]
    carry = jnp.exp(cumulative) * (seg_rows == seg_prior).astype(f32)
    tail = jnp.exp(last - cumulative) * (seg_rows == seg_last).astype(f32)
    live = lanes < heads
    carry = jnp.where(live, carry, 0.0)
    tail = jnp.where(live, tail, 0.0)
    return dict(
        seg_rows=seg_rows,
        seg_columns=seg_columns,
        row_ids=row_ids,
        column_ids=column_ids,
        same=same,
        step=step,
        shifted=shifted,
        cumulative=cumulative,
        carry=carry,
        tail=tail,
    )


def conv_sum(current, halo, weights, biases, same):
    full = jnp.concatenate([halo, current], axis=0)
    total = biases + weights(0) * current
    for lag in range(1, 4):
        total = total + weights(lag) * (pltpu.roll(full, lag, 0)[8:] * same[lag])
    return total


def logistic(value):
    return 1.0 / (1.0 + jnp.exp(-value))


def forward_kernel(heads, chunks, plan, *refs):
    (
        marks, vraw, vprev, vrim, craw, cprev, crim, sraw, cw, cb, ccw, ccb, sbias, rate, skip,
        sel, selcol,
    ) = refs[:17]
    arrays = plan.arrays
    weights, refs = refs[17 : 17 + arrays], refs[17 + arrays :]
    y_out, st_out, fin_out, bc_out, carry_out, cd_out, entering = refs[:7]
    fulls, refs = refs[7 : 7 + arrays], refs[7 + arrays :]
    (
        state, cumt, stack, cumpack, halo, same_s, bias_s, gram_s, cd_s, cparts, btparts,
        leaving, leave_send, leave_recv,
    ) = refs[:14]
    plan.bind(weights, fulls, refs[14:])
    grid_step = pl.program_id(0)
    steps = pl.num_programs(0)
    chunk = lax.rem(grid_step, chunks)
    micro = grid_step // chunks
    width = state.shape[0]
    early = {0: range(2)}
    for when in range(1, min(2 * chunks - 1, len(plan.order) - 1)):
        early[when] = [when + 1]
    placed = len(early)

    def leave_copy(which):
        return pltpu.make_async_remote_copy(
            src_ref=leaving.at[which], dst_ref=entering.at[which],
            send_sem=leave_send.at[which], recv_sem=leave_recv.at[which],
            device_id=plan.across, device_id_type=MESH,
        )

    for when, numbers in early.items():

        @pl.when(grid_step == when)
        def _(when=when, numbers=numbers):
            if when == 0:
                plan.greet()
            for number in numbers:
                plan.event(number)

    @pl.when(chunk == 0)
    def _():
        state[...] = jnp.zeros_like(state)
        cd_s[...] = jnp.ones_like(cd_s)
        cd_out[...] = jnp.zeros_like(cd_out)
        halo[...] = vrim[...]

    @pl.when(chunk > 0)
    def _():
        halo[...] = vprev[...]

    frame = chunk_frame([marks[micro, place] for place in range(3)], chunk, sraw[...], sbias[...], rate[...], heads)
    same = frame["same"]
    for lag in range(1, 4):
        same_s[lag - 1] = same[lag]
    joined = (frame["seg_rows"] == frame["seg_columns"]) & (frame["row_ids"] >= frame["column_ids"])
    bias_s[...] = jnp.where(joined, 0.0, -1e30)
    stack[0:CHUNK, :] = packed_parts(frame["step"], heads)
    stack[CHUNK : 2 * CHUNK, :] = packed_parts(frame["carry"], heads)
    stack[2 * CHUNK : 3 * CHUNK, :] = packed_parts(frame["tail"], heads)
    cumpack[...] = packed_parts(frame["cumulative"], heads)
    cumt[...] = jnp.transpose(frame["cumulative"])
    coupling_halo = jnp.where(chunk == 0, crim[...], cprev[...])
    wide_same = [None] + [jnp.concatenate([same[lag], same[lag]], axis=1) for lag in range(1, 4)]
    pre = conv_sum(
        craw[...], coupling_halo, lambda lag: ccw[lag : lag + 1, :], ccb[...], wide_same
    )
    coupled = pre * logistic(pre)
    bc_out[...] = coupled
    b_part = split_two(coupled[:, :width])
    c_part = split_two(coupled[:, width:])
    gram_s[...] = mm_three_nt(c_part, b_part)
    cparts[0] = c_part[0]
    cparts[1] = c_part[1]
    turned = jnp.transpose(coupled[:, :width])
    bt_part = split_two(turned)
    btparts[0] = bt_part[0]
    btparts[1] = bt_part[1]
    lane = lax.broadcasted_iota(jnp.int32, (CHUNK, LANES), 1)
    low_half = (lane < LANES // 2).astype(f32)
    high_half = 1.0 - low_half

    def pair(index, carried):
        cols = pl.ds(pl.multiple_of(index * LANES, LANES), LANES)
        wide = pl.ds(pl.multiple_of(index * 2 * LANES, 2 * LANES), 2 * LANES)
        pre_value = conv_sum(
            vraw[:, cols],
            halo[:, cols],
            lambda lag: cw[lag : lag + 1, cols],
            cb[:, cols],
            [None] + [same_s[lag - 1] for lag in range(1, 4)],
        )
        value = pre_value * logistic(pre_value)
        spread = mm(stack[...], sel[:, cols])
        step_e = spread[:CHUNK]
        carry_e = spread[CHUNK : 2 * CHUNK]
        tail_e = spread[2 * CHUNK :]
        inputs = step_e * value
        column = mm(cumpack[...], selcol[:, wide])
        row_pair = jnp.concatenate(
            [cumt[pl.ds(2 * index, 1), :], cumt[pl.ds(2 * index + 1, 1), :]], axis=1
        )
        bias = bias_s[...]
        gram = gram_s[...]
        mixing = jnp.concatenate([gram, gram], axis=1) * jnp.exp(
            column - row_pair + jnp.concatenate([bias, bias], axis=1)
        )
        mix_high, mix_low = split_two(mixing)
        in_low = split_two(inputs * low_half)
        in_high = split_two(inputs * high_half)
        diag_high = jnp.concatenate([in_low[0], in_high[0]], axis=0)
        diag_low = jnp.concatenate([in_low[1], in_high[1]], axis=0)
        both = mm(mix_high, jnp.concatenate([diag_high, diag_low], axis=1))
        inside = both[:, :LANES] + both[:, LANES:] + mm(mix_low, diag_high)
        held = state[:, cols]
        from_state = mm_three((cparts[0], cparts[1]), split_two(held))
        y_out[:, cols] = inside + carry_e * from_state + skip[:, cols] * value
        fresh = mm_three((btparts[0], btparts[1]), split_two(tail_e * inputs))
        through = carry_e[CHUNK - 1 :, :]
        st_out[0, :, cols] = held
        renewed = through * held + fresh
        state[:, cols] = renewed
        fin_out[:, cols] = renewed
        reach = cd_s[0:1, cols]
        carry_out[:, cols] = carry_e * reach
        cd_s[0:1, cols] = reach * through
        return carried

    eight_rows = lax.broadcasted_iota(jnp.int32, cd_out.shape, 0)
    cd_out[...] = jnp.where(eight_rows == chunk, cd_s[0:1, :], cd_out[...])
    lax.fori_loop(0, heads // 2, pair, 0, unroll=4)
    cd_out[...] = jnp.where(eight_rows == chunk + 1, cd_s[0:1, :], cd_out[...])

    @pl.when(chunk == chunks - 1)
    def _():
        leaving[micro] = state[...]
        leave_copy(micro).start()

    @pl.when(grid_step == steps - 1)
    def _():
        for number in range(placed + 1, len(plan.order)):
            plan.event(number)
        plan.finish()
        for which in range(leaving.shape[0]):
            leave_copy(which).wait()


def selectors(heads, head_size):
    inner = heads * head_size
    head_of_lane = np.arange(inner) // head_size
    narrow = np.zeros((LANES, inner), np.float32)
    wide = np.zeros((LANES, heads * LANES), np.float32)
    head_of_wide = np.arange(heads * LANES) // LANES
    for part in range(3):
        narrow[part * heads + head_of_lane, np.arange(inner)] = 1.0
        wide[part * heads + head_of_wide, np.arange(heads * LANES)] = 1.0
    return narrow, wide


def whole(shape):
    return pl.BlockSpec(shape, lambda index, *_: (0,) * len(shape))


def forward_ssd(
    marks, micros, raw, rims, inner, twice, tokens,
    cw, cb, ccw, ccb, sbias, rate, skip, sel, selcol, shards, shared, collective_id,
):
    width = twice // 2
    chunks = tokens // CHUNK
    heads = inner // (LANES // 2)
    eighth = CHUNK // 8
    pairs = lax.axis_size("fsdp") // 2
    shard_rows = shards[0].shape[0]
    plan = Gathering(shard_rows, pairs, [shard.shape[1] for shard in shards], 2, shared)

    def part(count, start):
        return pl.BlockSpec((CHUNK, count), lambda step: (step, start // count))

    def before(count, start):
        return pl.BlockSpec(
            (8, count), lambda step: (jnp.maximum(step * eighth - 1, 0), start // count)
        )

    def edge(count, start):
        return pl.BlockSpec((None, 8, count), lambda step: (step // chunks, 0, start // count))

    def each(*shape):
        return pl.BlockSpec((None, *shape), lambda step: (step // chunks, 0, 0))

    hbm = pl.BlockSpec(memory_space=pl.ANY)
    dma = pltpu.SemaphoreType.DMA
    return pl.pallas_call(
        functools.partial(forward_kernel, heads, chunks, plan),
        grid=(micros * chunks,),
        in_specs=[
            pl.BlockSpec(memory_space=pltpu.SMEM),
            part(inner, 0),
            before(inner, 0),
            edge(inner, 0),
            part(twice, inner),
            before(twice, inner),
            edge(twice, inner),
            part(LANES, inner + twice),
            whole(cw.shape),
            whole(cb.shape),
            whole(ccw.shape),
            whole(ccb.shape),
            whole(sbias.shape),
            whole(rate.shape),
            whole(skip.shape),
            whole(sel.shape),
            whole(selcol.shape),
        ]
        + [hbm] * len(shards),
        out_specs=[
            part(inner, 0),
            pl.BlockSpec((1, width, inner), lambda step: (step, 0, 0)),
            each(width, inner),
            part(twice, 0),
            part(inner, 0),
            each(8, inner),
            hbm,
        ]
        + [hbm] * len(shards),
        scratch_shapes=[
            pltpu.VMEM((width, inner), f32),
            pltpu.VMEM((LANES, CHUNK), f32),
            pltpu.VMEM((3 * CHUNK, LANES), bf16),
            pltpu.VMEM((CHUNK, LANES), bf16),
            pltpu.VMEM((8, inner), f32),
            pltpu.VMEM((3, CHUNK, LANES), f32),
            pltpu.VMEM((CHUNK, CHUNK), f32),
            pltpu.VMEM((CHUNK, CHUNK), f32),
            pltpu.VMEM((8, inner), f32),
            pltpu.VMEM((2, CHUNK, width), bf16),
            pltpu.VMEM((2, width, CHUNK), bf16),
            pltpu.VMEM((micros, width, inner), f32),
            dma((micros,)),
            dma((micros,)),
        ]
        + plan.scratch(),
        out_shape=[
            jax.ShapeDtypeStruct((micros * tokens, inner), f32),
            jax.ShapeDtypeStruct((micros * chunks, width, inner), f32),
            jax.ShapeDtypeStruct((micros, width, inner), f32),
            jax.ShapeDtypeStruct((micros * tokens, twice), f32),
            jax.ShapeDtypeStruct((micros * tokens, inner), f32),
            jax.ShapeDtypeStruct((micros, 8, inner), f32),
            jax.ShapeDtypeStruct((micros, width, inner), f32),
        ]
        + [
            jax.ShapeDtypeStruct((2 * pairs * shard_rows, shard.shape[1]), shard.dtype)
            for shard in shards
        ],
        compiler_params=pltpu.CompilerParams(
            collective_id=collective_id, has_side_effects=True, vmem_limit_bytes=48 * 1024 * 1024
        ),
    )(
        marks, raw, raw, rims, raw, raw, rims, raw, cw, cb, ccw, ccb, sbias, rate, skip, sel, selcol,
        *shards,
    )


def backward_kernel(heads, chunks, plan, waited, *refs):
    (
        marks, vraw, vprev, vrim, craw, cprev, crim, sraw, grad, mixer, st_now, st_next, fin,
        entering, cd, pulled, cw, cb, ccw, ccb, sbias, rate, skip, sel, selcol, selt,
    ) = refs[:26]
    arrays = len(plan.counts)
    refs = refs[26:]
    terms, refs = refs[:arrays], refs[arrays + waited :]
    (
        lead_g, vtail_g, vrim_g, craw_g, crim_g, cw_g, ccw_g, small_g, skip_g,
    ) = refs[:9]
    outs, refs = refs[9 : 9 + arrays], refs[9 + arrays :]
    (
        state, cumt, stack, cumpack, halo, same_s, bias_s, gram_s, cparts, bparts, ctparts,
        rim_s, crim_s, dgram, dcoup, dhead, cd_s,
    ) = refs[:17]
    plan.bind(terms, outs, refs[17:])
    grid_step = pl.program_id(0)
    step_id = lax.rem(grid_step, chunks)
    micro = grid_step // chunks
    chunk = chunks - 1 - step_id
    width = state.shape[0]
    inner = state.shape[1]
    per_step = -(-plan.steps // pl.num_programs(0))

    @pl.when(grid_step == 0)
    def _():
        plan.greet()
        cw_g[...] = jnp.zeros_like(cw_g)
        ccw_g[...] = jnp.zeros_like(ccw_g)
        small_g[...] = jnp.zeros_like(small_g)
        skip_g[...] = jnp.zeros_like(skip_g)

    def reduce_steps(first, count):
        def one(number, carried):
            plan.step(number)
            return carried

        start = grid_step * per_step + first
        lax.fori_loop(start, jnp.minimum(start + count, plan.steps), one, 0)

    @pl.when(step_id == 0)
    def _():
        state[...] = pulled[...]
        rim_s[...] = jnp.zeros_like(rim_s)
        crim_s[...] = jnp.zeros_like(crim_s)

    @pl.when(chunk == 0)
    def _():
        halo[...] = vrim[...]

    @pl.when(chunk > 0)
    def _():
        halo[...] = vprev[...]

    frame = chunk_frame([marks[micro, place] for place in range(3)], chunk, sraw[...], sbias[...], rate[...], heads)
    same = frame["same"]
    for lag in range(1, 4):
        same_s[lag - 1] = same[lag]
    joined = (frame["seg_rows"] == frame["seg_columns"]) & (frame["row_ids"] <= frame["column_ids"])
    bias_s[...] = jnp.where(joined, 0.0, -1e30)
    stack[0:CHUNK, :] = packed_parts(frame["step"], heads)
    stack[CHUNK : 2 * CHUNK, :] = packed_parts(frame["carry"], heads)
    stack[2 * CHUNK : 3 * CHUNK, :] = packed_parts(frame["tail"], heads)
    cumpack[...] = packed_parts(frame["cumulative"], heads)
    cumt[...] = jnp.transpose(frame["cumulative"])
    coupling_halo = jnp.where(chunk == 0, crim[...], cprev[...])
    wide_same = [None] + [jnp.concatenate([same[lag], same[lag]], axis=1) for lag in range(1, 4)]
    craw_now = craw[...]
    pre = conv_sum(craw_now, coupling_halo, lambda lag: ccw[lag : lag + 1, :], ccb[...], wide_same)
    csig = logistic(pre)
    coupled = pre * csig
    b_value = coupled[:, :width]
    c_value = coupled[:, width:]
    b_part = split_two(b_value)
    c_part = split_two(c_value)
    gram_s[...] = mm_three_nt(b_part, c_part)
    cparts[0] = c_part[0]
    cparts[1] = c_part[1]
    bparts[0] = b_part[0]
    bparts[1] = b_part[1]
    ct_part = split_two(jnp.transpose(c_value))
    ctparts[0] = ct_part[0]
    ctparts[1] = ct_part[1]
    dgram[...] = jnp.zeros_like(dgram)
    dcoup[...] = jnp.zeros_like(dcoup)
    dhead[...] = jnp.zeros_like(dhead)
    lane = lax.broadcasted_iota(jnp.int32, (CHUNK, LANES), 1)
    row = lax.broadcasted_iota(jnp.int32, (CHUNK, LANES), 0)
    low_half = (lane < LANES // 2).astype(f32)
    high_half = 1.0 - low_half
    last_row = (row == CHUNK - 1).astype(f32)
    is_end = step_id == 0
    eight_rows = lax.broadcasted_iota(jnp.int32, cd.shape, 0)
    for place in range(2):
        chosen = jnp.where(eight_rows == chunk + place, cd[...], 0.0)
        cd_s[place : place + 1, :] = jnp.sum(chosen, axis=0, keepdims=True)

    def pair(index):
        cols = pl.ds(pl.multiple_of(index * LANES, LANES), LANES)
        wide = pl.ds(pl.multiple_of(index * 2 * LANES, 2 * LANES), 2 * LANES)
        raw = vraw[:, cols]
        full = jnp.concatenate([halo[:, cols], raw], axis=0)
        lagged = [raw] + [pltpu.roll(full, lag, 0)[8:] * same_s[lag - 1] for lag in range(1, 4)]
        pre_value = cb[:, cols]
        for lag in range(4):
            pre_value = pre_value + cw[lag : lag + 1, cols] * lagged[lag]
        sig = logistic(pre_value)
        value = pre_value * sig
        spread = mm(stack[...], sel[:, cols])
        step_e = spread[:CHUNK]
        carry_e = spread[CHUNK : 2 * CHUNK]
        tail_e = spread[2 * CHUNK :]
        inputs = step_e * value
        grads = grad[:, cols]
        column = mm(cumpack[...], selcol[:, wide])
        row_pair = jnp.concatenate(
            [cumt[pl.ds(2 * index, 1), :], cumt[pl.ds(2 * index + 1, 1), :]], axis=1
        )
        bias = bias_s[...]
        gram = gram_s[...]
        decays = jnp.exp(row_pair - column + jnp.concatenate([bias, bias], axis=1))
        mixing = jnp.concatenate([gram, gram], axis=1) * decays
        mix_high, mix_low = split_two(mixing)
        g_low = split_two(grads * low_half)
        g_high = split_two(grads * high_half)
        diag_high = jnp.concatenate([g_low[0], g_high[0]], axis=0)
        diag_low = jnp.concatenate([g_low[1], g_high[1]], axis=0)
        both = mm(mix_high, jnp.concatenate([diag_high, diag_low], axis=1))
        input_g = both[:, :LANES] + both[:, LANES:] + mm(mix_low, diag_high)
        held_g = state[:, cols]
        held_parts = split_two(held_g)
        input_g = input_g + tail_e * mm_three((bparts[0], bparts[1]), held_parts)
        in_parts = split_two(inputs)
        outer = mm_three_nt(in_parts, (diag_high, diag_low)) * decays
        dgram[...] += outer[:, :CHUNK] + outer[:, CHUNK:]
        reach_now = cd_s[0:1, cols]
        reach_next = cd_s[1:2, cols]
        arriving = entering[:, cols]
        held = st_now[0, :, cols] + reach_now * arriving
        next_own = jnp.where(is_end, fin[:, cols], st_next[0, :, cols])
        following = next_own + reach_next * arriving
        carried_g = split_two(carry_e * grads)
        state[:, cols] = carry_e[CHUNK - 1 :, :] * held_g + mm_three(
            (ctparts[0], ctparts[1]), carried_g
        )
        dcoup[1] += mm_three_nt(carried_g, split_two(held))
        dcoup[0] += mm_three_nt(split_two(tail_e * inputs), held_parts)
        value_g = input_g * step_e + skip[:, cols] * grads
        kept = jnp.sum(held_g * following, axis=0, keepdims=True)
        balance = grads * (mixer[:, cols] - skip[:, cols] * value) - inputs * input_g
        balance = balance + last_row * kept
        sums = jnp.concatenate([balance, input_g * value], axis=0)
        sums_parts = split_three(sums)
        pick = selt[cols, :]
        dhead[...] += mm(sums_parts[0], pick) + mm(sums_parts[1], pick) + mm(sums_parts[2], pick)
        skip_g[0:1, cols] += jnp.sum(grads * value, axis=0, keepdims=True)
        pre_g = value_g * (sig * (1.0 + pre_value * (1.0 - sig)))
        cw_g[4:5, cols] += jnp.sum(pre_g, axis=0, keepdims=True)
        raw_g = cw[0:1, cols] * pre_g
        cw_g[0:1, cols] += jnp.sum(pre_g * raw, axis=0, keepdims=True)
        none = jnp.zeros((8, LANES), f32)
        edge = none
        for lag in range(1, 4):
            cw_g[lag : lag + 1, cols] += jnp.sum(pre_g * lagged[lag], axis=0, keepdims=True)
            weighted = cw[lag : lag + 1, cols] * (pre_g * same_s[lag - 1])
            padded = jnp.concatenate([none, weighted, none], axis=0)
            turned = pltpu.roll(padded, CHUNK + 16 - lag, 0)
            raw_g = raw_g + turned[8 : 8 + CHUNK]
            edge = edge + turned[:8]
        last_rows = raw_g[CHUNK - 8 :] + rim_s[:, cols]
        lead_g[:, cols] = jnp.concatenate([raw_g[: CHUNK - 8], last_rows], axis=0).astype(bf16)

        @pl.when(step_id == 0)
        def _():
            vtail_g[:, cols] = last_rows

        rim_s[:, cols] = edge
        vrim_g[:, cols] = edge

    groups = 4
    per_group = heads // 2 // groups

    def group(number, carried):
        for inside in range(per_group):
            pair(number * per_group + inside)
        share = per_step // (groups + 1)
        reduce_steps(number * share, share)
        return carried

    lax.fori_loop(0, groups, group, 0)
    used = groups * (per_step // (groups + 1))
    reduce_steps(used, per_step - used)

    total = dgram[...]
    total_parts = split_two(total)
    turned_parts = split_two(jnp.transpose(total))
    b_grad = dcoup[0] + mm_three(total_parts, (cparts[0], cparts[1]))
    c_grad = dcoup[1] + mm_three(turned_parts, (bparts[0], bparts[1]))
    coupled_g = jnp.concatenate([b_grad, c_grad], axis=1)
    pre_g = coupled_g * (csig * (1.0 + pre * (1.0 - csig)))
    ccw_g[4:5, :] += jnp.sum(pre_g, axis=0, keepdims=True)
    ccw_g[0:1, :] += jnp.sum(pre_g * craw_now, axis=0, keepdims=True)
    raw_g = ccw[0:1, :] * pre_g
    full = jnp.concatenate([coupling_halo, craw_now], axis=0)
    none = jnp.zeros((8, 2 * width), f32)
    edge = none
    for lag in range(1, 4):
        masked = pre_g * wide_same[lag]
        ccw_g[lag : lag + 1, :] += jnp.sum(
            masked * pltpu.roll(full, lag, 0)[8:], axis=0, keepdims=True
        )
        padded = jnp.concatenate([none, ccw[lag : lag + 1, :] * masked, none], axis=0)
        turned = pltpu.roll(padded, CHUNK + 16 - lag, 0)
        raw_g = raw_g + turned[8 : 8 + CHUNK]
        edge = edge + turned[:8]
    craw_g[...] = raw_g
    craw_g[CHUNK - 8 :, :] += crim_s[...]
    crim_s[...] = edge
    crim_g[...] = edge

    upper = (frame["row_ids"] <= frame["column_ids"]).astype(bf16)
    parts = split_three(dhead[:CHUNK])
    decay_g = mm(upper, parts[0]) + mm(upper, parts[1]) + mm(upper, parts[2])
    step_g = (dhead[CHUNK:] - rate[...] * decay_g) * logistic(frame["shifted"])
    lead_g[:, inner : inner + 2 * width] = jnp.zeros((CHUNK, 2 * width), bf16)
    lead_g[:, inner + 2 * width :] = step_g.astype(bf16)
    small_g[0:1, :] += jnp.sum(step_g, axis=0, keepdims=True)
    small_g[1:2, :] += jnp.sum(-frame["step"] * decay_g, axis=0, keepdims=True)


def backward_ssd(
    marks, micros, raw, rims, inner, twice, tokens, grad, mixer, states, fin, entering, cd, pulled,
    cw, cb, ccw, ccb, sbias, rate, skip, sel, selcol, selt, terms, first, collective_id,
):
    width = twice // 2
    chunks = tokens // CHUNK
    heads = inner // (LANES // 2)
    eighth = CHUNK // 8
    pairs = lax.axis_size("fsdp") // 2
    shard_rows = terms[0].shape[0] // (2 * pairs)
    plan = Reduction(shard_rows, pairs, [term.shape[1] for term in terms], 2)
    lead = inner + twice + LANES

    def row(step):
        return step // chunks * chunks + chunks - 1 - lax.rem(step, chunks)

    def part(count, start):
        return pl.BlockSpec((CHUNK, count), lambda step: (row(step), start // count))

    def before(count, start):
        return pl.BlockSpec(
            (8, count), lambda step: (jnp.maximum(row(step) * eighth - 1, 0), start // count)
        )

    def edge(count, start):
        return pl.BlockSpec(
            (None, 8, count), lambda step: (step // chunks, 0, start // count)
        )

    def held(offset):
        return pl.BlockSpec(
            (1, width, inner),
            lambda step: (
                jnp.minimum(row(step) + offset, (step // chunks + 1) * chunks - 1), 0, 0,
            ),
        )

    def each(*shape):
        return pl.BlockSpec((None, *shape), lambda step: (step // chunks, 0, 0))

    hbm = pl.BlockSpec(memory_space=pl.ANY)
    return pl.pallas_call(
        functools.partial(backward_kernel, heads, chunks, plan, len(first)),
        grid=(micros * chunks,),
        in_specs=[
            pl.BlockSpec(memory_space=pltpu.SMEM),
            part(inner, 0),
            before(inner, 0),
            edge(inner, 0),
            part(twice, inner),
            before(twice, inner),
            edge(twice, inner),
            part(LANES, inner + twice),
            part(inner, 0),
            part(inner, 0),
            held(0),
            held(1),
            each(width, inner),
            each(width, inner),
            each(8, inner),
            each(width, inner),
            whole(cw.shape),
            whole(cb.shape),
            whole(ccw.shape),
            whole(ccb.shape),
            whole(sbias.shape),
            whole(rate.shape),
            whole(skip.shape),
            whole(sel.shape),
            whole(selcol.shape),
            whole(selt.shape),
        ]
        + [hbm] * (len(terms) + len(first)),
        out_specs=[
            part(lead, 0),
            each(8, inner),
            each(8, inner),
            part(twice, 0),
            each(8, twice),
            whole((8, inner)),
            whole((8, twice)),
            whole((8, LANES)),
            whole((8, inner)),
        ]
        + [hbm] * len(terms),
        scratch_shapes=[
            pltpu.VMEM((width, inner), f32),
            pltpu.VMEM((LANES, CHUNK), f32),
            pltpu.VMEM((3 * CHUNK, LANES), bf16),
            pltpu.VMEM((CHUNK, LANES), bf16),
            pltpu.VMEM((8, inner), f32),
            pltpu.VMEM((3, CHUNK, LANES), f32),
            pltpu.VMEM((CHUNK, CHUNK), f32),
            pltpu.VMEM((CHUNK, CHUNK), f32),
            pltpu.VMEM((2, CHUNK, width), bf16),
            pltpu.VMEM((2, CHUNK, width), bf16),
            pltpu.VMEM((2, width, CHUNK), bf16),
            pltpu.VMEM((8, inner), f32),
            pltpu.VMEM((8, twice), f32),
            pltpu.VMEM((CHUNK, CHUNK), f32),
            pltpu.VMEM((2, CHUNK, width), f32),
            pltpu.VMEM((2 * CHUNK, LANES), f32),
            pltpu.VMEM((8, inner), f32),
        ]
        + plan.scratch(),
        out_shape=[
            jax.ShapeDtypeStruct((micros * tokens, lead), bf16),
            jax.ShapeDtypeStruct((micros, 8, inner), f32),
            jax.ShapeDtypeStruct((micros, 8, inner), f32),
            jax.ShapeDtypeStruct((micros * tokens, twice), f32),
            jax.ShapeDtypeStruct((micros, 8, twice), f32),
            jax.ShapeDtypeStruct((8, inner), f32),
            jax.ShapeDtypeStruct((8, twice), f32),
            jax.ShapeDtypeStruct((8, LANES), f32),
            jax.ShapeDtypeStruct((8, inner), f32),
        ]
        + [jax.ShapeDtypeStruct((shard_rows, term.shape[1]), f32) for term in terms],
        compiler_params=pltpu.CompilerParams(
            collective_id=collective_id, has_side_effects=True, vmem_limit_bytes=60 * 1024 * 1024
        ),
    )(
        marks, raw, raw, rims, raw, raw, rims, raw, grad, mixer, states, states, fin, entering,
        cd, pulled, cw, cb, ccw, ccb, sbias, rate, skip, sel, selcol, selt,
        *[term.reshape(pairs, 2, shard_rows, -1) for term in terms], *first,
    )


class Gathering:
    def __init__(self, rows, pairs, widths, cuts, shared):
        self.rows, self.pairs, self.shared = rows, pairs, shared
        self.arrays = len(widths)
        self.pieces = []
        for array, width in enumerate(widths):
            size = -(-width // LANES // cuts) * LANES
            self.pieces += [
                (array, start, min(size, width - start)) for start in range(0, width, size)
            ]
        self.moved = rows - shared
        self.early = min(rows // 8, self.moved - shared) // 16 * 16
        self.late = self.moved - self.early
        self.order = [(j, k) for j in range(len(self.pieces)) for k in range(pairs)]
        if pairs > 1:
            self.order.sort(key=lambda item: (item[0] * pairs + (item[1] or -0.5 - (item[0] > 0))))
        self.lag = 2

    def scratch(self):
        dma, pairs, arrays = pltpu.SemaphoreType.DMA, self.pairs, len(self.pieces)
        return [
            dma((arrays, max(pairs - 1, 1))),
            dma((arrays, max(pairs - 1, 1))),
            dma((arrays, pairs)),
            dma((arrays, pairs)),
            dma((arrays, 2 * pairs)),
            dma((arrays, 2 * pairs)),
            dma((arrays, 2 * pairs)),
            dma((arrays, 2 * pairs)),
            dma((arrays,)),
        ]

    def bind(self, weights, fulls, scratch):
        self.weights, self.fulls = weights, fulls
        (
            self.ring_send, self.ring_recv, self.pair_send, self.pair_recv,
            self.cross_send, self.cross_recv, self.early_send, self.early_recv, self.local,
        ) = scratch
        self.own, self.place = lax.axis_index("fsdp"), lax.axis_index("context")
        self.side = lax.axis_index("tensor")
        self.pair, self.member = self.own // 2, lax.rem(self.own, 2)
        pairs, pair, member = self.pairs, self.pair, self.member
        self.ahead = (2 * lax.rem(pair + 1, pairs) + member, self.place, self.side)
        self.behind = (2 * lax.rem(pair + pairs - 1, pairs) + member, self.place, self.side)
        self.partner = (2 * pair + 1 - member, self.place, self.side)
        self.across = (self.own, 1 - self.place, self.side)
        self.beside = (self.own, self.place, 1 - self.side)
        self.late_start = pl.multiple_of(self.place * (self.shared + self.early), 16)
        self.early_start = pl.multiple_of(
            self.place * self.shared + (1 - self.place) * self.late, 16
        )
        self.shared_start = pl.multiple_of(self.place * self.moved, 16)

    def greet(self, *others):
        barrier = pltpu.get_barrier_semaphore()
        devices = [self.ahead, self.behind, self.partner, self.across, *others]
        for device in devices:
            pl.semaphore_signal(barrier, inc=1, device_id=device, device_id_type=MESH)
        pl.semaphore_wait(barrier, len(devices))

    def part(self, j, k, which, start, size):
        there = lax.rem(self.pair + self.pairs - k, self.pairs)
        index = 2 * there + (self.member if which == 0 else 1 - self.member)
        array, first, width = self.pieces[j]
        rows = pl.ds(pl.multiple_of(index * self.rows + start, 16), size)
        return self.fulls[array].at[rows, pl.ds(first, width)]

    def source(self, j, k, which, start, size):
        if k == 0 and which == 0:
            array, first, width = self.pieces[j]
            return self.weights[array].at[pl.ds(start, size), pl.ds(first, width)]
        return self.part(j, k, which, start, size)

    def ring_copy(self, j, k):
        return pltpu.make_async_remote_copy(
            src_ref=self.source(j, k, 0, self.late_start, self.late),
            dst_ref=self.part(j, k, 0, self.late_start, self.late),
            send_sem=self.ring_send.at[j, k], recv_sem=self.ring_recv.at[j, k],
            device_id=self.ahead, device_id_type=MESH,
        )

    def pair_copy(self, j, k):
        return pltpu.make_async_remote_copy(
            src_ref=self.source(j, k, 0, self.late_start, self.late),
            dst_ref=self.part(j, k, 0, self.late_start, self.late),
            send_sem=self.pair_send.at[j, k], recv_sem=self.pair_recv.at[j, k],
            device_id=self.partner, device_id_type=MESH,
        )

    def early_copy(self, j, k, which):
        own = k == self.pairs - 1
        k = 0 if own else k
        slot = 2 * self.pairs - 2 if own else 2 * k + which
        return pltpu.make_async_remote_copy(
            src_ref=self.source(j, k, which, self.early_start, self.early),
            dst_ref=self.part(j, k, which, self.early_start, self.early),
            send_sem=self.early_send.at[j, slot], recv_sem=self.early_recv.at[j, slot],
            device_id=self.partner if own else self.ahead, device_id_type=MESH,
        )

    def early_event(self, j, k):
        last = self.pairs - 1
        if k == 0:
            self.early_copy(j, last, 0).start()
        else:
            self.early_copy(j, k - 1, 0).wait_recv()
        if k < last:
            self.early_copy(j, k, 0).start()
        if k == 1:
            self.early_copy(j, last, 0).wait_recv()
        elif k > 1:
            self.early_copy(j, k - 2, 1).wait_recv()
        if k > 0:
            self.early_copy(j, k - 1, 1).start()

    def cross_copy(self, j, k, which):
        here = self.part(j, k, which, self.shared_start, self.shared)
        return pltpu.make_async_remote_copy(
            src_ref=here, dst_ref=here,
            send_sem=self.cross_send.at[j, 2 * k + which], recv_sem=self.cross_recv.at[j, 2 * k + which],
            device_id=self.across, device_id_type=MESH,
        )

    def keep_copy(self, j):
        rows = pl.ds(pl.multiple_of(self.own * self.rows, 16), self.rows)
        return pltpu.make_async_copy(self.weights[j], self.fulls[j].at[rows, :], self.local.at[j])

    def event(self, number):
        j, k = self.order[number]
        if k > 0:
            self.ring_copy(j, k - 1).wait_recv()
        if number == 0:
            for array in range(self.arrays):
                self.keep_copy(array).start()
        if k < self.pairs - 1:
            self.ring_copy(j, k).start()
        self.pair_copy(j, k).start()
        if k > 0:
            self.cross_copy(j, k, 0).start()
        if self.early:
            self.early_event(j, k)
        if number >= self.lag:
            self.share(number - self.lag)

    def share(self, number):
        j, k = self.order[number]
        self.pair_copy(j, k).wait_recv()
        self.cross_copy(j, k, 1).start()

    def finish(self):
        for number in range(max(len(self.order) - self.lag, 0), len(self.order)):
            self.share(number)
        crossed = [(j, k, which) for j, k in self.order for which in range(2) if k or which]
        for item in crossed:
            self.cross_copy(*item).wait_recv()
        for j, k in self.order:
            if k < self.pairs - 1:
                self.ring_copy(j, k).wait_send()
            self.pair_copy(j, k).wait_send()
        for item in crossed:
            self.cross_copy(*item).wait_send()
        for j in range(len(self.pieces)):
            if self.early:
                last = self.pairs - 1
                if last:
                    self.early_copy(j, last - 1, 1).wait_recv()
                else:
                    self.early_copy(j, last, 0).wait_recv()
                self.early_copy(j, last, 0).wait_send()
                for k in range(last):
                    for which in range(2):
                        self.early_copy(j, k, which).wait_send()
        for array in range(self.arrays):
            self.keep_copy(array).wait()


def gather_kernel(plan, *refs):
    arrays = plan.arrays
    weights, tokens = refs[:arrays], refs[arrays]
    fulls, far = refs[arrays + 1 : 2 * arrays + 1], refs[2 * arrays + 1]
    extra_send, extra_recv = refs[2 * arrays + 2 : 2 * arrays + 4]
    plan.bind(weights, fulls, refs[2 * arrays + 4 :])
    plan.greet(plan.beside)
    half = tokens.shape[2] // 2
    lanes = pl.ds(pl.multiple_of(plan.side * half, 128), half)

    def token_copy(src, number, device):
        return pltpu.make_async_remote_copy(
            src_ref=src.at[:, :, lanes], dst_ref=far.at[:, :, lanes],
            send_sem=extra_send.at[number], recv_sem=extra_recv.at[number],
            device_id=device, device_id_type=MESH,
        )

    first, second = token_copy(tokens, 0, plan.across), token_copy(far, 1, plan.beside)
    first.start()
    for number in range(len(plan.order)):
        plan.event(number)
        if number == min(5, len(plan.order) - 1):
            first.wait_recv()
            second.start()
    second.wait_recv()
    plan.finish()
    first.wait_send()
    second.wait_send()


def gather_weights(shards, tokens, shared, collective_id):
    rows = shards[0].shape[0]
    pairs = lax.axis_size("fsdp") // 2
    count = len(shards)
    plan = Gathering(rows, pairs, [shard.shape[1] for shard in shards], 2, shared)
    hbm = pl.BlockSpec(memory_space=pl.ANY)
    dma = pltpu.SemaphoreType.DMA
    return pl.pallas_call(
        functools.partial(gather_kernel, plan),
        out_shape=[
            jax.ShapeDtypeStruct((2 * pairs * rows, shard.shape[1]), shard.dtype) for shard in shards
        ]
        + [jax.ShapeDtypeStruct(tokens.shape, tokens.dtype)],
        in_specs=[hbm] * (count + 1),
        out_specs=[hbm] * (count + 1),
        scratch_shapes=[dma((2,)), dma((2,))] + plan.scratch(),
        compiler_params=pltpu.CompilerParams(collective_id=collective_id, has_side_effects=True),
    )(*shards, tokens)


def order_kernel(near_index, far_index, is_near, near, far, gain, x_out, normed_out, scale_out):
    step = pl.program_id(0)
    near_now = is_near[step] == 1
    x = jnp.where(near_now, near[...], far[...])
    x_out[...] = x
    value = x.astype(f32)
    mean = jnp.sum(value * value, axis=-1, keepdims=True) * (1.0 / value.shape[-1])
    scale = lax.rsqrt(mean + epsilon)
    normed_out[...] = (value * scale * gain[...]).astype(bf16)
    scale_out[...] = jnp.broadcast_to(scale, scale_out.shape)


def ordered(near, far, near_index, far_index, is_near, gain):
    micros, count, length, model = near.shape
    blocks = micros * count

    def block(spec_index):
        return pl.BlockSpec((None, None, length, model), spec_index)

    def rows(lanes):
        return pl.BlockSpec((length, lanes), lambda step, *_: (step, 0))

    return pl.pallas_call(
        order_kernel,
        grid_spec=pltpu.PrefetchScalarGridSpec(
            num_scalar_prefetch=3,
            grid=(blocks,),
            in_specs=[
                block(lambda step, near_at, far_at, flags: (step // count, near_at[step], 0, 0)),
                block(lambda step, near_at, far_at, flags: (step // count, far_at[step], 0, 0)),
                pl.BlockSpec((1, model), lambda *_: (0, 0)),
            ],
            out_specs=[rows(model), rows(model), rows(LANES)],
        ),
        out_shape=[
            jax.ShapeDtypeStruct((blocks * length, model), bf16),
            jax.ShapeDtypeStruct((blocks * length, model), bf16),
            jax.ShapeDtypeStruct((blocks * length, LANES), f32),
        ],
        compiler_params=pltpu.CompilerParams(vmem_limit_bytes=32 * 1024 * 1024),
    )(near_index, far_index, is_near, near, far, gain)


def gate_kernel(
    normed, out_grad, gate_weight, out_weight, y_own, carry, coupled, entering, gain,
    mixer_out, gate_out, grad_out, sums_out,
):
    gate_in = mm(normed[...], gate_weight[...])
    grads = mm(out_grad[...], out_weight[...])
    width = entering.shape[0]
    arrived = mm_three(split_two(coupled[:, width:]), split_two(entering[...]))
    mixer = y_own[...] + carry[...] * arrived
    gated = mixer * (gate_in * logistic(gate_in))
    mixer_out[...] = mixer
    gate_out[...] = gate_in
    grad_out[...] = grads
    square = jnp.sum(gated * gated, axis=-1, keepdims=True)
    product = jnp.sum(grads * gain[...] * gated, axis=-1, keepdims=True)
    lane = lax.broadcasted_iota(jnp.int32, sums_out.shape, 1)
    sums_out[...] = jnp.where(lane == 0, square, jnp.where(lane == 1, product, 0.0))


def gate_stage(normed, out_grad, gate_weight, out_weight, y_own, carry, coupled, entering, gain):
    rows, model = normed.shape
    inner = y_own.shape[1]
    twice = coupled.shape[1]
    micros, width, _ = entering.shape
    size = 2 * CHUNK
    per_micro = rows // micros // size

    def block(lanes):
        return pl.BlockSpec((size, lanes), lambda step: (step, 0))

    return pl.pallas_call(
        gate_kernel,
        grid=(rows // size,),
        in_specs=[
            block(model),
            block(model),
            pl.BlockSpec((model, inner), lambda step: (0, 0), pipeline_mode=pl.Buffered(1)),
            pl.BlockSpec((model, inner), lambda step: (0, 0), pipeline_mode=pl.Buffered(1)),
            block(inner),
            block(inner),
            block(twice),
            pl.BlockSpec((None, width, inner), lambda step: (step // per_micro, 0, 0)),
            pl.BlockSpec((1, inner), lambda step: (0, 0)),
        ],
        out_specs=[block(inner), block(inner), block(inner), block(LANES)],
        out_shape=[jax.ShapeDtypeStruct((rows, inner), f32)] * 3
        + [jax.ShapeDtypeStruct((rows, LANES), f32)],
        compiler_params=pltpu.CompilerParams(vmem_limit_bytes=60 * 1024 * 1024),
        cost_estimate=pl.CostEstimate(
            flops=4 * rows * model * inner, bytes_accessed=24 * rows * inner, transcendentals=0
        ),
    )(normed, out_grad, gate_weight, out_weight, y_own, carry, coupled, entering, gain)


def gate_back_kernel(
    inner_total, per_micro, mixer, gate_in, grads, carry, coupled, sums, gain,
    norm_out, gate_out, mixer_out, pull_out, gain_out,
):
    step = pl.program_id(0)
    width = pull_out.shape[0]
    inv_norm = lax.rsqrt(sums[:, 0:1] / inner_total + epsilon)
    inner_dot = sums[:, 1:2] * (inv_norm * inv_norm * inv_norm) / inner_total
    mixer_now, gate_now, grad_now = mixer[...], gate_in[...], grads[...]
    sig = logistic(gate_now)
    act = gate_now * sig
    gated = mixer_now * act
    norm_out[...] = (gated * inv_norm * gain[...]).astype(bf16)
    gated_grad = grad_now * gain[...] * inv_norm - gated * inner_dot
    gate_out[...] = (gated_grad * mixer_now * sig * (1.0 + gate_now * (1.0 - sig))).astype(bf16)
    mixer_grad = gated_grad * act
    mixer_out[...] = mixer_grad

    @pl.when(step == 0)
    def _():
        gain_out[...] = jnp.zeros_like(gain_out)

    gain_out[0:1, :] += jnp.sum(grad_now * gated * inv_norm, axis=0, keepdims=True)

    @pl.when(lax.rem(step, per_micro) == 0)
    def _():
        pull_out[...] = jnp.zeros_like(pull_out)

    turned = split_two(jnp.transpose(coupled[:, width:]))
    pull_out[...] += mm_three(turned, split_two(carry[...] * mixer_grad))


def gate_back_stage(mixer, gate_in, grads, carry, coupled, sums, gain, micros, inner_total):
    rows, inner = mixer.shape
    twice = coupled.shape[1]
    width = twice // 2
    per_micro = rows // micros // CHUNK

    def block(lanes):
        return pl.BlockSpec((CHUNK, lanes), lambda step: (step, 0))

    return pl.pallas_call(
        functools.partial(gate_back_kernel, inner_total, per_micro),
        grid=(rows // CHUNK,),
        in_specs=[
            block(inner),
            block(inner),
            block(inner),
            block(inner),
            block(twice),
            block(LANES),
            pl.BlockSpec((1, inner), lambda step: (0, 0)),
        ],
        out_specs=[
            block(inner),
            block(inner),
            block(inner),
            pl.BlockSpec((None, width, inner), lambda step: (step // per_micro, 0, 0)),
            pl.BlockSpec((8, inner), lambda step: (0, 0)),
        ],
        out_shape=[
            jax.ShapeDtypeStruct((rows, inner), bf16),
            jax.ShapeDtypeStruct((rows, inner), bf16),
            jax.ShapeDtypeStruct((rows, inner), f32),
            jax.ShapeDtypeStruct((micros, width, inner), f32),
            jax.ShapeDtypeStruct((8, inner), f32),
        ],
        compiler_params=pltpu.CompilerParams(vmem_limit_bytes=48 * 1024 * 1024),
        cost_estimate=pl.CostEstimate(
            flops=8 * rows * width * inner, bytes_accessed=24 * rows * inner, transcendentals=0
        ),
    )(mixer, gate_in, grads, carry, coupled, sums, gain)


def weave_kernel(first, second, out):
    out[:, 0, :] = first[...]
    out[:, 1, :] = second[...]


def woven(first, second, columns):
    rows = first.shape[0]
    size = 32
    block = pl.BlockSpec((size, columns), lambda step: (step, 0))
    return pl.pallas_call(
        weave_kernel,
        grid=(rows // size,),
        in_specs=[block, block],
        out_specs=pl.BlockSpec((size, 2, columns), lambda step: (step, 0, 0)),
        out_shape=jax.ShapeDtypeStruct((rows, 2, columns), first.dtype),
    )(first, second)


class Reduction:
    def __init__(self, rows, pairs, columns, lag):
        self.rows, self.pairs, self.columns, self.lag = rows, pairs, columns, lag
        self.shared = rows // 4
        self.moved = rows - self.shared
        self.counts = [count // LANES for count in columns]
        self.count = sum(self.counts)
        self.steps = self.count + 4 * lag

    def scratch(self):
        shared, moved, pairs, count = self.shared, self.moved, self.pairs, self.count
        cross, pair, ring = 2 * pairs * shared + 16, pairs * moved + 16, moved + 16
        i16, dma = jnp.int16, pltpu.SemaphoreType.DMA
        return [
            pltpu.VMEM((count, cross, LANES), i16),
            pltpu.VMEM((count, pair, LANES), i16),
            pltpu.VMEM((count, pairs - 1, ring, LANES), i16),
            pltpu.VMEM((count, ring, LANES), i16),
            pltpu.VMEM((2, cross, LANES), i16),
            pltpu.VMEM((2, pair, LANES), i16),
            pltpu.VMEM((2, pairs - 1, ring, LANES), i16),
            pltpu.VMEM((2, ring, LANES), i16),
            pltpu.VMEM((2, pairs, 2, shared, LANES), f32),
            pltpu.VMEM((2, pairs, moved, LANES), f32),
            pltpu.VMEM((2, pairs, moved, LANES), f32),
            pltpu.VMEM((2 * self.lag, moved, LANES), f32),
            pltpu.VMEM((2 * self.lag, moved, LANES), f32),
            pltpu.VMEM((2, self.rows, LANES), f32),
            dma((count,)),
            dma((count,)),
            dma((pairs - 1, count)),
            dma((count,)),
            dma((2,)),
            dma((2,)),
            dma((pairs - 1, 2)),
            dma((2,)),
            dma((3, 2)),
            dma((2,)),
        ]

    def bind(self, terms, outs, scratch):
        self.terms, self.outs = terms, outs
        (
            self.cross_in, self.pair_in, self.ring_in, self.last_in,
            self.cross_out, self.pair_out, self.ring_out, self.last_out,
            self.cross_term, self.pair_term, self.ring_term,
            self.kept, self.held, self.result,
            self.cross_recv, self.pair_recv, self.ring_recv, self.last_recv,
            self.cross_sent, self.pair_sent, self.ring_sent, self.last_sent,
            self.loaded, self.stored,
        ) = scratch
        self.own, self.place = lax.axis_index("fsdp"), lax.axis_index("context")
        self.side = lax.axis_index("tensor")
        self.pair, self.member = self.own // 2, lax.rem(self.own, 2)
        self.across = (self.own, 1 - self.place, self.side)
        self.partner = (2 * self.pair + 1 - self.member, self.place, self.side)
        self.inset = pl.multiple_of(self.place * (self.moved - self.shared), 16)
        self.start = pl.multiple_of(self.place * self.shared, 16)

    def peer(self, offset):
        there = lax.rem(self.pair + offset, self.pairs)
        return (2 * there + self.member, self.place, self.side)

    def greet(self):
        barrier = pltpu.get_barrier_semaphore()
        devices = [self.across, self.partner] + [self.peer(k) for k in range(1, self.pairs)]
        for device in devices:
            pl.semaphore_signal(barrier, inc=1, device_id=device, device_id_type=MESH)
        pl.semaphore_wait(barrier, len(devices))

    def cross_copy(self, chunk):
        slot = lax.rem(chunk, 2)
        return pltpu.make_async_remote_copy(
            src_ref=self.cross_out.at[slot], dst_ref=self.cross_in.at[chunk],
            send_sem=self.cross_sent.at[slot], recv_sem=self.cross_recv.at[chunk],
            device_id=self.across, device_id_type=MESH,
        )

    def pair_copy(self, chunk):
        slot = lax.rem(chunk, 2)
        return pltpu.make_async_remote_copy(
            src_ref=self.pair_out.at[slot], dst_ref=self.pair_in.at[chunk],
            send_sem=self.pair_sent.at[slot], recv_sem=self.pair_recv.at[chunk],
            device_id=self.partner, device_id_type=MESH,
        )

    def ring_copy(self, chunk, offset):
        slot = lax.rem(chunk, 2)
        return pltpu.make_async_remote_copy(
            src_ref=self.ring_out.at[slot, offset - 1], dst_ref=self.ring_in.at[chunk, offset - 1],
            send_sem=self.ring_sent.at[offset - 1, slot],
            recv_sem=self.ring_recv.at[offset - 1, chunk],
            device_id=self.peer(offset), device_id_type=MESH,
        )

    def last_copy(self, chunk):
        slot = lax.rem(chunk, 2)
        return pltpu.make_async_remote_copy(
            src_ref=self.last_out.at[slot], dst_ref=self.last_in.at[chunk],
            send_sem=self.last_sent.at[slot], recv_sem=self.last_recv.at[chunk],
            device_id=self.across, device_id_type=MESH,
        )

    def load_copy(self, stage, term, cols, slot):
        if stage == 0:
            rows = pl.ds(pl.multiple_of((1 - self.place) * self.moved, 16), self.shared)
            src, dst = term.at[:, :, rows, cols], self.cross_term.at[slot]
        elif stage == 1:
            src = term.at[:, 1 - self.member, pl.ds(self.start, self.moved), cols]
            dst = self.pair_term.at[slot]
        else:
            src = term.at[:, self.member, pl.ds(self.start, self.moved), cols]
            dst = self.ring_term.at[slot]
        return pltpu.make_async_copy(src, dst, self.loaded.at[stage, slot])

    def each_array(self, chunk, act):
        first = 0
        for number, count in enumerate(self.counts):
            inside = (chunk >= first) & (chunk < first + count)
            offset = first

            @pl.when(inside)
            def _(number=number, offset=offset):
                act(number, pl.ds(pl.multiple_of((chunk - offset) * LANES, LANES), LANES))

            first += count

    def load(self, stage, chunk):
        @pl.when((chunk >= 0) & (chunk < self.count))
        def _():
            self.each_array(
                chunk,
                lambda number, cols: self.load_copy(
                    stage, self.terms[number], cols, lax.rem(chunk, 2)
                ).start(),
            )

    def loaded_now(self, stage, chunk):
        self.load_copy(stage, self.terms[0], pl.ds(0, LANES), lax.rem(chunk, 2)).wait()

    @staticmethod
    def encode(value, out, place):
        count = value.shape[0]
        peak = jnp.maximum(jnp.max(jnp.abs(value), axis=0, keepdims=True), 1e-30)
        exponent = jnp.ceil(jnp.log(peak) * 1.4426950408889634)
        factor = jnp.exp(exponent * -0.6931471805599453) * 32000.0
        out[place + (pl.ds(0, count), slice(None))] = (
            (value * factor + 12582912.0 - 12582912.0).astype(jnp.int32).astype(jnp.int16)
        )
        out[place + (pl.ds(count, 16), slice(None))] = (
            jnp.broadcast_to(exponent, (16, LANES)).astype(jnp.int32).astype(jnp.int16)
        )

    @staticmethod
    def unit(ref, place, count):
        exponents = ref[place + (pl.ds(count, 16), slice(None))].astype(jnp.int32).astype(f32)
        return jnp.exp(exponents[:1] * 0.6931471805599453) * (1.0 / 32000.0)

    @staticmethod
    def decode(ref, place, first, count, unit):
        first = pl.multiple_of(first, 16) if not isinstance(first, int) else first
        return ref[place + (pl.ds(first, count), slice(None))].astype(jnp.int32).astype(f32) * unit

    def step(self, number):
        lag, pairs, shared, moved = self.lag, self.pairs, self.shared, self.moved

        @pl.when(number == 0)
        def _():
            self.load(0, number)

        self.load(0, number + 1)
        self.load(1, number + 1 - lag)
        self.load(2, number + 1 - 2 * lag)

        def stage(index, act):
            chunk = number - index * lag

            @pl.when((chunk >= 0) & (chunk < self.count))
            def _():
                act(chunk, lax.rem(chunk, 2))

        def cross(chunk, slot):
            self.loaded_now(0, chunk)

            @pl.when(chunk >= 2)
            def _():
                self.cross_copy(chunk - 2).wait_send()

            value = self.cross_term[slot].reshape(2 * pairs * shared, LANES)
            self.encode(value, self.cross_out, (slot,))
            self.cross_copy(chunk).start()

        def pair(chunk, slot):
            self.loaded_now(1, chunk)
            self.cross_copy(chunk).wait_recv()

            @pl.when(chunk >= 2)
            def _():
                self.pair_copy(chunk - 2).wait_send()

            unit = self.unit(self.cross_in, (chunk,), 2 * pairs * shared)
            for there in range(pairs):
                first = (2 * there + 1 - self.member) * shared
                self.pair_term[slot, there, pl.ds(self.inset, shared), :] += self.decode(
                    self.cross_in, (chunk,), first, shared, unit
                )
            value = self.pair_term[slot].reshape(pairs * moved, LANES)
            self.encode(value, self.pair_out, (slot,))
            self.pair_copy(chunk).start()

        def ring(chunk, slot):
            self.loaded_now(2, chunk)
            self.pair_copy(chunk).wait_recv()

            @pl.when(chunk >= 2)
            def _():
                for offset in range(1, pairs):
                    self.ring_copy(chunk - 2, offset).wait_send()

            cross_unit = self.unit(self.cross_in, (chunk,), 2 * pairs * shared)
            pair_unit = self.unit(self.pair_in, (chunk,), pairs * moved)
            for offset in list(range(1, pairs)) + [0]:
                there = lax.rem(self.pair + offset, pairs)
                first = (2 * there + self.member) * shared
                self.ring_term[slot, there, pl.ds(self.inset, shared), :] += self.decode(
                    self.cross_in, (chunk,), first, shared, cross_unit
                )
                value = self.ring_term[slot, there] + self.decode(
                    self.pair_in, (chunk,), there * moved, moved, pair_unit
                )
                if offset:
                    self.encode(value, self.ring_out, (slot, offset - 1))
                    self.ring_copy(chunk, offset).start()
                else:
                    self.kept[lax.rem(chunk, 2 * lag)] = value

        def last(chunk, slot):
            for offset in range(1, pairs):
                self.ring_copy(chunk, offset).wait_recv()

            @pl.when(chunk >= 2)
            def _():
                self.last_copy(chunk - 2).wait_send()

            total = self.kept[lax.rem(chunk, 2 * lag)]
            for offset in range(1, pairs):
                place = (chunk, offset - 1)
                total = total + self.decode(
                    self.ring_in, place, 0, moved, self.unit(self.ring_in, place, moved)
                )
            self.encode(total, self.last_out, (slot,))
            self.held[lax.rem(chunk, 2 * lag)] = self.decode(
                self.last_out, (slot,), 0, moved, self.unit(self.last_out, (slot,), moved)
            )
            self.last_copy(chunk).start()

        def write_copy(number, cols, slot):
            return pltpu.make_async_copy(
                self.result.at[slot], self.outs[number].at[:, cols], self.stored.at[slot]
            )

        def write(chunk, slot):
            self.last_copy(chunk).wait_recv()

            @pl.when(chunk >= 2)
            def _():
                write_copy(0, pl.ds(0, LANES), slot).wait()

            mine = self.held[lax.rem(chunk, 2 * lag)]
            other = self.decode(
                self.last_in, (chunk,), 0, moved, self.unit(self.last_in, (chunk,), moved)
            )
            low = jnp.where(self.place == 0, mine, other)
            high = jnp.where(self.place == 0, other, mine)
            self.result[slot, pl.ds(0, shared), :] = low[:shared]
            self.result[slot, pl.ds(shared, moved - shared), :] = (
                low[shared:] + high[: moved - shared]
            )
            self.result[slot, pl.ds(moved, shared), :] = high[moved - shared :]
            self.each_array(chunk, lambda which, cols: write_copy(which, cols, slot).start())

        stage(4, write)
        stage(3, last)
        stage(2, ring)
        stage(1, pair)
        stage(0, cross)

        @pl.when(number == self.steps - 1)
        def _():
            for slot in range(2):
                write_copy(0, pl.ds(0, LANES), slot).wait()
                self.cross_copy(jnp.int32(self.count - 2 + slot)).wait_send()
                self.pair_copy(jnp.int32(self.count - 2 + slot)).wait_send()
                self.last_copy(jnp.int32(self.count - 2 + slot)).wait_send()
                for offset in range(1, pairs):
                    self.ring_copy(jnp.int32(self.count - 2 + slot), offset).wait_send()


def finish_kernel(plan, blocks, *refs):
    (
        term, x, cot, scale, keep, branch, branch_other, part, part_other, gain, small,
        out, block_out, input_out, small_out,
        gain_sum, cross_in, pair_out, pair_in, ring_in,
        cross_send, cross_recv, pair_send, pair_recv, ring_send, ring_recv, final_sem,
    ) = refs[:27]
    plan.bind([term], [out], refs[27:])
    step = pl.program_id(0)

    @pl.when(step == 0)
    def _():
        plan.greet()
        gain_sum[...] = jnp.zeros_like(gain_sum)

    @pl.when(step < plan.steps)
    def _():
        plan.step(step)

    @pl.when(step < blocks)
    def _():
        x_float = x[...].astype(f32)
        block_out[...] = (x_float + keep[:, 0:1] * (branch[...] + branch_other[...])).astype(bf16)
        inv_rms = scale[:, 0:1]
        x_hat = x_float * inv_rms
        normed_grad = part[...] + part_other[...]
        hat_grad = normed_grad * gain[...]
        mean = jnp.sum(hat_grad * x_hat, axis=-1, keepdims=True) * (1.0 / x_float.shape[-1])
        input_out[...] = (cot[...].astype(f32) + inv_rms * (hat_grad - x_hat * mean)).astype(bf16)
        gain_sum[0:1, :] += jnp.sum(normed_grad * x_hat, axis=0, keepdims=True)

    rows = small.shape[0]
    lines = gain_sum.shape[1] // LANES

    def cross_copy():
        return pltpu.make_async_remote_copy(
            src_ref=pair_out, dst_ref=cross_in, send_sem=cross_send.at[0], recv_sem=cross_recv.at[0],
            device_id=plan.across, device_id_type=MESH,
        )

    def pair_copy():
        return pltpu.make_async_remote_copy(
            src_ref=pair_out, dst_ref=pair_in, send_sem=pair_send.at[0], recv_sem=pair_recv.at[0],
            device_id=plan.partner, device_id_type=MESH,
        )

    def ring_copy(offset):
        return pltpu.make_async_remote_copy(
            src_ref=ring_in.at[0], dst_ref=ring_in.at[plan.pairs - offset],
            send_sem=ring_send.at[offset - 1], recv_sem=ring_recv.at[offset - 1],
            device_id=plan.peer(offset), device_id_type=MESH,
        )

    @pl.when(step == blocks)
    def _():
        pair_out[pl.ds(0, rows), :] = small[...]
        for line in range(lines):
            pair_out[rows + line : rows + line + 1, :] = gain_sum[
                0:1, line * LANES : (line + 1) * LANES
            ]
        cross_copy().start()

    @pl.when(step == blocks + 2)
    def _():
        cross_copy().wait()
        pair_out[...] += cross_in[...]
        pair_copy().start()

    @pl.when(step == blocks + 4)
    def _():
        pair_copy().wait()
        ring_in[0] = pair_out[...] + pair_in[...]
        for offset in range(1, plan.pairs):
            ring_copy(offset).start()

    @pl.when(step == blocks + 6)
    def _():
        for offset in range(1, plan.pairs):
            ring_copy(offset).wait()
        total = jnp.zeros_like(pair_out)
        for index in range(plan.pairs):
            total = total + ring_in[lax.rem(index + plan.pairs - plan.pair, plan.pairs)]
        pair_in[...] = total
        copy = pltpu.make_async_copy(pair_in, small_out, final_sem.at[0])
        copy.start()
        copy.wait()


def finish(term, x, cot, scale, keep, branch, branch_other, part, part_other, gain, small, collective_id):
    pairs = lax.axis_size("fsdp") // 2
    shard_rows = term.shape[0] // (2 * pairs)
    plan = Reduction(shard_rows, pairs, [term.shape[1]], 2)
    rows, model = x.shape
    size = 64
    blocks = rows // size
    steps = max(plan.steps, blocks + 7)
    total_rows = small.shape[0] + model // LANES
    hbm = pl.BlockSpec(memory_space=pl.ANY)
    dma = pltpu.SemaphoreType.DMA

    def block(lanes):
        return pl.BlockSpec((size, lanes), lambda step: (jnp.minimum(step, blocks - 1), 0))

    def constant(shape):
        return pl.BlockSpec(shape, lambda step: (0, 0))

    return pl.pallas_call(
        functools.partial(finish_kernel, plan, blocks),
        grid=(steps,),
        in_specs=[hbm]
        + [block(lanes) for lanes in (model, model, LANES, LANES, model, model, model, model)]
        + [constant((1, model)), constant(small.shape)],
        out_specs=[hbm, block(model), block(model), hbm],
        out_shape=[
            jax.ShapeDtypeStruct((shard_rows, term.shape[1]), f32),
            jax.ShapeDtypeStruct((rows, model), bf16),
            jax.ShapeDtypeStruct((rows, model), bf16),
            jax.ShapeDtypeStruct((total_rows, LANES), f32),
        ],
        scratch_shapes=[
            pltpu.VMEM((8, model), f32),
            pltpu.VMEM((total_rows, LANES), f32),
            pltpu.VMEM((total_rows, LANES), f32),
            pltpu.VMEM((total_rows, LANES), f32),
            pltpu.VMEM((pairs, total_rows, LANES), f32),
            dma((1,)),
            dma((1,)),
            dma((1,)),
            dma((1,)),
            dma((max(pairs - 1, 1),)),
            dma((max(pairs - 1, 1),)),
            dma((1,)),
        ]
        + plan.scratch(),
        compiler_params=pltpu.CompilerParams(
            collective_id=collective_id, has_side_effects=True, vmem_limit_bytes=56 * 1024 * 1024
        ),
    )(
        term.reshape(pairs, 2, shard_rows, -1), x, cot, scale, keep, branch, branch_other, part,
        part_other, gain, small,
    )


def passed_along(value, axis, steps):
    count = lax.axis_size(axis)
    initial, last = (max(0, -steps), min(count, count - steps))
    return lax.ppermute(value, axis, [(source, source + steps) for source in range(initial, last)])


def paired(value, axis):
    count = lax.axis_size(axis)
    return lax.ppermute(value, axis, [(source, source ^ 1) for source in range(count)])


def ring_shift(value, axis, steps):
    count = lax.axis_size(axis)
    return lax.ppermute(
        value, axis, [(source, (source + 2 * steps) % count) for source in range(count)]
    )


def packed_rows(values):
    flat = jnp.concatenate([value.reshape(-1) for value in values])
    return jnp.pad(flat, (0, -flat.shape[0] % 1024)).reshape(-1, LANES)


def unpacked(flat, values):
    results, start = [], 0
    for value in values:
        results.append(flat[start : start + value.size].reshape(value.shape))
        start += value.size
    return results


def shards(
    tokens,
    lengths,
    block_order,
    cotangent,
    norm_gain,
    in_weight,
    coupling_weight,
    step_weight,
    out_weight,
    conv_weight,
    conv_bias,
    coupling_conv,
    coupling_bias,
    step_bias,
    decay_rate,
    skip_gain,
    inner_gain,
):
    micros = tokens.shape[0]
    count = tokens.shape[2]
    model = tokens.shape[3]
    inner = inner_gain.shape[0]
    heads = step_bias.shape[0]
    head_size = inner // heads
    twice = coupling_weight.shape[1]
    width = twice // 2
    blocks_row = block_order.shape[2]
    block_len = count * lax.axis_size("context") // blocks_row
    own_blocks = count // block_len
    inner_total = inner * lax.axis_size("tensor")
    side = lax.axis_index("tensor")
    place = lax.axis_index("context")
    base = place * count
    shard_rows = in_weight.shape[0]

    narrow, wide_columns = selectors(heads, head_size)
    sel = jnp.asarray(narrow, bf16)
    selcol = jnp.asarray(wide_columns, bf16)
    selt = jnp.asarray(narrow[:heads].T, bf16)
    selt = jnp.pad(selt, ((0, 0), (0, LANES - heads)))

    lead = jnp.concatenate(
        [
            in_weight[:, 1, :],
            coupling_weight,
            jnp.pad(step_weight, ((0, 0), (0, LANES - heads))),
        ],
        axis=1,
    )
    def sharing(parts):
        return max(shard_rows * parts // 16 // 16 * 16, 16)

    lead_full, far = gather_weights([lead], tokens[:, 0], sharing(3), 1)

    near = tokens[:, 0].reshape(micros, own_blocks, block_len, model)
    far = far.reshape(micros, own_blocks, block_len, model)
    slots = jnp.arange(blocks_row, dtype=jnp.int32)
    wanted = place * own_blocks + jnp.arange(own_blocks, dtype=jnp.int32)
    found = block_order[:, 0, None, :] == wanted[None, :, None]
    slot = jnp.sum(jnp.where(found, slots, 0), axis=2).reshape(-1)
    is_near = (slot // own_blocks == place).astype(jnp.int32)
    inside = slot % own_blocks
    x_input, normed, scales = ordered(
        near, far, inside * is_near, inside * (1 - is_near), is_near, norm_gain.reshape(1, model)
    )

    first_end = lengths[:, 0, 0]
    second_end = first_end + lengths[:, 0, 1]
    marks = [
        jnp.stack([first_end[micro], second_end[micro], base]).astype(jnp.int32)
        for micro in range(micros)
    ]
    positions = base + jnp.arange(count, dtype=jnp.int32)
    keep = jnp.concatenate([(positions < second_end[micro]) for micro in range(micros)])
    keep = keep.astype(f32)[:, None]

    cw, cb = conv_weight, conv_bias.reshape(1, inner)
    ccw, ccb = coupling_conv, coupling_bias.reshape(1, twice)
    sbias = jnp.pad(step_bias, (0, LANES - heads)).reshape(1, LANES)
    rate = jnp.pad(decay_rate, (0, LANES - heads)).reshape(1, LANES)
    skip = jnp.dot(
        skip_gain.reshape(1, heads), jnp.asarray(narrow[:heads], f32), precision=lax.Precision.HIGHEST
    )

    raw = jnp.dot(normed, lead_full, preferred_element_type=f32)
    rims = passed_along(
        jnp.stack([raw[(micro + 1) * count - 8 : (micro + 1) * count] for micro in range(micros)]),
        "context",
        1,
    )
    (y_own, states, finals, coupled, carry, reach, entering, gate_full, out_full) = forward_ssd(
        jnp.stack(marks), micros, raw, rims, inner, twice, count,
        cw, cb, ccw, ccb, sbias, rate, skip, sel, selcol,
        [in_weight[:, 0, :], jnp.transpose(out_weight)], sharing(4), 3,
    )
    entering = jnp.where(place == 0, 0.0, entering)
    cot = cotangent[:, 0].reshape(micros * count, model)
    out_grad = cot * keep.astype(bf16)
    gain_row = inner_gain.reshape(1, inner)
    mixer, gate_in, norm_grad, row_sums = gate_stage(
        normed, out_grad, gate_full, out_full, y_own, carry, coupled, entering, gain_row
    )
    row_sums = row_sums + paired(row_sums, "tensor")
    gated_norm, gate_grad, mixer_grad, own_pulls, inner_gain_rows = gate_back_stage(
        mixer, gate_in, norm_grad, carry, coupled, row_sums, gain_row, micros, inner_total
    )
    pulled = passed_along(own_pulls, "context", -1)
    out_term = contract_rows(out_grad, gated_norm)
    gate_term = contract_rows(normed, gate_grad)
    branch = contract_cols(gated_norm, out_full)
    gate_part = contract_cols(gate_grad, gate_full)
    branch_other = paired(branch, "tensor")

    (
        lead_grad, tails, rims_grad, coupling_raw_grad, coupling_rims_grad,
        value_sums, coupling_sums, small_sums, skip_sums, out_shard, gate_shard,
    ) = backward_ssd(
        jnp.stack(marks), micros, raw, rims, inner, twice, count, mixer_grad, mixer, states,
        finals, entering, reach, pulled,
        cw, cb, ccw, ccb, sbias, rate, skip, sel, selcol, selt, [out_term, gate_term], [branch, gate_part], 2,
    )
    edges = passed_along(jnp.concatenate([rims_grad, coupling_rims_grad], axis=2), "context", -1)
    coupling_raw_grad = coupling_raw_grad.reshape(micros, count, twice) + jnp.pad(
        edges[:, :, inner:], ((0, 0), (count - 8, 0), (0, 0))
    )
    coupling_raw_grad = coupling_raw_grad + paired(coupling_raw_grad, "tensor")
    lane_ids = jnp.arange(twice, dtype=jnp.int32)
    own_lanes = ((lane_ids // width) == side).astype(bf16)
    coupling_low = (coupling_raw_grad.astype(bf16) * own_lanes).reshape(micros * count, twice)
    lead_grad = lax.dynamic_update_slice(lead_grad, coupling_low, (0, inner))
    tails = (tails + edges[:, :, :inner]).astype(bf16)
    for micro in range(micros):
        lead_grad = lax.dynamic_update_slice(
            lead_grad, tails[micro], ((micro + 1) * count - 8, 0)
        )
    normed_part = gate_part + contract_cols(lead_grad, lead_full)
    skip_sums = skip_sums[0].reshape(heads, head_size).sum(axis=1)
    coupling_sums = coupling_sums + paired(coupling_sums, "tensor")
    small = [value_sums[:5], coupling_sums[:5], small_sums[:2], skip_sums, inner_gain_rows[0]]
    small_rows = packed_rows(small)
    lead_shard, block_out, input_grad, summed = finish(
        contract_rows(normed, lead_grad), x_input, cot, scales,
        jnp.broadcast_to(keep, (micros * count, LANES)), branch, branch_other,
        normed_part, paired(normed_part, "tensor"), norm_gain.reshape(1, model), small_rows, 4,
    )
    flat = summed.reshape(-1)
    value_all, coupling_all, small_all, skip_all, inner_all = unpacked(flat, small)
    norm_all = flat[small_rows.size :]
    coupling_shard = lead_shard[:, inner : inner + twice]
    coupling_shard = coupling_shard + paired(coupling_shard, "tensor")
    return (
        block_out.reshape(micros, 1, count, model),
        input_grad.reshape(micros, 1, count, model),
        norm_all,
        woven(gate_shard, lead_shard, inner),
        coupling_shard,
        lead_shard[:, inner + twice : inner + twice + heads],
        jnp.transpose(out_shard),
        value_all[:4],
        value_all[4],
        coupling_all[:4],
        coupling_all[4],
        small_all[0, :heads],
        small_all[1, :heads],
        skip_all,
        inner_all,
    )


def contract_rows(left, right):
    return lax.dot_general(
        left, right, (((0,), (0,)), ((), ())), preferred_element_type=jnp.float32
    )


def contract_cols(left, right):
    return lax.dot_general(
        left, right, (((1,), (1,)), ((), ())), preferred_element_type=jnp.float32
    )


def solution(mesh):
    return jax.shard_map(
        shards,
        mesh=mesh,
        in_specs=(
            P(None, "fsdp", "context", None),
            P(None, "fsdp", None),
            P(None, "fsdp", None),
            P(None, "fsdp", "context", None),
            P(),
            P("fsdp", None, "tensor"),
            P("fsdp", None),
            P("fsdp", "tensor"),
            P("tensor", "fsdp"),
            P(None, "tensor"),
            P("tensor"),
            P(),
            P(),
            P("tensor"),
            P("tensor"),
            P("tensor"),
            P("tensor"),
        ),
        out_specs=(
            P(None, "fsdp", "context", None),
            P(None, "fsdp", "context", None),
            P(),
            P("fsdp", None, "tensor"),
            P("fsdp", None),
            P("fsdp", "tensor"),
            P("tensor", "fsdp"),
            P(None, "tensor"),
            P("tensor"),
            P(),
            P(),
            P("tensor"),
            P("tensor"),
            P("tensor"),
            P("tensor"),
        ),
        check_vma=False,
    )
```

```python
import functools

import jax
import jax.numpy as jnp
import numpy as np
from jax import lax
from jax.experimental import pallas as pl
from jax.experimental.pallas import tpu as pltpu
from jax.sharding import PartitionSpec as P

CHUNK = 128
LANES = 128
MESH = pl.DeviceIdType.MESH
f32 = jnp.float32
bf16 = jnp.bfloat16
epsilon = 1e-05


def split_two(value):
    high = value.astype(bf16)
    return high, (value - high.astype(f32)).astype(bf16)


def split_three(value):
    high = value.astype(bf16)
    rest = value - high.astype(f32)
    middle = rest.astype(bf16)
    return high, middle, (rest - middle.astype(f32)).astype(bf16)


def mm(left, right):
    return jnp.dot(left, right, preferred_element_type=f32)


def mm_nt(left, right):
    return lax.dot_general(left, right, (((1,), (1,)), ((), ())), preferred_element_type=f32)


def mm_three(left, right):
    wide = mm(left[0], jnp.concatenate([right[0], right[1]], axis=1))
    count = right[0].shape[1]
    return wide[:, :count] + wide[:, count:] + mm(left[1], right[0])


def mm_three_nt(left, right):
    return mm_nt(left[0], right[0]) + mm_nt(left[0], right[1]) + mm_nt(left[1], right[0])


def packed_parts(value, heads):
    high, middle, lowest = split_three(value)
    joined = (
        high.astype(f32)
        + pltpu.roll(middle.astype(f32), heads, 1)
        + pltpu.roll(lowest.astype(f32), 2 * heads, 1)
    )
    return joined.astype(bf16)


def segment_at(position, first_end, second_end):
    first_part = (position >= first_end).astype(jnp.int32)
    second_part = (position >= second_end).astype(jnp.int32)
    return jnp.where(position < 0, -1, first_part + second_part)


def chunk_frame(marks, chunk, step_raw, step_bias, rate, heads):
    first_end, second_end, base = marks[0], marks[1], marks[2]
    start = base + chunk * CHUNK
    rows = start + lax.broadcasted_iota(jnp.int32, (CHUNK, LANES), 0)
    columns = start + lax.broadcasted_iota(jnp.int32, (CHUNK, CHUNK), 1)
    seg_rows = segment_at(rows, first_end, second_end)
    seg_columns = segment_at(columns, first_end, second_end)
    seg_prior = segment_at(start - 1, first_end, second_end)
    seg_last = segment_at(start + CHUNK - 1, first_end, second_end)
    same = [
        (segment_at(rows - lag, first_end, second_end) == seg_rows).astype(f32) for lag in range(4)
    ]
    shifted = step_raw + step_bias
    step = jnp.maximum(shifted, 0.0) + jnp.log1p(jnp.exp(-jnp.abs(shifted)))
    lanes = lax.broadcasted_iota(jnp.int32, (CHUNK, LANES), 1)
    step = jnp.where(lanes < heads, step, 0.0)
    log_decay = -step * rate
    row_ids = lax.broadcasted_iota(jnp.int32, (CHUNK, CHUNK), 0)
    column_ids = lax.broadcasted_iota(jnp.int32, (CHUNK, CHUNK), 1)
    lower = (row_ids >= column_ids).astype(bf16)
    parts = split_three(log_decay)
    cumulative = mm(lower, parts[0]) + mm(lower, parts[1]) + mm(lower, parts[2])
    last = cumulative[CHUNK - 1 :, :]
    carry = jnp.exp(cumulative) * (seg_rows == seg_prior).astype(f32)
    tail = jnp.exp(last - cumulative) * (seg_rows == seg_last).astype(f32)
    live = lanes < heads
    carry = jnp.where(live, carry, 0.0)
    tail = jnp.where(live, tail, 0.0)
    return dict(
        seg_rows=seg_rows,
        seg_columns=seg_columns,
        row_ids=row_ids,
        column_ids=column_ids,
        same=same,
        step=step,
        shifted=shifted,
        cumulative=cumulative,
        carry=carry,
        tail=tail,
    )


def conv_sum(current, halo, weights, biases, same):
    full = jnp.concatenate([halo, current], axis=0)
    total = biases + weights(0) * current
    for lag in range(1, 4):
        total = total + weights(lag) * (pltpu.roll(full, lag, 0)[8:] * same[lag])
    return total


def logistic(value):
    return 1.0 / (1.0 + jnp.exp(-value))


def forward_kernel(heads, chunks, plan, *refs):
    (
        marks, vraw, vprev, vrim, craw, cprev, crim, sraw, cw, cb, ccw, ccb, sbias, rate, skip,
        sel, selcol,
    ) = refs[:17]
    arrays = plan.arrays
    weights, refs = refs[17 : 17 + arrays], refs[17 + arrays :]
    y_out, st_out, fin_out, bc_out, carry_out, cd_out, entering = refs[:7]
    fulls, refs = refs[7 : 7 + arrays], refs[7 + arrays :]
    (
        state, cumt, stack, cumpack, halo, same_s, bias_s, gram_s, cd_s, cparts, btparts,
        leaving, leave_send, leave_recv,
    ) = refs[:14]
    plan.bind(weights, fulls, refs[14:])
    grid_step = pl.program_id(0)
    steps = pl.num_programs(0)
    chunk = lax.rem(grid_step, chunks)
    micro = grid_step // chunks
    width = state.shape[0]
    early = {0: range(2)}
    for when in range(1, min(2 * chunks - 1, len(plan.order) - 1)):
        early[when] = [when + 1]
    placed = len(early)

    def leave_copy(which):
        return pltpu.make_async_remote_copy(
            src_ref=leaving.at[which], dst_ref=entering.at[which],
            send_sem=leave_send.at[which], recv_sem=leave_recv.at[which],
            device_id=plan.across, device_id_type=MESH,
        )

    for when, numbers in early.items():

        @pl.when(grid_step == when)
        def _(when=when, numbers=numbers):
            if when == 0:
                plan.greet()
            for number in numbers:
                plan.event(number)

    @pl.when(chunk == 0)
    def _():
        state[...] = jnp.zeros_like(state)
        cd_s[...] = jnp.ones_like(cd_s)
        cd_out[...] = jnp.zeros_like(cd_out)
        halo[...] = vrim[...]

    @pl.when(chunk > 0)
    def _():
        halo[...] = vprev[...]

    frame = chunk_frame([marks[micro, place] for place in range(3)], chunk, sraw[...], sbias[...], rate[...], heads)
    same = frame["same"]
    for lag in range(1, 4):
        same_s[lag - 1] = same[lag]
    joined = (frame["seg_rows"] == frame["seg_columns"]) & (frame["row_ids"] >= frame["column_ids"])
    bias_s[...] = jnp.where(joined, 0.0, -1e30)
    stack[0:CHUNK, :] = packed_parts(frame["step"], heads)
    stack[CHUNK : 2 * CHUNK, :] = packed_parts(frame["carry"], heads)
    stack[2 * CHUNK : 3 * CHUNK, :] = packed_parts(frame["tail"], heads)
    cumpack[...] = packed_parts(frame["cumulative"], heads)
    cumt[...] = jnp.transpose(frame["cumulative"])
    coupling_halo = jnp.where(chunk == 0, crim[...], cprev[...])
    wide_same = [None] + [jnp.concatenate([same[lag], same[lag]], axis=1) for lag in range(1, 4)]
    pre = conv_sum(
        craw[...], coupling_halo, lambda lag: ccw[lag : lag + 1, :], ccb[...], wide_same
    )
    coupled = pre * logistic(pre)
    bc_out[...] = coupled
    b_part = split_two(coupled[:, :width])
    c_part = split_two(coupled[:, width:])
    gram_s[...] = mm_three_nt(c_part, b_part)
    cparts[0] = c_part[0]
    cparts[1] = c_part[1]
    turned = jnp.transpose(coupled[:, :width])
    bt_part = split_two(turned)
    btparts[0] = bt_part[0]
    btparts[1] = bt_part[1]
    lane = lax.broadcasted_iota(jnp.int32, (CHUNK, LANES), 1)
    low_half = (lane < LANES // 2).astype(f32)
    high_half = 1.0 - low_half

    def pair(index, carried):
        cols = pl.ds(pl.multiple_of(index * LANES, LANES), LANES)
        wide = pl.ds(pl.multiple_of(index * 2 * LANES, 2 * LANES), 2 * LANES)
        pre_value = conv_sum(
            vraw[:, cols],
            halo[:, cols],
            lambda lag: cw[lag : lag + 1, cols],
            cb[:, cols],
            [None] + [same_s[lag - 1] for lag in range(1, 4)],
        )
        value = pre_value * logistic(pre_value)
        spread = mm(stack[...], sel[:, cols])
        step_e = spread[:CHUNK]
        carry_e = spread[CHUNK : 2 * CHUNK]
        tail_e = spread[2 * CHUNK :]
        inputs = step_e * value
        column = mm(cumpack[...], selcol[:, wide])
        row_pair = jnp.concatenate(
            [cumt[pl.ds(2 * index, 1), :], cumt[pl.ds(2 * index + 1, 1), :]], axis=1
        )
        bias = bias_s[...]
        gram = gram_s[...]
        mixing = jnp.concatenate([gram, gram], axis=1) * jnp.exp(
            column - row_pair + jnp.concatenate([bias, bias], axis=1)
        )
        mix_high, mix_low = split_two(mixing)
        in_low = split_two(inputs * low_half)
        in_high = split_two(inputs * high_half)
        diag_high = jnp.concatenate([in_low[0], in_high[0]], axis=0)
        diag_low = jnp.concatenate([in_low[1], in_high[1]], axis=0)
        both = mm(mix_high, jnp.concatenate([diag_high, diag_low], axis=1))
        inside = both[:, :LANES] + both[:, LANES:] + mm(mix_low, diag_high)
        held = state[:, cols]
        from_state = mm_three((cparts[0], cparts[1]), split_two(held))
        y_out[:, cols] = inside + carry_e * from_state + skip[:, cols] * value
        fresh = mm_three((btparts[0], btparts[1]), split_two(tail_e * inputs))
        through = carry_e[CHUNK - 1 :, :]
        st_out[0, :, cols] = held
        renewed = through * held + fresh
        state[:, cols] = renewed
        fin_out[:, cols] = renewed
        reach = cd_s[0:1, cols]
        carry_out[:, cols] = carry_e * reach
        cd_s[0:1, cols] = reach * through
        return carried

    eight_rows = lax.broadcasted_iota(jnp.int32, cd_out.shape, 0)
    cd_out[...] = jnp.where(eight_rows == chunk, cd_s[0:1, :], cd_out[...])
    lax.fori_loop(0, heads // 2, pair, 0, unroll=4)
    cd_out[...] = jnp.where(eight_rows == chunk + 1, cd_s[0:1, :], cd_out[...])

    @pl.when(chunk == chunks - 1)
    def _():
        leaving[micro] = state[...]
        leave_copy(micro).start()

    @pl.when(grid_step == steps - 1)
    def _():
        for number in range(placed + 1, len(plan.order)):
            plan.event(number)
        plan.finish()
        for which in range(leaving.shape[0]):
            leave_copy(which).wait()


def selectors(heads, head_size):
    inner = heads * head_size
    head_of_lane = np.arange(inner) // head_size
    narrow = np.zeros((LANES, inner), np.float32)
    wide = np.zeros((LANES, heads * LANES), np.float32)
    head_of_wide = np.arange(heads * LANES) // LANES
    for part in range(3):
        narrow[part * heads + head_of_lane, np.arange(inner)] = 1.0
        wide[part * heads + head_of_wide, np.arange(heads * LANES)] = 1.0
    return narrow, wide


def whole(shape):
    return pl.BlockSpec(shape, lambda index, *_: (0,) * len(shape))


def forward_ssd(
    marks, micros, raw, rims, inner, twice, tokens,
    cw, cb, ccw, ccb, sbias, rate, skip, sel, selcol, shards, shared, collective_id,
):
    width = twice // 2
    chunks = tokens // CHUNK
    heads = inner // (LANES // 2)
    eighth = CHUNK // 8
    pairs = lax.axis_size("fsdp") // 2
    shard_rows = shards[0].shape[0]
    plan = Gathering(shard_rows, pairs, [shard.shape[1] for shard in shards], 2, shared)

    def part(count, start):
        return pl.BlockSpec((CHUNK, count), lambda step: (step, start // count))

    def before(count, start):
        return pl.BlockSpec(
            (8, count), lambda step: (jnp.maximum(step * eighth - 1, 0), start // count)
        )

    def edge(count, start):
        return pl.BlockSpec((None, 8, count), lambda step: (step // chunks, 0, start // count))

    def each(*shape):
        return pl.BlockSpec((None, *shape), lambda step: (step // chunks, 0, 0))

    hbm = pl.BlockSpec(memory_space=pl.ANY)
    dma = pltpu.SemaphoreType.DMA
    return pl.pallas_call(
        functools.partial(forward_kernel, heads, chunks, plan),
        grid=(micros * chunks,),
        in_specs=[
            pl.BlockSpec(memory_space=pltpu.SMEM),
            part(inner, 0),
            before(inner, 0),
            edge(inner, 0),
            part(twice, inner),
            before(twice, inner),
            edge(twice, inner),
            part(LANES, inner + twice),
            whole(cw.shape),
            whole(cb.shape),
            whole(ccw.shape),
            whole(ccb.shape),
            whole(sbias.shape),
            whole(rate.shape),
            whole(skip.shape),
            whole(sel.shape),
            whole(selcol.shape),
        ]
        + [hbm] * len(shards),
        out_specs=[
            part(inner, 0),
            pl.BlockSpec((1, width, inner), lambda step: (step, 0, 0)),
            each(width, inner),
            part(twice, 0),
            part(inner, 0),
            each(8, inner),
            hbm,
        ]
        + [hbm] * len(shards),
        scratch_shapes=[
            pltpu.VMEM((width, inner), f32),
            pltpu.VMEM((LANES, CHUNK), f32),
            pltpu.VMEM((3 * CHUNK, LANES), bf16),
            pltpu.VMEM((CHUNK, LANES), bf16),
            pltpu.VMEM((8, inner), f32),
            pltpu.VMEM((3, CHUNK, LANES), f32),
            pltpu.VMEM((CHUNK, CHUNK), f32),
            pltpu.VMEM((CHUNK, CHUNK), f32),
            pltpu.VMEM((8, inner), f32),
            pltpu.VMEM((2, CHUNK, width), bf16),
            pltpu.VMEM((2, width, CHUNK), bf16),
            pltpu.VMEM((micros, width, inner), f32),
            dma((micros,)),
            dma((micros,)),
        ]
        + plan.scratch(),
        out_shape=[
            jax.ShapeDtypeStruct((micros * tokens, inner), f32),
            jax.ShapeDtypeStruct((micros * chunks, width, inner), f32),
            jax.ShapeDtypeStruct((micros, width, inner), f32),
            jax.ShapeDtypeStruct((micros * tokens, twice), f32),
            jax.ShapeDtypeStruct((micros * tokens, inner), f32),
            jax.ShapeDtypeStruct((micros, 8, inner), f32),
            jax.ShapeDtypeStruct((micros, width, inner), f32),
        ]
        + [
            jax.ShapeDtypeStruct((2 * pairs * shard_rows, shard.shape[1]), shard.dtype)
            for shard in shards
        ],
        compiler_params=pltpu.CompilerParams(
            collective_id=collective_id, has_side_effects=True, vmem_limit_bytes=48 * 1024 * 1024
        ),
    )(
        marks, raw, raw, rims, raw, raw, rims, raw, cw, cb, ccw, ccb, sbias, rate, skip, sel, selcol,
        *shards,
    )


def backward_kernel(heads, chunks, plan, waited, *refs):
    (
        marks, vraw, vprev, vrim, craw, cprev, crim, sraw, grad, mixer, st_now, st_next, fin,
        entering, cd, pulled, cw, cb, ccw, ccb, sbias, rate, skip, sel, selcol, selt,
    ) = refs[:26]
    arrays = len(plan.counts)
    refs = refs[26:]
    terms, refs = refs[:arrays], refs[arrays + waited :]
    (
        lead_g, vtail_g, vrim_g, craw_g, crim_g, cw_g, ccw_g, small_g, skip_g,
    ) = refs[:9]
    outs, refs = refs[9 : 9 + arrays], refs[9 + arrays :]
    (
        state, cumt, stack, cumpack, halo, same_s, bias_s, gram_s, cparts, bparts, ctparts,
        rim_s, crim_s, dgram, dcoup, dhead, cd_s,
    ) = refs[:17]
    plan.bind(terms, outs, refs[17:])
    grid_step = pl.program_id(0)
    step_id = lax.rem(grid_step, chunks)
    micro = grid_step // chunks
    chunk = chunks - 1 - step_id
    width = state.shape[0]
    inner = state.shape[1]
    per_step = -(-plan.steps // pl.num_programs(0))

    @pl.when(grid_step == 0)
    def _():
        plan.greet()
        cw_g[...] = jnp.zeros_like(cw_g)
        ccw_g[...] = jnp.zeros_like(ccw_g)
        small_g[...] = jnp.zeros_like(small_g)
        skip_g[...] = jnp.zeros_like(skip_g)

    def reduce_steps(first, count):
        def one(number, carried):
            plan.step(number)
            return carried

        start = grid_step * per_step + first
        lax.fori_loop(start, jnp.minimum(start + count, plan.steps), one, 0)

    @pl.when(step_id == 0)
    def _():
        state[...] = pulled[...]
        rim_s[...] = jnp.zeros_like(rim_s)
        crim_s[...] = jnp.zeros_like(crim_s)

    @pl.when(chunk == 0)
    def _():
        halo[...] = vrim[...]

    @pl.when(chunk > 0)
    def _():
        halo[...] = vprev[...]

    frame = chunk_frame([marks[micro, place] for place in range(3)], chunk, sraw[...], sbias[...], rate[...], heads)
    same = frame["same"]
    for lag in range(1, 4):
        same_s[lag - 1] = same[lag]
    joined = (frame["seg_rows"] == frame["seg_columns"]) & (frame["row_ids"] <= frame["column_ids"])
    bias_s[...] = jnp.where(joined, 0.0, -1e30)
    stack[0:CHUNK, :] = packed_parts(frame["step"], heads)
    stack[CHUNK : 2 * CHUNK, :] = packed_parts(frame["carry"], heads)
    stack[2 * CHUNK : 3 * CHUNK, :] = packed_parts(frame["tail"], heads)
    cumpack[...] = packed_parts(frame["cumulative"], heads)
    cumt[...] = jnp.transpose(frame["cumulative"])
    coupling_halo = jnp.where(chunk == 0, crim[...], cprev[...])
    wide_same = [None] + [jnp.concatenate([same[lag], same[lag]], axis=1) for lag in range(1, 4)]
    craw_now = craw[...]
    pre = conv_sum(craw_now, coupling_halo, lambda lag: ccw[lag : lag + 1, :], ccb[...], wide_same)
    csig = logistic(pre)
    coupled = pre * csig
    b_value = coupled[:, :width]
    c_value = coupled[:, width:]
    b_part = split_two(b_value)
    c_part = split_two(c_value)
    gram_s[...] = mm_three_nt(b_part, c_part)
    cparts[0] = c_part[0]
    cparts[1] = c_part[1]
    bparts[0] = b_part[0]
    bparts[1] = b_part[1]
    ct_part = split_two(jnp.transpose(c_value))
    ctparts[0] = ct_part[0]
    ctparts[1] = ct_part[1]
    dgram[...] = jnp.zeros_like(dgram)
    dcoup[...] = jnp.zeros_like(dcoup)
    dhead[...] = jnp.zeros_like(dhead)
    lane = lax.broadcasted_iota(jnp.int32, (CHUNK, LANES), 1)
    row = lax.broadcasted_iota(jnp.int32, (CHUNK, LANES), 0)
    low_half = (lane < LANES // 2).astype(f32)
    high_half = 1.0 - low_half
    last_row = (row == CHUNK - 1).astype(f32)
    is_end = step_id == 0
    eight_rows = lax.broadcasted_iota(jnp.int32, cd.shape, 0)
    for place in range(2):
        chosen = jnp.where(eight_rows == chunk + place, cd[...], 0.0)
        cd_s[place : place + 1, :] = jnp.sum(chosen, axis=0, keepdims=True)

    def pair(index):
        cols = pl.ds(pl.multiple_of(index * LANES, LANES), LANES)
        wide = pl.ds(pl.multiple_of(index * 2 * LANES, 2 * LANES), 2 * LANES)
        raw = vraw[:, cols]
        full = jnp.concatenate([halo[:, cols], raw], axis=0)
        lagged = [raw] + [pltpu.roll(full, lag, 0)[8:] * same_s[lag - 1] for lag in range(1, 4)]
        pre_value = cb[:, cols]
        for lag in range(4):
            pre_value = pre_value + cw[lag : lag + 1, cols] * lagged[lag]
        sig = logistic(pre_value)
        value = pre_value * sig
        spread = mm(stack[...], sel[:, cols])
        step_e = spread[:CHUNK]
        carry_e = spread[CHUNK : 2 * CHUNK]
        tail_e = spread[2 * CHUNK :]
        inputs = step_e * value
        grads = grad[:, cols]
        column = mm(cumpack[...], selcol[:, wide])
        row_pair = jnp.concatenate(
            [cumt[pl.ds(2 * index, 1), :], cumt[pl.ds(2 * index + 1, 1), :]], axis=1
        )
        bias = bias_s[...]
        gram = gram_s[...]
        decays = jnp.exp(row_pair - column + jnp.concatenate([bias, bias], axis=1))
        mixing = jnp.concatenate([gram, gram], axis=1) * decays
        mix_high, mix_low = split_two(mixing)
        g_low = split_two(grads * low_half)
        g_high = split_two(grads * high_half)
        diag_high = jnp.concatenate([g_low[0], g_high[0]], axis=0)
        diag_low = jnp.concatenate([g_low[1], g_high[1]], axis=0)
        both = mm(mix_high, jnp.concatenate([diag_high, diag_low], axis=1))
        input_g = both[:, :LANES] + both[:, LANES:] + mm(mix_low, diag_high)
        held_g = state[:, cols]
        held_parts = split_two(held_g)
        input_g = input_g + tail_e * mm_three((bparts[0], bparts[1]), held_parts)
        in_parts = split_two(inputs)
        outer = mm_three_nt(in_parts, (diag_high, diag_low)) * decays
        dgram[...] += outer[:, :CHUNK] + outer[:, CHUNK:]
        reach_now = cd_s[0:1, cols]
        reach_next = cd_s[1:2, cols]
        arriving = entering[:, cols]
        held = st_now[0, :, cols] + reach_now * arriving
        next_own = jnp.where(is_end, fin[:, cols], st_next[0, :, cols])
        following = next_own + reach_next * arriving
        carried_g = split_two(carry_e * grads)
        state[:, cols] = carry_e[CHUNK - 1 :, :] * held_g + mm_three(
            (ctparts[0], ctparts[1]), carried_g
        )
        dcoup[1] += mm_three_nt(carried_g, split_two(held))
        dcoup[0] += mm_three_nt(split_two(tail_e * inputs), held_parts)
        value_g = input_g * step_e + skip[:, cols] * grads
        kept = jnp.sum(held_g * following, axis=0, keepdims=True)
        balance = grads * (mixer[:, cols] - skip[:, cols] * value) - inputs * input_g
        balance = balance + last_row * kept
        sums = jnp.concatenate([balance, input_g * value], axis=0)
        sums_parts = split_three(sums)
        pick = selt[cols, :]
        dhead[...] += mm(sums_parts[0], pick) + mm(sums_parts[1], pick) + mm(sums_parts[2], pick)
        skip_g[0:1, cols] += jnp.sum(grads * value, axis=0, keepdims=True)
        pre_g = value_g * (sig * (1.0 + pre_value * (1.0 - sig)))
        cw_g[4:5, cols] += jnp.sum(pre_g, axis=0, keepdims=True)
        raw_g = cw[0:1, cols] * pre_g
        cw_g[0:1, cols] += jnp.sum(pre_g * raw, axis=0, keepdims=True)
        none = jnp.zeros((8, LANES), f32)
        edge = none
        for lag in range(1, 4):
            cw_g[lag : lag + 1, cols] += jnp.sum(pre_g * lagged[lag], axis=0, keepdims=True)
            weighted = cw[lag : lag + 1, cols] * (pre_g * same_s[lag - 1])
            padded = jnp.concatenate([none, weighted, none], axis=0)
            turned = pltpu.roll(padded, CHUNK + 16 - lag, 0)
            raw_g = raw_g + turned[8 : 8 + CHUNK]
            edge = edge + turned[:8]
        last_rows = raw_g[CHUNK - 8 :] + rim_s[:, cols]
        lead_g[:, cols] = jnp.concatenate([raw_g[: CHUNK - 8], last_rows], axis=0).astype(bf16)

        @pl.when(step_id == 0)
        def _():
            vtail_g[:, cols] = last_rows

        rim_s[:, cols] = edge
        vrim_g[:, cols] = edge

    groups = 4
    per_group = heads // 2 // groups

    def group(number, carried):
        for inside in range(per_group):
            pair(number * per_group + inside)
        share = per_step // (groups + 1)
        reduce_steps(number * share, share)
        return carried

    lax.fori_loop(0, groups, group, 0)
    used = groups * (per_step // (groups + 1))
    reduce_steps(used, per_step - used)

    total = dgram[...]
    total_parts = split_two(total)
    turned_parts = split_two(jnp.transpose(total))
    b_grad = dcoup[0] + mm_three(total_parts, (cparts[0], cparts[1]))
    c_grad = dcoup[1] + mm_three(turned_parts, (bparts[0], bparts[1]))
    coupled_g = jnp.concatenate([b_grad, c_grad], axis=1)
    pre_g = coupled_g * (csig * (1.0 + pre * (1.0 - csig)))
    ccw_g[4:5, :] += jnp.sum(pre_g, axis=0, keepdims=True)
    ccw_g[0:1, :] += jnp.sum(pre_g * craw_now, axis=0, keepdims=True)
    raw_g = ccw[0:1, :] * pre_g
    full = jnp.concatenate([coupling_halo, craw_now], axis=0)
    none = jnp.zeros((8, 2 * width), f32)
    edge = none
    for lag in range(1, 4):
        masked = pre_g * wide_same[lag]
        ccw_g[lag : lag + 1, :] += jnp.sum(
            masked * pltpu.roll(full, lag, 0)[8:], axis=0, keepdims=True
        )
        padded = jnp.concatenate([none, ccw[lag : lag + 1, :] * masked, none], axis=0)
        turned = pltpu.roll(padded, CHUNK + 16 - lag, 0)
        raw_g = raw_g + turned[8 : 8 + CHUNK]
        edge = edge + turned[:8]
    craw_g[...] = raw_g
    craw_g[CHUNK - 8 :, :] += crim_s[...]
    crim_s[...] = edge
    crim_g[...] = edge

    upper = (frame["row_ids"] <= frame["column_ids"]).astype(bf16)
    parts = split_three(dhead[:CHUNK])
    decay_g = mm(upper, parts[0]) + mm(upper, parts[1]) + mm(upper, parts[2])
    step_g = (dhead[CHUNK:] - rate[...] * decay_g) * logistic(frame["shifted"])
    lead_g[:, inner : inner + 2 * width] = jnp.zeros((CHUNK, 2 * width), bf16)
    lead_g[:, inner + 2 * width :] = step_g.astype(bf16)
    small_g[0:1, :] += jnp.sum(step_g, axis=0, keepdims=True)
    small_g[1:2, :] += jnp.sum(-frame["step"] * decay_g, axis=0, keepdims=True)


def backward_ssd(
    marks, micros, raw, rims, inner, twice, tokens, grad, mixer, states, fin, entering, cd, pulled,
    cw, cb, ccw, ccb, sbias, rate, skip, sel, selcol, selt, terms, first, collective_id,
):
    width = twice // 2
    chunks = tokens // CHUNK
    heads = inner // (LANES // 2)
    eighth = CHUNK // 8
    pairs = lax.axis_size("fsdp") // 2
    shard_rows = terms[0].shape[0] // (2 * pairs)
    plan = Reduction(shard_rows, pairs, [term.shape[1] for term in terms], 2)
    lead = inner + twice + LANES

    def row(step):
        return step // chunks * chunks + chunks - 1 - lax.rem(step, chunks)

    def part(count, start):
        return pl.BlockSpec((CHUNK, count), lambda step: (row(step), start // count))

    def before(count, start):
        return pl.BlockSpec(
            (8, count), lambda step: (jnp.maximum(row(step) * eighth - 1, 0), start // count)
        )

    def edge(count, start):
        return pl.BlockSpec(
            (None, 8, count), lambda step: (step // chunks, 0, start // count)
        )

    def held(offset):
        return pl.BlockSpec(
            (1, width, inner),
            lambda step: (
                jnp.minimum(row(step) + offset, (step // chunks + 1) * chunks - 1), 0, 0,
            ),
        )

    def each(*shape):
        return pl.BlockSpec((None, *shape), lambda step: (step // chunks, 0, 0))

    hbm = pl.BlockSpec(memory_space=pl.ANY)
    return pl.pallas_call(
        functools.partial(backward_kernel, heads, chunks, plan, len(first)),
        grid=(micros * chunks,),
        in_specs=[
            pl.BlockSpec(memory_space=pltpu.SMEM),
            part(inner, 0),
            before(inner, 0),
            edge(inner, 0),
            part(twice, inner),
            before(twice, inner),
            edge(twice, inner),
            part(LANES, inner + twice),
            part(inner, 0),
            part(inner, 0),
            held(0),
            held(1),
            each(width, inner),
            each(width, inner),
            each(8, inner),
            each(width, inner),
            whole(cw.shape),
            whole(cb.shape),
            whole(ccw.shape),
            whole(ccb.shape),
            whole(sbias.shape),
            whole(rate.shape),
            whole(skip.shape),
            whole(sel.shape),
            whole(selcol.shape),
            whole(selt.shape),
        ]
        + [hbm] * (len(terms) + len(first)),
        out_specs=[
            part(lead, 0),
            each(8, inner),
            each(8, inner),
            part(twice, 0),
            each(8, twice),
            whole((8, inner)),
            whole((8, twice)),
            whole((8, LANES)),
            whole((8, inner)),
        ]
        + [hbm] * len(terms),
        scratch_shapes=[
            pltpu.VMEM((width, inner), f32),
            pltpu.VMEM((LANES, CHUNK), f32),
            pltpu.VMEM((3 * CHUNK, LANES), bf16),
            pltpu.VMEM((CHUNK, LANES), bf16),
            pltpu.VMEM((8, inner), f32),
            pltpu.VMEM((3, CHUNK, LANES), f32),
            pltpu.VMEM((CHUNK, CHUNK), f32),
            pltpu.VMEM((CHUNK, CHUNK), f32),
            pltpu.VMEM((2, CHUNK, width), bf16),
            pltpu.VMEM((2, CHUNK, width), bf16),
            pltpu.VMEM((2, width, CHUNK), bf16),
            pltpu.VMEM((8, inner), f32),
            pltpu.VMEM((8, twice), f32),
            pltpu.VMEM((CHUNK, CHUNK), f32),
            pltpu.VMEM((2, CHUNK, width), f32),
            pltpu.VMEM((2 * CHUNK, LANES), f32),
            pltpu.VMEM((8, inner), f32),
        ]
        + plan.scratch(),
        out_shape=[
            jax.ShapeDtypeStruct((micros * tokens, lead), bf16),
            jax.ShapeDtypeStruct((micros, 8, inner), f32),
            jax.ShapeDtypeStruct((micros, 8, inner), f32),
            jax.ShapeDtypeStruct((micros * tokens, twice), f32),
            jax.ShapeDtypeStruct((micros, 8, twice), f32),
            jax.ShapeDtypeStruct((8, inner), f32),
            jax.ShapeDtypeStruct((8, twice), f32),
            jax.ShapeDtypeStruct((8, LANES), f32),
            jax.ShapeDtypeStruct((8, inner), f32),
        ]
        + [jax.ShapeDtypeStruct((shard_rows, term.shape[1]), f32) for term in terms],
        compiler_params=pltpu.CompilerParams(
            collective_id=collective_id, has_side_effects=True, vmem_limit_bytes=60 * 1024 * 1024
        ),
    )(
        marks, raw, raw, rims, raw, raw, rims, raw, grad, mixer, states, states, fin, entering,
        cd, pulled, cw, cb, ccw, ccb, sbias, rate, skip, sel, selcol, selt,
        *[term.reshape(pairs, 2, shard_rows, -1) for term in terms], *first,
    )


class Gathering:
    def __init__(self, rows, pairs, widths, cuts, shared):
        self.rows, self.pairs, self.shared = rows, pairs, shared
        self.arrays = len(widths)
        self.pieces = []
        for array, width in enumerate(widths):
            size = -(-width // LANES // cuts) * LANES
            self.pieces += [
                (array, start, min(size, width - start)) for start in range(0, width, size)
            ]
        self.moved = rows - shared
        self.early = min(rows // 8, self.moved - shared) // 16 * 16
        self.late = self.moved - self.early
        self.order = [(j, k) for j in range(len(self.pieces)) for k in range(pairs)]
        if pairs > 1:
            self.order.sort(key=lambda item: (item[0] * pairs + (item[1] or -0.5 - (item[0] > 0))))
        self.lag = 2

    def scratch(self):
        dma, pairs, arrays = pltpu.SemaphoreType.DMA, self.pairs, len(self.pieces)
        return [
            dma((arrays, max(pairs - 1, 1))),
            dma((arrays, max(pairs - 1, 1))),
            dma((arrays, pairs)),
            dma((arrays, pairs)),
            dma((arrays, 2 * pairs)),
            dma((arrays, 2 * pairs)),
            dma((arrays, 2 * pairs)),
            dma((arrays, 2 * pairs)),
            dma((arrays,)),
        ]

    def bind(self, weights, fulls, scratch):
        self.weights, self.fulls = weights, fulls
        (
            self.ring_send, self.ring_recv, self.pair_send, self.pair_recv,
            self.cross_send, self.cross_recv, self.early_send, self.early_recv, self.local,
        ) = scratch
        self.own, self.place = lax.axis_index("fsdp"), lax.axis_index("context")
        self.side = lax.axis_index("tensor")
        self.pair, self.member = self.own // 2, lax.rem(self.own, 2)
        pairs, pair, member = self.pairs, self.pair, self.member
        self.ahead = (2 * lax.rem(pair + 1, pairs) + member, self.place, self.side)
        self.behind = (2 * lax.rem(pair + pairs - 1, pairs) + member, self.place, self.side)
        self.partner = (2 * pair + 1 - member, self.place, self.side)
        self.across = (self.own, 1 - self.place, self.side)
        self.beside = (self.own, self.place, 1 - self.side)
        self.late_start = pl.multiple_of(self.place * (self.shared + self.early), 16)
        self.early_start = pl.multiple_of(
            self.place * self.shared + (1 - self.place) * self.late, 16
        )
        self.shared_start = pl.multiple_of(self.place * self.moved, 16)

    def greet(self, *others):
        barrier = pltpu.get_barrier_semaphore()
        devices = [self.ahead, self.behind, self.partner, self.across, *others]
        for device in devices:
            pl.semaphore_signal(barrier, inc=1, device_id=device, device_id_type=MESH)
        pl.semaphore_wait(barrier, len(devices))

    def part(self, j, k, which, start, size):
        there = lax.rem(self.pair + self.pairs - k, self.pairs)
        index = 2 * there + (self.member if which == 0 else 1 - self.member)
        array, first, width = self.pieces[j]
        rows = pl.ds(pl.multiple_of(index * self.rows + start, 16), size)
        return self.fulls[array].at[rows, pl.ds(first, width)]

    def source(self, j, k, which, start, size):
        if k == 0 and which == 0:
            array, first, width = self.pieces[j]
            return self.weights[array].at[pl.ds(start, size), pl.ds(first, width)]
        return self.part(j, k, which, start, size)

    def ring_copy(self, j, k):
        return pltpu.make_async_remote_copy(
            src_ref=self.source(j, k, 0, self.late_start, self.late),
            dst_ref=self.part(j, k, 0, self.late_start, self.late),
            send_sem=self.ring_send.at[j, k], recv_sem=self.ring_recv.at[j, k],
            device_id=self.ahead, device_id_type=MESH,
        )

    def pair_copy(self, j, k):
        return pltpu.make_async_remote_copy(
            src_ref=self.source(j, k, 0, self.late_start, self.late),
            dst_ref=self.part(j, k, 0, self.late_start, self.late),
            send_sem=self.pair_send.at[j, k], recv_sem=self.pair_recv.at[j, k],
            device_id=self.partner, device_id_type=MESH,
        )

    def early_copy(self, j, k, which):
        own = k == self.pairs - 1
        k = 0 if own else k
        slot = 2 * self.pairs - 2 if own else 2 * k + which
        return pltpu.make_async_remote_copy(
            src_ref=self.source(j, k, which, self.early_start, self.early),
            dst_ref=self.part(j, k, which, self.early_start, self.early),
            send_sem=self.early_send.at[j, slot], recv_sem=self.early_recv.at[j, slot],
            device_id=self.partner if own else self.ahead, device_id_type=MESH,
        )

    def early_event(self, j, k):
        last = self.pairs - 1
        if k == 0:
            self.early_copy(j, last, 0).start()
        else:
            self.early_copy(j, k - 1, 0).wait_recv()
        if k < last:
            self.early_copy(j, k, 0).start()
        if k == 1:
            self.early_copy(j, last, 0).wait_recv()
        elif k > 1:
            self.early_copy(j, k - 2, 1).wait_recv()
        if k > 0:
            self.early_copy(j, k - 1, 1).start()

    def cross_copy(self, j, k, which):
        here = self.part(j, k, which, self.shared_start, self.shared)
        return pltpu.make_async_remote_copy(
            src_ref=here, dst_ref=here,
            send_sem=self.cross_send.at[j, 2 * k + which], recv_sem=self.cross_recv.at[j, 2 * k + which],
            device_id=self.across, device_id_type=MESH,
        )

    def keep_copy(self, j):
        rows = pl.ds(pl.multiple_of(self.own * self.rows, 16), self.rows)
        return pltpu.make_async_copy(self.weights[j], self.fulls[j].at[rows, :], self.local.at[j])

    def event(self, number):
        j, k = self.order[number]
        if k > 0:
            self.ring_copy(j, k - 1).wait_recv()
        if number == 0:
            for array in range(self.arrays):
                self.keep_copy(array).start()
        if k < self.pairs - 1:
            self.ring_copy(j, k).start()
        self.pair_copy(j, k).start()
        if k > 0:
            self.cross_copy(j, k, 0).start()
        if self.early:
            self.early_event(j, k)
        if number >= self.lag:
            self.share(number - self.lag)

    def share(self, number):
        j, k = self.order[number]
        self.pair_copy(j, k).wait_recv()
        self.cross_copy(j, k, 1).start()

    def finish(self):
        for number in range(max(len(self.order) - self.lag, 0), len(self.order)):
            self.share(number)
        crossed = [(j, k, which) for j, k in self.order for which in range(2) if k or which]
        for item in crossed:
            self.cross_copy(*item).wait_recv()
        for j, k in self.order:
            if k < self.pairs - 1:
                self.ring_copy(j, k).wait_send()
            self.pair_copy(j, k).wait_send()
        for item in crossed:
            self.cross_copy(*item).wait_send()
        for j in range(len(self.pieces)):
            if self.early:
                last = self.pairs - 1
                if last:
                    self.early_copy(j, last - 1, 1).wait_recv()
                else:
                    self.early_copy(j, last, 0).wait_recv()
                self.early_copy(j, last, 0).wait_send()
                for k in range(last):
                    for which in range(2):
                        self.early_copy(j, k, which).wait_send()
        for array in range(self.arrays):
            self.keep_copy(array).wait()


def gather_kernel(plan, *refs):
    arrays = plan.arrays
    weights, tokens = refs[:arrays], refs[arrays]
    fulls, far = refs[arrays + 1 : 2 * arrays + 1], refs[2 * arrays + 1]
    extra_send, extra_recv = refs[2 * arrays + 2 : 2 * arrays + 4]
    plan.bind(weights, fulls, refs[2 * arrays + 4 :])
    plan.greet(plan.beside)
    half = tokens.shape[2] // 2
    lanes = pl.ds(pl.multiple_of(plan.side * half, 128), half)

    def token_copy(src, number, device):
        return pltpu.make_async_remote_copy(
            src_ref=src.at[:, :, lanes], dst_ref=far.at[:, :, lanes],
            send_sem=extra_send.at[number], recv_sem=extra_recv.at[number],
            device_id=device, device_id_type=MESH,
        )

    first, second = token_copy(tokens, 0, plan.across), token_copy(far, 1, plan.beside)
    first.start()
    for number in range(len(plan.order)):
        plan.event(number)
        if number == min(5, len(plan.order) - 1):
            first.wait_recv()
            second.start()
    second.wait_recv()
    plan.finish()
    first.wait_send()
    second.wait_send()


def gather_weights(shards, tokens, shared, collective_id):
    rows = shards[0].shape[0]
    pairs = lax.axis_size("fsdp") // 2
    count = len(shards)
    plan = Gathering(rows, pairs, [shard.shape[1] for shard in shards], 2, shared)
    hbm = pl.BlockSpec(memory_space=pl.ANY)
    dma = pltpu.SemaphoreType.DMA
    return pl.pallas_call(
        functools.partial(gather_kernel, plan),
        out_shape=[
            jax.ShapeDtypeStruct((2 * pairs * rows, shard.shape[1]), shard.dtype) for shard in shards
        ]
        + [jax.ShapeDtypeStruct(tokens.shape, tokens.dtype)],
        in_specs=[hbm] * (count + 1),
        out_specs=[hbm] * (count + 1),
        scratch_shapes=[dma((2,)), dma((2,))] + plan.scratch(),
        compiler_params=pltpu.CompilerParams(collective_id=collective_id, has_side_effects=True),
    )(*shards, tokens)


def order_kernel(near_index, far_index, is_near, near, far, gain, x_out, normed_out, scale_out):
    step = pl.program_id(0)
    near_now = is_near[step] == 1
    x = jnp.where(near_now, near[...], far[...])
    x_out[...] = x
    value = x.astype(f32)
    mean = jnp.sum(value * value, axis=-1, keepdims=True) * (1.0 / value.shape[-1])
    scale = lax.rsqrt(mean + epsilon)
    normed_out[...] = (value * scale * gain[...]).astype(bf16)
    scale_out[...] = jnp.broadcast_to(scale, scale_out.shape)


def ordered(near, far, near_index, far_index, is_near, gain):
    micros, count, length, model = near.shape
    blocks = micros * count

    def block(spec_index):
        return pl.BlockSpec((None, None, length, model), spec_index)

    def rows(lanes):
        return pl.BlockSpec((length, lanes), lambda step, *_: (step, 0))

    return pl.pallas_call(
        order_kernel,
        grid_spec=pltpu.PrefetchScalarGridSpec(
            num_scalar_prefetch=3,
            grid=(blocks,),
            in_specs=[
                block(lambda step, near_at, far_at, flags: (step // count, near_at[step], 0, 0)),
                block(lambda step, near_at, far_at, flags: (step // count, far_at[step], 0, 0)),
                pl.BlockSpec((1, model), lambda *_: (0, 0)),
            ],
            out_specs=[rows(model), rows(model), rows(LANES)],
        ),
        out_shape=[
            jax.ShapeDtypeStruct((blocks * length, model), bf16),
            jax.ShapeDtypeStruct((blocks * length, model), bf16),
            jax.ShapeDtypeStruct((blocks * length, LANES), f32),
        ],
        compiler_params=pltpu.CompilerParams(vmem_limit_bytes=32 * 1024 * 1024),
    )(near_index, far_index, is_near, near, far, gain)


def gate_kernel(
    normed, out_grad, gate_weight, out_weight, y_own, carry, coupled, entering, gain,
    mixer_out, gate_out, grad_out, sums_out,
):
    gate_in = mm(normed[...], gate_weight[...])
    grads = mm(out_grad[...], out_weight[...])
    width = entering.shape[0]
    arrived = mm_three(split_two(coupled[:, width:]), split_two(entering[...]))
    mixer = y_own[...] + carry[...] * arrived
    gated = mixer * (gate_in * logistic(gate_in))
    mixer_out[...] = mixer
    gate_out[...] = gate_in
    grad_out[...] = grads
    square = jnp.sum(gated * gated, axis=-1, keepdims=True)
    product = jnp.sum(grads * gain[...] * gated, axis=-1, keepdims=True)
    lane = lax.broadcasted_iota(jnp.int32, sums_out.shape, 1)
    sums_out[...] = jnp.where(lane == 0, square, jnp.where(lane == 1, product, 0.0))


def gate_stage(normed, out_grad, gate_weight, out_weight, y_own, carry, coupled, entering, gain):
    rows, model = normed.shape
    inner = y_own.shape[1]
    twice = coupled.shape[1]
    micros, width, _ = entering.shape
    size = 2 * CHUNK
    per_micro = rows // micros // size

    def block(lanes):
        return pl.BlockSpec((size, lanes), lambda step: (step, 0))

    return pl.pallas_call(
        gate_kernel,
        grid=(rows // size,),
        in_specs=[
            block(model),
            block(model),
            pl.BlockSpec((model, inner), lambda step: (0, 0), pipeline_mode=pl.Buffered(1)),
            pl.BlockSpec((model, inner), lambda step: (0, 0), pipeline_mode=pl.Buffered(1)),
            block(inner),
            block(inner),
            block(twice),
            pl.BlockSpec((None, width, inner), lambda step: (step // per_micro, 0, 0)),
            pl.BlockSpec((1, inner), lambda step: (0, 0)),
        ],
        out_specs=[block(inner), block(inner), block(inner), block(LANES)],
        out_shape=[jax.ShapeDtypeStruct((rows, inner), f32)] * 3
        + [jax.ShapeDtypeStruct((rows, LANES), f32)],
        compiler_params=pltpu.CompilerParams(vmem_limit_bytes=60 * 1024 * 1024),
        cost_estimate=pl.CostEstimate(
            flops=4 * rows * model * inner, bytes_accessed=24 * rows * inner, transcendentals=0
        ),
    )(normed, out_grad, gate_weight, out_weight, y_own, carry, coupled, entering, gain)


def gate_back_kernel(
    inner_total, per_micro, mixer, gate_in, grads, carry, coupled, sums, gain,
    norm_out, gate_out, mixer_out, pull_out, gain_out,
):
    step = pl.program_id(0)
    width = pull_out.shape[0]
    inv_norm = lax.rsqrt(sums[:, 0:1] / inner_total + epsilon)
    inner_dot = sums[:, 1:2] * (inv_norm * inv_norm * inv_norm) / inner_total
    mixer_now, gate_now, grad_now = mixer[...], gate_in[...], grads[...]
    sig = logistic(gate_now)
    act = gate_now * sig
    gated = mixer_now * act
    norm_out[...] = (gated * inv_norm * gain[...]).astype(bf16)
    gated_grad = grad_now * gain[...] * inv_norm - gated * inner_dot
    gate_out[...] = (gated_grad * mixer_now * sig * (1.0 + gate_now * (1.0 - sig))).astype(bf16)
    mixer_grad = gated_grad * act
    mixer_out[...] = mixer_grad

    @pl.when(step == 0)
    def _():
        gain_out[...] = jnp.zeros_like(gain_out)

    gain_out[0:1, :] += jnp.sum(grad_now * gated * inv_norm, axis=0, keepdims=True)

    @pl.when(lax.rem(step, per_micro) == 0)
    def _():
        pull_out[...] = jnp.zeros_like(pull_out)

    turned = split_two(jnp.transpose(coupled[:, width:]))
    pull_out[...] += mm_three(turned, split_two(carry[...] * mixer_grad))


def gate_back_stage(mixer, gate_in, grads, carry, coupled, sums, gain, micros, inner_total):
    rows, inner = mixer.shape
    twice = coupled.shape[1]
    width = twice // 2
    per_micro = rows // micros // CHUNK

    def block(lanes):
        return pl.BlockSpec((CHUNK, lanes), lambda step: (step, 0))

    return pl.pallas_call(
        functools.partial(gate_back_kernel, inner_total, per_micro),
        grid=(rows // CHUNK,),
        in_specs=[
            block(inner),
            block(inner),
            block(inner),
            block(inner),
            block(twice),
            block(LANES),
            pl.BlockSpec((1, inner), lambda step: (0, 0)),
        ],
        out_specs=[
            block(inner),
            block(inner),
            block(inner),
            pl.BlockSpec((None, width, inner), lambda step: (step // per_micro, 0, 0)),
            pl.BlockSpec((8, inner), lambda step: (0, 0)),
        ],
        out_shape=[
            jax.ShapeDtypeStruct((rows, inner), bf16),
            jax.ShapeDtypeStruct((rows, inner), bf16),
            jax.ShapeDtypeStruct((rows, inner), f32),
            jax.ShapeDtypeStruct((micros, width, inner), f32),
            jax.ShapeDtypeStruct((8, inner), f32),
        ],
        compiler_params=pltpu.CompilerParams(vmem_limit_bytes=48 * 1024 * 1024),
        cost_estimate=pl.CostEstimate(
            flops=8 * rows * width * inner, bytes_accessed=24 * rows * inner, transcendentals=0
        ),
    )(mixer, gate_in, grads, carry, coupled, sums, gain)


def weave_kernel(first, second, out):
    out[:, 0, :] = first[...]
    out[:, 1, :] = second[...]


def woven(first, second, columns):
    rows = first.shape[0]
    size = 32
    block = pl.BlockSpec((size, columns), lambda step: (step, 0))
    return pl.pallas_call(
        weave_kernel,
        grid=(rows // size,),
        in_specs=[block, block],
        out_specs=pl.BlockSpec((size, 2, columns), lambda step: (step, 0, 0)),
        out_shape=jax.ShapeDtypeStruct((rows, 2, columns), first.dtype),
    )(first, second)


class Reduction:
    def __init__(self, rows, pairs, columns, lag):
        self.rows, self.pairs, self.columns, self.lag = rows, pairs, columns, lag
        self.shared = rows // 4
        self.moved = rows - self.shared
        self.counts = [count // LANES for count in columns]
        self.count = sum(self.counts)
        self.steps = self.count + 4 * lag

    def scratch(self):
        shared, moved, pairs, count = self.shared, self.moved, self.pairs, self.count
        cross, pair, ring = 2 * pairs * shared + 16, pairs * moved + 16, moved + 16
        i16, dma = jnp.int16, pltpu.SemaphoreType.DMA
        return [
            pltpu.VMEM((count, cross, LANES), i16),
            pltpu.VMEM((count, pair, LANES), i16),
            pltpu.VMEM((count, pairs - 1, ring, LANES), i16),
            pltpu.VMEM((count, ring, LANES), i16),
            pltpu.VMEM((2, cross, LANES), i16),
            pltpu.VMEM((2, pair, LANES), i16),
            pltpu.VMEM((2, pairs - 1, ring, LANES), i16),
            pltpu.VMEM((2, ring, LANES), i16),
            pltpu.VMEM((2, pairs, 2, shared, LANES), f32),
            pltpu.VMEM((2, pairs, moved, LANES), f32),
            pltpu.VMEM((2, pairs, moved, LANES), f32),
            pltpu.VMEM((2 * self.lag, moved, LANES), f32),
            pltpu.VMEM((2 * self.lag, moved, LANES), f32),
            pltpu.VMEM((2, self.rows, LANES), f32),
            dma((count,)),
            dma((count,)),
            dma((pairs - 1, count)),
            dma((count,)),
            dma((2,)),
            dma((2,)),
            dma((pairs - 1, 2)),
            dma((2,)),
            dma((3, 2)),
            dma((2,)),
        ]

    def bind(self, terms, outs, scratch):
        self.terms, self.outs = terms, outs
        (
            self.cross_in, self.pair_in, self.ring_in, self.last_in,
            self.cross_out, self.pair_out, self.ring_out, self.last_out,
            self.cross_term, self.pair_term, self.ring_term,
            self.kept, self.held, self.result,
            self.cross_recv, self.pair_recv, self.ring_recv, self.last_recv,
            self.cross_sent, self.pair_sent, self.ring_sent, self.last_sent,
            self.loaded, self.stored,
        ) = scratch
        self.own, self.place = lax.axis_index("fsdp"), lax.axis_index("context")
        self.side = lax.axis_index("tensor")
        self.pair, self.member = self.own // 2, lax.rem(self.own, 2)
        self.across = (self.own, 1 - self.place, self.side)
        self.partner = (2 * self.pair + 1 - self.member, self.place, self.side)
        self.inset = pl.multiple_of(self.place * (self.moved - self.shared), 16)
        self.start = pl.multiple_of(self.place * self.shared, 16)

    def peer(self, offset):
        there = lax.rem(self.pair + offset, self.pairs)
        return (2 * there + self.member, self.place, self.side)

    def greet(self):
        barrier = pltpu.get_barrier_semaphore()
        devices = [self.across, self.partner] + [self.peer(k) for k in range(1, self.pairs)]
        for device in devices:
            pl.semaphore_signal(barrier, inc=1, device_id=device, device_id_type=MESH)
        pl.semaphore_wait(barrier, len(devices))

    def cross_copy(self, chunk):
        slot = lax.rem(chunk, 2)
        return pltpu.make_async_remote_copy(
            src_ref=self.cross_out.at[slot], dst_ref=self.cross_in.at[chunk],
            send_sem=self.cross_sent.at[slot], recv_sem=self.cross_recv.at[chunk],
            device_id=self.across, device_id_type=MESH,
        )

    def pair_copy(self, chunk):
        slot = lax.rem(chunk, 2)
        return pltpu.make_async_remote_copy(
            src_ref=self.pair_out.at[slot], dst_ref=self.pair_in.at[chunk],
            send_sem=self.pair_sent.at[slot], recv_sem=self.pair_recv.at[chunk],
            device_id=self.partner, device_id_type=MESH,
        )

    def ring_copy(self, chunk, offset):
        slot = lax.rem(chunk, 2)
        return pltpu.make_async_remote_copy(
            src_ref=self.ring_out.at[slot, offset - 1], dst_ref=self.ring_in.at[chunk, offset - 1],
            send_sem=self.ring_sent.at[offset - 1, slot],
            recv_sem=self.ring_recv.at[offset - 1, chunk],
            device_id=self.peer(offset), device_id_type=MESH,
        )

    def last_copy(self, chunk):
        slot = lax.rem(chunk, 2)
        return pltpu.make_async_remote_copy(
            src_ref=self.last_out.at[slot], dst_ref=self.last_in.at[chunk],
            send_sem=self.last_sent.at[slot], recv_sem=self.last_recv.at[chunk],
            device_id=self.across, device_id_type=MESH,
        )

    def load_copy(self, stage, term, cols, slot):
        if stage == 0:
            rows = pl.ds(pl.multiple_of((1 - self.place) * self.moved, 16), self.shared)
            src, dst = term.at[:, :, rows, cols], self.cross_term.at[slot]
        elif stage == 1:
            src = term.at[:, 1 - self.member, pl.ds(self.start, self.moved), cols]
            dst = self.pair_term.at[slot]
        else:
            src = term.at[:, self.member, pl.ds(self.start, self.moved), cols]
            dst = self.ring_term.at[slot]
        return pltpu.make_async_copy(src, dst, self.loaded.at[stage, slot])

    def each_array(self, chunk, act):
        first = 0
        for number, count in enumerate(self.counts):
            inside = (chunk >= first) & (chunk < first + count)
            offset = first

            @pl.when(inside)
            def _(number=number, offset=offset):
                act(number, pl.ds(pl.multiple_of((chunk - offset) * LANES, LANES), LANES))

            first += count

    def load(self, stage, chunk):
        @pl.when((chunk >= 0) & (chunk < self.count))
        def _():
            self.each_array(
                chunk,
                lambda number, cols: self.load_copy(
                    stage, self.terms[number], cols, lax.rem(chunk, 2)
                ).start(),
            )

    def loaded_now(self, stage, chunk):
        self.load_copy(stage, self.terms[0], pl.ds(0, LANES), lax.rem(chunk, 2)).wait()

    @staticmethod
    def encode(value, out, place):
        count = value.shape[0]
        peak = jnp.maximum(jnp.max(jnp.abs(value), axis=0, keepdims=True), 1e-30)
        exponent = jnp.ceil(jnp.log(peak) * 1.4426950408889634)
        factor = jnp.exp(exponent * -0.6931471805599453) * 32000.0
        out[place + (pl.ds(0, count), slice(None))] = (
            (value * factor + 12582912.0 - 12582912.0).astype(jnp.int32).astype(jnp.int16)
        )
        out[place + (pl.ds(count, 16), slice(None))] = (
            jnp.broadcast_to(exponent, (16, LANES)).astype(jnp.int32).astype(jnp.int16)
        )

    @staticmethod
    def unit(ref, place, count):
        exponents = ref[place + (pl.ds(count, 16), slice(None))].astype(jnp.int32).astype(f32)
        return jnp.exp(exponents[:1] * 0.6931471805599453) * (1.0 / 32000.0)

    @staticmethod
    def decode(ref, place, first, count, unit):
        first = pl.multiple_of(first, 16) if not isinstance(first, int) else first
        return ref[place + (pl.ds(first, count), slice(None))].astype(jnp.int32).astype(f32) * unit

    def step(self, number):
        lag, pairs, shared, moved = self.lag, self.pairs, self.shared, self.moved

        @pl.when(number == 0)
        def _():
            self.load(0, number)

        self.load(0, number + 1)
        self.load(1, number + 1 - lag)
        self.load(2, number + 1 - 2 * lag)

        def stage(index, act):
            chunk = number - index * lag

            @pl.when((chunk >= 0) & (chunk < self.count))
            def _():
                act(chunk, lax.rem(chunk, 2))

        def cross(chunk, slot):
            self.loaded_now(0, chunk)

            @pl.when(chunk >= 2)
            def _():
                self.cross_copy(chunk - 2).wait_send()

            value = self.cross_term[slot].reshape(2 * pairs * shared, LANES)
            self.encode(value, self.cross_out, (slot,))
            self.cross_copy(chunk).start()

        def pair(chunk, slot):
            self.loaded_now(1, chunk)
            self.cross_copy(chunk).wait_recv()

            @pl.when(chunk >= 2)
            def _():
                self.pair_copy(chunk - 2).wait_send()

            unit = self.unit(self.cross_in, (chunk,), 2 * pairs * shared)
            for there in range(pairs):
                first = (2 * there + 1 - self.member) * shared
                self.pair_term[slot, there, pl.ds(self.inset, shared), :] += self.decode(
                    self.cross_in, (chunk,), first, shared, unit
                )
            value = self.pair_term[slot].reshape(pairs * moved, LANES)
            self.encode(value, self.pair_out, (slot,))
            self.pair_copy(chunk).start()

        def ring(chunk, slot):
            self.loaded_now(2, chunk)
            self.pair_copy(chunk).wait_recv()

            @pl.when(chunk >= 2)
            def _():
                for offset in range(1, pairs):
                    self.ring_copy(chunk - 2, offset).wait_send()

            cross_unit = self.unit(self.cross_in, (chunk,), 2 * pairs * shared)
            pair_unit = self.unit(self.pair_in, (chunk,), pairs * moved)
            for offset in list(range(1, pairs)) + [0]:
                there = lax.rem(self.pair + offset, pairs)
                first = (2 * there + self.member) * shared
                self.ring_term[slot, there, pl.ds(self.inset, shared), :] += self.decode(
                    self.cross_in, (chunk,), first, shared, cross_unit
                )
                value = self.ring_term[slot, there] + self.decode(
                    self.pair_in, (chunk,), there * moved, moved, pair_unit
                )
                if offset:
                    self.encode(value, self.ring_out, (slot, offset - 1))
                    self.ring_copy(chunk, offset).start()
                else:
                    self.kept[lax.rem(chunk, 2 * lag)] = value

        def last(chunk, slot):
            for offset in range(1, pairs):
                self.ring_copy(chunk, offset).wait_recv()

            @pl.when(chunk >= 2)
            def _():
                self.last_copy(chunk - 2).wait_send()

            total = self.kept[lax.rem(chunk, 2 * lag)]
            for offset in range(1, pairs):
                place = (chunk, offset - 1)
                total = total + self.decode(
                    self.ring_in, place, 0, moved, self.unit(self.ring_in, place, moved)
                )
            self.encode(total, self.last_out, (slot,))
            self.held[lax.rem(chunk, 2 * lag)] = self.decode(
                self.last_out, (slot,), 0, moved, self.unit(self.last_out, (slot,), moved)
            )
            self.last_copy(chunk).start()

        def write_copy(number, cols, slot):
            return pltpu.make_async_copy(
                self.result.at[slot], self.outs[number].at[:, cols], self.stored.at[slot]
            )

        def write(chunk, slot):
            self.last_copy(chunk).wait_recv()

            @pl.when(chunk >= 2)
            def _():
                write_copy(0, pl.ds(0, LANES), slot).wait()

            mine = self.held[lax.rem(chunk, 2 * lag)]
            other = self.decode(
                self.last_in, (chunk,), 0, moved, self.unit(self.last_in, (chunk,), moved)
            )
            low = jnp.where(self.place == 0, mine, other)
            high = jnp.where(self.place == 0, other, mine)
            self.result[slot, pl.ds(0, shared), :] = low[:shared]
            self.result[slot, pl.ds(shared, moved - shared), :] = (
                low[shared:] + high[: moved - shared]
            )
            self.result[slot, pl.ds(moved, shared), :] = high[moved - shared :]
            self.each_array(chunk, lambda which, cols: write_copy(which, cols, slot).start())

        stage(4, write)
        stage(3, last)
        stage(2, ring)
        stage(1, pair)
        stage(0, cross)

        @pl.when(number == self.steps - 1)
        def _():
            for slot in range(2):
                write_copy(0, pl.ds(0, LANES), slot).wait()
                self.cross_copy(jnp.int32(self.count - 2 + slot)).wait_send()
                self.pair_copy(jnp.int32(self.count - 2 + slot)).wait_send()
                self.last_copy(jnp.int32(self.count - 2 + slot)).wait_send()
                for offset in range(1, pairs):
                    self.ring_copy(jnp.int32(self.count - 2 + slot), offset).wait_send()


def finish_kernel(plan, blocks, *refs):
    (
        term, x, cot, scale, keep, branch, branch_other, part, part_other, gain, small,
        out, block_out, input_out, small_out,
        gain_sum, cross_in, pair_out, pair_in, ring_in,
        cross_send, cross_recv, pair_send, pair_recv, ring_send, ring_recv, final_sem,
    ) = refs[:27]
    plan.bind([term], [out], refs[27:])
    step = pl.program_id(0)

    @pl.when(step == 0)
    def _():
        plan.greet()
        gain_sum[...] = jnp.zeros_like(gain_sum)

    @pl.when(step < plan.steps)
    def _():
        plan.step(step)

    @pl.when(step < blocks)
    def _():
        x_float = x[...].astype(f32)
        block_out[...] = (x_float + keep[:, 0:1] * (branch[...] + branch_other[...])).astype(bf16)
        inv_rms = scale[:, 0:1]
        x_hat = x_float * inv_rms
        normed_grad = part[...] + part_other[...]
        hat_grad = normed_grad * gain[...]
        mean = jnp.sum(hat_grad * x_hat, axis=-1, keepdims=True) * (1.0 / x_float.shape[-1])
        input_out[...] = (cot[...].astype(f32) + inv_rms * (hat_grad - x_hat * mean)).astype(bf16)
        gain_sum[0:1, :] += jnp.sum(normed_grad * x_hat, axis=0, keepdims=True)

    rows = small.shape[0]
    lines = gain_sum.shape[1] // LANES

    def cross_copy():
        return pltpu.make_async_remote_copy(
            src_ref=pair_out, dst_ref=cross_in, send_sem=cross_send.at[0], recv_sem=cross_recv.at[0],
            device_id=plan.across, device_id_type=MESH,
        )

    def pair_copy():
        return pltpu.make_async_remote_copy(
            src_ref=pair_out, dst_ref=pair_in, send_sem=pair_send.at[0], recv_sem=pair_recv.at[0],
            device_id=plan.partner, device_id_type=MESH,
        )

    def ring_copy(offset):
        return pltpu.make_async_remote_copy(
            src_ref=ring_in.at[0], dst_ref=ring_in.at[plan.pairs - offset],
            send_sem=ring_send.at[offset - 1], recv_sem=ring_recv.at[offset - 1],
            device_id=plan.peer(offset), device_id_type=MESH,
        )

    @pl.when(step == blocks)
    def _():
        pair_out[pl.ds(0, rows), :] = small[...]
        for line in range(lines):
            pair_out[rows + line : rows + line + 1, :] = gain_sum[
                0:1, line * LANES : (line + 1) * LANES
            ]
        cross_copy().start()

    @pl.when(step == blocks + 2)
    def _():
        cross_copy().wait()
        pair_out[...] += cross_in[...]
        pair_copy().start()

    @pl.when(step == blocks + 4)
    def _():
        pair_copy().wait()
        ring_in[0] = pair_out[...] + pair_in[...]
        for offset in range(1, plan.pairs):
            ring_copy(offset).start()

    @pl.when(step == blocks + 6)
    def _():
        for offset in range(1, plan.pairs):
            ring_copy(offset).wait()
        total = jnp.zeros_like(pair_out)
        for index in range(plan.pairs):
            total = total + ring_in[lax.rem(index + plan.pairs - plan.pair, plan.pairs)]
        pair_in[...] = total
        copy = pltpu.make_async_copy(pair_in, small_out, final_sem.at[0])
        copy.start()
        copy.wait()


def finish(term, x, cot, scale, keep, branch, branch_other, part, part_other, gain, small, collective_id):
    pairs = lax.axis_size("fsdp") // 2
    shard_rows = term.shape[0] // (2 * pairs)
    plan = Reduction(shard_rows, pairs, [term.shape[1]], 2)
    rows, model = x.shape
    size = 64
    blocks = rows // size
    steps = max(plan.steps, blocks + 7)
    total_rows = small.shape[0] + model // LANES
    hbm = pl.BlockSpec(memory_space=pl.ANY)
    dma = pltpu.SemaphoreType.DMA

    def block(lanes):
        return pl.BlockSpec((size, lanes), lambda step: (jnp.minimum(step, blocks - 1), 0))

    def constant(shape):
        return pl.BlockSpec(shape, lambda step: (0, 0))

    return pl.pallas_call(
        functools.partial(finish_kernel, plan, blocks),
        grid=(steps,),
        in_specs=[hbm]
        + [block(lanes) for lanes in (model, model, LANES, LANES, model, model, model, model)]
        + [constant((1, model)), constant(small.shape)],
        out_specs=[hbm, block(model), block(model), hbm],
        out_shape=[
            jax.ShapeDtypeStruct((shard_rows, term.shape[1]), f32),
            jax.ShapeDtypeStruct((rows, model), bf16),
            jax.ShapeDtypeStruct((rows, model), bf16),
            jax.ShapeDtypeStruct((total_rows, LANES), f32),
        ],
        scratch_shapes=[
            pltpu.VMEM((8, model), f32),
            pltpu.VMEM((total_rows, LANES), f32),
            pltpu.VMEM((total_rows, LANES), f32),
            pltpu.VMEM((total_rows, LANES), f32),
            pltpu.VMEM((pairs, total_rows, LANES), f32),
            dma((1,)),
            dma((1,)),
            dma((1,)),
            dma((1,)),
            dma((max(pairs - 1, 1),)),
            dma((max(pairs - 1, 1),)),
            dma((1,)),
        ]
        + plan.scratch(),
        compiler_params=pltpu.CompilerParams(
            collective_id=collective_id, has_side_effects=True, vmem_limit_bytes=56 * 1024 * 1024
        ),
    )(
        term.reshape(pairs, 2, shard_rows, -1), x, cot, scale, keep, branch, branch_other, part,
        part_other, gain, small,
    )


def passed_along(value, axis, steps):
    count = lax.axis_size(axis)
    initial, last = (max(0, -steps), min(count, count - steps))
    return lax.ppermute(value, axis, [(source, source + steps) for source in range(initial, last)])


def paired(value, axis):
    count = lax.axis_size(axis)
    return lax.ppermute(value, axis, [(source, source ^ 1) for source in range(count)])


def ring_shift(value, axis, steps):
    count = lax.axis_size(axis)
    return lax.ppermute(
        value, axis, [(source, (source + 2 * steps) % count) for source in range(count)]
    )


def packed_rows(values):
    flat = jnp.concatenate([value.reshape(-1) for value in values])
    return jnp.pad(flat, (0, -flat.shape[0] % 1024)).reshape(-1, LANES)


def unpacked(flat, values):
    results, start = [], 0
    for value in values:
        results.append(flat[start : start + value.size].reshape(value.shape))
        start += value.size
    return results


def shards(
    tokens,
    lengths,
    block_order,
    cotangent,
    norm_gain,
    in_weight,
    coupling_weight,
    step_weight,
    out_weight,
    conv_weight,
    conv_bias,
    coupling_conv,
    coupling_bias,
    step_bias,
    decay_rate,
    skip_gain,
    inner_gain,
):
    micros = tokens.shape[0]
    count = tokens.shape[2]
    model = tokens.shape[3]
    inner = inner_gain.shape[0]
    heads = step_bias.shape[0]
    head_size = inner // heads
    twice = coupling_weight.shape[1]
    width = twice // 2
    blocks_row = block_order.shape[2]
    block_len = count * lax.axis_size("context") // blocks_row
    own_blocks = count // block_len
    inner_total = inner * lax.axis_size("tensor")
    side = lax.axis_index("tensor")
    place = lax.axis_index("context")
    base = place * count
    shard_rows = in_weight.shape[0]

    narrow, wide_columns = selectors(heads, head_size)
    sel = jnp.asarray(narrow, bf16)
    selcol = jnp.asarray(wide_columns, bf16)
    selt = jnp.asarray(narrow[:heads].T, bf16)
    selt = jnp.pad(selt, ((0, 0), (0, LANES - heads)))

    lead = jnp.concatenate(
        [
            in_weight[:, 1, :],
            coupling_weight,
            jnp.pad(step_weight, ((0, 0), (0, LANES - heads))),
        ],
        axis=1,
    )
    def sharing(parts):
        return max(shard_rows * parts // 16 // 16 * 16, 16)

    lead_full, far = gather_weights([lead], tokens[:, 0], sharing(3), 1)

    near = tokens[:, 0].reshape(micros, own_blocks, block_len, model)
    far = far.reshape(micros, own_blocks, block_len, model)
    slots = jnp.arange(blocks_row, dtype=jnp.int32)
    wanted = place * own_blocks + jnp.arange(own_blocks, dtype=jnp.int32)
    found = block_order[:, 0, None, :] == wanted[None, :, None]
    slot = jnp.sum(jnp.where(found, slots, 0), axis=2).reshape(-1)
    is_near = (slot // own_blocks == place).astype(jnp.int32)
    inside = slot % own_blocks
    x_input, normed, scales = ordered(
        near, far, inside * is_near, inside * (1 - is_near), is_near, norm_gain.reshape(1, model)
    )

    first_end = lengths[:, 0, 0]
    second_end = first_end + lengths[:, 0, 1]
    marks = [
        jnp.stack([first_end[micro], second_end[micro], base]).astype(jnp.int32)
        for micro in range(micros)
    ]
    positions = base + jnp.arange(count, dtype=jnp.int32)
    keep = jnp.concatenate([(positions < second_end[micro]) for micro in range(micros)])
    keep = keep.astype(f32)[:, None]

    cw, cb = conv_weight, conv_bias.reshape(1, inner)
    ccw, ccb = coupling_conv, coupling_bias.reshape(1, twice)
    sbias = jnp.pad(step_bias, (0, LANES - heads)).reshape(1, LANES)
    rate = jnp.pad(decay_rate, (0, LANES - heads)).reshape(1, LANES)
    skip = jnp.dot(
        skip_gain.reshape(1, heads), jnp.asarray(narrow[:heads], f32), precision=lax.Precision.HIGHEST
    )

    raw = jnp.dot(normed, lead_full, preferred_element_type=f32)
    rims = passed_along(
        jnp.stack([raw[(micro + 1) * count - 8 : (micro + 1) * count] for micro in range(micros)]),
        "context",
        1,
    )
    (y_own, states, finals, coupled, carry, reach, entering, gate_full, out_full) = forward_ssd(
        jnp.stack(marks), micros, raw, rims, inner, twice, count,
        cw, cb, ccw, ccb, sbias, rate, skip, sel, selcol,
        [in_weight[:, 0, :], jnp.transpose(out_weight)], sharing(3), 3,
    )
    entering = jnp.where(place == 0, 0.0, entering)
    cot = cotangent[:, 0].reshape(micros * count, model)
    out_grad = cot * keep.astype(bf16)
    gain_row = inner_gain.reshape(1, inner)
    mixer, gate_in, norm_grad, row_sums = gate_stage(
        normed, out_grad, gate_full, out_full, y_own, carry, coupled, entering, gain_row
    )
    row_sums = row_sums + paired(row_sums, "tensor")
    gated_norm, gate_grad, mixer_grad, own_pulls, inner_gain_rows = gate_back_stage(
        mixer, gate_in, norm_grad, carry, coupled, row_sums, gain_row, micros, inner_total
    )
    pulled = passed_along(own_pulls, "context", -1)
    out_term = lax.optimization_barrier(contract_rows(out_grad, gated_norm))
    gate_term = contract_rows(normed, gate_grad)
    branch = contract_cols(gated_norm, out_full)
    gate_part = contract_cols(gate_grad, gate_full)
    branch_other = paired(branch, "tensor")

    (
        lead_grad, tails, rims_grad, coupling_raw_grad, coupling_rims_grad,
        value_sums, coupling_sums, small_sums, skip_sums, out_shard, gate_shard,
    ) = backward_ssd(
        jnp.stack(marks), micros, raw, rims, inner, twice, count, mixer_grad, mixer, states,
        finals, entering, reach, pulled,
        cw, cb, ccw, ccb, sbias, rate, skip, sel, selcol, selt, [out_term, gate_term], [branch, gate_part], 2,
    )
    edges = passed_along(jnp.concatenate([rims_grad, coupling_rims_grad], axis=2), "context", -1)
    coupling_raw_grad = coupling_raw_grad.reshape(micros, count, twice) + jnp.pad(
        edges[:, :, inner:], ((0, 0), (count - 8, 0), (0, 0))
    )
    coupling_raw_grad = coupling_raw_grad + paired(coupling_raw_grad, "tensor")
    lane_ids = jnp.arange(twice, dtype=jnp.int32)
    own_lanes = ((lane_ids // width) == side).astype(bf16)
    coupling_low = (coupling_raw_grad.astype(bf16) * own_lanes).reshape(micros * count, twice)
    lead_grad = lax.dynamic_update_slice(lead_grad, coupling_low, (0, inner))
    tails = (tails + edges[:, :, :inner]).astype(bf16)
    for micro in range(micros):
        lead_grad = lax.dynamic_update_slice(
            lead_grad, tails[micro], ((micro + 1) * count - 8, 0)
        )
    normed_part = gate_part + contract_cols(lead_grad, lead_full)
    skip_sums = skip_sums[0].reshape(heads, head_size).sum(axis=1)
    coupling_sums = coupling_sums + paired(coupling_sums, "tensor")
    small = [value_sums[:5], coupling_sums[:5], small_sums[:2], skip_sums, inner_gain_rows[0]]
    small_rows = packed_rows(small)
    lead_shard, block_out, input_grad, summed = finish(
        contract_rows(normed, lead_grad), x_input, cot, scales,
        jnp.broadcast_to(keep, (micros * count, LANES)), branch, branch_other,
        normed_part, paired(normed_part, "tensor"), norm_gain.reshape(1, model), small_rows, 4,
    )
    flat = summed.reshape(-1)
    value_all, coupling_all, small_all, skip_all, inner_all = unpacked(flat, small)
    norm_all = flat[small_rows.size :]
    coupling_shard = lead_shard[:, inner : inner + twice]
    coupling_shard = coupling_shard + paired(coupling_shard, "tensor")
    return (
        block_out.reshape(micros, 1, count, model),
        input_grad.reshape(micros, 1, count, model),
        norm_all,
        woven(gate_shard, lead_shard, inner),
        coupling_shard,
        lead_shard[:, inner + twice : inner + twice + heads],
        jnp.transpose(out_shard),
        value_all[:4],
        value_all[4],
        coupling_all[:4],
        coupling_all[4],
        small_all[0, :heads],
        small_all[1, :heads],
        skip_all,
        inner_all,
    )


def contract_rows(left, right):
    return lax.dot_general(
        left, right, (((0,), (0,)), ((), ())), preferred_element_type=jnp.float32
    )


def contract_cols(left, right):
    return lax.dot_general(
        left, right, (((1,), (1,)), ((), ())), preferred_element_type=jnp.float32
    )


def solution(mesh):
    return jax.shard_map(
        shards,
        mesh=mesh,
        in_specs=(
            P(None, "fsdp", "context", None),
            P(None, "fsdp", None),
            P(None, "fsdp", None),
            P(None, "fsdp", "context", None),
            P(),
            P("fsdp", None, "tensor"),
            P("fsdp", None),
            P("fsdp", "tensor"),
            P("tensor", "fsdp"),
            P(None, "tensor"),
            P("tensor"),
            P(),
            P(),
            P("tensor"),
            P("tensor"),
            P("tensor"),
            P("tensor"),
        ),
        out_specs=(
            P(None, "fsdp", "context", None),
            P(None, "fsdp", "context", None),
            P(),
            P("fsdp", None, "tensor"),
            P("fsdp", None),
            P("fsdp", "tensor"),
            P("tensor", "fsdp"),
            P(None, "tensor"),
            P("tensor"),
            P(),
            P(),
            P("tensor"),
            P("tensor"),
            P("tensor"),
            P("tensor"),
        ),
        check_vma=False,
    )
```

```python
import functools

import jax
import jax.numpy as jnp
import numpy as np
from jax import lax
from jax.experimental import pallas as pl
from jax.experimental.pallas import tpu as pltpu
from jax.sharding import PartitionSpec as P

CHUNK = 128
LANES = 128
MESH = pl.DeviceIdType.MESH
f32 = jnp.float32
bf16 = jnp.bfloat16
epsilon = 1e-05


def split_two(value):
    high = value.astype(bf16)
    return high, (value - high.astype(f32)).astype(bf16)


def split_three(value):
    high = value.astype(bf16)
    rest = value - high.astype(f32)
    middle = rest.astype(bf16)
    return high, middle, (rest - middle.astype(f32)).astype(bf16)


def mm(left, right):
    return jnp.dot(left, right, preferred_element_type=f32)


def mm_nt(left, right):
    return lax.dot_general(left, right, (((1,), (1,)), ((), ())), preferred_element_type=f32)


def mm_three(left, right):
    wide = mm(left[0], jnp.concatenate([right[0], right[1]], axis=1))
    count = right[0].shape[1]
    return wide[:, :count] + wide[:, count:] + mm(left[1], right[0])


def mm_three_nt(left, right):
    return mm_nt(left[0], right[0]) + mm_nt(left[0], right[1]) + mm_nt(left[1], right[0])


def packed_parts(value, heads):
    high, middle, lowest = split_three(value)
    joined = (
        high.astype(f32)
        + pltpu.roll(middle.astype(f32), heads, 1)
        + pltpu.roll(lowest.astype(f32), 2 * heads, 1)
    )
    return joined.astype(bf16)


def segment_at(position, first_end, second_end):
    first_part = (position >= first_end).astype(jnp.int32)
    second_part = (position >= second_end).astype(jnp.int32)
    return jnp.where(position < 0, -1, first_part + second_part)


def chunk_frame(marks, chunk, step_raw, step_bias, rate, heads):
    first_end, second_end, base = marks[0], marks[1], marks[2]
    start = base + chunk * CHUNK
    rows = start + lax.broadcasted_iota(jnp.int32, (CHUNK, LANES), 0)
    columns = start + lax.broadcasted_iota(jnp.int32, (CHUNK, CHUNK), 1)
    seg_rows = segment_at(rows, first_end, second_end)
    seg_columns = segment_at(columns, first_end, second_end)
    seg_prior = segment_at(start - 1, first_end, second_end)
    seg_last = segment_at(start + CHUNK - 1, first_end, second_end)
    same = [
        (segment_at(rows - lag, first_end, second_end) == seg_rows).astype(f32) for lag in range(4)
    ]
    shifted = step_raw + step_bias
    step = jnp.maximum(shifted, 0.0) + jnp.log1p(jnp.exp(-jnp.abs(shifted)))
    lanes = lax.broadcasted_iota(jnp.int32, (CHUNK, LANES), 1)
    step = jnp.where(lanes < heads, step, 0.0)
    log_decay = -step * rate
    row_ids = lax.broadcasted_iota(jnp.int32, (CHUNK, CHUNK), 0)
    column_ids = lax.broadcasted_iota(jnp.int32, (CHUNK, CHUNK), 1)
    lower = (row_ids >= column_ids).astype(bf16)
    parts = split_three(log_decay)
    cumulative = mm(lower, parts[0]) + mm(lower, parts[1]) + mm(lower, parts[2])
    last = cumulative[CHUNK - 1 :, :]
    carry = jnp.exp(cumulative) * (seg_rows == seg_prior).astype(f32)
    tail = jnp.exp(last - cumulative) * (seg_rows == seg_last).astype(f32)
    live = lanes < heads
    carry = jnp.where(live, carry, 0.0)
    tail = jnp.where(live, tail, 0.0)
    return dict(
        seg_rows=seg_rows,
        seg_columns=seg_columns,
        row_ids=row_ids,
        column_ids=column_ids,
        same=same,
        step=step,
        shifted=shifted,
        cumulative=cumulative,
        carry=carry,
        tail=tail,
    )


def conv_sum(current, halo, weights, biases, same):
    full = jnp.concatenate([halo, current], axis=0)
    total = biases + weights(0) * current
    for lag in range(1, 4):
        total = total + weights(lag) * (pltpu.roll(full, lag, 0)[8:] * same[lag])
    return total


def logistic(value):
    return 1.0 / (1.0 + jnp.exp(-value))


def forward_kernel(heads, chunks, plan, *refs):
    (
        marks, vraw, vprev, vrim, craw, cprev, crim, sraw, cw, cb, ccw, ccb, sbias, rate, skip,
        sel, selcol,
    ) = refs[:17]
    arrays = plan.arrays
    weights, refs = refs[17 : 17 + arrays], refs[17 + arrays :]
    y_out, st_out, fin_out, bc_out, carry_out, cd_out, entering = refs[:7]
    fulls, refs = refs[7 : 7 + arrays], refs[7 + arrays :]
    (
        state, cumt, stack, cumpack, halo, same_s, bias_s, gram_s, cd_s, cparts, btparts,
        leaving, leave_send, leave_recv,
    ) = refs[:14]
    plan.bind(weights, fulls, refs[14:])
    grid_step = pl.program_id(0)
    steps = pl.num_programs(0)
    chunk = lax.rem(grid_step, chunks)
    micro = grid_step // chunks
    width = state.shape[0]
    early = {0: range(2)}
    for when in range(1, min(2 * chunks - 1, len(plan.order) - 1)):
        early[when] = [when + 1]
    placed = len(early)

    def leave_copy(which):
        return pltpu.make_async_remote_copy(
            src_ref=leaving.at[which], dst_ref=entering.at[which],
            send_sem=leave_send.at[which], recv_sem=leave_recv.at[which],
            device_id=plan.across, device_id_type=MESH,
        )

    for when, numbers in early.items():

        @pl.when(grid_step == when)
        def _(when=when, numbers=numbers):
            if when == 0:
                plan.greet()
            for number in numbers:
                plan.event(number)

    @pl.when(chunk == 0)
    def _():
        state[...] = jnp.zeros_like(state)
        cd_s[...] = jnp.ones_like(cd_s)
        cd_out[...] = jnp.zeros_like(cd_out)
        halo[...] = vrim[...]

    @pl.when(chunk > 0)
    def _():
        halo[...] = vprev[...]

    frame = chunk_frame([marks[micro, place] for place in range(3)], chunk, sraw[...], sbias[...], rate[...], heads)
    same = frame["same"]
    for lag in range(1, 4):
        same_s[lag - 1] = same[lag]
    joined = (frame["seg_rows"] == frame["seg_columns"]) & (frame["row_ids"] >= frame["column_ids"])
    bias_s[...] = jnp.where(joined, 0.0, -1e30)
    stack[0:CHUNK, :] = packed_parts(frame["step"], heads)
    stack[CHUNK : 2 * CHUNK, :] = packed_parts(frame["carry"], heads)
    stack[2 * CHUNK : 3 * CHUNK, :] = packed_parts(frame["tail"], heads)
    cumpack[...] = packed_parts(frame["cumulative"], heads)
    cumt[...] = jnp.transpose(frame["cumulative"])
    coupling_halo = jnp.where(chunk == 0, crim[...], cprev[...])
    wide_same = [None] + [jnp.concatenate([same[lag], same[lag]], axis=1) for lag in range(1, 4)]
    pre = conv_sum(
        craw[...], coupling_halo, lambda lag: ccw[lag : lag + 1, :], ccb[...], wide_same
    )
    coupled = pre * logistic(pre)
    bc_out[...] = coupled
    b_part = split_two(coupled[:, :width])
    c_part = split_two(coupled[:, width:])
    gram_s[...] = mm_three_nt(c_part, b_part)
    cparts[0] = c_part[0]
    cparts[1] = c_part[1]
    turned = jnp.transpose(coupled[:, :width])
    bt_part = split_two(turned)
    btparts[0] = bt_part[0]
    btparts[1] = bt_part[1]
    lane = lax.broadcasted_iota(jnp.int32, (CHUNK, LANES), 1)
    low_half = (lane < LANES // 2).astype(f32)
    high_half = 1.0 - low_half

    def pair(index, carried):
        cols = pl.ds(pl.multiple_of(index * LANES, LANES), LANES)
        wide = pl.ds(pl.multiple_of(index * 2 * LANES, 2 * LANES), 2 * LANES)
        pre_value = conv_sum(
            vraw[:, cols],
            halo[:, cols],
            lambda lag: cw[lag : lag + 1, cols],
            cb[:, cols],
            [None] + [same_s[lag - 1] for lag in range(1, 4)],
        )
        value = pre_value * logistic(pre_value)
        spread = mm(stack[...], sel[:, cols])
        step_e = spread[:CHUNK]
        carry_e = spread[CHUNK : 2 * CHUNK]
        tail_e = spread[2 * CHUNK :]
        inputs = step_e * value
        column = mm(cumpack[...], selcol[:, wide])
        row_pair = jnp.concatenate(
            [cumt[pl.ds(2 * index, 1), :], cumt[pl.ds(2 * index + 1, 1), :]], axis=1
        )
        bias = bias_s[...]
        gram = gram_s[...]
        mixing = jnp.concatenate([gram, gram], axis=1) * jnp.exp(
            column - row_pair + jnp.concatenate([bias, bias], axis=1)
        )
        mix_high, mix_low = split_two(mixing)
        in_low = split_two(inputs * low_half)
        in_high = split_two(inputs * high_half)
        diag_high = jnp.concatenate([in_low[0], in_high[0]], axis=0)
        diag_low = jnp.concatenate([in_low[1], in_high[1]], axis=0)
        both = mm(mix_high, jnp.concatenate([diag_high, diag_low], axis=1))
        inside = both[:, :LANES] + both[:, LANES:] + mm(mix_low, diag_high)
        held = state[:, cols]
        from_state = mm_three((cparts[0], cparts[1]), split_two(held))
        y_out[:, cols] = inside + carry_e * from_state + skip[:, cols] * value
        fresh = mm_three((btparts[0], btparts[1]), split_two(tail_e * inputs))
        through = carry_e[CHUNK - 1 :, :]
        st_out[0, :, cols] = held
        renewed = through * held + fresh
        state[:, cols] = renewed
        fin_out[:, cols] = renewed
        reach = cd_s[0:1, cols]
        carry_out[:, cols] = carry_e * reach
        cd_s[0:1, cols] = reach * through
        return carried

    eight_rows = lax.broadcasted_iota(jnp.int32, cd_out.shape, 0)
    cd_out[...] = jnp.where(eight_rows == chunk, cd_s[0:1, :], cd_out[...])
    lax.fori_loop(0, heads // 2, pair, 0, unroll=4)
    cd_out[...] = jnp.where(eight_rows == chunk + 1, cd_s[0:1, :], cd_out[...])

    @pl.when(chunk == chunks - 1)
    def _():
        leaving[micro] = state[...]
        leave_copy(micro).start()

    @pl.when(grid_step == steps - 1)
    def _():
        for number in range(placed + 1, len(plan.order)):
            plan.event(number)
        plan.finish()
        for which in range(leaving.shape[0]):
            leave_copy(which).wait()


def selectors(heads, head_size):
    inner = heads * head_size
    head_of_lane = np.arange(inner) // head_size
    narrow = np.zeros((LANES, inner), np.float32)
    wide = np.zeros((LANES, heads * LANES), np.float32)
    head_of_wide = np.arange(heads * LANES) // LANES
    for part in range(3):
        narrow[part * heads + head_of_lane, np.arange(inner)] = 1.0
        wide[part * heads + head_of_wide, np.arange(heads * LANES)] = 1.0
    return narrow, wide


def whole(shape):
    return pl.BlockSpec(shape, lambda index, *_: (0,) * len(shape))


def forward_ssd(
    marks, micros, raw, rims, inner, twice, tokens,
    cw, cb, ccw, ccb, sbias, rate, skip, sel, selcol, shards, shared, collective_id,
):
    width = twice // 2
    chunks = tokens // CHUNK
    heads = inner // (LANES // 2)
    eighth = CHUNK // 8
    pairs = lax.axis_size("fsdp") // 2
    shard_rows = shards[0].shape[0]
    plan = Gathering(shard_rows, pairs, [shard.shape[1] for shard in shards], 3, shared)

    def part(count, start):
        return pl.BlockSpec((CHUNK, count), lambda step: (step, start // count))

    def before(count, start):
        return pl.BlockSpec(
            (8, count), lambda step: (jnp.maximum(step * eighth - 1, 0), start // count)
        )

    def edge(count, start):
        return pl.BlockSpec((None, 8, count), lambda step: (step // chunks, 0, start // count))

    def each(*shape):
        return pl.BlockSpec((None, *shape), lambda step: (step // chunks, 0, 0))

    hbm = pl.BlockSpec(memory_space=pl.ANY)
    dma = pltpu.SemaphoreType.DMA
    return pl.pallas_call(
        functools.partial(forward_kernel, heads, chunks, plan),
        grid=(micros * chunks,),
        in_specs=[
            pl.BlockSpec(memory_space=pltpu.SMEM),
            part(inner, 0),
            before(inner, 0),
            edge(inner, 0),
            part(twice, inner),
            before(twice, inner),
            edge(twice, inner),
            part(LANES, inner + twice),
            whole(cw.shape),
            whole(cb.shape),
            whole(ccw.shape),
            whole(ccb.shape),
            whole(sbias.shape),
            whole(rate.shape),
            whole(skip.shape),
            whole(sel.shape),
            whole(selcol.shape),
        ]
        + [hbm] * len(shards),
        out_specs=[
            part(inner, 0),
            pl.BlockSpec((1, width, inner), lambda step: (step, 0, 0)),
            each(width, inner),
            part(twice, 0),
            part(inner, 0),
            each(8, inner),
            hbm,
        ]
        + [hbm] * len(shards),
        scratch_shapes=[
            pltpu.VMEM((width, inner), f32),
            pltpu.VMEM((LANES, CHUNK), f32),
            pltpu.VMEM((3 * CHUNK, LANES), bf16),
            pltpu.VMEM((CHUNK, LANES), bf16),
            pltpu.VMEM((8, inner), f32),
            pltpu.VMEM((3, CHUNK, LANES), f32),
            pltpu.VMEM((CHUNK, CHUNK), f32),
            pltpu.VMEM((CHUNK, CHUNK), f32),
            pltpu.VMEM((8, inner), f32),
            pltpu.VMEM((2, CHUNK, width), bf16),
            pltpu.VMEM((2, width, CHUNK), bf16),
            pltpu.VMEM((micros, width, inner), f32),
            dma((micros,)),
            dma((micros,)),
        ]
        + plan.scratch(),
        out_shape=[
            jax.ShapeDtypeStruct((micros * tokens, inner), f32),
            jax.ShapeDtypeStruct((micros * chunks, width, inner), f32),
            jax.ShapeDtypeStruct((micros, width, inner), f32),
            jax.ShapeDtypeStruct((micros * tokens, twice), f32),
            jax.ShapeDtypeStruct((micros * tokens, inner), f32),
            jax.ShapeDtypeStruct((micros, 8, inner), f32),
            jax.ShapeDtypeStruct((micros, width, inner), f32),
        ]
        + [
            jax.ShapeDtypeStruct((2 * pairs * shard_rows, shard.shape[1]), shard.dtype)
            for shard in shards
        ],
        compiler_params=pltpu.CompilerParams(
            collective_id=collective_id, has_side_effects=True, vmem_limit_bytes=48 * 1024 * 1024
        ),
    )(
        marks, raw, raw, rims, raw, raw, rims, raw, cw, cb, ccw, ccb, sbias, rate, skip, sel, selcol,
        *shards,
    )


def backward_kernel(heads, chunks, plan, waited, *refs):
    (
        marks, vraw, vprev, vrim, craw, cprev, crim, sraw, grad, mixer, st_now, st_next, fin,
        entering, cd, pulled, cw, cb, ccw, ccb, sbias, rate, skip, sel, selcol, selt,
    ) = refs[:26]
    arrays = len(plan.counts)
    refs = refs[26:]
    terms, refs = refs[:arrays], refs[arrays + waited :]
    (
        lead_g, vtail_g, vrim_g, craw_g, crim_g, cw_g, ccw_g, small_g, skip_g,
    ) = refs[:9]
    outs, refs = refs[9 : 9 + arrays], refs[9 + arrays :]
    (
        state, cumt, stack, cumpack, halo, same_s, bias_s, gram_s, cparts, bparts, ctparts,
        rim_s, crim_s, dgram, dcoup, dhead, cd_s,
    ) = refs[:17]
    plan.bind(terms, outs, refs[17:])
    grid_step = pl.program_id(0)
    step_id = lax.rem(grid_step, chunks)
    micro = grid_step // chunks
    chunk = chunks - 1 - step_id
    width = state.shape[0]
    inner = state.shape[1]
    per_step = -(-plan.steps // pl.num_programs(0))

    @pl.when(grid_step == 0)
    def _():
        plan.greet()
        cw_g[...] = jnp.zeros_like(cw_g)
        ccw_g[...] = jnp.zeros_like(ccw_g)
        small_g[...] = jnp.zeros_like(small_g)
        skip_g[...] = jnp.zeros_like(skip_g)

    def reduce_steps(first, count):
        def one(number, carried):
            plan.step(number)
            return carried

        start = grid_step * per_step + first
        lax.fori_loop(start, jnp.minimum(start + count, plan.steps), one, 0)

    @pl.when(step_id == 0)
    def _():
        state[...] = pulled[...]
        rim_s[...] = jnp.zeros_like(rim_s)
        crim_s[...] = jnp.zeros_like(crim_s)

    @pl.when(chunk == 0)
    def _():
        halo[...] = vrim[...]

    @pl.when(chunk > 0)
    def _():
        halo[...] = vprev[...]

    frame = chunk_frame([marks[micro, place] for place in range(3)], chunk, sraw[...], sbias[...], rate[...], heads)
    same = frame["same"]
    for lag in range(1, 4):
        same_s[lag - 1] = same[lag]
    joined = (frame["seg_rows"] == frame["seg_columns"]) & (frame["row_ids"] <= frame["column_ids"])
    bias_s[...] = jnp.where(joined, 0.0, -1e30)
    stack[0:CHUNK, :] = packed_parts(frame["step"], heads)
    stack[CHUNK : 2 * CHUNK, :] = packed_parts(frame["carry"], heads)
    stack[2 * CHUNK : 3 * CHUNK, :] = packed_parts(frame["tail"], heads)
    cumpack[...] = packed_parts(frame["cumulative"], heads)
    cumt[...] = jnp.transpose(frame["cumulative"])
    coupling_halo = jnp.where(chunk == 0, crim[...], cprev[...])
    wide_same = [None] + [jnp.concatenate([same[lag], same[lag]], axis=1) for lag in range(1, 4)]
    craw_now = craw[...]
    pre = conv_sum(craw_now, coupling_halo, lambda lag: ccw[lag : lag + 1, :], ccb[...], wide_same)
    csig = logistic(pre)
    coupled = pre * csig
    b_value = coupled[:, :width]
    c_value = coupled[:, width:]
    b_part = split_two(b_value)
    c_part = split_two(c_value)
    gram_s[...] = mm_three_nt(b_part, c_part)
    cparts[0] = c_part[0]
    cparts[1] = c_part[1]
    bparts[0] = b_part[0]
    bparts[1] = b_part[1]
    ct_part = split_two(jnp.transpose(c_value))
    ctparts[0] = ct_part[0]
    ctparts[1] = ct_part[1]
    dgram[...] = jnp.zeros_like(dgram)
    dcoup[...] = jnp.zeros_like(dcoup)
    dhead[...] = jnp.zeros_like(dhead)
    lane = lax.broadcasted_iota(jnp.int32, (CHUNK, LANES), 1)
    row = lax.broadcasted_iota(jnp.int32, (CHUNK, LANES), 0)
    low_half = (lane < LANES // 2).astype(f32)
    high_half = 1.0 - low_half
    last_row = (row == CHUNK - 1).astype(f32)
    is_end = step_id == 0
    eight_rows = lax.broadcasted_iota(jnp.int32, cd.shape, 0)
    for place in range(2):
        chosen = jnp.where(eight_rows == chunk + place, cd[...], 0.0)
        cd_s[place : place + 1, :] = jnp.sum(chosen, axis=0, keepdims=True)

    def pair(index):
        cols = pl.ds(pl.multiple_of(index * LANES, LANES), LANES)
        wide = pl.ds(pl.multiple_of(index * 2 * LANES, 2 * LANES), 2 * LANES)
        raw = vraw[:, cols]
        full = jnp.concatenate([halo[:, cols], raw], axis=0)
        lagged = [raw] + [pltpu.roll(full, lag, 0)[8:] * same_s[lag - 1] for lag in range(1, 4)]
        pre_value = cb[:, cols]
        for lag in range(4):
            pre_value = pre_value + cw[lag : lag + 1, cols] * lagged[lag]
        sig = logistic(pre_value)
        value = pre_value * sig
        spread = mm(stack[...], sel[:, cols])
        step_e = spread[:CHUNK]
        carry_e = spread[CHUNK : 2 * CHUNK]
        tail_e = spread[2 * CHUNK :]
        inputs = step_e * value
        grads = grad[:, cols]
        column = mm(cumpack[...], selcol[:, wide])
        row_pair = jnp.concatenate(
            [cumt[pl.ds(2 * index, 1), :], cumt[pl.ds(2 * index + 1, 1), :]], axis=1
        )
        bias = bias_s[...]
        gram = gram_s[...]
        decays = jnp.exp(row_pair - column + jnp.concatenate([bias, bias], axis=1))
        mixing = jnp.concatenate([gram, gram], axis=1) * decays
        mix_high, mix_low = split_two(mixing)
        g_low = split_two(grads * low_half)
        g_high = split_two(grads * high_half)
        diag_high = jnp.concatenate([g_low[0], g_high[0]], axis=0)
        diag_low = jnp.concatenate([g_low[1], g_high[1]], axis=0)
        both = mm(mix_high, jnp.concatenate([diag_high, diag_low], axis=1))
        input_g = both[:, :LANES] + both[:, LANES:] + mm(mix_low, diag_high)
        held_g = state[:, cols]
        held_parts = split_two(held_g)
        input_g = input_g + tail_e * mm_three((bparts[0], bparts[1]), held_parts)
        in_parts = split_two(inputs)
        outer = mm_three_nt(in_parts, (diag_high, diag_low)) * decays
        dgram[...] += outer[:, :CHUNK] + outer[:, CHUNK:]
        reach_now = cd_s[0:1, cols]
        reach_next = cd_s[1:2, cols]
        arriving = entering[:, cols]
        held = st_now[0, :, cols] + reach_now * arriving
        next_own = jnp.where(is_end, fin[:, cols], st_next[0, :, cols])
        following = next_own + reach_next * arriving
        carried_g = split_two(carry_e * grads)
        state[:, cols] = carry_e[CHUNK - 1 :, :] * held_g + mm_three(
            (ctparts[0], ctparts[1]), carried_g
        )
        dcoup[1] += mm_three_nt(carried_g, split_two(held))
        dcoup[0] += mm_three_nt(split_two(tail_e * inputs), held_parts)
        value_g = input_g * step_e + skip[:, cols] * grads
        kept = jnp.sum(held_g * following, axis=0, keepdims=True)
        balance = grads * (mixer[:, cols] - skip[:, cols] * value) - inputs * input_g
        balance = balance + last_row * kept
        sums = jnp.concatenate([balance, input_g * value], axis=0)
        sums_parts = split_three(sums)
        pick = selt[cols, :]
        dhead[...] += mm(sums_parts[0], pick) + mm(sums_parts[1], pick) + mm(sums_parts[2], pick)
        skip_g[0:1, cols] += jnp.sum(grads * value, axis=0, keepdims=True)
        pre_g = value_g * (sig * (1.0 + pre_value * (1.0 - sig)))
        cw_g[4:5, cols] += jnp.sum(pre_g, axis=0, keepdims=True)
        raw_g = cw[0:1, cols] * pre_g
        cw_g[0:1, cols] += jnp.sum(pre_g * raw, axis=0, keepdims=True)
        none = jnp.zeros((8, LANES), f32)
        edge = none
        for lag in range(1, 4):
            cw_g[lag : lag + 1, cols] += jnp.sum(pre_g * lagged[lag], axis=0, keepdims=True)
            weighted = cw[lag : lag + 1, cols] * (pre_g * same_s[lag - 1])
            padded = jnp.concatenate([none, weighted, none], axis=0)
            turned = pltpu.roll(padded, CHUNK + 16 - lag, 0)
            raw_g = raw_g + turned[8 : 8 + CHUNK]
            edge = edge + turned[:8]
        last_rows = raw_g[CHUNK - 8 :] + rim_s[:, cols]
        lead_g[:, cols] = jnp.concatenate([raw_g[: CHUNK - 8], last_rows], axis=0).astype(bf16)

        @pl.when(step_id == 0)
        def _():
            vtail_g[:, cols] = last_rows

        rim_s[:, cols] = edge
        vrim_g[:, cols] = edge

    groups = 4
    per_group = heads // 2 // groups

    def group(number, carried):
        for inside in range(per_group):
            pair(number * per_group + inside)
        share = per_step // (groups + 1)
        reduce_steps(number * share, share)
        return carried

    lax.fori_loop(0, groups, group, 0)
    used = groups * (per_step // (groups + 1))
    reduce_steps(used, per_step - used)

    total = dgram[...]
    total_parts = split_two(total)
    turned_parts = split_two(jnp.transpose(total))
    b_grad = dcoup[0] + mm_three(total_parts, (cparts[0], cparts[1]))
    c_grad = dcoup[1] + mm_three(turned_parts, (bparts[0], bparts[1]))
    coupled_g = jnp.concatenate([b_grad, c_grad], axis=1)
    pre_g = coupled_g * (csig * (1.0 + pre * (1.0 - csig)))
    ccw_g[4:5, :] += jnp.sum(pre_g, axis=0, keepdims=True)
    ccw_g[0:1, :] += jnp.sum(pre_g * craw_now, axis=0, keepdims=True)
    raw_g = ccw[0:1, :] * pre_g
    full = jnp.concatenate([coupling_halo, craw_now], axis=0)
    none = jnp.zeros((8, 2 * width), f32)
    edge = none
    for lag in range(1, 4):
        masked = pre_g * wide_same[lag]
        ccw_g[lag : lag + 1, :] += jnp.sum(
            masked * pltpu.roll(full, lag, 0)[8:], axis=0, keepdims=True
        )
        padded = jnp.concatenate([none, ccw[lag : lag + 1, :] * masked, none], axis=0)
        turned = pltpu.roll(padded, CHUNK + 16 - lag, 0)
        raw_g = raw_g + turned[8 : 8 + CHUNK]
        edge = edge + turned[:8]
    craw_g[...] = raw_g
    craw_g[CHUNK - 8 :, :] += crim_s[...]
    crim_s[...] = edge
    crim_g[...] = edge

    upper = (frame["row_ids"] <= frame["column_ids"]).astype(bf16)
    parts = split_three(dhead[:CHUNK])
    decay_g = mm(upper, parts[0]) + mm(upper, parts[1]) + mm(upper, parts[2])
    step_g = (dhead[CHUNK:] - rate[...] * decay_g) * logistic(frame["shifted"])
    lead_g[:, inner : inner + 2 * width] = jnp.zeros((CHUNK, 2 * width), bf16)
    lead_g[:, inner + 2 * width :] = step_g.astype(bf16)
    small_g[0:1, :] += jnp.sum(step_g, axis=0, keepdims=True)
    small_g[1:2, :] += jnp.sum(-frame["step"] * decay_g, axis=0, keepdims=True)


def backward_ssd(
    marks, micros, raw, rims, inner, twice, tokens, grad, mixer, states, fin, entering, cd, pulled,
    cw, cb, ccw, ccb, sbias, rate, skip, sel, selcol, selt, terms, first, collective_id,
):
    width = twice // 2
    chunks = tokens // CHUNK
    heads = inner // (LANES // 2)
    eighth = CHUNK // 8
    pairs = lax.axis_size("fsdp") // 2
    shard_rows = terms[0].shape[0] // (2 * pairs)
    plan = Reduction(shard_rows, pairs, [term.shape[1] for term in terms], 2)
    lead = inner + twice + LANES

    def row(step):
        return step // chunks * chunks + chunks - 1 - lax.rem(step, chunks)

    def part(count, start):
        return pl.BlockSpec((CHUNK, count), lambda step: (row(step), start // count))

    def before(count, start):
        return pl.BlockSpec(
            (8, count), lambda step: (jnp.maximum(row(step) * eighth - 1, 0), start // count)
        )

    def edge(count, start):
        return pl.BlockSpec(
            (None, 8, count), lambda step: (step // chunks, 0, start // count)
        )

    def held(offset):
        return pl.BlockSpec(
            (1, width, inner),
            lambda step: (
                jnp.minimum(row(step) + offset, (step // chunks + 1) * chunks - 1), 0, 0,
            ),
        )

    def each(*shape):
        return pl.BlockSpec((None, *shape), lambda step: (step // chunks, 0, 0))

    hbm = pl.BlockSpec(memory_space=pl.ANY)
    return pl.pallas_call(
        functools.partial(backward_kernel, heads, chunks, plan, len(first)),
        grid=(micros * chunks,),
        in_specs=[
            pl.BlockSpec(memory_space=pltpu.SMEM),
            part(inner, 0),
            before(inner, 0),
            edge(inner, 0),
            part(twice, inner),
            before(twice, inner),
            edge(twice, inner),
            part(LANES, inner + twice),
            part(inner, 0),
            part(inner, 0),
            held(0),
            held(1),
            each(width, inner),
            each(width, inner),
            each(8, inner),
            each(width, inner),
            whole(cw.shape),
            whole(cb.shape),
            whole(ccw.shape),
            whole(ccb.shape),
            whole(sbias.shape),
            whole(rate.shape),
            whole(skip.shape),
            whole(sel.shape),
            whole(selcol.shape),
            whole(selt.shape),
        ]
        + [hbm] * (len(terms) + len(first)),
        out_specs=[
            part(lead, 0),
            each(8, inner),
            each(8, inner),
            part(twice, 0),
            each(8, twice),
            whole((8, inner)),
            whole((8, twice)),
            whole((8, LANES)),
            whole((8, inner)),
        ]
        + [hbm] * len(terms),
        scratch_shapes=[
            pltpu.VMEM((width, inner), f32),
            pltpu.VMEM((LANES, CHUNK), f32),
            pltpu.VMEM((3 * CHUNK, LANES), bf16),
            pltpu.VMEM((CHUNK, LANES), bf16),
            pltpu.VMEM((8, inner), f32),
            pltpu.VMEM((3, CHUNK, LANES), f32),
            pltpu.VMEM((CHUNK, CHUNK), f32),
            pltpu.VMEM((CHUNK, CHUNK), f32),
            pltpu.VMEM((2, CHUNK, width), bf16),
            pltpu.VMEM((2, CHUNK, width), bf16),
            pltpu.VMEM((2, width, CHUNK), bf16),
            pltpu.VMEM((8, inner), f32),
            pltpu.VMEM((8, twice), f32),
            pltpu.VMEM((CHUNK, CHUNK), f32),
            pltpu.VMEM((2, CHUNK, width), f32),
            pltpu.VMEM((2 * CHUNK, LANES), f32),
            pltpu.VMEM((8, inner), f32),
        ]
        + plan.scratch(),
        out_shape=[
            jax.ShapeDtypeStruct((micros * tokens, lead), bf16),
            jax.ShapeDtypeStruct((micros, 8, inner), f32),
            jax.ShapeDtypeStruct((micros, 8, inner), f32),
            jax.ShapeDtypeStruct((micros * tokens, twice), f32),
            jax.ShapeDtypeStruct((micros, 8, twice), f32),
            jax.ShapeDtypeStruct((8, inner), f32),
            jax.ShapeDtypeStruct((8, twice), f32),
            jax.ShapeDtypeStruct((8, LANES), f32),
            jax.ShapeDtypeStruct((8, inner), f32),
        ]
        + [jax.ShapeDtypeStruct((shard_rows, term.shape[1]), f32) for term in terms],
        compiler_params=pltpu.CompilerParams(
            collective_id=collective_id, has_side_effects=True, vmem_limit_bytes=60 * 1024 * 1024
        ),
    )(
        marks, raw, raw, rims, raw, raw, rims, raw, grad, mixer, states, states, fin, entering,
        cd, pulled, cw, cb, ccw, ccb, sbias, rate, skip, sel, selcol, selt,
        *[term.reshape(pairs, 2, shard_rows, -1) for term in terms], *first,
    )


class Gathering:
    def __init__(self, rows, pairs, widths, cuts, shared):
        self.rows, self.pairs, self.shared = rows, pairs, shared
        self.arrays = len(widths)
        self.pieces = []
        for array, width in enumerate(widths):
            size = -(-width // LANES // cuts) * LANES
            self.pieces += [
                (array, start, min(size, width - start)) for start in range(0, width, size)
            ]
        self.moved = rows - shared
        self.early = min(rows // 8, self.moved - shared) // 16 * 16
        self.late = self.moved - self.early
        self.order = [(j, k) for j in range(len(self.pieces)) for k in range(pairs)]
        if pairs > 1:
            self.order.sort(key=lambda item: (item[0] * pairs + (item[1] or -0.5 - (item[0] > 0))))
        self.lag = 2

    def scratch(self):
        dma, pairs, arrays = pltpu.SemaphoreType.DMA, self.pairs, len(self.pieces)
        return [
            dma((arrays, max(pairs - 1, 1))),
            dma((arrays, max(pairs - 1, 1))),
            dma((arrays, pairs)),
            dma((arrays, pairs)),
            dma((arrays, 2 * pairs)),
            dma((arrays, 2 * pairs)),
            dma((arrays, 2 * pairs)),
            dma((arrays, 2 * pairs)),
            dma((arrays,)),
        ]

    def bind(self, weights, fulls, scratch):
        self.weights, self.fulls = weights, fulls
        (
            self.ring_send, self.ring_recv, self.pair_send, self.pair_recv,
            self.cross_send, self.cross_recv, self.early_send, self.early_recv, self.local,
        ) = scratch
        self.own, self.place = lax.axis_index("fsdp"), lax.axis_index("context")
        self.side = lax.axis_index("tensor")
        self.pair, self.member = self.own // 2, lax.rem(self.own, 2)
        pairs, pair, member = self.pairs, self.pair, self.member
        self.ahead = (2 * lax.rem(pair + 1, pairs) + member, self.place, self.side)
        self.behind = (2 * lax.rem(pair + pairs - 1, pairs) + member, self.place, self.side)
        self.partner = (2 * pair + 1 - member, self.place, self.side)
        self.across = (self.own, 1 - self.place, self.side)
        self.beside = (self.own, self.place, 1 - self.side)
        self.late_start = pl.multiple_of(self.place * (self.shared + self.early), 16)
        self.early_start = pl.multiple_of(
            self.place * self.shared + (1 - self.place) * self.late, 16
        )
        self.shared_start = pl.multiple_of(self.place * self.moved, 16)

    def greet(self, *others):
        barrier = pltpu.get_barrier_semaphore()
        devices = [self.ahead, self.behind, self.partner, self.across, *others]
        for device in devices:
            pl.semaphore_signal(barrier, inc=1, device_id=device, device_id_type=MESH)
        pl.semaphore_wait(barrier, len(devices))

    def part(self, j, k, which, start, size):
        there = lax.rem(self.pair + self.pairs - k, self.pairs)
        index = 2 * there + (self.member if which == 0 else 1 - self.member)
        array, first, width = self.pieces[j]
        rows = pl.ds(pl.multiple_of(index * self.rows + start, 16), size)
        return self.fulls[array].at[rows, pl.ds(first, width)]

    def source(self, j, k, which, start, size):
        if k == 0 and which == 0:
            array, first, width = self.pieces[j]
            return self.weights[array].at[pl.ds(start, size), pl.ds(first, width)]
        return self.part(j, k, which, start, size)

    def ring_copy(self, j, k):
        return pltpu.make_async_remote_copy(
            src_ref=self.source(j, k, 0, self.late_start, self.late),
            dst_ref=self.part(j, k, 0, self.late_start, self.late),
            send_sem=self.ring_send.at[j, k], recv_sem=self.ring_recv.at[j, k],
            device_id=self.ahead, device_id_type=MESH,
        )

    def pair_copy(self, j, k):
        return pltpu.make_async_remote_copy(
            src_ref=self.source(j, k, 0, self.late_start, self.late),
            dst_ref=self.part(j, k, 0, self.late_start, self.late),
            send_sem=self.pair_send.at[j, k], recv_sem=self.pair_recv.at[j, k],
            device_id=self.partner, device_id_type=MESH,
        )

    def early_copy(self, j, k, which):
        own = k == self.pairs - 1
        k = 0 if own else k
        slot = 2 * self.pairs - 2 if own else 2 * k + which
        return pltpu.make_async_remote_copy(
            src_ref=self.source(j, k, which, self.early_start, self.early),
            dst_ref=self.part(j, k, which, self.early_start, self.early),
            send_sem=self.early_send.at[j, slot], recv_sem=self.early_recv.at[j, slot],
            device_id=self.partner if own else self.ahead, device_id_type=MESH,
        )

    def early_event(self, j, k):
        last = self.pairs - 1
        if k == 0:
            self.early_copy(j, last, 0).start()
        else:
            self.early_copy(j, k - 1, 0).wait_recv()
        if k < last:
            self.early_copy(j, k, 0).start()
        if k == 1:
            self.early_copy(j, last, 0).wait_recv()
        elif k > 1:
            self.early_copy(j, k - 2, 1).wait_recv()
        if k > 0:
            self.early_copy(j, k - 1, 1).start()

    def cross_copy(self, j, k, which):
        here = self.part(j, k, which, self.shared_start, self.shared)
        return pltpu.make_async_remote_copy(
            src_ref=here, dst_ref=here,
            send_sem=self.cross_send.at[j, 2 * k + which], recv_sem=self.cross_recv.at[j, 2 * k + which],
            device_id=self.across, device_id_type=MESH,
        )

    def keep_copy(self, j):
        rows = pl.ds(pl.multiple_of(self.own * self.rows, 16), self.rows)
        return pltpu.make_async_copy(self.weights[j], self.fulls[j].at[rows, :], self.local.at[j])

    def event(self, number):
        j, k = self.order[number]
        if k > 0:
            self.ring_copy(j, k - 1).wait_recv()
        if number == 0:
            for array in range(self.arrays):
                self.keep_copy(array).start()
        if k < self.pairs - 1:
            self.ring_copy(j, k).start()
        self.pair_copy(j, k).start()
        if k > 0:
            self.cross_copy(j, k, 0).start()
        if self.early:
            self.early_event(j, k)
        if number >= self.lag:
            self.share(number - self.lag)

    def share(self, number):
        j, k = self.order[number]
        self.pair_copy(j, k).wait_recv()
        self.cross_copy(j, k, 1).start()

    def finish(self):
        for number in range(max(len(self.order) - self.lag, 0), len(self.order)):
            self.share(number)
        crossed = [(j, k, which) for j, k in self.order for which in range(2) if k or which]
        for item in crossed:
            self.cross_copy(*item).wait_recv()
        for j, k in self.order:
            if k < self.pairs - 1:
                self.ring_copy(j, k).wait_send()
            self.pair_copy(j, k).wait_send()
        for item in crossed:
            self.cross_copy(*item).wait_send()
        for j in range(len(self.pieces)):
            if self.early:
                last = self.pairs - 1
                if last:
                    self.early_copy(j, last - 1, 1).wait_recv()
                else:
                    self.early_copy(j, last, 0).wait_recv()
                self.early_copy(j, last, 0).wait_send()
                for k in range(last):
                    for which in range(2):
                        self.early_copy(j, k, which).wait_send()
        for array in range(self.arrays):
            self.keep_copy(array).wait()


def gather_kernel(plan, *refs):
    arrays = plan.arrays
    weights, tokens = refs[:arrays], refs[arrays]
    fulls, far = refs[arrays + 1 : 2 * arrays + 1], refs[2 * arrays + 1]
    extra_send, extra_recv = refs[2 * arrays + 2 : 2 * arrays + 4]
    plan.bind(weights, fulls, refs[2 * arrays + 4 :])
    plan.greet(plan.beside)
    half = tokens.shape[2] // 2
    lanes = pl.ds(pl.multiple_of(plan.side * half, 128), half)

    def token_copy(src, number, device):
        return pltpu.make_async_remote_copy(
            src_ref=src.at[:, :, lanes], dst_ref=far.at[:, :, lanes],
            send_sem=extra_send.at[number], recv_sem=extra_recv.at[number],
            device_id=device, device_id_type=MESH,
        )

    first, second = token_copy(tokens, 0, plan.across), token_copy(far, 1, plan.beside)
    first.start()
    for number in range(len(plan.order)):
        plan.event(number)
        if number == min(5, len(plan.order) - 1):
            first.wait_recv()
            second.start()
    second.wait_recv()
    plan.finish()
    first.wait_send()
    second.wait_send()


def gather_weights(shards, tokens, shared, collective_id):
    rows = shards[0].shape[0]
    pairs = lax.axis_size("fsdp") // 2
    count = len(shards)
    plan = Gathering(rows, pairs, [shard.shape[1] for shard in shards], 3, shared)
    hbm = pl.BlockSpec(memory_space=pl.ANY)
    dma = pltpu.SemaphoreType.DMA
    return pl.pallas_call(
        functools.partial(gather_kernel, plan),
        out_shape=[
            jax.ShapeDtypeStruct((2 * pairs * rows, shard.shape[1]), shard.dtype) for shard in shards
        ]
        + [jax.ShapeDtypeStruct(tokens.shape, tokens.dtype)],
        in_specs=[hbm] * (count + 1),
        out_specs=[hbm] * (count + 1),
        scratch_shapes=[dma((2,)), dma((2,))] + plan.scratch(),
        compiler_params=pltpu.CompilerParams(collective_id=collective_id, has_side_effects=True),
    )(*shards, tokens)


def order_kernel(near_index, far_index, is_near, near, far, gain, x_out, normed_out, scale_out):
    step = pl.program_id(0)
    near_now = is_near[step] == 1
    x = jnp.where(near_now, near[...], far[...])
    x_out[...] = x
    value = x.astype(f32)
    mean = jnp.sum(value * value, axis=-1, keepdims=True) * (1.0 / value.shape[-1])
    scale = lax.rsqrt(mean + epsilon)
    normed_out[...] = (value * scale * gain[...]).astype(bf16)
    scale_out[...] = jnp.broadcast_to(scale, scale_out.shape)


def ordered(near, far, near_index, far_index, is_near, gain):
    micros, count, length, model = near.shape
    blocks = micros * count

    def block(spec_index):
        return pl.BlockSpec((None, None, length, model), spec_index)

    def rows(lanes):
        return pl.BlockSpec((length, lanes), lambda step, *_: (step, 0))

    return pl.pallas_call(
        order_kernel,
        grid_spec=pltpu.PrefetchScalarGridSpec(
            num_scalar_prefetch=3,
            grid=(blocks,),
            in_specs=[
                block(lambda step, near_at, far_at, flags: (step // count, near_at[step], 0, 0)),
                block(lambda step, near_at, far_at, flags: (step // count, far_at[step], 0, 0)),
                pl.BlockSpec((1, model), lambda *_: (0, 0)),
            ],
            out_specs=[rows(model), rows(model), rows(LANES)],
        ),
        out_shape=[
            jax.ShapeDtypeStruct((blocks * length, model), bf16),
            jax.ShapeDtypeStruct((blocks * length, model), bf16),
            jax.ShapeDtypeStruct((blocks * length, LANES), f32),
        ],
        compiler_params=pltpu.CompilerParams(vmem_limit_bytes=32 * 1024 * 1024),
    )(near_index, far_index, is_near, near, far, gain)


def gate_kernel(
    normed, out_grad, gate_weight, out_weight, y_own, carry, coupled, entering, gain,
    mixer_out, gate_out, grad_out, sums_out,
):
    gate_in = mm(normed[...], gate_weight[...])
    grads = mm(out_grad[...], out_weight[...])
    width = entering.shape[0]
    arrived = mm_three(split_two(coupled[:, width:]), split_two(entering[...]))
    mixer = y_own[...] + carry[...] * arrived
    gated = mixer * (gate_in * logistic(gate_in))
    mixer_out[...] = mixer
    gate_out[...] = gate_in
    grad_out[...] = grads
    square = jnp.sum(gated * gated, axis=-1, keepdims=True)
    product = jnp.sum(grads * gain[...] * gated, axis=-1, keepdims=True)
    lane = lax.broadcasted_iota(jnp.int32, sums_out.shape, 1)
    sums_out[...] = jnp.where(lane == 0, square, jnp.where(lane == 1, product, 0.0))


def gate_stage(normed, out_grad, gate_weight, out_weight, y_own, carry, coupled, entering, gain):
    rows, model = normed.shape
    inner = y_own.shape[1]
    twice = coupled.shape[1]
    micros, width, _ = entering.shape
    size = 2 * CHUNK
    per_micro = rows // micros // size

    def block(lanes):
        return pl.BlockSpec((size, lanes), lambda step: (step, 0))

    return pl.pallas_call(
        gate_kernel,
        grid=(rows // size,),
        in_specs=[
            block(model),
            block(model),
            pl.BlockSpec((model, inner), lambda step: (0, 0), pipeline_mode=pl.Buffered(1)),
            pl.BlockSpec((model, inner), lambda step: (0, 0), pipeline_mode=pl.Buffered(1)),
            block(inner),
            block(inner),
            block(twice),
            pl.BlockSpec((None, width, inner), lambda step: (step // per_micro, 0, 0)),
            pl.BlockSpec((1, inner), lambda step: (0, 0)),
        ],
        out_specs=[block(inner), block(inner), block(inner), block(LANES)],
        out_shape=[jax.ShapeDtypeStruct((rows, inner), f32)] * 3
        + [jax.ShapeDtypeStruct((rows, LANES), f32)],
        compiler_params=pltpu.CompilerParams(vmem_limit_bytes=60 * 1024 * 1024),
        cost_estimate=pl.CostEstimate(
            flops=4 * rows * model * inner, bytes_accessed=24 * rows * inner, transcendentals=0
        ),
    )(normed, out_grad, gate_weight, out_weight, y_own, carry, coupled, entering, gain)


def gate_back_kernel(
    inner_total, per_micro, mixer, gate_in, grads, carry, coupled, sums, gain,
    norm_out, gate_out, mixer_out, pull_out, gain_out,
):
    step = pl.program_id(0)
    width = pull_out.shape[0]
    inv_norm = lax.rsqrt(sums[:, 0:1] / inner_total + epsilon)
    inner_dot = sums[:, 1:2] * (inv_norm * inv_norm * inv_norm) / inner_total
    mixer_now, gate_now, grad_now = mixer[...], gate_in[...], grads[...]
    sig = logistic(gate_now)
    act = gate_now * sig
    gated = mixer_now * act
    norm_out[...] = (gated * inv_norm * gain[...]).astype(bf16)
    gated_grad = grad_now * gain[...] * inv_norm - gated * inner_dot
    gate_out[...] = (gated_grad * mixer_now * sig * (1.0 + gate_now * (1.0 - sig))).astype(bf16)
    mixer_grad = gated_grad * act
    mixer_out[...] = mixer_grad

    @pl.when(step == 0)
    def _():
        gain_out[...] = jnp.zeros_like(gain_out)

    gain_out[0:1, :] += jnp.sum(grad_now * gated * inv_norm, axis=0, keepdims=True)

    @pl.when(lax.rem(step, per_micro) == 0)
    def _():
        pull_out[...] = jnp.zeros_like(pull_out)

    turned = split_two(jnp.transpose(coupled[:, width:]))
    pull_out[...] += mm_three(turned, split_two(carry[...] * mixer_grad))


def gate_back_stage(mixer, gate_in, grads, carry, coupled, sums, gain, micros, inner_total):
    rows, inner = mixer.shape
    twice = coupled.shape[1]
    width = twice // 2
    per_micro = rows // micros // CHUNK

    def block(lanes):
        return pl.BlockSpec((CHUNK, lanes), lambda step: (step, 0))

    return pl.pallas_call(
        functools.partial(gate_back_kernel, inner_total, per_micro),
        grid=(rows // CHUNK,),
        in_specs=[
            block(inner),
            block(inner),
            block(inner),
            block(inner),
            block(twice),
            block(LANES),
            pl.BlockSpec((1, inner), lambda step: (0, 0)),
        ],
        out_specs=[
            block(inner),
            block(inner),
            block(inner),
            pl.BlockSpec((None, width, inner), lambda step: (step // per_micro, 0, 0)),
            pl.BlockSpec((8, inner), lambda step: (0, 0)),
        ],
        out_shape=[
            jax.ShapeDtypeStruct((rows, inner), bf16),
            jax.ShapeDtypeStruct((rows, inner), bf16),
            jax.ShapeDtypeStruct((rows, inner), f32),
            jax.ShapeDtypeStruct((micros, width, inner), f32),
            jax.ShapeDtypeStruct((8, inner), f32),
        ],
        compiler_params=pltpu.CompilerParams(vmem_limit_bytes=48 * 1024 * 1024),
        cost_estimate=pl.CostEstimate(
            flops=8 * rows * width * inner, bytes_accessed=24 * rows * inner, transcendentals=0
        ),
    )(mixer, gate_in, grads, carry, coupled, sums, gain)


def weave_kernel(first, second, out):
    out[:, 0, :] = first[...]
    out[:, 1, :] = second[...]


def woven(first, second, columns):
    rows = first.shape[0]
    size = 32
    block = pl.BlockSpec((size, columns), lambda step: (step, 0))
    return pl.pallas_call(
        weave_kernel,
        grid=(rows // size,),
        in_specs=[block, block],
        out_specs=pl.BlockSpec((size, 2, columns), lambda step: (step, 0, 0)),
        out_shape=jax.ShapeDtypeStruct((rows, 2, columns), first.dtype),
    )(first, second)


class Reduction:
    def __init__(self, rows, pairs, columns, lag):
        self.rows, self.pairs, self.columns, self.lag = rows, pairs, columns, lag
        self.shared = rows // 4
        self.moved = rows - self.shared
        self.counts = [count // LANES for count in columns]
        self.count = sum(self.counts)
        self.steps = self.count + 4 * lag

    def scratch(self):
        shared, moved, pairs, count = self.shared, self.moved, self.pairs, self.count
        cross, pair, ring = 2 * pairs * shared + 16, pairs * moved + 16, moved + 16
        i16, dma = jnp.int16, pltpu.SemaphoreType.DMA
        return [
            pltpu.VMEM((count, cross, LANES), i16),
            pltpu.VMEM((count, pair, LANES), i16),
            pltpu.VMEM((count, pairs - 1, ring, LANES), i16),
            pltpu.VMEM((count, ring, LANES), i16),
            pltpu.VMEM((2, cross, LANES), i16),
            pltpu.VMEM((2, pair, LANES), i16),
            pltpu.VMEM((2, pairs - 1, ring, LANES), i16),
            pltpu.VMEM((2, ring, LANES), i16),
            pltpu.VMEM((2, pairs, 2, shared, LANES), f32),
            pltpu.VMEM((2, pairs, moved, LANES), f32),
            pltpu.VMEM((2, pairs, moved, LANES), f32),
            pltpu.VMEM((2 * self.lag, moved, LANES), f32),
            pltpu.VMEM((2 * self.lag, moved, LANES), f32),
            pltpu.VMEM((2, self.rows, LANES), f32),
            dma((count,)),
            dma((count,)),
            dma((pairs - 1, count)),
            dma((count,)),
            dma((2,)),
            dma((2,)),
            dma((pairs - 1, 2)),
            dma((2,)),
            dma((3, 2)),
            dma((2,)),
        ]

    def bind(self, terms, outs, scratch):
        self.terms, self.outs = terms, outs
        (
            self.cross_in, self.pair_in, self.ring_in, self.last_in,
            self.cross_out, self.pair_out, self.ring_out, self.last_out,
            self.cross_term, self.pair_term, self.ring_term,
            self.kept, self.held, self.result,
            self.cross_recv, self.pair_recv, self.ring_recv, self.last_recv,
            self.cross_sent, self.pair_sent, self.ring_sent, self.last_sent,
            self.loaded, self.stored,
        ) = scratch
        self.own, self.place = lax.axis_index("fsdp"), lax.axis_index("context")
        self.side = lax.axis_index("tensor")
        self.pair, self.member = self.own // 2, lax.rem(self.own, 2)
        self.across = (self.own, 1 - self.place, self.side)
        self.partner = (2 * self.pair + 1 - self.member, self.place, self.side)
        self.inset = pl.multiple_of(self.place * (self.moved - self.shared), 16)
        self.start = pl.multiple_of(self.place * self.shared, 16)

    def peer(self, offset):
        there = lax.rem(self.pair + offset, self.pairs)
        return (2 * there + self.member, self.place, self.side)

    def greet(self):
        barrier = pltpu.get_barrier_semaphore()
        devices = [self.across, self.partner] + [self.peer(k) for k in range(1, self.pairs)]
        for device in devices:
            pl.semaphore_signal(barrier, inc=1, device_id=device, device_id_type=MESH)
        pl.semaphore_wait(barrier, len(devices))

    def cross_copy(self, chunk):
        slot = lax.rem(chunk, 2)
        return pltpu.make_async_remote_copy(
            src_ref=self.cross_out.at[slot], dst_ref=self.cross_in.at[chunk],
            send_sem=self.cross_sent.at[slot], recv_sem=self.cross_recv.at[chunk],
            device_id=self.across, device_id_type=MESH,
        )

    def pair_copy(self, chunk):
        slot = lax.rem(chunk, 2)
        return pltpu.make_async_remote_copy(
            src_ref=self.pair_out.at[slot], dst_ref=self.pair_in.at[chunk],
            send_sem=self.pair_sent.at[slot], recv_sem=self.pair_recv.at[chunk],
            device_id=self.partner, device_id_type=MESH,
        )

    def ring_copy(self, chunk, offset):
        slot = lax.rem(chunk, 2)
        return pltpu.make_async_remote_copy(
            src_ref=self.ring_out.at[slot, offset - 1], dst_ref=self.ring_in.at[chunk, offset - 1],
            send_sem=self.ring_sent.at[offset - 1, slot],
            recv_sem=self.ring_recv.at[offset - 1, chunk],
            device_id=self.peer(offset), device_id_type=MESH,
        )

    def last_copy(self, chunk):
        slot = lax.rem(chunk, 2)
        return pltpu.make_async_remote_copy(
            src_ref=self.last_out.at[slot], dst_ref=self.last_in.at[chunk],
            send_sem=self.last_sent.at[slot], recv_sem=self.last_recv.at[chunk],
            device_id=self.across, device_id_type=MESH,
        )

    def load_copy(self, stage, term, cols, slot):
        if stage == 0:
            rows = pl.ds(pl.multiple_of((1 - self.place) * self.moved, 16), self.shared)
            src, dst = term.at[:, :, rows, cols], self.cross_term.at[slot]
        elif stage == 1:
            src = term.at[:, 1 - self.member, pl.ds(self.start, self.moved), cols]
            dst = self.pair_term.at[slot]
        else:
            src = term.at[:, self.member, pl.ds(self.start, self.moved), cols]
            dst = self.ring_term.at[slot]
        return pltpu.make_async_copy(src, dst, self.loaded.at[stage, slot])

    def each_array(self, chunk, act):
        first = 0
        for number, count in enumerate(self.counts):
            inside = (chunk >= first) & (chunk < first + count)
            offset = first

            @pl.when(inside)
            def _(number=number, offset=offset):
                act(number, pl.ds(pl.multiple_of((chunk - offset) * LANES, LANES), LANES))

            first += count

    def load(self, stage, chunk):
        @pl.when((chunk >= 0) & (chunk < self.count))
        def _():
            self.each_array(
                chunk,
                lambda number, cols: self.load_copy(
                    stage, self.terms[number], cols, lax.rem(chunk, 2)
                ).start(),
            )

    def loaded_now(self, stage, chunk):
        self.load_copy(stage, self.terms[0], pl.ds(0, LANES), lax.rem(chunk, 2)).wait()

    @staticmethod
    def encode(value, out, place):
        count = value.shape[0]
        peak = jnp.maximum(jnp.max(jnp.abs(value), axis=0, keepdims=True), 1e-30)
        exponent = jnp.ceil(jnp.log(peak) * 1.4426950408889634)
        factor = jnp.exp(exponent * -0.6931471805599453) * 32000.0
        out[place + (pl.ds(0, count), slice(None))] = (
            (value * factor + 12582912.0 - 12582912.0).astype(jnp.int32).astype(jnp.int16)
        )
        out[place + (pl.ds(count, 16), slice(None))] = (
            jnp.broadcast_to(exponent, (16, LANES)).astype(jnp.int32).astype(jnp.int16)
        )

    @staticmethod
    def unit(ref, place, count):
        exponents = ref[place + (pl.ds(count, 16), slice(None))].astype(jnp.int32).astype(f32)
        return jnp.exp(exponents[:1] * 0.6931471805599453) * (1.0 / 32000.0)

    @staticmethod
    def decode(ref, place, first, count, unit):
        first = pl.multiple_of(first, 16) if not isinstance(first, int) else first
        return ref[place + (pl.ds(first, count), slice(None))].astype(jnp.int32).astype(f32) * unit

    def step(self, number):
        lag, pairs, shared, moved = self.lag, self.pairs, self.shared, self.moved

        @pl.when(number == 0)
        def _():
            self.load(0, number)

        self.load(0, number + 1)
        self.load(1, number + 1 - lag)
        self.load(2, number + 1 - 2 * lag)

        def stage(index, act):
            chunk = number - index * lag

            @pl.when((chunk >= 0) & (chunk < self.count))
            def _():
                act(chunk, lax.rem(chunk, 2))

        def cross(chunk, slot):
            self.loaded_now(0, chunk)

            @pl.when(chunk >= 2)
            def _():
                self.cross_copy(chunk - 2).wait_send()

            value = self.cross_term[slot].reshape(2 * pairs * shared, LANES)
            self.encode(value, self.cross_out, (slot,))
            self.cross_copy(chunk).start()

        def pair(chunk, slot):
            self.loaded_now(1, chunk)
            self.cross_copy(chunk).wait_recv()

            @pl.when(chunk >= 2)
            def _():
                self.pair_copy(chunk - 2).wait_send()

            unit = self.unit(self.cross_in, (chunk,), 2 * pairs * shared)
            for there in range(pairs):
                first = (2 * there + 1 - self.member) * shared
                self.pair_term[slot, there, pl.ds(self.inset, shared), :] += self.decode(
                    self.cross_in, (chunk,), first, shared, unit
                )
            value = self.pair_term[slot].reshape(pairs * moved, LANES)
            self.encode(value, self.pair_out, (slot,))
            self.pair_copy(chunk).start()

        def ring(chunk, slot):
            self.loaded_now(2, chunk)
            self.pair_copy(chunk).wait_recv()

            @pl.when(chunk >= 2)
            def _():
                for offset in range(1, pairs):
                    self.ring_copy(chunk - 2, offset).wait_send()

            cross_unit = self.unit(self.cross_in, (chunk,), 2 * pairs * shared)
            pair_unit = self.unit(self.pair_in, (chunk,), pairs * moved)
            for offset in list(range(1, pairs)) + [0]:
                there = lax.rem(self.pair + offset, pairs)
                first = (2 * there + self.member) * shared
                self.ring_term[slot, there, pl.ds(self.inset, shared), :] += self.decode(
                    self.cross_in, (chunk,), first, shared, cross_unit
                )
                value = self.ring_term[slot, there] + self.decode(
                    self.pair_in, (chunk,), there * moved, moved, pair_unit
                )
                if offset:
                    self.encode(value, self.ring_out, (slot, offset - 1))
                    self.ring_copy(chunk, offset).start()
                else:
                    self.kept[lax.rem(chunk, 2 * lag)] = value

        def last(chunk, slot):
            for offset in range(1, pairs):
                self.ring_copy(chunk, offset).wait_recv()

            @pl.when(chunk >= 2)
            def _():
                self.last_copy(chunk - 2).wait_send()

            total = self.kept[lax.rem(chunk, 2 * lag)]
            for offset in range(1, pairs):
                place = (chunk, offset - 1)
                total = total + self.decode(
                    self.ring_in, place, 0, moved, self.unit(self.ring_in, place, moved)
                )
            self.encode(total, self.last_out, (slot,))
            self.held[lax.rem(chunk, 2 * lag)] = self.decode(
                self.last_out, (slot,), 0, moved, self.unit(self.last_out, (slot,), moved)
            )
            self.last_copy(chunk).start()

        def write_copy(number, cols, slot):
            return pltpu.make_async_copy(
                self.result.at[slot], self.outs[number].at[:, cols], self.stored.at[slot]
            )

        def write(chunk, slot):
            self.last_copy(chunk).wait_recv()

            @pl.when(chunk >= 2)
            def _():
                write_copy(0, pl.ds(0, LANES), slot).wait()

            mine = self.held[lax.rem(chunk, 2 * lag)]
            other = self.decode(
                self.last_in, (chunk,), 0, moved, self.unit(self.last_in, (chunk,), moved)
            )
            low = jnp.where(self.place == 0, mine, other)
            high = jnp.where(self.place == 0, other, mine)
            self.result[slot, pl.ds(0, shared), :] = low[:shared]
            self.result[slot, pl.ds(shared, moved - shared), :] = (
                low[shared:] + high[: moved - shared]
            )
            self.result[slot, pl.ds(moved, shared), :] = high[moved - shared :]
            self.each_array(chunk, lambda which, cols: write_copy(which, cols, slot).start())

        stage(4, write)
        stage(3, last)
        stage(2, ring)
        stage(1, pair)
        stage(0, cross)

        @pl.when(number == self.steps - 1)
        def _():
            for slot in range(2):
                write_copy(0, pl.ds(0, LANES), slot).wait()
                self.cross_copy(jnp.int32(self.count - 2 + slot)).wait_send()
                self.pair_copy(jnp.int32(self.count - 2 + slot)).wait_send()
                self.last_copy(jnp.int32(self.count - 2 + slot)).wait_send()
                for offset in range(1, pairs):
                    self.ring_copy(jnp.int32(self.count - 2 + slot), offset).wait_send()


def finish_kernel(plan, blocks, *refs):
    (
        term, x, cot, scale, keep, branch, branch_other, part, part_other, gain, small,
        out, block_out, input_out, small_out,
        gain_sum, cross_in, pair_out, pair_in, ring_in,
        cross_send, cross_recv, pair_send, pair_recv, ring_send, ring_recv, final_sem,
    ) = refs[:27]
    plan.bind([term], [out], refs[27:])
    step = pl.program_id(0)

    @pl.when(step == 0)
    def _():
        plan.greet()
        gain_sum[...] = jnp.zeros_like(gain_sum)

    @pl.when(step < plan.steps)
    def _():
        plan.step(step)

    @pl.when(step < blocks)
    def _():
        x_float = x[...].astype(f32)
        block_out[...] = (x_float + keep[:, 0:1] * (branch[...] + branch_other[...])).astype(bf16)
        inv_rms = scale[:, 0:1]
        x_hat = x_float * inv_rms
        normed_grad = part[...] + part_other[...]
        hat_grad = normed_grad * gain[...]
        mean = jnp.sum(hat_grad * x_hat, axis=-1, keepdims=True) * (1.0 / x_float.shape[-1])
        input_out[...] = (cot[...].astype(f32) + inv_rms * (hat_grad - x_hat * mean)).astype(bf16)
        gain_sum[0:1, :] += jnp.sum(normed_grad * x_hat, axis=0, keepdims=True)

    rows = small.shape[0]
    lines = gain_sum.shape[1] // LANES

    def cross_copy():
        return pltpu.make_async_remote_copy(
            src_ref=pair_out, dst_ref=cross_in, send_sem=cross_send.at[0], recv_sem=cross_recv.at[0],
            device_id=plan.across, device_id_type=MESH,
        )

    def pair_copy():
        return pltpu.make_async_remote_copy(
            src_ref=pair_out, dst_ref=pair_in, send_sem=pair_send.at[0], recv_sem=pair_recv.at[0],
            device_id=plan.partner, device_id_type=MESH,
        )

    def ring_copy(offset):
        return pltpu.make_async_remote_copy(
            src_ref=ring_in.at[0], dst_ref=ring_in.at[plan.pairs - offset],
            send_sem=ring_send.at[offset - 1], recv_sem=ring_recv.at[offset - 1],
            device_id=plan.peer(offset), device_id_type=MESH,
        )

    @pl.when(step == blocks)
    def _():
        pair_out[pl.ds(0, rows), :] = small[...]
        for line in range(lines):
            pair_out[rows + line : rows + line + 1, :] = gain_sum[
                0:1, line * LANES : (line + 1) * LANES
            ]
        cross_copy().start()

    @pl.when(step == blocks + 2)
    def _():
        cross_copy().wait()
        pair_out[...] += cross_in[...]
        pair_copy().start()

    @pl.when(step == blocks + 4)
    def _():
        pair_copy().wait()
        ring_in[0] = pair_out[...] + pair_in[...]
        for offset in range(1, plan.pairs):
            ring_copy(offset).start()

    @pl.when(step == blocks + 6)
    def _():
        for offset in range(1, plan.pairs):
            ring_copy(offset).wait()
        total = jnp.zeros_like(pair_out)
        for index in range(plan.pairs):
            total = total + ring_in[lax.rem(index + plan.pairs - plan.pair, plan.pairs)]
        pair_in[...] = total
        copy = pltpu.make_async_copy(pair_in, small_out, final_sem.at[0])
        copy.start()
        copy.wait()


def finish(term, x, cot, scale, keep, branch, branch_other, part, part_other, gain, small, collective_id):
    pairs = lax.axis_size("fsdp") // 2
    shard_rows = term.shape[0] // (2 * pairs)
    plan = Reduction(shard_rows, pairs, [term.shape[1]], 2)
    rows, model = x.shape
    size = 64
    blocks = rows // size
    steps = max(plan.steps, blocks + 7)
    total_rows = small.shape[0] + model // LANES
    hbm = pl.BlockSpec(memory_space=pl.ANY)
    dma = pltpu.SemaphoreType.DMA

    def block(lanes):
        return pl.BlockSpec((size, lanes), lambda step: (jnp.minimum(step, blocks - 1), 0))

    def constant(shape):
        return pl.BlockSpec(shape, lambda step: (0, 0))

    return pl.pallas_call(
        functools.partial(finish_kernel, plan, blocks),
        grid=(steps,),
        in_specs=[hbm]
        + [block(lanes) for lanes in (model, model, LANES, LANES, model, model, model, model)]
        + [constant((1, model)), constant(small.shape)],
        out_specs=[hbm, block(model), block(model), hbm],
        out_shape=[
            jax.ShapeDtypeStruct((shard_rows, term.shape[1]), f32),
            jax.ShapeDtypeStruct((rows, model), bf16),
            jax.ShapeDtypeStruct((rows, model), bf16),
            jax.ShapeDtypeStruct((total_rows, LANES), f32),
        ],
        scratch_shapes=[
            pltpu.VMEM((8, model), f32),
            pltpu.VMEM((total_rows, LANES), f32),
            pltpu.VMEM((total_rows, LANES), f32),
            pltpu.VMEM((total_rows, LANES), f32),
            pltpu.VMEM((pairs, total_rows, LANES), f32),
            dma((1,)),
            dma((1,)),
            dma((1,)),
            dma((1,)),
            dma((max(pairs - 1, 1),)),
            dma((max(pairs - 1, 1),)),
            dma((1,)),
        ]
        + plan.scratch(),
        compiler_params=pltpu.CompilerParams(
            collective_id=collective_id, has_side_effects=True, vmem_limit_bytes=56 * 1024 * 1024
        ),
    )(
        term.reshape(pairs, 2, shard_rows, -1), x, cot, scale, keep, branch, branch_other, part,
        part_other, gain, small,
    )


def passed_along(value, axis, steps):
    count = lax.axis_size(axis)
    initial, last = (max(0, -steps), min(count, count - steps))
    return lax.ppermute(value, axis, [(source, source + steps) for source in range(initial, last)])


def paired(value, axis):
    count = lax.axis_size(axis)
    return lax.ppermute(value, axis, [(source, source ^ 1) for source in range(count)])


def ring_shift(value, axis, steps):
    count = lax.axis_size(axis)
    return lax.ppermute(
        value, axis, [(source, (source + 2 * steps) % count) for source in range(count)]
    )


def packed_rows(values):
    flat = jnp.concatenate([value.reshape(-1) for value in values])
    return jnp.pad(flat, (0, -flat.shape[0] % 1024)).reshape(-1, LANES)


def unpacked(flat, values):
    results, start = [], 0
    for value in values:
        results.append(flat[start : start + value.size].reshape(value.shape))
        start += value.size
    return results


def shards(
    tokens,
    lengths,
    block_order,
    cotangent,
    norm_gain,
    in_weight,
    coupling_weight,
    step_weight,
    out_weight,
    conv_weight,
    conv_bias,
    coupling_conv,
    coupling_bias,
    step_bias,
    decay_rate,
    skip_gain,
    inner_gain,
):
    micros = tokens.shape[0]
    count = tokens.shape[2]
    model = tokens.shape[3]
    inner = inner_gain.shape[0]
    heads = step_bias.shape[0]
    head_size = inner // heads
    twice = coupling_weight.shape[1]
    width = twice // 2
    blocks_row = block_order.shape[2]
    block_len = count * lax.axis_size("context") // blocks_row
    own_blocks = count // block_len
    inner_total = inner * lax.axis_size("tensor")
    side = lax.axis_index("tensor")
    place = lax.axis_index("context")
    base = place * count
    shard_rows = in_weight.shape[0]

    narrow, wide_columns = selectors(heads, head_size)
    sel = jnp.asarray(narrow, bf16)
    selcol = jnp.asarray(wide_columns, bf16)
    selt = jnp.asarray(narrow[:heads].T, bf16)
    selt = jnp.pad(selt, ((0, 0), (0, LANES - heads)))

    lead = jnp.concatenate(
        [
            in_weight[:, 1, :],
            coupling_weight,
            jnp.pad(step_weight, ((0, 0), (0, LANES - heads))),
        ],
        axis=1,
    )
    def sharing(parts):
        return max(shard_rows * parts // 16 // 16 * 16, 16)

    lead_full, far = gather_weights([lead], tokens[:, 0], sharing(3), 1)

    near = tokens[:, 0].reshape(micros, own_blocks, block_len, model)
    far = far.reshape(micros, own_blocks, block_len, model)
    slots = jnp.arange(blocks_row, dtype=jnp.int32)
    wanted = place * own_blocks + jnp.arange(own_blocks, dtype=jnp.int32)
    found = block_order[:, 0, None, :] == wanted[None, :, None]
    slot = jnp.sum(jnp.where(found, slots, 0), axis=2).reshape(-1)
    is_near = (slot // own_blocks == place).astype(jnp.int32)
    inside = slot % own_blocks
    x_input, normed, scales = ordered(
        near, far, inside * is_near, inside * (1 - is_near), is_near, norm_gain.reshape(1, model)
    )

    first_end = lengths[:, 0, 0]
    second_end = first_end + lengths[:, 0, 1]
    marks = [
        jnp.stack([first_end[micro], second_end[micro], base]).astype(jnp.int32)
        for micro in range(micros)
    ]
    positions = base + jnp.arange(count, dtype=jnp.int32)
    keep = jnp.concatenate([(positions < second_end[micro]) for micro in range(micros)])
    keep = keep.astype(f32)[:, None]

    cw, cb = conv_weight, conv_bias.reshape(1, inner)
    ccw, ccb = coupling_conv, coupling_bias.reshape(1, twice)
    sbias = jnp.pad(step_bias, (0, LANES - heads)).reshape(1, LANES)
    rate = jnp.pad(decay_rate, (0, LANES - heads)).reshape(1, LANES)
    skip = jnp.dot(
        skip_gain.reshape(1, heads), jnp.asarray(narrow[:heads], f32), precision=lax.Precision.HIGHEST
    )

    raw = jnp.dot(normed, lead_full, preferred_element_type=f32)
    rims = passed_along(
        jnp.stack([raw[(micro + 1) * count - 8 : (micro + 1) * count] for micro in range(micros)]),
        "context",
        1,
    )
    (y_own, states, finals, coupled, carry, reach, entering, gate_full, out_full) = forward_ssd(
        jnp.stack(marks), micros, raw, rims, inner, twice, count,
        cw, cb, ccw, ccb, sbias, rate, skip, sel, selcol,
        [in_weight[:, 0, :], jnp.transpose(out_weight)], sharing(3), 3,
    )
    entering = jnp.where(place == 0, 0.0, entering)
    cot = cotangent[:, 0].reshape(micros * count, model)
    out_grad = cot * keep.astype(bf16)
    gain_row = inner_gain.reshape(1, inner)
    mixer, gate_in, norm_grad, row_sums = gate_stage(
        normed, out_grad, gate_full, out_full, y_own, carry, coupled, entering, gain_row
    )
    row_sums = row_sums + paired(row_sums, "tensor")
    gated_norm, gate_grad, mixer_grad, own_pulls, inner_gain_rows = gate_back_stage(
        mixer, gate_in, norm_grad, carry, coupled, row_sums, gain_row, micros, inner_total
    )
    pulled = passed_along(own_pulls, "context", -1)
    out_term = lax.optimization_barrier(contract_rows(out_grad, gated_norm))
    gate_term = contract_rows(normed, gate_grad)
    branch = contract_cols(gated_norm, out_full)
    gate_part = contract_cols(gate_grad, gate_full)
    branch_other = paired(branch, "tensor")

    (
        lead_grad, tails, rims_grad, coupling_raw_grad, coupling_rims_grad,
        value_sums, coupling_sums, small_sums, skip_sums, out_shard, gate_shard,
    ) = backward_ssd(
        jnp.stack(marks), micros, raw, rims, inner, twice, count, mixer_grad, mixer, states,
        finals, entering, reach, pulled,
        cw, cb, ccw, ccb, sbias, rate, skip, sel, selcol, selt, [out_term, gate_term], [branch, gate_part], 2,
    )
    edges = passed_along(jnp.concatenate([rims_grad, coupling_rims_grad], axis=2), "context", -1)
    coupling_raw_grad = coupling_raw_grad.reshape(micros, count, twice) + jnp.pad(
        edges[:, :, inner:], ((0, 0), (count - 8, 0), (0, 0))
    )
    coupling_raw_grad = coupling_raw_grad + paired(coupling_raw_grad, "tensor")
    lane_ids = jnp.arange(twice, dtype=jnp.int32)
    own_lanes = ((lane_ids // width) == side).astype(bf16)
    coupling_low = (coupling_raw_grad.astype(bf16) * own_lanes).reshape(micros * count, twice)
    lead_grad = lax.dynamic_update_slice(lead_grad, coupling_low, (0, inner))
    tails = (tails + edges[:, :, :inner]).astype(bf16)
    for micro in range(micros):
        lead_grad = lax.dynamic_update_slice(
            lead_grad, tails[micro], ((micro + 1) * count - 8, 0)
        )
    normed_part = gate_part + contract_cols(lead_grad, lead_full)
    skip_sums = skip_sums[0].reshape(heads, head_size).sum(axis=1)
    coupling_sums = coupling_sums + paired(coupling_sums, "tensor")
    small = [value_sums[:5], coupling_sums[:5], small_sums[:2], skip_sums, inner_gain_rows[0]]
    small_rows = packed_rows(small)
    lead_shard, block_out, input_grad, summed = finish(
        contract_rows(normed, lead_grad), x_input, cot, scales,
        jnp.broadcast_to(keep, (micros * count, LANES)), branch, branch_other,
        normed_part, paired(normed_part, "tensor"), norm_gain.reshape(1, model), small_rows, 4,
    )
    flat = summed.reshape(-1)
    value_all, coupling_all, small_all, skip_all, inner_all = unpacked(flat, small)
    norm_all = flat[small_rows.size :]
    coupling_shard = lead_shard[:, inner : inner + twice]
    coupling_shard = coupling_shard + paired(coupling_shard, "tensor")
    return (
        block_out.reshape(micros, 1, count, model),
        input_grad.reshape(micros, 1, count, model),
        norm_all,
        woven(gate_shard, lead_shard, inner),
        coupling_shard,
        lead_shard[:, inner + twice : inner + twice + heads],
        jnp.transpose(out_shard),
        value_all[:4],
        value_all[4],
        coupling_all[:4],
        coupling_all[4],
        small_all[0, :heads],
        small_all[1, :heads],
        skip_all,
        inner_all,
    )


def contract_rows(left, right):
    return lax.dot_general(
        left, right, (((0,), (0,)), ((), ())), preferred_element_type=jnp.float32
    )


def contract_cols(left, right):
    return lax.dot_general(
        left, right, (((1,), (1,)), ((), ())), preferred_element_type=jnp.float32
    )


def solution(mesh):
    return jax.shard_map(
        shards,
        mesh=mesh,
        in_specs=(
            P(None, "fsdp", "context", None),
            P(None, "fsdp", None),
            P(None, "fsdp", None),
            P(None, "fsdp", "context", None),
            P(),
            P("fsdp", None, "tensor"),
            P("fsdp", None),
            P("fsdp", "tensor"),
            P("tensor", "fsdp"),
            P(None, "tensor"),
            P("tensor"),
            P(),
            P(),
            P("tensor"),
            P("tensor"),
            P("tensor"),
            P("tensor"),
        ),
        out_specs=(
            P(None, "fsdp", "context", None),
            P(None, "fsdp", "context", None),
            P(),
            P("fsdp", None, "tensor"),
            P("fsdp", None),
            P("fsdp", "tensor"),
            P("tensor", "fsdp"),
            P(None, "tensor"),
            P("tensor"),
            P(),
            P(),
            P("tensor"),
            P("tensor"),
            P("tensor"),
            P("tensor"),
        ),
        check_vma=False,
    )
```

```python
import functools

import jax
import jax.numpy as jnp
import numpy as np
from jax import lax
from jax.experimental import pallas as pl
from jax.experimental.pallas import tpu as pltpu
from jax.sharding import PartitionSpec as P

CHUNK = 128
LANES = 128
MESH = pl.DeviceIdType.MESH
f32 = jnp.float32
bf16 = jnp.bfloat16
epsilon = 1e-05


def split_two(value):
    high = value.astype(bf16)
    return high, (value - high.astype(f32)).astype(bf16)


def split_three(value):
    high = value.astype(bf16)
    rest = value - high.astype(f32)
    middle = rest.astype(bf16)
    return high, middle, (rest - middle.astype(f32)).astype(bf16)


def mm(left, right):
    return jnp.dot(left, right, preferred_element_type=f32)


def mm_nt(left, right):
    return lax.dot_general(left, right, (((1,), (1,)), ((), ())), preferred_element_type=f32)


def mm_three(left, right):
    wide = mm(left[0], jnp.concatenate([right[0], right[1]], axis=1))
    count = right[0].shape[1]
    return wide[:, :count] + wide[:, count:] + mm(left[1], right[0])


def mm_three_nt(left, right):
    return mm_nt(left[0], right[0]) + mm_nt(left[0], right[1]) + mm_nt(left[1], right[0])


def packed_parts(value, heads):
    high, middle, lowest = split_three(value)
    joined = (
        high.astype(f32)
        + pltpu.roll(middle.astype(f32), heads, 1)
        + pltpu.roll(lowest.astype(f32), 2 * heads, 1)
    )
    return joined.astype(bf16)


def segment_at(position, first_end, second_end):
    first_part = (position >= first_end).astype(jnp.int32)
    second_part = (position >= second_end).astype(jnp.int32)
    return jnp.where(position < 0, -1, first_part + second_part)


def chunk_frame(marks, chunk, step_raw, step_bias, rate, heads):
    first_end, second_end, base = marks[0], marks[1], marks[2]
    start = base + chunk * CHUNK
    rows = start + lax.broadcasted_iota(jnp.int32, (CHUNK, LANES), 0)
    columns = start + lax.broadcasted_iota(jnp.int32, (CHUNK, CHUNK), 1)
    seg_rows = segment_at(rows, first_end, second_end)
    seg_columns = segment_at(columns, first_end, second_end)
    seg_prior = segment_at(start - 1, first_end, second_end)
    seg_last = segment_at(start + CHUNK - 1, first_end, second_end)
    same = [
        (segment_at(rows - lag, first_end, second_end) == seg_rows).astype(f32) for lag in range(4)
    ]
    shifted = step_raw + step_bias
    step = jnp.maximum(shifted, 0.0) + jnp.log1p(jnp.exp(-jnp.abs(shifted)))
    lanes = lax.broadcasted_iota(jnp.int32, (CHUNK, LANES), 1)
    step = jnp.where(lanes < heads, step, 0.0)
    log_decay = -step * rate
    row_ids = lax.broadcasted_iota(jnp.int32, (CHUNK, CHUNK), 0)
    column_ids = lax.broadcasted_iota(jnp.int32, (CHUNK, CHUNK), 1)
    lower = (row_ids >= column_ids).astype(bf16)
    parts = split_three(log_decay)
    cumulative = mm(lower, parts[0]) + mm(lower, parts[1]) + mm(lower, parts[2])
    last = cumulative[CHUNK - 1 :, :]
    carry = jnp.exp(cumulative) * (seg_rows == seg_prior).astype(f32)
    tail = jnp.exp(last - cumulative) * (seg_rows == seg_last).astype(f32)
    live = lanes < heads
    carry = jnp.where(live, carry, 0.0)
    tail = jnp.where(live, tail, 0.0)
    return dict(
        seg_rows=seg_rows,
        seg_columns=seg_columns,
        row_ids=row_ids,
        column_ids=column_ids,
        same=same,
        step=step,
        shifted=shifted,
        cumulative=cumulative,
        carry=carry,
        tail=tail,
    )


def conv_sum(current, halo, weights, biases, same):
    full = jnp.concatenate([halo, current], axis=0)
    total = biases + weights(0) * current
    for lag in range(1, 4):
        total = total + weights(lag) * (pltpu.roll(full, lag, 0)[8:] * same[lag])
    return total


def logistic(value):
    return 1.0 / (1.0 + jnp.exp(-value))


def forward_kernel(heads, chunks, plan, *refs):
    (
        marks, vraw, vprev, vrim, craw, cprev, crim, sraw, cw, cb, ccw, ccb, sbias, rate, skip,
        sel, selcol,
    ) = refs[:17]
    arrays = plan.arrays
    weights, refs = refs[17 : 17 + arrays], refs[17 + arrays :]
    y_out, st_out, fin_out, bc_out, carry_out, cd_out, entering = refs[:7]
    fulls, refs = refs[7 : 7 + arrays], refs[7 + arrays :]
    (
        state, cumt, stack, cumpack, halo, same_s, bias_s, gram_s, cd_s, cparts, btparts,
        leaving, leave_send, leave_recv,
    ) = refs[:14]
    plan.bind(weights, fulls, refs[14:])
    grid_step = pl.program_id(0)
    steps = pl.num_programs(0)
    chunk = lax.rem(grid_step, chunks)
    micro = grid_step // chunks
    width = state.shape[0]
    early = {0: range(2)}
    for when in range(1, min(2 * chunks - 1, len(plan.order) - 1)):
        early[when] = [when + 1]
    placed = len(early)

    def leave_copy(which):
        return pltpu.make_async_remote_copy(
            src_ref=leaving.at[which], dst_ref=entering.at[which],
            send_sem=leave_send.at[which], recv_sem=leave_recv.at[which],
            device_id=plan.across, device_id_type=MESH,
        )

    for when, numbers in early.items():

        @pl.when(grid_step == when)
        def _(when=when, numbers=numbers):
            if when == 0:
                plan.greet()
            for number in numbers:
                plan.event(number)

    @pl.when(chunk == 0)
    def _():
        state[...] = jnp.zeros_like(state)
        cd_s[...] = jnp.ones_like(cd_s)
        cd_out[...] = jnp.zeros_like(cd_out)
        halo[...] = vrim[...]

    @pl.when(chunk > 0)
    def _():
        halo[...] = vprev[...]

    frame = chunk_frame([marks[micro, place] for place in range(3)], chunk, sraw[...], sbias[...], rate[...], heads)
    same = frame["same"]
    for lag in range(1, 4):
        same_s[lag - 1] = same[lag]
    joined = (frame["seg_rows"] == frame["seg_columns"]) & (frame["row_ids"] >= frame["column_ids"])
    bias_s[...] = jnp.where(joined, 0.0, -1e30)
    stack[0:CHUNK, :] = packed_parts(frame["step"], heads)
    stack[CHUNK : 2 * CHUNK, :] = packed_parts(frame["carry"], heads)
    stack[2 * CHUNK : 3 * CHUNK, :] = packed_parts(frame["tail"], heads)
    cumpack[...] = packed_parts(frame["cumulative"], heads)
    cumt[...] = jnp.transpose(frame["cumulative"])
    coupling_halo = jnp.where(chunk == 0, crim[...], cprev[...])
    wide_same = [None] + [jnp.concatenate([same[lag], same[lag]], axis=1) for lag in range(1, 4)]
    pre = conv_sum(
        craw[...], coupling_halo, lambda lag: ccw[lag : lag + 1, :], ccb[...], wide_same
    )
    coupled = pre * logistic(pre)
    bc_out[...] = coupled
    b_part = split_two(coupled[:, :width])
    c_part = split_two(coupled[:, width:])
    gram_s[...] = mm_three_nt(c_part, b_part)
    cparts[0] = c_part[0]
    cparts[1] = c_part[1]
    turned = jnp.transpose(coupled[:, :width])
    bt_part = split_two(turned)
    btparts[0] = bt_part[0]
    btparts[1] = bt_part[1]
    lane = lax.broadcasted_iota(jnp.int32, (CHUNK, LANES), 1)
    low_half = (lane < LANES // 2).astype(f32)
    high_half = 1.0 - low_half

    def pair(index, carried):
        cols = pl.ds(pl.multiple_of(index * LANES, LANES), LANES)
        wide = pl.ds(pl.multiple_of(index * 2 * LANES, 2 * LANES), 2 * LANES)
        pre_value = conv_sum(
            vraw[:, cols],
            halo[:, cols],
            lambda lag: cw[lag : lag + 1, cols],
            cb[:, cols],
            [None] + [same_s[lag - 1] for lag in range(1, 4)],
        )
        value = pre_value * logistic(pre_value)
        spread = mm(stack[...], sel[:, cols])
        step_e = spread[:CHUNK]
        carry_e = spread[CHUNK : 2 * CHUNK]
        tail_e = spread[2 * CHUNK :]
        inputs = step_e * value
        column = mm(cumpack[...], selcol[:, wide])
        row_pair = jnp.concatenate(
            [cumt[pl.ds(2 * index, 1), :], cumt[pl.ds(2 * index + 1, 1), :]], axis=1
        )
        bias = bias_s[...]
        gram = gram_s[...]
        mixing = jnp.concatenate([gram, gram], axis=1) * jnp.exp(
            column - row_pair + jnp.concatenate([bias, bias], axis=1)
        )
        mix_high, mix_low = split_two(mixing)
        in_low = split_two(inputs * low_half)
        in_high = split_two(inputs * high_half)
        diag_high = jnp.concatenate([in_low[0], in_high[0]], axis=0)
        diag_low = jnp.concatenate([in_low[1], in_high[1]], axis=0)
        both = mm(mix_high, jnp.concatenate([diag_high, diag_low], axis=1))
        inside = both[:, :LANES] + both[:, LANES:] + mm(mix_low, diag_high)
        held = state[:, cols]
        from_state = mm_three((cparts[0], cparts[1]), split_two(held))
        y_out[:, cols] = inside + carry_e * from_state + skip[:, cols] * value
        fresh = mm_three((btparts[0], btparts[1]), split_two(tail_e * inputs))
        through = carry_e[CHUNK - 1 :, :]
        st_out[0, :, cols] = held
        renewed = through * held + fresh
        state[:, cols] = renewed
        fin_out[:, cols] = renewed
        reach = cd_s[0:1, cols]
        carry_out[:, cols] = carry_e * reach
        cd_s[0:1, cols] = reach * through
        return carried

    eight_rows = lax.broadcasted_iota(jnp.int32, cd_out.shape, 0)
    cd_out[...] = jnp.where(eight_rows == chunk, cd_s[0:1, :], cd_out[...])
    lax.fori_loop(0, heads // 2, pair, 0, unroll=4)
    cd_out[...] = jnp.where(eight_rows == chunk + 1, cd_s[0:1, :], cd_out[...])

    @pl.when(chunk == chunks - 1)
    def _():
        leaving[micro] = state[...]
        leave_copy(micro).start()

    @pl.when(grid_step == steps - 1)
    def _():
        for number in range(placed + 1, len(plan.order)):
            plan.event(number)
        plan.finish()
        for which in range(leaving.shape[0]):
            leave_copy(which).wait()


def selectors(heads, head_size):
    inner = heads * head_size
    head_of_lane = np.arange(inner) // head_size
    narrow = np.zeros((LANES, inner), np.float32)
    wide = np.zeros((LANES, heads * LANES), np.float32)
    head_of_wide = np.arange(heads * LANES) // LANES
    for part in range(3):
        narrow[part * heads + head_of_lane, np.arange(inner)] = 1.0
        wide[part * heads + head_of_wide, np.arange(heads * LANES)] = 1.0
    return narrow, wide


def whole(shape):
    return pl.BlockSpec(shape, lambda index, *_: (0,) * len(shape))


def forward_ssd(
    marks, micros, raw, rims, inner, twice, tokens,
    cw, cb, ccw, ccb, sbias, rate, skip, sel, selcol, shards, shared, collective_id,
):
    width = twice // 2
    chunks = tokens // CHUNK
    heads = inner // (LANES // 2)
    eighth = CHUNK // 8
    pairs = lax.axis_size("fsdp") // 2
    shard_rows = shards[0].shape[0]
    plan = Gathering(shard_rows, pairs, [shard.shape[1] for shard in shards], 2, shared)

    def part(count, start):
        return pl.BlockSpec((CHUNK, count), lambda step: (step, start // count))

    def before(count, start):
        return pl.BlockSpec(
            (8, count), lambda step: (jnp.maximum(step * eighth - 1, 0), start // count)
        )

    def edge(count, start):
        return pl.BlockSpec((None, 8, count), lambda step: (step // chunks, 0, start // count))

    def each(*shape):
        return pl.BlockSpec((None, *shape), lambda step: (step // chunks, 0, 0))

    hbm = pl.BlockSpec(memory_space=pl.ANY)
    dma = pltpu.SemaphoreType.DMA
    return pl.pallas_call(
        functools.partial(forward_kernel, heads, chunks, plan),
        grid=(micros * chunks,),
        in_specs=[
            pl.BlockSpec(memory_space=pltpu.SMEM),
            part(inner, 0),
            before(inner, 0),
            edge(inner, 0),
            part(twice, inner),
            before(twice, inner),
            edge(twice, inner),
            part(LANES, inner + twice),
            whole(cw.shape),
            whole(cb.shape),
            whole(ccw.shape),
            whole(ccb.shape),
            whole(sbias.shape),
            whole(rate.shape),
            whole(skip.shape),
            whole(sel.shape),
            whole(selcol.shape),
        ]
        + [hbm] * len(shards),
        out_specs=[
            part(inner, 0),
            pl.BlockSpec((1, width, inner), lambda step: (step, 0, 0)),
            each(width, inner),
            part(twice, 0),
            part(inner, 0),
            each(8, inner),
            hbm,
        ]
        + [hbm] * len(shards),
        scratch_shapes=[
            pltpu.VMEM((width, inner), f32),
            pltpu.VMEM((LANES, CHUNK), f32),
            pltpu.VMEM((3 * CHUNK, LANES), bf16),
            pltpu.VMEM((CHUNK, LANES), bf16),
            pltpu.VMEM((8, inner), f32),
            pltpu.VMEM((3, CHUNK, LANES), f32),
            pltpu.VMEM((CHUNK, CHUNK), f32),
            pltpu.VMEM((CHUNK, CHUNK), f32),
            pltpu.VMEM((8, inner), f32),
            pltpu.VMEM((2, CHUNK, width), bf16),
            pltpu.VMEM((2, width, CHUNK), bf16),
            pltpu.VMEM((micros, width, inner), f32),
            dma((micros,)),
            dma((micros,)),
        ]
        + plan.scratch(),
        out_shape=[
            jax.ShapeDtypeStruct((micros * tokens, inner), f32),
            jax.ShapeDtypeStruct((micros * chunks, width, inner), f32),
            jax.ShapeDtypeStruct((micros, width, inner), f32),
            jax.ShapeDtypeStruct((micros * tokens, twice), f32),
            jax.ShapeDtypeStruct((micros * tokens, inner), f32),
            jax.ShapeDtypeStruct((micros, 8, inner), f32),
            jax.ShapeDtypeStruct((micros, width, inner), f32),
        ]
        + [
            jax.ShapeDtypeStruct((2 * pairs * shard_rows, shard.shape[1]), shard.dtype)
            for shard in shards
        ],
        compiler_params=pltpu.CompilerParams(
            collective_id=collective_id, has_side_effects=True, vmem_limit_bytes=60 * 1024 * 1024
        ),
    )(
        marks, raw, raw, rims, raw, raw, rims, raw, cw, cb, ccw, ccb, sbias, rate, skip, sel, selcol,
        *shards,
    )


def backward_kernel(heads, chunks, plan, waited, *refs):
    (
        marks, vraw, vprev, vrim, craw, cprev, crim, sraw, grad, mixer, st_now, st_next, fin,
        entering, cd, pulled, cw, cb, ccw, ccb, sbias, rate, skip, sel, selcol, selt,
    ) = refs[:26]
    arrays = len(plan.counts)
    refs = refs[26:]
    terms, refs = refs[:arrays], refs[arrays + waited :]
    (
        lead_g, vtail_g, vrim_g, craw_g, crim_g, cw_g, ccw_g, small_g, skip_g,
    ) = refs[:9]
    outs, refs = refs[9 : 9 + arrays], refs[9 + arrays :]
    (
        state, cumt, stack, cumpack, halo, same_s, bias_s, gram_s, cparts, bparts, ctparts,
        rim_s, crim_s, dgram, dcoup, dhead, cd_s,
    ) = refs[:17]
    plan.bind(terms, outs, refs[17:])
    grid_step = pl.program_id(0)
    step_id = lax.rem(grid_step, chunks)
    micro = grid_step // chunks
    chunk = chunks - 1 - step_id
    width = state.shape[0]
    inner = state.shape[1]
    per_step = -(-plan.steps // pl.num_programs(0))

    @pl.when(grid_step == 0)
    def _():
        plan.greet()
        cw_g[...] = jnp.zeros_like(cw_g)
        ccw_g[...] = jnp.zeros_like(ccw_g)
        small_g[...] = jnp.zeros_like(small_g)
        skip_g[...] = jnp.zeros_like(skip_g)

    def reduce_steps(first, count):
        def one(number, carried):
            plan.step(number)
            return carried

        start = grid_step * per_step + first
        lax.fori_loop(start, jnp.minimum(start + count, plan.steps), one, 0)

    @pl.when(step_id == 0)
    def _():
        state[...] = pulled[...]
        rim_s[...] = jnp.zeros_like(rim_s)
        crim_s[...] = jnp.zeros_like(crim_s)

    @pl.when(chunk == 0)
    def _():
        halo[...] = vrim[...]

    @pl.when(chunk > 0)
    def _():
        halo[...] = vprev[...]

    frame = chunk_frame([marks[micro, place] for place in range(3)], chunk, sraw[...], sbias[...], rate[...], heads)
    same = frame["same"]
    for lag in range(1, 4):
        same_s[lag - 1] = same[lag]
    joined = (frame["seg_rows"] == frame["seg_columns"]) & (frame["row_ids"] <= frame["column_ids"])
    bias_s[...] = jnp.where(joined, 0.0, -1e30)
    stack[0:CHUNK, :] = packed_parts(frame["step"], heads)
    stack[CHUNK : 2 * CHUNK, :] = packed_parts(frame["carry"], heads)
    stack[2 * CHUNK : 3 * CHUNK, :] = packed_parts(frame["tail"], heads)
    cumpack[...] = packed_parts(frame["cumulative"], heads)
    cumt[...] = jnp.transpose(frame["cumulative"])
    coupling_halo = jnp.where(chunk == 0, crim[...], cprev[...])
    wide_same = [None] + [jnp.concatenate([same[lag], same[lag]], axis=1) for lag in range(1, 4)]
    craw_now = craw[...]
    pre = conv_sum(craw_now, coupling_halo, lambda lag: ccw[lag : lag + 1, :], ccb[...], wide_same)
    csig = logistic(pre)
    coupled = pre * csig
    b_value = coupled[:, :width]
    c_value = coupled[:, width:]
    b_part = split_two(b_value)
    c_part = split_two(c_value)
    gram_s[...] = mm_three_nt(b_part, c_part)
    cparts[0] = c_part[0]
    cparts[1] = c_part[1]
    bparts[0] = b_part[0]
    bparts[1] = b_part[1]
    ct_part = split_two(jnp.transpose(c_value))
    ctparts[0] = ct_part[0]
    ctparts[1] = ct_part[1]
    dgram[...] = jnp.zeros_like(dgram)
    dcoup[...] = jnp.zeros_like(dcoup)
    dhead[...] = jnp.zeros_like(dhead)
    lane = lax.broadcasted_iota(jnp.int32, (CHUNK, LANES), 1)
    row = lax.broadcasted_iota(jnp.int32, (CHUNK, LANES), 0)
    low_half = (lane < LANES // 2).astype(f32)
    high_half = 1.0 - low_half
    last_row = (row == CHUNK - 1).astype(f32)
    is_end = step_id == 0
    eight_rows = lax.broadcasted_iota(jnp.int32, cd.shape, 0)
    for place in range(2):
        chosen = jnp.where(eight_rows == chunk + place, cd[...], 0.0)
        cd_s[place : place + 1, :] = jnp.sum(chosen, axis=0, keepdims=True)

    def pair(index):
        cols = pl.ds(pl.multiple_of(index * LANES, LANES), LANES)
        wide = pl.ds(pl.multiple_of(index * 2 * LANES, 2 * LANES), 2 * LANES)
        raw = vraw[:, cols]
        full = jnp.concatenate([halo[:, cols], raw], axis=0)
        lagged = [raw] + [pltpu.roll(full, lag, 0)[8:] * same_s[lag - 1] for lag in range(1, 4)]
        pre_value = cb[:, cols]
        for lag in range(4):
            pre_value = pre_value + cw[lag : lag + 1, cols] * lagged[lag]
        sig = logistic(pre_value)
        value = pre_value * sig
        spread = mm(stack[...], sel[:, cols])
        step_e = spread[:CHUNK]
        carry_e = spread[CHUNK : 2 * CHUNK]
        tail_e = spread[2 * CHUNK :]
        inputs = step_e * value
        grads = grad[:, cols]
        column = mm(cumpack[...], selcol[:, wide])
        row_pair = jnp.concatenate(
            [cumt[pl.ds(2 * index, 1), :], cumt[pl.ds(2 * index + 1, 1), :]], axis=1
        )
        bias = bias_s[...]
        gram = gram_s[...]
        decays = jnp.exp(row_pair - column + jnp.concatenate([bias, bias], axis=1))
        mixing = jnp.concatenate([gram, gram], axis=1) * decays
        mix_high, mix_low = split_two(mixing)
        g_low = split_two(grads * low_half)
        g_high = split_two(grads * high_half)
        diag_high = jnp.concatenate([g_low[0], g_high[0]], axis=0)
        diag_low = jnp.concatenate([g_low[1], g_high[1]], axis=0)
        both = mm(mix_high, jnp.concatenate([diag_high, diag_low], axis=1))
        input_g = both[:, :LANES] + both[:, LANES:] + mm(mix_low, diag_high)
        held_g = state[:, cols]
        held_parts = split_two(held_g)
        input_g = input_g + tail_e * mm_three((bparts[0], bparts[1]), held_parts)
        in_parts = split_two(inputs)
        outer = mm_three_nt(in_parts, (diag_high, diag_low)) * decays
        dgram[...] += outer[:, :CHUNK] + outer[:, CHUNK:]
        reach_now = cd_s[0:1, cols]
        reach_next = cd_s[1:2, cols]
        arriving = entering[:, cols]
        held = st_now[0, :, cols] + reach_now * arriving
        next_own = jnp.where(is_end, fin[:, cols], st_next[0, :, cols])
        following = next_own + reach_next * arriving
        carried_g = split_two(carry_e * grads)
        state[:, cols] = carry_e[CHUNK - 1 :, :] * held_g + mm_three(
            (ctparts[0], ctparts[1]), carried_g
        )
        dcoup[1] += mm_three_nt(carried_g, split_two(held))
        dcoup[0] += mm_three_nt(split_two(tail_e * inputs), held_parts)
        value_g = input_g * step_e + skip[:, cols] * grads
        kept = jnp.sum(held_g * following, axis=0, keepdims=True)
        balance = grads * (mixer[:, cols] - skip[:, cols] * value) - inputs * input_g
        balance = balance + last_row * kept
        sums = jnp.concatenate([balance, input_g * value], axis=0)
        sums_parts = split_three(sums)
        pick = selt[cols, :]
        dhead[...] += mm(sums_parts[0], pick) + mm(sums_parts[1], pick) + mm(sums_parts[2], pick)
        skip_g[0:1, cols] += jnp.sum(grads * value, axis=0, keepdims=True)
        pre_g = value_g * (sig * (1.0 + pre_value * (1.0 - sig)))
        cw_g[4:5, cols] += jnp.sum(pre_g, axis=0, keepdims=True)
        raw_g = cw[0:1, cols] * pre_g
        cw_g[0:1, cols] += jnp.sum(pre_g * raw, axis=0, keepdims=True)
        none = jnp.zeros((8, LANES), f32)
        edge = none
        for lag in range(1, 4):
            cw_g[lag : lag + 1, cols] += jnp.sum(pre_g * lagged[lag], axis=0, keepdims=True)
            weighted = cw[lag : lag + 1, cols] * (pre_g * same_s[lag - 1])
            padded = jnp.concatenate([none, weighted, none], axis=0)
            turned = pltpu.roll(padded, CHUNK + 16 - lag, 0)
            raw_g = raw_g + turned[8 : 8 + CHUNK]
            edge = edge + turned[:8]
        last_rows = raw_g[CHUNK - 8 :] + rim_s[:, cols]
        lead_g[:, cols] = jnp.concatenate([raw_g[: CHUNK - 8], last_rows], axis=0).astype(bf16)

        @pl.when(step_id == 0)
        def _():
            vtail_g[:, cols] = last_rows

        rim_s[:, cols] = edge
        vrim_g[:, cols] = edge

    groups = 4
    per_group = heads // 2 // groups

    def group(number, carried):
        for inside in range(per_group):
            pair(number * per_group + inside)
        share = per_step // (groups + 1)
        reduce_steps(number * share, share)
        return carried

    lax.fori_loop(0, groups, group, 0)
    used = groups * (per_step // (groups + 1))
    reduce_steps(used, per_step - used)

    total = dgram[...]
    total_parts = split_two(total)
    turned_parts = split_two(jnp.transpose(total))
    b_grad = dcoup[0] + mm_three(total_parts, (cparts[0], cparts[1]))
    c_grad = dcoup[1] + mm_three(turned_parts, (bparts[0], bparts[1]))
    coupled_g = jnp.concatenate([b_grad, c_grad], axis=1)
    pre_g = coupled_g * (csig * (1.0 + pre * (1.0 - csig)))
    ccw_g[4:5, :] += jnp.sum(pre_g, axis=0, keepdims=True)
    ccw_g[0:1, :] += jnp.sum(pre_g * craw_now, axis=0, keepdims=True)
    raw_g = ccw[0:1, :] * pre_g
    full = jnp.concatenate([coupling_halo, craw_now], axis=0)
    none = jnp.zeros((8, 2 * width), f32)
    edge = none
    for lag in range(1, 4):
        masked = pre_g * wide_same[lag]
        ccw_g[lag : lag + 1, :] += jnp.sum(
            masked * pltpu.roll(full, lag, 0)[8:], axis=0, keepdims=True
        )
        padded = jnp.concatenate([none, ccw[lag : lag + 1, :] * masked, none], axis=0)
        turned = pltpu.roll(padded, CHUNK + 16 - lag, 0)
        raw_g = raw_g + turned[8 : 8 + CHUNK]
        edge = edge + turned[:8]
    craw_g[...] = raw_g
    craw_g[CHUNK - 8 :, :] += crim_s[...]
    crim_s[...] = edge
    crim_g[...] = edge

    upper = (frame["row_ids"] <= frame["column_ids"]).astype(bf16)
    parts = split_three(dhead[:CHUNK])
    decay_g = mm(upper, parts[0]) + mm(upper, parts[1]) + mm(upper, parts[2])
    step_g = (dhead[CHUNK:] - rate[...] * decay_g) * logistic(frame["shifted"])
    lead_g[:, inner : inner + 2 * width] = jnp.zeros((CHUNK, 2 * width), bf16)
    lead_g[:, inner + 2 * width :] = step_g.astype(bf16)
    small_g[0:1, :] += jnp.sum(step_g, axis=0, keepdims=True)
    small_g[1:2, :] += jnp.sum(-frame["step"] * decay_g, axis=0, keepdims=True)


def backward_ssd(
    marks, micros, raw, rims, inner, twice, tokens, grad, mixer, states, fin, entering, cd, pulled,
    cw, cb, ccw, ccb, sbias, rate, skip, sel, selcol, selt, terms, first, collective_id,
):
    width = twice // 2
    chunks = tokens // CHUNK
    heads = inner // (LANES // 2)
    eighth = CHUNK // 8
    pairs = lax.axis_size("fsdp") // 2
    shard_rows = terms[0].shape[0] // (2 * pairs)
    plan = Reduction(shard_rows, pairs, [term.shape[1] for term in terms], 2)
    lead = inner + twice + LANES

    def row(step):
        return step // chunks * chunks + chunks - 1 - lax.rem(step, chunks)

    def part(count, start):
        return pl.BlockSpec((CHUNK, count), lambda step: (row(step), start // count))

    def before(count, start):
        return pl.BlockSpec(
            (8, count), lambda step: (jnp.maximum(row(step) * eighth - 1, 0), start // count)
        )

    def edge(count, start):
        return pl.BlockSpec(
            (None, 8, count), lambda step: (step // chunks, 0, start // count)
        )

    def held(offset):
        return pl.BlockSpec(
            (1, width, inner),
            lambda step: (
                jnp.minimum(row(step) + offset, (step // chunks + 1) * chunks - 1), 0, 0,
            ),
        )

    def each(*shape):
        return pl.BlockSpec((None, *shape), lambda step: (step // chunks, 0, 0))

    hbm = pl.BlockSpec(memory_space=pl.ANY)
    return pl.pallas_call(
        functools.partial(backward_kernel, heads, chunks, plan, len(first)),
        grid=(micros * chunks,),
        in_specs=[
            pl.BlockSpec(memory_space=pltpu.SMEM),
            part(inner, 0),
            before(inner, 0),
            edge(inner, 0),
            part(twice, inner),
            before(twice, inner),
            edge(twice, inner),
            part(LANES, inner + twice),
            part(inner, 0),
            part(inner, 0),
            held(0),
            held(1),
            each(width, inner),
            each(width, inner),
            each(8, inner),
            each(width, inner),
            whole(cw.shape),
            whole(cb.shape),
            whole(ccw.shape),
            whole(ccb.shape),
            whole(sbias.shape),
            whole(rate.shape),
            whole(skip.shape),
            whole(sel.shape),
            whole(selcol.shape),
            whole(selt.shape),
        ]
        + [hbm] * (len(terms) + len(first)),
        out_specs=[
            part(lead, 0),
            each(8, inner),
            each(8, inner),
            part(twice, 0),
            each(8, twice),
            whole((8, inner)),
            whole((8, twice)),
            whole((8, LANES)),
            whole((8, inner)),
        ]
        + [hbm] * len(terms),
        scratch_shapes=[
            pltpu.VMEM((width, inner), f32),
            pltpu.VMEM((LANES, CHUNK), f32),
            pltpu.VMEM((3 * CHUNK, LANES), bf16),
            pltpu.VMEM((CHUNK, LANES), bf16),
            pltpu.VMEM((8, inner), f32),
            pltpu.VMEM((3, CHUNK, LANES), f32),
            pltpu.VMEM((CHUNK, CHUNK), f32),
            pltpu.VMEM((CHUNK, CHUNK), f32),
            pltpu.VMEM((2, CHUNK, width), bf16),
            pltpu.VMEM((2, CHUNK, width), bf16),
            pltpu.VMEM((2, width, CHUNK), bf16),
            pltpu.VMEM((8, inner), f32),
            pltpu.VMEM((8, twice), f32),
            pltpu.VMEM((CHUNK, CHUNK), f32),
            pltpu.VMEM((2, CHUNK, width), f32),
            pltpu.VMEM((2 * CHUNK, LANES), f32),
            pltpu.VMEM((8, inner), f32),
        ]
        + plan.scratch(),
        out_shape=[
            jax.ShapeDtypeStruct((micros * tokens, lead), bf16),
            jax.ShapeDtypeStruct((micros, 8, inner), f32),
            jax.ShapeDtypeStruct((micros, 8, inner), f32),
            jax.ShapeDtypeStruct((micros * tokens, twice), f32),
            jax.ShapeDtypeStruct((micros, 8, twice), f32),
            jax.ShapeDtypeStruct((8, inner), f32),
            jax.ShapeDtypeStruct((8, twice), f32),
            jax.ShapeDtypeStruct((8, LANES), f32),
            jax.ShapeDtypeStruct((8, inner), f32),
        ]
        + [jax.ShapeDtypeStruct((shard_rows, term.shape[1]), f32) for term in terms],
        compiler_params=pltpu.CompilerParams(
            collective_id=collective_id, has_side_effects=True, vmem_limit_bytes=60 * 1024 * 1024
        ),
    )(
        marks, raw, raw, rims, raw, raw, rims, raw, grad, mixer, states, states, fin, entering,
        cd, pulled, cw, cb, ccw, ccb, sbias, rate, skip, sel, selcol, selt,
        *[term.reshape(pairs, 2, shard_rows, -1) for term in terms], *first,
    )


class Gathering:
    def __init__(self, rows, pairs, widths, cuts, shared):
        self.rows, self.pairs, self.shared = rows, pairs, shared
        self.arrays = len(widths)
        self.pieces = []
        for array, width in enumerate(widths):
            size = -(-width // LANES // cuts) * LANES
            self.pieces += [
                (array, start, min(size, width - start)) for start in range(0, width, size)
            ]
        self.moved = rows - shared
        self.early = min(rows // 8, self.moved - shared) // 16 * 16
        self.late = self.moved - self.early
        self.order = [(j, k) for j in range(len(self.pieces)) for k in range(pairs)]
        if pairs > 1:
            self.order.sort(key=lambda item: (item[0] * pairs + (item[1] or -0.5 - (item[0] > 0))))
        self.lag = 2

    def scratch(self):
        dma, pairs, arrays = pltpu.SemaphoreType.DMA, self.pairs, len(self.pieces)
        return [
            dma((arrays, max(pairs - 1, 1))),
            dma((arrays, max(pairs - 1, 1))),
            dma((arrays, pairs)),
            dma((arrays, pairs)),
            dma((arrays, 2 * pairs)),
            dma((arrays, 2 * pairs)),
            dma((arrays, 2 * pairs)),
            dma((arrays, 2 * pairs)),
            dma((arrays,)),
        ]

    def bind(self, weights, fulls, scratch):
        self.weights, self.fulls = weights, fulls
        (
            self.ring_send, self.ring_recv, self.pair_send, self.pair_recv,
            self.cross_send, self.cross_recv, self.early_send, self.early_recv, self.local,
        ) = scratch
        self.own, self.place = lax.axis_index("fsdp"), lax.axis_index("context")
        self.side = lax.axis_index("tensor")
        self.pair, self.member = self.own // 2, lax.rem(self.own, 2)
        pairs, pair, member = self.pairs, self.pair, self.member
        self.ahead = (2 * lax.rem(pair + 1, pairs) + member, self.place, self.side)
        self.behind = (2 * lax.rem(pair + pairs - 1, pairs) + member, self.place, self.side)
        self.partner = (2 * pair + 1 - member, self.place, self.side)
        self.across = (self.own, 1 - self.place, self.side)
        self.beside = (self.own, self.place, 1 - self.side)
        self.late_start = pl.multiple_of(self.place * (self.shared + self.early), 16)
        self.early_start = pl.multiple_of(
            self.place * self.shared + (1 - self.place) * self.late, 16
        )
        self.shared_start = pl.multiple_of(self.place * self.moved, 16)

    def greet(self, *others):
        barrier = pltpu.get_barrier_semaphore()
        devices = [self.ahead, self.behind, self.partner, self.across, *others]
        for device in devices:
            pl.semaphore_signal(barrier, inc=1, device_id=device, device_id_type=MESH)
        pl.semaphore_wait(barrier, len(devices))

    def part(self, j, k, which, start, size):
        there = lax.rem(self.pair + self.pairs - k, self.pairs)
        index = 2 * there + (self.member if which == 0 else 1 - self.member)
        array, first, width = self.pieces[j]
        rows = pl.ds(pl.multiple_of(index * self.rows + start, 16), size)
        return self.fulls[array].at[rows, pl.ds(first, width)]

    def source(self, j, k, which, start, size):
        if k == 0 and which == 0:
            array, first, width = self.pieces[j]
            return self.weights[array].at[pl.ds(start, size), pl.ds(first, width)]
        return self.part(j, k, which, start, size)

    def ring_copy(self, j, k):
        return pltpu.make_async_remote_copy(
            src_ref=self.source(j, k, 0, self.late_start, self.late),
            dst_ref=self.part(j, k, 0, self.late_start, self.late),
            send_sem=self.ring_send.at[j, k], recv_sem=self.ring_recv.at[j, k],
            device_id=self.ahead, device_id_type=MESH,
        )

    def pair_copy(self, j, k):
        return pltpu.make_async_remote_copy(
            src_ref=self.source(j, k, 0, self.late_start, self.late),
            dst_ref=self.part(j, k, 0, self.late_start, self.late),
            send_sem=self.pair_send.at[j, k], recv_sem=self.pair_recv.at[j, k],
            device_id=self.partner, device_id_type=MESH,
        )

    def early_copy(self, j, k, which):
        own = k == self.pairs - 1
        k = 0 if own else k
        slot = 2 * self.pairs - 2 if own else 2 * k + which
        return pltpu.make_async_remote_copy(
            src_ref=self.source(j, k, which, self.early_start, self.early),
            dst_ref=self.part(j, k, which, self.early_start, self.early),
            send_sem=self.early_send.at[j, slot], recv_sem=self.early_recv.at[j, slot],
            device_id=self.partner if own else self.ahead, device_id_type=MESH,
        )

    def early_event(self, j, k):
        last = self.pairs - 1
        if k == 0:
            self.early_copy(j, last, 0).start()
        else:
            self.early_copy(j, k - 1, 0).wait_recv()
        if k < last:
            self.early_copy(j, k, 0).start()
        if k == 1:
            self.early_copy(j, last, 0).wait_recv()
        elif k > 1:
            self.early_copy(j, k - 2, 1).wait_recv()
        if k > 0:
            self.early_copy(j, k - 1, 1).start()

    def cross_copy(self, j, k, which):
        here = self.part(j, k, which, self.shared_start, self.shared)
        return pltpu.make_async_remote_copy(
            src_ref=here, dst_ref=here,
            send_sem=self.cross_send.at[j, 2 * k + which], recv_sem=self.cross_recv.at[j, 2 * k + which],
            device_id=self.across, device_id_type=MESH,
        )

    def keep_copy(self, j):
        rows = pl.ds(pl.multiple_of(self.own * self.rows, 16), self.rows)
        return pltpu.make_async_copy(self.weights[j], self.fulls[j].at[rows, :], self.local.at[j])

    def event(self, number):
        j, k = self.order[number]
        if k > 0:
            self.ring_copy(j, k - 1).wait_recv()
        if number == 0:
            for array in range(self.arrays):
                self.keep_copy(array).start()
        if k < self.pairs - 1:
            self.ring_copy(j, k).start()
        self.pair_copy(j, k).start()
        if k > 0:
            self.cross_copy(j, k, 0).start()
        if self.early:
            self.early_event(j, k)
        if number >= self.lag:
            self.share(number - self.lag)

    def share(self, number):
        j, k = self.order[number]
        self.pair_copy(j, k).wait_recv()
        self.cross_copy(j, k, 1).start()

    def finish(self):
        for number in range(max(len(self.order) - self.lag, 0), len(self.order)):
            self.share(number)
        crossed = [(j, k, which) for j, k in self.order for which in range(2) if k or which]
        for item in crossed:
            self.cross_copy(*item).wait_recv()
        for j, k in self.order:
            if k < self.pairs - 1:
                self.ring_copy(j, k).wait_send()
            self.pair_copy(j, k).wait_send()
        for item in crossed:
            self.cross_copy(*item).wait_send()
        for j in range(len(self.pieces)):
            if self.early:
                last = self.pairs - 1
                if last:
                    self.early_copy(j, last - 1, 1).wait_recv()
                else:
                    self.early_copy(j, last, 0).wait_recv()
                self.early_copy(j, last, 0).wait_send()
                for k in range(last):
                    for which in range(2):
                        self.early_copy(j, k, which).wait_send()
        for array in range(self.arrays):
            self.keep_copy(array).wait()


def gather_kernel(plan, *refs):
    arrays = plan.arrays
    weights, tokens = refs[:arrays], refs[arrays]
    fulls, far = refs[arrays + 1 : 2 * arrays + 1], refs[2 * arrays + 1]
    extra_send, extra_recv = refs[2 * arrays + 2 : 2 * arrays + 4]
    plan.bind(weights, fulls, refs[2 * arrays + 4 :])
    plan.greet(plan.beside)
    half = tokens.shape[2] // 2
    lanes = pl.ds(pl.multiple_of(plan.side * half, 128), half)

    def token_copy(src, number, device):
        return pltpu.make_async_remote_copy(
            src_ref=src.at[:, :, lanes], dst_ref=far.at[:, :, lanes],
            send_sem=extra_send.at[number], recv_sem=extra_recv.at[number],
            device_id=device, device_id_type=MESH,
        )

    first, second = token_copy(tokens, 0, plan.across), token_copy(far, 1, plan.beside)
    first.start()
    for number in range(len(plan.order)):
        plan.event(number)
        if number == min(5, len(plan.order) - 1):
            first.wait_recv()
            second.start()
    second.wait_recv()
    plan.finish()
    first.wait_send()
    second.wait_send()


def gather_weights(shards, tokens, shared, collective_id):
    rows = shards[0].shape[0]
    pairs = lax.axis_size("fsdp") // 2
    count = len(shards)
    plan = Gathering(rows, pairs, [shard.shape[1] for shard in shards], 2, shared)
    hbm = pl.BlockSpec(memory_space=pl.ANY)
    dma = pltpu.SemaphoreType.DMA
    return pl.pallas_call(
        functools.partial(gather_kernel, plan),
        out_shape=[
            jax.ShapeDtypeStruct((2 * pairs * rows, shard.shape[1]), shard.dtype) for shard in shards
        ]
        + [jax.ShapeDtypeStruct(tokens.shape, tokens.dtype)],
        in_specs=[hbm] * (count + 1),
        out_specs=[hbm] * (count + 1),
        scratch_shapes=[dma((2,)), dma((2,))] + plan.scratch(),
        compiler_params=pltpu.CompilerParams(collective_id=collective_id, has_side_effects=True),
    )(*shards, tokens)


def order_kernel(near_index, far_index, is_near, near, far, gain, x_out, normed_out, scale_out):
    step = pl.program_id(0)
    near_now = is_near[step] == 1
    x = jnp.where(near_now, near[...], far[...])
    x_out[...] = x
    value = x.astype(f32)
    mean = jnp.sum(value * value, axis=-1, keepdims=True) * (1.0 / value.shape[-1])
    scale = lax.rsqrt(mean + epsilon)
    normed_out[...] = (value * scale * gain[...]).astype(bf16)
    scale_out[...] = jnp.broadcast_to(scale, scale_out.shape)


def ordered(near, far, near_index, far_index, is_near, gain):
    micros, count, length, model = near.shape
    blocks = micros * count

    def block(spec_index):
        return pl.BlockSpec((None, None, length, model), spec_index)

    def rows(lanes):
        return pl.BlockSpec((length, lanes), lambda step, *_: (step, 0))

    return pl.pallas_call(
        order_kernel,
        grid_spec=pltpu.PrefetchScalarGridSpec(
            num_scalar_prefetch=3,
            grid=(blocks,),
            in_specs=[
                block(lambda step, near_at, far_at, flags: (step // count, near_at[step], 0, 0)),
                block(lambda step, near_at, far_at, flags: (step // count, far_at[step], 0, 0)),
                pl.BlockSpec((1, model), lambda *_: (0, 0)),
            ],
            out_specs=[rows(model), rows(model), rows(LANES)],
        ),
        out_shape=[
            jax.ShapeDtypeStruct((blocks * length, model), bf16),
            jax.ShapeDtypeStruct((blocks * length, model), bf16),
            jax.ShapeDtypeStruct((blocks * length, LANES), f32),
        ],
        compiler_params=pltpu.CompilerParams(vmem_limit_bytes=32 * 1024 * 1024),
    )(near_index, far_index, is_near, near, far, gain)


def gate_kernel(
    normed, out_grad, gate_weight, out_weight, y_own, carry, coupled, entering, gain,
    mixer_out, gate_out, grad_out, sums_out,
):
    gate_in = mm(normed[...], gate_weight[...])
    grads = mm(out_grad[...], out_weight[...])
    width = entering.shape[0]
    arrived = mm_three(split_two(coupled[:, width:]), split_two(entering[...]))
    mixer = y_own[...] + carry[...] * arrived
    gated = mixer * (gate_in * logistic(gate_in))
    mixer_out[...] = mixer
    gate_out[...] = gate_in
    grad_out[...] = grads
    square = jnp.sum(gated * gated, axis=-1, keepdims=True)
    product = jnp.sum(grads * gain[...] * gated, axis=-1, keepdims=True)
    lane = lax.broadcasted_iota(jnp.int32, sums_out.shape, 1)
    sums_out[...] = jnp.where(lane == 0, square, jnp.where(lane == 1, product, 0.0))


def gate_stage(normed, out_grad, gate_weight, out_weight, y_own, carry, coupled, entering, gain):
    rows, model = normed.shape
    inner = y_own.shape[1]
    twice = coupled.shape[1]
    micros, width, _ = entering.shape
    size = 2 * CHUNK
    per_micro = rows // micros // size

    def block(lanes):
        return pl.BlockSpec((size, lanes), lambda step: (step, 0))

    return pl.pallas_call(
        gate_kernel,
        grid=(rows // size,),
        in_specs=[
            block(model),
            block(model),
            pl.BlockSpec((model, inner), lambda step: (0, 0), pipeline_mode=pl.Buffered(1)),
            pl.BlockSpec((model, inner), lambda step: (0, 0), pipeline_mode=pl.Buffered(1)),
            block(inner),
            block(inner),
            block(twice),
            pl.BlockSpec((None, width, inner), lambda step: (step // per_micro, 0, 0)),
            pl.BlockSpec((1, inner), lambda step: (0, 0)),
        ],
        out_specs=[block(inner), block(inner), block(inner), block(LANES)],
        out_shape=[jax.ShapeDtypeStruct((rows, inner), f32)] * 3
        + [jax.ShapeDtypeStruct((rows, LANES), f32)],
        compiler_params=pltpu.CompilerParams(vmem_limit_bytes=60 * 1024 * 1024),
        cost_estimate=pl.CostEstimate(
            flops=4 * rows * model * inner, bytes_accessed=24 * rows * inner, transcendentals=0
        ),
    )(normed, out_grad, gate_weight, out_weight, y_own, carry, coupled, entering, gain)


def gate_back_kernel(
    inner_total, per_micro, mixer, gate_in, grads, carry, coupled, sums, gain,
    norm_out, gate_out, mixer_out, pull_out, gain_out,
):
    step = pl.program_id(0)
    width = pull_out.shape[0]
    inv_norm = lax.rsqrt(sums[:, 0:1] / inner_total + epsilon)
    inner_dot = sums[:, 1:2] * (inv_norm * inv_norm * inv_norm) / inner_total
    mixer_now, gate_now, grad_now = mixer[...], gate_in[...], grads[...]
    sig = logistic(gate_now)
    act = gate_now * sig
    gated = mixer_now * act
    norm_out[...] = (gated * inv_norm * gain[...]).astype(bf16)
    gated_grad = grad_now * gain[...] * inv_norm - gated * inner_dot
    gate_out[...] = (gated_grad * mixer_now * sig * (1.0 + gate_now * (1.0 - sig))).astype(bf16)
    mixer_grad = gated_grad * act
    mixer_out[...] = mixer_grad

    @pl.when(step == 0)
    def _():
        gain_out[...] = jnp.zeros_like(gain_out)

    gain_out[0:1, :] += jnp.sum(grad_now * gated * inv_norm, axis=0, keepdims=True)

    @pl.when(lax.rem(step, per_micro) == 0)
    def _():
        pull_out[...] = jnp.zeros_like(pull_out)

    turned = split_two(jnp.transpose(coupled[:, width:]))
    pull_out[...] += mm_three(turned, split_two(carry[...] * mixer_grad))


def gate_back_stage(mixer, gate_in, grads, carry, coupled, sums, gain, micros, inner_total):
    rows, inner = mixer.shape
    twice = coupled.shape[1]
    width = twice // 2
    per_micro = rows // micros // CHUNK

    def block(lanes):
        return pl.BlockSpec((CHUNK, lanes), lambda step: (step, 0))

    return pl.pallas_call(
        functools.partial(gate_back_kernel, inner_total, per_micro),
        grid=(rows // CHUNK,),
        in_specs=[
            block(inner),
            block(inner),
            block(inner),
            block(inner),
            block(twice),
            block(LANES),
            pl.BlockSpec((1, inner), lambda step: (0, 0)),
        ],
        out_specs=[
            block(inner),
            block(inner),
            block(inner),
            pl.BlockSpec((None, width, inner), lambda step: (step // per_micro, 0, 0)),
            pl.BlockSpec((8, inner), lambda step: (0, 0)),
        ],
        out_shape=[
            jax.ShapeDtypeStruct((rows, inner), bf16),
            jax.ShapeDtypeStruct((rows, inner), bf16),
            jax.ShapeDtypeStruct((rows, inner), f32),
            jax.ShapeDtypeStruct((micros, width, inner), f32),
            jax.ShapeDtypeStruct((8, inner), f32),
        ],
        compiler_params=pltpu.CompilerParams(vmem_limit_bytes=48 * 1024 * 1024),
        cost_estimate=pl.CostEstimate(
            flops=8 * rows * width * inner, bytes_accessed=24 * rows * inner, transcendentals=0
        ),
    )(mixer, gate_in, grads, carry, coupled, sums, gain)


def weave_kernel(first, second, out):
    out[:, 0, :] = first[...]
    out[:, 1, :] = second[...]


def woven(first, second, columns):
    rows = first.shape[0]
    size = 32
    block = pl.BlockSpec((size, columns), lambda step: (step, 0))
    return pl.pallas_call(
        weave_kernel,
        grid=(rows // size,),
        in_specs=[block, block],
        out_specs=pl.BlockSpec((size, 2, columns), lambda step: (step, 0, 0)),
        out_shape=jax.ShapeDtypeStruct((rows, 2, columns), first.dtype),
    )(first, second)


class Reduction:
    def __init__(self, rows, pairs, columns, lag):
        self.rows, self.pairs, self.columns, self.lag = rows, pairs, columns, lag
        self.shared = rows // 4
        self.moved = rows - self.shared
        self.counts = [count // LANES for count in columns]
        self.count = sum(self.counts)
        self.steps = self.count + 4 * lag

    def scratch(self):
        shared, moved, pairs, count = self.shared, self.moved, self.pairs, self.count
        cross, pair, ring = 2 * pairs * shared + 16, pairs * moved + 16, moved + 16
        i16, dma = jnp.int16, pltpu.SemaphoreType.DMA
        return [
            pltpu.VMEM((count, cross, LANES), i16),
            pltpu.VMEM((count, pair, LANES), i16),
            pltpu.VMEM((count, pairs - 1, ring, LANES), i16),
            pltpu.VMEM((count, ring, LANES), i16),
            pltpu.VMEM((2, cross, LANES), i16),
            pltpu.VMEM((2, pair, LANES), i16),
            pltpu.VMEM((2, pairs - 1, ring, LANES), i16),
            pltpu.VMEM((2, ring, LANES), i16),
            pltpu.VMEM((2, pairs, 2, shared, LANES), f32),
            pltpu.VMEM((2, pairs, moved, LANES), f32),
            pltpu.VMEM((2, pairs, moved, LANES), f32),
            pltpu.VMEM((2 * self.lag, moved, LANES), f32),
            pltpu.VMEM((2 * self.lag, moved, LANES), f32),
            pltpu.VMEM((2, self.rows, LANES), f32),
            dma((count,)),
            dma((count,)),
            dma((pairs - 1, count)),
            dma((count,)),
            dma((2,)),
            dma((2,)),
            dma((pairs - 1, 2)),
            dma((2,)),
            dma((3, 2)),
            dma((2,)),
        ]

    def bind(self, terms, outs, scratch):
        self.terms, self.outs = terms, outs
        (
            self.cross_in, self.pair_in, self.ring_in, self.last_in,
            self.cross_out, self.pair_out, self.ring_out, self.last_out,
            self.cross_term, self.pair_term, self.ring_term,
            self.kept, self.held, self.result,
            self.cross_recv, self.pair_recv, self.ring_recv, self.last_recv,
            self.cross_sent, self.pair_sent, self.ring_sent, self.last_sent,
            self.loaded, self.stored,
        ) = scratch
        self.own, self.place = lax.axis_index("fsdp"), lax.axis_index("context")
        self.side = lax.axis_index("tensor")
        self.pair, self.member = self.own // 2, lax.rem(self.own, 2)
        self.across = (self.own, 1 - self.place, self.side)
        self.partner = (2 * self.pair + 1 - self.member, self.place, self.side)
        self.inset = pl.multiple_of(self.place * (self.moved - self.shared), 16)
        self.start = pl.multiple_of(self.place * self.shared, 16)

    def peer(self, offset):
        there = lax.rem(self.pair + offset, self.pairs)
        return (2 * there + self.member, self.place, self.side)

    def greet(self):
        barrier = pltpu.get_barrier_semaphore()
        devices = [self.across, self.partner] + [self.peer(k) for k in range(1, self.pairs)]
        for device in devices:
            pl.semaphore_signal(barrier, inc=1, device_id=device, device_id_type=MESH)
        pl.semaphore_wait(barrier, len(devices))

    def cross_copy(self, chunk):
        slot = lax.rem(chunk, 2)
        return pltpu.make_async_remote_copy(
            src_ref=self.cross_out.at[slot], dst_ref=self.cross_in.at[chunk],
            send_sem=self.cross_sent.at[slot], recv_sem=self.cross_recv.at[chunk],
            device_id=self.across, device_id_type=MESH,
        )

    def pair_copy(self, chunk):
        slot = lax.rem(chunk, 2)
        return pltpu.make_async_remote_copy(
            src_ref=self.pair_out.at[slot], dst_ref=self.pair_in.at[chunk],
            send_sem=self.pair_sent.at[slot], recv_sem=self.pair_recv.at[chunk],
            device_id=self.partner, device_id_type=MESH,
        )

    def ring_copy(self, chunk, offset):
        slot = lax.rem(chunk, 2)
        return pltpu.make_async_remote_copy(
            src_ref=self.ring_out.at[slot, offset - 1], dst_ref=self.ring_in.at[chunk, offset - 1],
            send_sem=self.ring_sent.at[offset - 1, slot],
            recv_sem=self.ring_recv.at[offset - 1, chunk],
            device_id=self.peer(offset), device_id_type=MESH,
        )

    def last_copy(self, chunk):
        slot = lax.rem(chunk, 2)
        return pltpu.make_async_remote_copy(
            src_ref=self.last_out.at[slot], dst_ref=self.last_in.at[chunk],
            send_sem=self.last_sent.at[slot], recv_sem=self.last_recv.at[chunk],
            device_id=self.across, device_id_type=MESH,
        )

    def load_copy(self, stage, term, cols, slot):
        if stage == 0:
            rows = pl.ds(pl.multiple_of((1 - self.place) * self.moved, 16), self.shared)
            src, dst = term.at[:, :, rows, cols], self.cross_term.at[slot]
        elif stage == 1:
            src = term.at[:, 1 - self.member, pl.ds(self.start, self.moved), cols]
            dst = self.pair_term.at[slot]
        else:
            src = term.at[:, self.member, pl.ds(self.start, self.moved), cols]
            dst = self.ring_term.at[slot]
        return pltpu.make_async_copy(src, dst, self.loaded.at[stage, slot])

    def each_array(self, chunk, act):
        first = 0
        for number, count in enumerate(self.counts):
            inside = (chunk >= first) & (chunk < first + count)
            offset = first

            @pl.when(inside)
            def _(number=number, offset=offset):
                act(number, pl.ds(pl.multiple_of((chunk - offset) * LANES, LANES), LANES))

            first += count

    def load(self, stage, chunk):
        @pl.when((chunk >= 0) & (chunk < self.count))
        def _():
            self.each_array(
                chunk,
                lambda number, cols: self.load_copy(
                    stage, self.terms[number], cols, lax.rem(chunk, 2)
                ).start(),
            )

    def loaded_now(self, stage, chunk):
        self.load_copy(stage, self.terms[0], pl.ds(0, LANES), lax.rem(chunk, 2)).wait()

    @staticmethod
    def encode(value, out, place):
        count = value.shape[0]
        peak = jnp.maximum(jnp.max(jnp.abs(value), axis=0, keepdims=True), 1e-30)
        exponent = jnp.ceil(jnp.log(peak) * 1.4426950408889634)
        factor = jnp.exp(exponent * -0.6931471805599453) * 32000.0
        out[place + (pl.ds(0, count), slice(None))] = (
            (value * factor + 12582912.0 - 12582912.0).astype(jnp.int32).astype(jnp.int16)
        )
        out[place + (pl.ds(count, 16), slice(None))] = (
            jnp.broadcast_to(exponent, (16, LANES)).astype(jnp.int32).astype(jnp.int16)
        )

    @staticmethod
    def unit(ref, place, count):
        exponents = ref[place + (pl.ds(count, 16), slice(None))].astype(jnp.int32).astype(f32)
        return jnp.exp(exponents[:1] * 0.6931471805599453) * (1.0 / 32000.0)

    @staticmethod
    def decode(ref, place, first, count, unit):
        first = pl.multiple_of(first, 16) if not isinstance(first, int) else first
        return ref[place + (pl.ds(first, count), slice(None))].astype(jnp.int32).astype(f32) * unit

    def step(self, number):
        lag, pairs, shared, moved = self.lag, self.pairs, self.shared, self.moved

        @pl.when(number == 0)
        def _():
            self.load(0, number)

        self.load(0, number + 1)
        self.load(1, number + 1 - lag)
        self.load(2, number + 1 - 2 * lag)

        def stage(index, act):
            chunk = number - index * lag

            @pl.when((chunk >= 0) & (chunk < self.count))
            def _():
                act(chunk, lax.rem(chunk, 2))

        def cross(chunk, slot):
            self.loaded_now(0, chunk)

            @pl.when(chunk >= 2)
            def _():
                self.cross_copy(chunk - 2).wait_send()

            value = self.cross_term[slot].reshape(2 * pairs * shared, LANES)
            self.encode(value, self.cross_out, (slot,))
            self.cross_copy(chunk).start()

        def pair(chunk, slot):
            self.loaded_now(1, chunk)
            self.cross_copy(chunk).wait_recv()

            @pl.when(chunk >= 2)
            def _():
                self.pair_copy(chunk - 2).wait_send()

            unit = self.unit(self.cross_in, (chunk,), 2 * pairs * shared)
            for there in range(pairs):
                first = (2 * there + 1 - self.member) * shared
                self.pair_term[slot, there, pl.ds(self.inset, shared), :] += self.decode(
                    self.cross_in, (chunk,), first, shared, unit
                )
            value = self.pair_term[slot].reshape(pairs * moved, LANES)
            self.encode(value, self.pair_out, (slot,))
            self.pair_copy(chunk).start()

        def ring(chunk, slot):
            self.loaded_now(2, chunk)
            self.pair_copy(chunk).wait_recv()

            @pl.when(chunk >= 2)
            def _():
                for offset in range(1, pairs):
                    self.ring_copy(chunk - 2, offset).wait_send()

            cross_unit = self.unit(self.cross_in, (chunk,), 2 * pairs * shared)
            pair_unit = self.unit(self.pair_in, (chunk,), pairs * moved)
            for offset in list(range(1, pairs)) + [0]:
                there = lax.rem(self.pair + offset, pairs)
                first = (2 * there + self.member) * shared
                self.ring_term[slot, there, pl.ds(self.inset, shared), :] += self.decode(
                    self.cross_in, (chunk,), first, shared, cross_unit
                )
                value = self.ring_term[slot, there] + self.decode(
                    self.pair_in, (chunk,), there * moved, moved, pair_unit
                )
                if offset:
                    self.encode(value, self.ring_out, (slot, offset - 1))
                    self.ring_copy(chunk, offset).start()
                else:
                    self.kept[lax.rem(chunk, 2 * lag)] = value

        def last(chunk, slot):
            for offset in range(1, pairs):
                self.ring_copy(chunk, offset).wait_recv()

            @pl.when(chunk >= 2)
            def _():
                self.last_copy(chunk - 2).wait_send()

            total = self.kept[lax.rem(chunk, 2 * lag)]
            for offset in range(1, pairs):
                place = (chunk, offset - 1)
                total = total + self.decode(
                    self.ring_in, place, 0, moved, self.unit(self.ring_in, place, moved)
                )
            self.encode(total, self.last_out, (slot,))
            self.held[lax.rem(chunk, 2 * lag)] = self.decode(
                self.last_out, (slot,), 0, moved, self.unit(self.last_out, (slot,), moved)
            )
            self.last_copy(chunk).start()

        def write_copy(number, cols, slot):
            return pltpu.make_async_copy(
                self.result.at[slot], self.outs[number].at[:, cols], self.stored.at[slot]
            )

        def write(chunk, slot):
            self.last_copy(chunk).wait_recv()

            @pl.when(chunk >= 2)
            def _():
                write_copy(0, pl.ds(0, LANES), slot).wait()

            mine = self.held[lax.rem(chunk, 2 * lag)]
            other = self.decode(
                self.last_in, (chunk,), 0, moved, self.unit(self.last_in, (chunk,), moved)
            )
            low = jnp.where(self.place == 0, mine, other)
            high = jnp.where(self.place == 0, other, mine)
            self.result[slot, pl.ds(0, shared), :] = low[:shared]
            self.result[slot, pl.ds(shared, moved - shared), :] = (
                low[shared:] + high[: moved - shared]
            )
            self.result[slot, pl.ds(moved, shared), :] = high[moved - shared :]
            self.each_array(chunk, lambda which, cols: write_copy(which, cols, slot).start())

        stage(4, write)
        stage(3, last)
        stage(2, ring)
        stage(1, pair)
        stage(0, cross)

        @pl.when(number == self.steps - 1)
        def _():
            for slot in range(2):
                write_copy(0, pl.ds(0, LANES), slot).wait()
                self.cross_copy(jnp.int32(self.count - 2 + slot)).wait_send()
                self.pair_copy(jnp.int32(self.count - 2 + slot)).wait_send()
                self.last_copy(jnp.int32(self.count - 2 + slot)).wait_send()
                for offset in range(1, pairs):
                    self.ring_copy(jnp.int32(self.count - 2 + slot), offset).wait_send()


def finish_kernel(plan, blocks, *refs):
    (
        term, x, cot, scale, keep, branch, branch_other, part, part_other, gain, small,
        out, block_out, input_out, small_out,
        gain_sum, cross_in, pair_out, pair_in, ring_in,
        cross_send, cross_recv, pair_send, pair_recv, ring_send, ring_recv, final_sem,
    ) = refs[:27]
    plan.bind([term], [out], refs[27:])
    step = pl.program_id(0)

    @pl.when(step == 0)
    def _():
        plan.greet()
        gain_sum[...] = jnp.zeros_like(gain_sum)

    @pl.when(step < plan.steps)
    def _():
        plan.step(step)

    @pl.when(step < blocks)
    def _():
        x_float = x[...].astype(f32)
        block_out[...] = (x_float + keep[:, 0:1] * (branch[...] + branch_other[...])).astype(bf16)
        inv_rms = scale[:, 0:1]
        x_hat = x_float * inv_rms
        normed_grad = part[...] + part_other[...]
        hat_grad = normed_grad * gain[...]
        mean = jnp.sum(hat_grad * x_hat, axis=-1, keepdims=True) * (1.0 / x_float.shape[-1])
        input_out[...] = (cot[...].astype(f32) + inv_rms * (hat_grad - x_hat * mean)).astype(bf16)
        gain_sum[0:1, :] += jnp.sum(normed_grad * x_hat, axis=0, keepdims=True)

    rows = small.shape[0]
    lines = gain_sum.shape[1] // LANES

    def cross_copy():
        return pltpu.make_async_remote_copy(
            src_ref=pair_out, dst_ref=cross_in, send_sem=cross_send.at[0], recv_sem=cross_recv.at[0],
            device_id=plan.across, device_id_type=MESH,
        )

    def pair_copy():
        return pltpu.make_async_remote_copy(
            src_ref=pair_out, dst_ref=pair_in, send_sem=pair_send.at[0], recv_sem=pair_recv.at[0],
            device_id=plan.partner, device_id_type=MESH,
        )

    def ring_copy(offset):
        return pltpu.make_async_remote_copy(
            src_ref=ring_in.at[0], dst_ref=ring_in.at[plan.pairs - offset],
            send_sem=ring_send.at[offset - 1], recv_sem=ring_recv.at[offset - 1],
            device_id=plan.peer(offset), device_id_type=MESH,
        )

    @pl.when(step == blocks)
    def _():
        pair_out[pl.ds(0, rows), :] = small[...]
        for line in range(lines):
            pair_out[rows + line : rows + line + 1, :] = gain_sum[
                0:1, line * LANES : (line + 1) * LANES
            ]
        cross_copy().start()

    @pl.when(step == blocks + 2)
    def _():
        cross_copy().wait()
        pair_out[...] += cross_in[...]
        pair_copy().start()

    @pl.when(step == blocks + 4)
    def _():
        pair_copy().wait()
        ring_in[0] = pair_out[...] + pair_in[...]
        for offset in range(1, plan.pairs):
            ring_copy(offset).start()

    @pl.when(step == blocks + 6)
    def _():
        for offset in range(1, plan.pairs):
            ring_copy(offset).wait()
        total = jnp.zeros_like(pair_out)
        for index in range(plan.pairs):
            total = total + ring_in[lax.rem(index + plan.pairs - plan.pair, plan.pairs)]
        pair_in[...] = total
        copy = pltpu.make_async_copy(pair_in, small_out, final_sem.at[0])
        copy.start()
        copy.wait()


def finish(term, x, cot, scale, keep, branch, branch_other, part, part_other, gain, small, collective_id):
    pairs = lax.axis_size("fsdp") // 2
    shard_rows = term.shape[0] // (2 * pairs)
    plan = Reduction(shard_rows, pairs, [term.shape[1]], 2)
    rows, model = x.shape
    size = 64
    blocks = rows // size
    steps = max(plan.steps, blocks + 7)
    total_rows = small.shape[0] + model // LANES
    hbm = pl.BlockSpec(memory_space=pl.ANY)
    dma = pltpu.SemaphoreType.DMA

    def block(lanes):
        return pl.BlockSpec((size, lanes), lambda step: (jnp.minimum(step, blocks - 1), 0))

    def constant(shape):
        return pl.BlockSpec(shape, lambda step: (0, 0))

    return pl.pallas_call(
        functools.partial(finish_kernel, plan, blocks),
        grid=(steps,),
        in_specs=[hbm]
        + [block(lanes) for lanes in (model, model, LANES, LANES, model, model, model, model)]
        + [constant((1, model)), constant(small.shape)],
        out_specs=[hbm, block(model), block(model), hbm],
        out_shape=[
            jax.ShapeDtypeStruct((shard_rows, term.shape[1]), f32),
            jax.ShapeDtypeStruct((rows, model), bf16),
            jax.ShapeDtypeStruct((rows, model), bf16),
            jax.ShapeDtypeStruct((total_rows, LANES), f32),
        ],
        scratch_shapes=[
            pltpu.VMEM((8, model), f32),
            pltpu.VMEM((total_rows, LANES), f32),
            pltpu.VMEM((total_rows, LANES), f32),
            pltpu.VMEM((total_rows, LANES), f32),
            pltpu.VMEM((pairs, total_rows, LANES), f32),
            dma((1,)),
            dma((1,)),
            dma((1,)),
            dma((1,)),
            dma((max(pairs - 1, 1),)),
            dma((max(pairs - 1, 1),)),
            dma((1,)),
        ]
        + plan.scratch(),
        compiler_params=pltpu.CompilerParams(
            collective_id=collective_id, has_side_effects=True, vmem_limit_bytes=56 * 1024 * 1024
        ),
    )(
        term.reshape(pairs, 2, shard_rows, -1), x, cot, scale, keep, branch, branch_other, part,
        part_other, gain, small,
    )


def passed_along(value, axis, steps):
    count = lax.axis_size(axis)
    initial, last = (max(0, -steps), min(count, count - steps))
    return lax.ppermute(value, axis, [(source, source + steps) for source in range(initial, last)])


def paired(value, axis):
    count = lax.axis_size(axis)
    return lax.ppermute(value, axis, [(source, source ^ 1) for source in range(count)])


def ring_shift(value, axis, steps):
    count = lax.axis_size(axis)
    return lax.ppermute(
        value, axis, [(source, (source + 2 * steps) % count) for source in range(count)]
    )


def packed_rows(values):
    flat = jnp.concatenate([value.reshape(-1) for value in values])
    return jnp.pad(flat, (0, -flat.shape[0] % 1024)).reshape(-1, LANES)


def unpacked(flat, values):
    results, start = [], 0
    for value in values:
        results.append(flat[start : start + value.size].reshape(value.shape))
        start += value.size
    return results


def shards(
    tokens,
    lengths,
    block_order,
    cotangent,
    norm_gain,
    in_weight,
    coupling_weight,
    step_weight,
    out_weight,
    conv_weight,
    conv_bias,
    coupling_conv,
    coupling_bias,
    step_bias,
    decay_rate,
    skip_gain,
    inner_gain,
):
    micros = tokens.shape[0]
    count = tokens.shape[2]
    model = tokens.shape[3]
    inner = inner_gain.shape[0]
    heads = step_bias.shape[0]
    head_size = inner // heads
    twice = coupling_weight.shape[1]
    width = twice // 2
    blocks_row = block_order.shape[2]
    block_len = count * lax.axis_size("context") // blocks_row
    own_blocks = count // block_len
    inner_total = inner * lax.axis_size("tensor")
    side = lax.axis_index("tensor")
    place = lax.axis_index("context")
    base = place * count
    shard_rows = in_weight.shape[0]

    narrow, wide_columns = selectors(heads, head_size)
    sel = jnp.asarray(narrow, bf16)
    selcol = jnp.asarray(wide_columns, bf16)
    selt = jnp.asarray(narrow[:heads].T, bf16)
    selt = jnp.pad(selt, ((0, 0), (0, LANES - heads)))

    lead = jnp.concatenate(
        [
            in_weight[:, 1, :],
            coupling_weight,
            jnp.pad(step_weight, ((0, 0), (0, LANES - heads))),
        ],
        axis=1,
    )
    def sharing(parts):
        return max(shard_rows * parts // 16 // 16 * 16, 16)

    lead_full, far = gather_weights([lead], tokens[:, 0], sharing(3), 1)

    near = tokens[:, 0].reshape(micros, own_blocks, block_len, model)
    far = far.reshape(micros, own_blocks, block_len, model)
    slots = jnp.arange(blocks_row, dtype=jnp.int32)
    wanted = place * own_blocks + jnp.arange(own_blocks, dtype=jnp.int32)
    found = block_order[:, 0, None, :] == wanted[None, :, None]
    slot = jnp.sum(jnp.where(found, slots, 0), axis=2).reshape(-1)
    is_near = (slot // own_blocks == place).astype(jnp.int32)
    inside = slot % own_blocks
    x_input, normed, scales = ordered(
        near, far, inside * is_near, inside * (1 - is_near), is_near, norm_gain.reshape(1, model)
    )

    first_end = lengths[:, 0, 0]
    second_end = first_end + lengths[:, 0, 1]
    marks = [
        jnp.stack([first_end[micro], second_end[micro], base]).astype(jnp.int32)
        for micro in range(micros)
    ]
    positions = base + jnp.arange(count, dtype=jnp.int32)
    keep = jnp.concatenate([(positions < second_end[micro]) for micro in range(micros)])
    keep = keep.astype(f32)[:, None]

    cw, cb = conv_weight, conv_bias.reshape(1, inner)
    ccw, ccb = coupling_conv, coupling_bias.reshape(1, twice)
    sbias = jnp.pad(step_bias, (0, LANES - heads)).reshape(1, LANES)
    rate = jnp.pad(decay_rate, (0, LANES - heads)).reshape(1, LANES)
    skip = jnp.dot(
        skip_gain.reshape(1, heads), jnp.asarray(narrow[:heads], f32), precision=lax.Precision.HIGHEST
    )

    raw = jnp.dot(normed, lead_full, preferred_element_type=f32)
    rims = passed_along(
        jnp.stack([raw[(micro + 1) * count - 8 : (micro + 1) * count] for micro in range(micros)]),
        "context",
        1,
    )
    (y_own, states, finals, coupled, carry, reach, entering, gate_full, out_full) = forward_ssd(
        jnp.stack(marks), micros, raw, rims, inner, twice, count,
        cw, cb, ccw, ccb, sbias, rate, skip, sel, selcol,
        [in_weight[:, 0, :], jnp.transpose(out_weight)], sharing(3), 3,
    )
    entering = jnp.where(place == 0, 0.0, entering)
    cot = cotangent[:, 0].reshape(micros * count, model)
    out_grad = cot * keep.astype(bf16)
    gain_row = inner_gain.reshape(1, inner)
    mixer, gate_in, norm_grad, row_sums = gate_stage(
        normed, out_grad, gate_full, out_full, y_own, carry, coupled, entering, gain_row
    )
    row_sums = row_sums + paired(row_sums, "tensor")
    gated_norm, gate_grad, mixer_grad, own_pulls, inner_gain_rows = gate_back_stage(
        mixer, gate_in, norm_grad, carry, coupled, row_sums, gain_row, micros, inner_total
    )
    pulled = passed_along(own_pulls, "context", -1)
    out_term = lax.optimization_barrier(contract_rows(out_grad, gated_norm))
    gate_term = contract_rows(normed, gate_grad)
    branch = contract_cols(gated_norm, out_full)
    gate_part = contract_cols(gate_grad, gate_full)
    branch_other = paired(branch, "tensor")

    (
        lead_grad, tails, rims_grad, coupling_raw_grad, coupling_rims_grad,
        value_sums, coupling_sums, small_sums, skip_sums, out_shard, gate_shard,
    ) = backward_ssd(
        jnp.stack(marks), micros, raw, rims, inner, twice, count, mixer_grad, mixer, states,
        finals, entering, reach, pulled,
        cw, cb, ccw, ccb, sbias, rate, skip, sel, selcol, selt, [out_term, gate_term], [branch, gate_part], 2,
    )
    edges = passed_along(jnp.concatenate([rims_grad, coupling_rims_grad], axis=2), "context", -1)
    coupling_raw_grad = coupling_raw_grad.reshape(micros, count, twice) + jnp.pad(
        edges[:, :, inner:], ((0, 0), (count - 8, 0), (0, 0))
    )
    coupling_raw_grad = coupling_raw_grad + paired(coupling_raw_grad, "tensor")
    lane_ids = jnp.arange(twice, dtype=jnp.int32)
    own_lanes = ((lane_ids // width) == side).astype(bf16)
    coupling_low = (coupling_raw_grad.astype(bf16) * own_lanes).reshape(micros * count, twice)
    lead_grad = lax.dynamic_update_slice(lead_grad, coupling_low, (0, inner))
    tails = (tails + edges[:, :, :inner]).astype(bf16)
    for micro in range(micros):
        lead_grad = lax.dynamic_update_slice(
            lead_grad, tails[micro], ((micro + 1) * count - 8, 0)
        )
    normed_part = gate_part + contract_cols(lead_grad, lead_full)
    skip_sums = skip_sums[0].reshape(heads, head_size).sum(axis=1)
    coupling_sums = coupling_sums + paired(coupling_sums, "tensor")
    small = [value_sums[:5], coupling_sums[:5], small_sums[:2], skip_sums, inner_gain_rows[0]]
    small_rows = packed_rows(small)
    lead_shard, block_out, input_grad, summed = finish(
        contract_rows(normed, lead_grad), x_input, cot, scales,
        jnp.broadcast_to(keep, (micros * count, LANES)), branch, branch_other,
        normed_part, paired(normed_part, "tensor"), norm_gain.reshape(1, model), small_rows, 4,
    )
    flat = summed.reshape(-1)
    value_all, coupling_all, small_all, skip_all, inner_all = unpacked(flat, small)
    norm_all = flat[small_rows.size :]
    coupling_shard = lead_shard[:, inner : inner + twice]
    coupling_shard = coupling_shard + paired(coupling_shard, "tensor")
    return (
        block_out.reshape(micros, 1, count, model),
        input_grad.reshape(micros, 1, count, model),
        norm_all,
        woven(gate_shard, lead_shard, inner),
        coupling_shard,
        lead_shard[:, inner + twice : inner + twice + heads],
        jnp.transpose(out_shard),
        value_all[:4],
        value_all[4],
        coupling_all[:4],
        coupling_all[4],
        small_all[0, :heads],
        small_all[1, :heads],
        skip_all,
        inner_all,
    )


def contract_rows(left, right):
    return lax.dot_general(
        left, right, (((0,), (0,)), ((), ())), preferred_element_type=jnp.float32
    )


def contract_cols(left, right):
    return lax.dot_general(
        left, right, (((1,), (1,)), ((), ())), preferred_element_type=jnp.float32
    )


def solution(mesh):
    return jax.shard_map(
        shards,
        mesh=mesh,
        in_specs=(
            P(None, "fsdp", "context", None),
            P(None, "fsdp", None),
            P(None, "fsdp", None),
            P(None, "fsdp", "context", None),
            P(),
            P("fsdp", None, "tensor"),
            P("fsdp", None),
            P("fsdp", "tensor"),
            P("tensor", "fsdp"),
            P(None, "tensor"),
            P("tensor"),
            P(),
            P(),
            P("tensor"),
            P("tensor"),
            P("tensor"),
            P("tensor"),
        ),
        out_specs=(
            P(None, "fsdp", "context", None),
            P(None, "fsdp", "context", None),
            P(),
            P("fsdp", None, "tensor"),
            P("fsdp", None),
            P("fsdp", "tensor"),
            P("tensor", "fsdp"),
            P(None, "tensor"),
            P("tensor"),
            P(),
            P(),
            P("tensor"),
            P("tensor"),
            P("tensor"),
            P("tensor"),
        ),
        check_vma=False,
    )
```
